32 devices in a mesh: seq: 16 (over z, x, core), head: 2 (over y).
Axes of the slice: x: 2, y: 2, z: 4, core: 2. Of those that a mesh axis runs over, the one named last changes fastest.
Arguments:
- queries: bfloat16 [2048, 2560], P('seq', 'head'), may hold values from -6 to 6
- keys: bfloat16 [2048, 2560], P('seq', 'head'), may hold values from -6 to 6
- values: bfloat16 [2048, 2560], P('seq', 'head'), may hold values from -6 to 6
- grad_out: bfloat16 [2048, 2560], P('seq', 'head'), may hold values from -6 to 6
- cache: bfloat16 [2048, 2560], P('seq', 'head'), may hold values from -6 to 6
- w_kv: bfloat16 [2, 2560, 2560], P(None, 'seq', 'head'), may hold values from -0.125 to 0.125
- doc_ids: int32 [2048], replicated, may hold values from 0 to 15, never falling along the last dimension, each value on 1 to 256 neighbouring positions
- routes: int32 [2048], replicated, may hold values from 0 to 15, as said below
Outputs:
- output: bfloat16 [2048, 2560], P('seq', 'head')
- grad_q: bfloat16 [2048, 2560], P('seq', 'head')
- grad_k: bfloat16 [2048, 2560], P('seq', 'head')
- grad_v: bfloat16 [2048, 2560], P('seq', 'head')
The draws below stay inside these ranges and needn't reach their ends.
Inputs may be any that keep to these rules, and one draw needn't show every extreme that they name: `routes`: each device's aligned block of 128 rows names every destination at most 16 times; in every draw some destination is named exactly 16 times by every block.
All inputs are finite; a program needn't handle non-finite values.
Results may differ from the reference program's by a relative error of at most 0.03.
Values may be sent and summed in bfloat16 or wider, within the bound.
No kernel may reach another device: no remote copies, remote signals or barrier semaphores. Data moves between devices by JAX's collectives and lax.ppermute only.
A program may use at most 128 MiB of HBM per device.

```python
import math
import jax
import jax.numpy as jnp
import numpy as np
from jax import lax

H = 20
HD = 128
CW = 2560
SPAN = 2
S = 128
CACHE_DEV = 128
HF = 2560
TOKENS = 2048
CACHES = 2048
CAP = 16
DOC_MAX = 256
DOCS = 16
N_SEQ = 16


def draw_queries(key, part):
    drawn = jax.random.truncated_normal(jax.random.fold_in(key, 5), -6.0, 6.0, (TOKENS, HF), jnp.float32)
    return drawn.astype(jnp.bfloat16)


def draw_keys(key, part):
    drawn = jax.random.truncated_normal(jax.random.fold_in(key, 6), -6.0, 6.0, (TOKENS, HF), jnp.float32)
    return drawn.astype(jnp.bfloat16)


def draw_routes(key, part):
    hottest = jax.random.randint(jax.random.fold_in(key, 1), (), 0, N_SEQ)
    offsets = jax.random.randint(jax.random.fold_in(key, 2), (N_SEQ, 1), 0, N_SEQ - 1)
    ordinal = jnp.arange(CACHE_DEV, dtype=jnp.int32)[None, :] - CAP
    others = (offsets + jnp.maximum(ordinal, 0)) % (N_SEQ - 1)
    others = others + (others >= hottest).astype(jnp.int32)
    targets = jnp.where(ordinal < 0, hottest, others)
    shuffle_keys = jax.random.split(jax.random.fold_in(key, 3), N_SEQ)
    orders = jax.vmap(lambda one_key: jax.random.permutation(one_key, CACHE_DEV))(shuffle_keys)
    targets = jnp.take_along_axis(targets, orders, axis=1)
    return targets.reshape(-1).astype(jnp.int32)


def block_scale(rng, dims, cuts, least, largest):
    loudness = 1.0
    for position, parts in cuts:
        heights = jax.random.uniform(jax.random.fold_in(jax.random.fold_in(rng, 6), position), (parts,), jnp.float32, least / len(cuts), largest / len(cuts))
        loudness = loudness * jnp.repeat(jnp.exp(heights), dims[position] // parts).reshape((-1,) + (1,) * (len(dims) - 1 - position))
    return loudness


def length_profile(number_of, total, most, slope):
    portions = [(1 << 20) // math.isqrt(rank ** slope) + 1 for rank in range(2, number_of + 1)]
    surplus, counts = total - most - (number_of - 1), [1] * (number_of - 1)
    while surplus > 0:
        movable = [i for i in range(number_of - 1) if counts[i] < most]
        whole, budget = sum([portions[i] for i in movable]), surplus
        for i in movable:
            more = min(most - counts[i], max(1, budget * portions[i] // whole), surplus)
            counts[i] = counts[i] + more
            surplus = surplus - more
    return np.array([most] + counts)


def uneven(stream_key, amount, total, bound, slope):
    if amount == 2:
        one = jax.random.randint(stream_key, (), max(1, total - bound), min(bound, total - 1) + 1)
        return jnp.stack([one, total - one])
    lengths = jnp.asarray(length_profile(amount, total, bound, slope), jnp.int32)
    pairs = (amount - 1) // 2
    donor, receiver = lengths[1:1 + 2 * pairs:2], lengths[2:2 + 2 * pairs:2]
    margin = jnp.minimum(donor - 1, bound - receiver)
    shifted = jax.random.randint(jax.random.fold_in(stream_key, 1), (pairs,), 0, 1 << 20) % (margin + 1)
    lengths = lengths.at[1:1 + 2 * pairs:2].set(donor - shifted).at[2:2 + 2 * pairs:2].set(receiver + shifted)
    return lengths[jax.random.permutation(jax.random.fold_in(stream_key, 2), amount)]


def scatter_about(own_key, dims, width, bound, pieces=(), held_as=jnp.bfloat16):
    gain = block_scale(own_key, dims, pieces, -0.22, 0.18) if pieces else 1.0
    result = jax.random.normal(own_key, dims, jnp.float32) * width * gain
    return jnp.minimum(jnp.maximum(result, -bound), bound).astype(held_as)


def setup_inputs(seed: int = 0) -> dict:
    key_of = jax.random.split(jax.random.key(seed), 9)
    return {
        "queries": draw_queries(jax.random.fold_in(key_of[8], 71), 0),
        "keys": draw_keys(jax.random.fold_in(key_of[8], 71), 0),
        "values": scatter_about(key_of[2], (TOKENS, HF), 1.0, 6.0, ((0, 16), (1, 2))),
        "grad_out": scatter_about(key_of[3], (TOKENS, HF), 1.0, 6.0, ((0, 16), (1, 2))),
        "cache": scatter_about(key_of[4], (CACHES, CW), 1.0, 6.0, ((0, 16), (1, 2))),
        "w_kv": scatter_about(key_of[5], (2, CW, HF), CW ** -0.5, 0.125, ((1, 16), (2, 2))),
        "doc_ids": jnp.searchsorted(jnp.cumsum(uneven(key_of[6], DOCS, TOKENS, DOC_MAX, 0)), jnp.arange(TOKENS), side="right").astype(jnp.int32),
        "routes": draw_routes(jax.random.fold_in(key_of[8], 71), 0),
    }


def attend(queries, key_set, value_set, grad_out, allowed, head_count):
    seg_rows = queries.shape[0]
    key_len = key_set.shape[0]
    head_dim = queries.shape[1] // head_count
    scaling = head_dim ** -0.5
    q_heads = queries.astype(jnp.float32).reshape(seg_rows, head_count, head_dim)
    k_heads = key_set.astype(jnp.float32).reshape(key_len, head_count, head_dim)
    v_heads = value_set.astype(jnp.float32).reshape(key_len, head_count, head_dim)
    g_heads = grad_out.astype(jnp.float32).reshape(seg_rows, head_count, head_dim)
    scores = jnp.einsum("qhd,khd->hqk", q_heads, k_heads) * scaling
    scores = jnp.where(allowed[None], scores, -1e30)
    row_max = jnp.max(scores, axis=-1, keepdims=True)
    weights = jnp.where(allowed[None], jnp.exp(scores - row_max), 0.0)
    prob = weights / jnp.sum(weights, axis=-1, keepdims=True)
    prob_b = lax.optimization_barrier(prob.astype(jnp.bfloat16)).astype(jnp.float32)
    output = jnp.einsum("hqk,khd->qhd", prob_b, v_heads)
    output_b = lax.optimization_barrier(output.astype(jnp.bfloat16))
    output_f = output_b.astype(jnp.float32)
    dprob = jnp.einsum("qhd,khd->hqk", g_heads, v_heads)
    delta = jnp.sum(g_heads * output_f, axis=-1)
    dscore = prob * (dprob - jnp.transpose(delta)[:, :, None]) * scaling
    dscore_b = lax.optimization_barrier(dscore.astype(jnp.bfloat16)).astype(jnp.float32)
    grad_q = jnp.einsum("hqk,khd->qhd", dscore_b, k_heads).astype(jnp.bfloat16)
    grad_k = jnp.einsum("hqk,qhd->khd", dscore_b, q_heads)
    grad_v = jnp.einsum("hqk,qhd->khd", prob_b, g_heads)
    return (output_b.reshape(seg_rows, -1), grad_q.reshape(seg_rows, -1),
            grad_k.reshape(key_len, -1), grad_v.reshape(key_len, -1))


def reference(queries, keys, values, grad_out, cache, w_kv, doc_ids, routes):
    capacity = 2 * CACHE_DEV // N_SEQ
    slot_count = capacity * N_SEQ
    window = (SPAN + 1) * S
    pad_rows = SPAN * S
    features = H * HD

    def project(block):
        proj_k = jnp.dot(block.astype(jnp.float32), w_kv[0].astype(jnp.float32), preferred_element_type=jnp.float32)
        proj_v = jnp.dot(block.astype(jnp.float32), w_kv[1].astype(jnp.float32), preferred_element_type=jnp.float32)
        return jnp.stack([proj_k.astype(jnp.bfloat16), proj_v.astype(jnp.bfloat16)], 1)

    memory = lax.map(project, cache.reshape(N_SEQ, CACHE_DEV, CW)).reshape(N_SEQ * CACHE_DEV, 2, features)
    by_block = routes.reshape(N_SEQ, CACHE_DEV)
    targets = jnp.arange(N_SEQ, dtype=jnp.int32)
    onehot = (by_block[:, :, None] == targets[None, None, :]).astype(jnp.int32)
    ranks = jnp.sum((jnp.cumsum(onehot, axis=1) - onehot) * onehot, axis=2).astype(jnp.int32)
    sources = targets[:, None]
    place = (by_block * slot_count + sources * capacity + ranks).reshape(-1).astype(jnp.int32)
    table = jnp.zeros((N_SEQ * slot_count,), jnp.int32).at[place].set(jnp.arange(N_SEQ * CACHE_DEV, dtype=jnp.int32))
    filled = jnp.zeros((N_SEQ * slot_count,), jnp.bool_).at[place].set(True)
    key_pad = jnp.concatenate([jnp.zeros((pad_rows, features), keys.dtype), keys], 0)
    value_pad = jnp.concatenate([jnp.zeros((pad_rows, features), values.dtype), values], 0)
    id_pad = jnp.concatenate([jnp.full((pad_rows,), -1, jnp.int32), doc_ids.astype(jnp.int32)])

    def one_segment(accum, device):
        picked = lax.dynamic_slice_in_dim(table, device * slot_count, slot_count)
        live = lax.dynamic_slice_in_dim(filled, device * slot_count, slot_count)
        mem_rows = memory[picked]
        start = (device * S).astype(jnp.int32)
        seg_q = lax.dynamic_slice_in_dim(queries, start, S)
        seg_g = lax.dynamic_slice_in_dim(grad_out, start, S)
        win_k = lax.dynamic_slice_in_dim(key_pad, start, window)
        win_v = lax.dynamic_slice_in_dim(value_pad, start, window)
        q_ids = lax.dynamic_slice_in_dim(doc_ids.astype(jnp.int32), start, S)
        k_ids = lax.dynamic_slice_in_dim(id_pad, start, window)
        q_pos = start + jnp.arange(S, dtype=jnp.int32)
        k_pos = start - pad_rows + jnp.arange(window, dtype=jnp.int32)
        allowed_win = (k_pos[None, :] <= q_pos[:, None]) & (k_ids[None, :] == q_ids[:, None])
        allowed = jnp.concatenate([jnp.broadcast_to(live[None, :], (S, slot_count)), allowed_win], 1)
        key_set = jnp.concatenate([mem_rows[:, 0], win_k], 0)
        value_set = jnp.concatenate([mem_rows[:, 1], win_v], 0)
        output, grad_q, grad_k, grad_v = attend(seg_q, key_set, value_set, seg_g, allowed, H)
        update = jnp.stack([grad_k[slot_count:], grad_v[slot_count:]], 1)
        current = lax.dynamic_slice_in_dim(accum, start, window)
        accum = lax.dynamic_update_slice_in_dim(accum, current + update, start, 0)
        return accum, (output, grad_q)

    accum_start = jnp.zeros((pad_rows + TOKENS, 2, features), jnp.float32)
    accum, (outputs, grads) = lax.scan(one_segment, accum_start, jnp.arange(N_SEQ, dtype=jnp.int32))
    grad_kv = accum[pad_rows:]
    return (outputs.reshape(TOKENS, features), grads.reshape(TOKENS, features),
            grad_kv[:, 0].astype(jnp.bfloat16), grad_kv[:, 1].astype(jnp.bfloat16))
```

```python
import jax
import jax.numpy as jnp
from jax import lax
from jax.sharding import Mesh, PartitionSpec as P

HD = 128
SPAN = 2
GROUPS = 4
SEQ = ("z", "p")


def shifted(value, by):
    n_z, n_p = lax.axis_size("z"), lax.axis_size("p")
    length = n_z * n_p
    pairs = [(i, i + by) for i in range(length) if 0 <= i + by < length]
    return lax.ppermute(value, SEQ, pairs)


def attend(queries, key_set, value_set, grad_out, allowed, head_count):
    seg_rows = queries.shape[0]
    key_len = key_set.shape[0]
    head_dim = queries.shape[1] // head_count
    scaling = head_dim ** (-0.5)
    q_heads = queries.reshape(seg_rows, head_count, head_dim)
    k_heads = key_set.reshape(key_len, head_count, head_dim)
    v_heads = value_set.reshape(key_len, head_count, head_dim)
    g_heads = grad_out.reshape(seg_rows, head_count, head_dim)
    scores = (
        jnp.einsum("qhd,khd->hqk", q_heads, k_heads, preferred_element_type=jnp.float32) * scaling
    )
    scores = jnp.where(allowed[None], scores, -1e30)
    row_max = jnp.max(scores, axis=-1, keepdims=True)
    weights = jnp.where(allowed[None], jnp.exp(scores - row_max), 0.0)
    prob = weights / jnp.sum(weights, axis=-1, keepdims=True)
    prob_b = prob.astype(jnp.bfloat16)
    output_b = jnp.einsum(
        "hqk,khd->qhd", prob_b, v_heads, preferred_element_type=jnp.float32
    ).astype(jnp.bfloat16)
    dprob = jnp.einsum("qhd,khd->hqk", g_heads, v_heads, preferred_element_type=jnp.float32)
    delta = jnp.sum(g_heads.astype(jnp.float32) * output_b.astype(jnp.float32), axis=-1)
    dscore_b = (prob * (dprob - jnp.transpose(delta)[:, :, None]) * scaling).astype(jnp.bfloat16)
    grad_q = jnp.einsum(
        "hqk,khd->qhd", dscore_b, k_heads, preferred_element_type=jnp.float32
    ).astype(jnp.bfloat16)
    grad_k = jnp.einsum("hqk,qhd->khd", dscore_b, q_heads, preferred_element_type=jnp.float32)
    grad_v = jnp.einsum("hqk,qhd->khd", prob_b, g_heads, preferred_element_type=jnp.float32)
    return (
        output_b.reshape(seg_rows, -1),
        grad_q.reshape(seg_rows, -1),
        grad_k.reshape(key_len, -1),
        grad_v.reshape(key_len, -1),
    )


def slot_matrix(routes, n_z, n_p, cache_rows, capacity):
    mine = lax.dynamic_index_in_dim(
        routes.reshape(n_z, n_p, cache_rows), lax.axis_index("p"), 1, keepdims=False
    )
    ids = jnp.arange(cache_rows, dtype=jnp.int32)
    same = mine[:, :, None] == mine[:, None, :]
    ranks = jnp.sum((same & (ids[None, :] < ids[:, None])[None]).astype(jnp.int32), axis=2)
    place = mine * capacity + ranks
    slots = jnp.arange(n_z * n_p * capacity, dtype=jnp.int32)
    return (slots[None, :, None] == place[:, None, :]).astype(jnp.bfloat16)


def body(queries, keys, values, grad_out, cache, w_kv, doc_ids, routes):
    n_z, n_p = lax.axis_size("z"), lax.axis_size("p")
    devices = n_z * n_p
    my_index = lax.axis_index(SEQ)
    seg_rows = queries.shape[0]
    features = queries.shape[1]
    head_count = features // HD
    cache_rows = cache.shape[0]
    capacity = 2 * cache_rows // devices
    slot_count = capacity * devices
    pad_rows = SPAN * seg_rows
    window = pad_rows + seg_rows
    w_rows = w_kv.shape[1]
    halves = n_z // 2
    block = features // halves

    blocks = w_kv.reshape(2, w_rows, halves, block).transpose(2, 0, 1, 3)
    blocks = blocks.reshape(n_z, w_rows, block)
    w_z = lax.all_to_all(blocks, "z", split_axis=0, concat_axis=0, tiled=True)
    w_all = lax.all_gather(w_z, "p", axis=1, tiled=True).reshape(n_z * n_p * w_rows, block)
    rows = lax.all_gather(cache, ("head", "z"), axis=0, tiled=True)
    rows = rows.reshape(-1, n_z * cache_rows, cache.shape[1])
    proj = sum(
        jnp.dot(
            rows[i],
            w_all[i * cache.shape[1] : (i + 1) * cache.shape[1]],
            preferred_element_type=jnp.float32,
        )
        for i in range(rows.shape[0])
    ).astype(jnp.bfloat16)
    chosen = slot_matrix(routes, n_z, n_p, cache_rows, capacity)
    slots = jnp.einsum(
        "zsi,zic->zsc",
        chosen,
        proj.reshape(n_z, cache_rows, block),
        preferred_element_type=jnp.float32,
    ).astype(jnp.bfloat16)
    slots = slots.reshape(n_z, devices, capacity, block).transpose(1, 0, 2, 3)
    memory = lax.all_to_all(slots, SEQ, split_axis=0, concat_axis=0, tiled=True)
    memory = memory.reshape(halves, 2, slot_count, block)
    mem_keys = memory[:, 0].transpose(1, 0, 2).reshape(slot_count, features)
    mem_values = memory[:, 1].transpose(1, 0, 2).reshape(slot_count, features)
    incoming = jnp.sum(
        (routes.reshape(n_z, n_p, cache_rows) == my_index).astype(jnp.int32), axis=2
    ).T
    live = jnp.arange(capacity, dtype=jnp.int32)[None, None, :] < incoming[:, :, None]
    live = live.reshape(slot_count)

    current = jnp.stack([keys, values], 0)
    received = [current]
    for cycle_step in range(SPAN):
        current = shifted(current, 1)
        received.append(current)
    window_kv = jnp.concatenate(received[::-1], axis=1)
    start = my_index * seg_rows
    id_pad = jnp.concatenate([jnp.full((pad_rows,), -1, jnp.int32), doc_ids])
    q_ids = lax.dynamic_slice_in_dim(doc_ids, start, seg_rows)
    k_ids = lax.dynamic_slice_in_dim(id_pad, start, window)
    q_pos = start + jnp.arange(seg_rows, dtype=jnp.int32)
    k_pos = start - pad_rows + jnp.arange(window, dtype=jnp.int32)
    allowed_win = (k_pos[None, :] <= q_pos[:, None]) & (k_ids[None, :] == q_ids[:, None])
    allowed = jnp.concatenate(
        [jnp.broadcast_to(live[None, :], (seg_rows, slot_count)), allowed_win], 1
    )
    key_set = jnp.concatenate([mem_keys, window_kv[0]], 0)
    value_set = jnp.concatenate([mem_values, window_kv[1]], 0)
    output, grad_q, grad_k, grad_v = attend(
        queries, key_set, value_set, grad_out, allowed, head_count
    )
    pairs = jnp.stack([grad_k[slot_count:], grad_v[slot_count:]], 0)

    def piece_for(offset):
        lower = (SPAN - offset) * seg_rows
        return pairs[:, lower : lower + seg_rows]

    totals = piece_for(SPAN)
    for offset in range(SPAN - 1, -1, -1):
        totals = shifted(totals.astype(jnp.bfloat16), -1).astype(totals.dtype) + piece_for(offset)
    return (output, grad_q, totals[0].astype(jnp.bfloat16), totals[1].astype(jnp.bfloat16))


def solution(mesh):
    n_seq, n_head = mesh.devices.shape
    grid = Mesh(mesh.devices.reshape(GROUPS, n_seq // GROUPS, n_head), ("z", "p", "head"))
    rows = P(SEQ, "head")
    return jax.shard_map(
        body,
        mesh=grid,
        in_specs=(rows, rows, rows, rows, rows, P(None, SEQ, "head"), P(), P()),
        out_specs=(rows, rows, rows, rows),
        check_vma=False,
    )
```

```python
import functools

import jax
import jax.numpy as jnp
from jax import lax
from jax.experimental import pallas as pl
from jax.experimental.pallas import tpu as pltpu
from jax.sharding import Mesh, PartitionSpec as P

HD = 128
SPAN = 2
GROUPS = 4
SEQ = ("z", "p")
ROW_TILE = 16
VMEM = 48 * 1024 * 1024


def shifted(value, by):
    length = lax.axis_size("z") * lax.axis_size("p")
    pairs = [(i, i + by) for i in range(length) if 0 <= i + by < length]
    return lax.ppermute(value, SEQ, pairs)


def swapped(value, axis, mask):
    return lax.ppermute(value, axis, [(i, i ^ mask) for i in range(lax.axis_size(axis))])


def dot_t(a, b, dims):
    return lax.dot_general(a, b, (dims, ((), ())), preferred_element_type=jnp.float32)


def attend_kernel(
    q_ref, g_ref, k_ref, v_ref, kv1_ref, kv2_ref, mem_ref, bias_ref,
    out_ref, gq_ref, far_ref, near_ref, own_ref,
):
    rows, width = q_ref.shape
    slots = mem_ref.shape[1]
    scaling = HD ** (-0.5)
    bias = bias_ref[...]
    for head in range(width // HD):
        cols = slice(head * HD, (head + 1) * HD)
        qh, gh = q_ref[:, cols], g_ref[:, cols]
        kh = jnp.concatenate(
            [mem_ref[0, :, cols], kv2_ref[0, :, cols], kv1_ref[0, :, cols], k_ref[:, cols]], 0
        )
        vh = jnp.concatenate(
            [mem_ref[1, :, cols], kv2_ref[1, :, cols], kv1_ref[1, :, cols], v_ref[:, cols]], 0
        )
        scores = dot_t(qh, kh, ((1,), (1,))) * scaling + bias
        weights = jnp.exp(scores - jnp.max(scores, axis=-1, keepdims=True))
        prob = weights / jnp.sum(weights, axis=-1, keepdims=True)
        prob_b = prob.astype(jnp.bfloat16)
        out_b = dot_t(prob_b, vh, ((1,), (0,))).astype(jnp.bfloat16)
        out_ref[:, cols] = out_b
        dprob = dot_t(gh, vh, ((1,), (1,)))
        delta = jnp.sum(
            gh.astype(jnp.float32) * out_b.astype(jnp.float32), axis=-1, keepdims=True
        )
        dscore = (prob * (dprob - delta) * scaling).astype(jnp.bfloat16)
        gq_ref[:, cols] = dot_t(dscore, kh, ((1,), (0,))).astype(jnp.bfloat16)
        grad_k = dot_t(dscore[:, slots:], qh, ((0,), (0,)))
        grad_v = dot_t(prob_b[:, slots:], gh, ((0,), (0,)))
        for i, grad in enumerate((grad_k, grad_v)):
            far_ref[i, :, cols] = grad[:rows].astype(jnp.bfloat16)
            near_ref[i, :, cols] = grad[rows : 2 * rows]
            own_ref[i, :, cols] = grad[2 * rows :]


def attend(queries, grad_out, keys, values, kv1, kv2, memory, bias):
    rows, features = queries.shape
    steps = memory.shape[0] // 2
    block = features // steps
    slots = memory.shape[1]
    flat = pl.BlockSpec((rows, block), lambda i: (0, i))
    pair = pl.BlockSpec((2, rows, block), lambda i: (0, 0, i))
    heads = features // HD
    keys_all = slots + 3 * rows
    return pl.pallas_call(
        attend_kernel,
        grid=(steps,),
        in_specs=[
            flat, flat, flat, flat, pair, pair,
            pl.BlockSpec((2, slots, block), lambda i: (i, 0, 0)),
            pl.BlockSpec((rows, keys_all), lambda i: (0, 0)),
        ],
        out_specs=[flat, flat, pair, pair, pair],
        out_shape=[
            jax.ShapeDtypeStruct((rows, features), jnp.bfloat16),
            jax.ShapeDtypeStruct((rows, features), jnp.bfloat16),
            jax.ShapeDtypeStruct((2, rows, features), jnp.bfloat16),
            jax.ShapeDtypeStruct((2, rows, features), jnp.float32),
            jax.ShapeDtypeStruct((2, rows, features), jnp.float32),
        ],
        compiler_params=pltpu.CompilerParams(vmem_limit_bytes=VMEM),
        cost_estimate=pl.CostEstimate(
            flops=2 * 5 * rows * keys_all * HD * heads,
            bytes_accessed=8 * 1024 * 1024,
            transcendentals=rows * keys_all * heads,
        ),
        name="attend",
    )(queries, grad_out, keys, values, kv1, kv2, memory, bias)


def project_kernel(order_ref, rows_ref, place_ref, *refs):
    pieces, (out_ref, w_ref, a_ref, sems) = refs[:-4], refs[-4:]
    halves, n_z, cache_rows, depth = a_ref.shape
    n_p, w_rows, block = len(pieces), w_ref.shape[2], w_ref.shape[3]
    devices, _, capacity, _ = out_ref.shape
    copies = [pltpu.make_async_copy(rows_ref, a_ref, sems.at[n_p * n_z])]
    for m in range(n_p):
        for k in range(n_z):
            copies.append(
                pltpu.make_async_copy(
                    pieces[m].at[k],
                    w_ref.at[order_ref[k], order_ref[n_z + m]],
                    sems.at[m * n_z + k],
                )
            )
    for copy in copies:
        copy.start()
    for copy in copies:
        copy.wait()
    per_half = n_z // halves
    total = None
    for half in range(halves):
        a = a_ref[half].reshape(n_z * cache_rows, depth)
        w = w_ref[half * per_half : (half + 1) * per_half].reshape(depth, block)
        part = jnp.dot(a, w, preferred_element_type=jnp.float32)
        total = part if total is None else total + part
    proj = total.astype(jnp.bfloat16)
    slot_ids = lax.broadcasted_iota(jnp.int32, (devices * capacity, cache_rows), 0)
    for z in range(n_z):
        chosen = jnp.where(slot_ids == place_ref[z], 1.0, 0.0).astype(jnp.bfloat16)
        slots = jnp.dot(
            chosen,
            proj[z * cache_rows : (z + 1) * cache_rows],
            preferred_element_type=jnp.float32,
        ).astype(jnp.bfloat16)
        out_ref[:, z] = slots.reshape(devices, capacity, block)


def project(order, rows, place, pieces, devices, capacity):
    halves, n_z, cache_rows, depth = rows.shape
    n_p = len(pieces)
    _, w_rows, block = pieces[0].shape
    whole = pl.BlockSpec(memory_space=pl.ANY)
    return pl.pallas_call(
        project_kernel,
        in_specs=[
            pl.BlockSpec(memory_space=pltpu.SMEM),
            whole,
            pl.BlockSpec(memory_space=pltpu.VMEM),
            *([whole] * n_p),
        ],
        out_specs=pl.BlockSpec(memory_space=pltpu.VMEM),
        out_shape=jax.ShapeDtypeStruct((devices, n_z, capacity, block), jnp.bfloat16),
        scratch_shapes=[
            pltpu.VMEM((n_z, n_p, w_rows, block), jnp.bfloat16),
            pltpu.VMEM((halves, n_z, cache_rows, depth), jnp.bfloat16),
            pltpu.SemaphoreType.DMA((n_p * n_z + 1,)),
        ],
        compiler_params=pltpu.CompilerParams(vmem_limit_bytes=VMEM),
        cost_estimate=pl.CostEstimate(
            flops=2 * n_z * cache_rows * halves * depth * block,
            bytes_accessed=8 * 1024 * 1024,
            transcendentals=0,
        ),
        name="project",
    )(order, rows, place, *pieces)


def slot_places(routes, n_z, n_p, cache_rows, capacity):
    mine = lax.dynamic_index_in_dim(
        routes.reshape(n_z, n_p, cache_rows), lax.axis_index("p"), 1, keepdims=False
    )
    ids = jnp.arange(cache_rows, dtype=jnp.int32)
    same = mine[:, :, None] == mine[:, None, :]
    ranks = jnp.sum((same & (ids[None, :] < ids[:, None])[None]).astype(jnp.int32), axis=2)
    return mine * capacity + ranks


def memory_slots(cache, w_kv, place, capacity):
    n_z, n_p = lax.axis_size("z"), lax.axis_size("p")
    devices = n_z * n_p
    cache_rows = cache.shape[0]
    _, w_rows, features = w_kv.shape
    halves = n_z // 2
    block = features // halves
    rows = lax.all_gather(cache, ("head", "z"), axis=0, tiled=False)
    rows = rows.reshape(-1, n_z, cache_rows, cache.shape[1])
    z, p = lax.axis_index("z"), lax.axis_index("p")
    if n_p == 4 and capacity % ROW_TILE == 0 and w_rows % ROW_TILE == 0:

        def block_for(target):
            start = ((target % 2), 0, (target // 2) * block)
            return lax.dynamic_slice(w_kv, start, (1, w_rows, block))[0]

        arrived = [block_for(z)]
        for mask in range(1, n_z):
            arrived.append(swapped(block_for(z ^ mask), "z", mask))
        own = jnp.stack(arrived, 0)
        across = swapped(own, "p", 2)
        pieces = [own, swapped(own, "p", 1), across, swapped(across, "p", 1)]
        order = jnp.concatenate([z ^ jnp.arange(n_z), p ^ jnp.arange(n_p)]).astype(jnp.int32)
        return project(order, rows, place.reshape(n_z, 1, cache_rows), pieces, devices, capacity)
    blocks = w_kv.reshape(2, w_rows, halves, block).transpose(2, 0, 1, 3)
    w_z = lax.all_to_all(
        blocks.reshape(n_z, w_rows, block), "z", split_axis=0, concat_axis=0, tiled=True
    )
    w_all = lax.all_gather(w_z, "p", axis=1, tiled=True).reshape(devices * w_rows, block)
    rows = rows.reshape(-1, n_z * cache_rows, cache.shape[1])
    proj = sum(
        jnp.dot(
            rows[i],
            w_all[i * cache.shape[1] : (i + 1) * cache.shape[1]],
            preferred_element_type=jnp.float32,
        )
        for i in range(rows.shape[0])
    ).astype(jnp.bfloat16)
    slot_ids = jnp.arange(devices * capacity, dtype=jnp.int32)
    chosen = (slot_ids[None, :, None] == place[:, None, :]).astype(jnp.bfloat16)
    slots = jnp.einsum(
        "zsi,zic->zsc",
        chosen,
        proj.reshape(n_z, cache_rows, block),
        preferred_element_type=jnp.float32,
    ).astype(jnp.bfloat16)
    return slots.reshape(n_z, devices, capacity, block).transpose(1, 0, 2, 3)


def body(queries, keys, values, grad_out, cache, w_kv, doc_ids, routes):
    n_z, n_p = lax.axis_size("z"), lax.axis_size("p")
    devices = n_z * n_p
    my_index = lax.axis_index(SEQ)
    seg_rows = queries.shape[0]
    cache_rows = cache.shape[0]
    capacity = 2 * cache_rows // devices
    slot_count = capacity * devices
    pad_rows = SPAN * seg_rows
    window = pad_rows + seg_rows

    place = slot_places(routes, n_z, n_p, cache_rows, capacity)
    slots = memory_slots(cache, w_kv, place, capacity)
    kv1 = shifted(jnp.stack([keys, values], 0), 1)
    kv2 = shifted(kv1, 1)
    memory = lax.all_to_all(slots, SEQ, split_axis=0, concat_axis=0, tiled=True)
    memory = memory.reshape(n_z, slot_count, slots.shape[-1])

    incoming = jnp.sum(
        (routes.reshape(n_z, n_p, cache_rows) == my_index).astype(jnp.int32), axis=2
    ).T
    live = jnp.arange(capacity, dtype=jnp.int32)[None, None, :] < incoming[:, :, None]
    live = live.reshape(slot_count)
    start = my_index * seg_rows
    id_pad = jnp.concatenate([jnp.full((pad_rows,), -1, jnp.int32), doc_ids])
    q_ids = lax.dynamic_slice_in_dim(doc_ids, start, seg_rows)
    k_ids = lax.dynamic_slice_in_dim(id_pad, start, window)
    q_pos = start + jnp.arange(seg_rows, dtype=jnp.int32)
    k_pos = start - pad_rows + jnp.arange(window, dtype=jnp.int32)
    allowed_win = (k_pos[None, :] <= q_pos[:, None]) & (k_ids[None, :] == q_ids[:, None])
    allowed = jnp.concatenate(
        [jnp.broadcast_to(live[None, :], (seg_rows, slot_count)), allowed_win], 1
    )
    bias = jnp.where(allowed, 0.0, -1e30).astype(jnp.float32)

    output, grad_q, far, near, own = attend(
        queries, grad_out, keys, values, kv1, kv2, memory, bias
    )
    near = shifted(far, -1).astype(jnp.float32) + near
    own = shifted(near.astype(jnp.bfloat16), -1).astype(jnp.float32) + own
    return (output, grad_q, own[0].astype(jnp.bfloat16), own[1].astype(jnp.bfloat16))


def solution(mesh):
    n_seq, n_head = mesh.devices.shape
    grid = Mesh(mesh.devices.reshape(GROUPS, n_seq // GROUPS, n_head), ("z", "p", "head"))
    rows = P(SEQ, "head")
    return jax.shard_map(
        body,
        mesh=grid,
        in_specs=(rows, rows, rows, rows, rows, P(None, SEQ, "head"), P(), P()),
        out_specs=(rows, rows, rows, rows),
        check_vma=False,
    )
```

```python
import functools

import jax
import jax.numpy as jnp
from jax import lax
from jax.experimental import pallas as pl
from jax.experimental.pallas import tpu as pltpu
from jax.sharding import Mesh, PartitionSpec as P

HD = 128
SPAN = 2
GROUPS = 4
SEQ = ("z", "p")
ROW_TILE = 16
RING = [0, 1, 3, 2]
VMEM = 48 * 1024 * 1024


def shifted(value, by):
    length = lax.axis_size("z") * lax.axis_size("p")
    pairs = [(i, i + by) for i in range(length) if 0 <= i + by < length]
    return lax.ppermute(value, SEQ, pairs)


def swapped(value, axis, mask):
    return lax.ppermute(value, axis, [(i, i ^ mask) for i in range(lax.axis_size(axis))])


def dot_t(a, b, dims):
    return lax.dot_general(a, b, (dims, ((), ())), preferred_element_type=jnp.float32)


def attend_kernel(
    q_ref, g_ref, k_ref, v_ref, kv1_ref, kv2_ref, mem_ref, bias_ref, *refs
):
    out_ref, gq_ref, far_ref, near_ref, own_ref = refs[-5:]
    rows, width = q_ref.shape
    slots = mem_ref.shape[1]
    scaling = HD ** (-0.5)
    bias = bias_ref[...]
    for head in range(width // HD):
        cols = slice(head * HD, (head + 1) * HD)
        qh, gh = q_ref[:, cols], g_ref[:, cols]
        kh = jnp.concatenate(
            [mem_ref[0, :, cols], kv2_ref[0, :, cols], kv1_ref[0, :, cols], k_ref[:, cols]], 0
        )
        vh = jnp.concatenate(
            [mem_ref[1, :, cols], kv2_ref[1, :, cols], kv1_ref[1, :, cols], v_ref[:, cols]], 0
        )
        scores = dot_t(qh, kh, ((1,), (1,))) + bias
        weights = jnp.exp((scores - jnp.max(scores, axis=-1, keepdims=True)) * scaling)
        prob = weights * (1.0 / jnp.sum(weights, axis=-1, keepdims=True))
        prob_b = prob.astype(jnp.bfloat16)
        out_b = dot_t(prob_b, vh, ((1,), (0,))).astype(jnp.bfloat16)
        out_ref[:, cols] = out_b
        dprob = dot_t(gh, vh, ((1,), (1,)))
        delta = jnp.sum(
            gh.astype(jnp.float32) * out_b.astype(jnp.float32), axis=-1, keepdims=True
        )
        dscore = (prob * (dprob - delta) * scaling).astype(jnp.bfloat16)
        gq_ref[:, cols] = dot_t(dscore, kh, ((1,), (0,))).astype(jnp.bfloat16)
        grad_k = dot_t(dscore[:, slots:], qh, ((0,), (0,)))
        grad_v = dot_t(prob_b[:, slots:], gh, ((0,), (0,)))
        for i, grad in enumerate((grad_k, grad_v)):
            far_ref[i, :, cols] = grad[:rows].astype(jnp.bfloat16)
            near_ref[i, :, cols] = grad[rows : 2 * rows]
            own_ref[i, :, cols] = grad[2 * rows :]


def attend(first, queries, grad_out, keys, values, kv1, kv2, memory, bias, earlier):
    rows, features = queries.shape
    steps = memory.shape[0] // 2
    slots, block = memory.shape[1:]
    heads = steps * block // HD
    offset = first // block
    flat = pl.BlockSpec((rows, block), lambda i: (0, i + offset))
    pair = pl.BlockSpec((2, rows, block), lambda i: (0, 0, i + offset))
    grad = pl.BlockSpec((2, rows, block), lambda i: (0, 0, i))
    whole = pl.BlockSpec(memory_space=pl.ANY)
    keys_all = slots + 3 * rows
    return pl.pallas_call(
        attend_kernel,
        grid=(steps,),
        in_specs=[
            flat, flat, flat, flat, pair, pair,
            pl.BlockSpec((2, slots, block), lambda i: (i, 0, 0)),
            pl.BlockSpec((rows, keys_all), lambda i: (0, 0)),
            *([whole] * len(earlier)),
        ],
        out_specs=[flat, flat, grad, grad, grad],
        out_shape=[
            jax.ShapeDtypeStruct((rows, features), jnp.bfloat16),
            jax.ShapeDtypeStruct((rows, features), jnp.bfloat16),
            jax.ShapeDtypeStruct((2, rows, steps * block), jnp.bfloat16),
            jax.ShapeDtypeStruct((2, rows, steps * block), jnp.float32),
            jax.ShapeDtypeStruct((2, rows, steps * block), jnp.float32),
        ],
        input_output_aliases={8 + i: i for i in range(len(earlier))},
        compiler_params=pltpu.CompilerParams(vmem_limit_bytes=VMEM),
        cost_estimate=pl.CostEstimate(
            flops=2 * 5 * rows * keys_all * HD * heads,
            bytes_accessed=8 * 1024 * 1024,
            transcendentals=rows * keys_all * heads,
        ),
        name="attend",
    )(queries, grad_out, keys, values, kv1, kv2, memory, bias, *earlier)


def project_kernel(first, order_ref, place_ref, *refs):
    n_z = place_ref.shape[0]
    out_ref, w_ref, a_ref, sems = refs[-4:]
    rows = refs[: 2 * n_z]
    pieces = refs[2 * n_z : -4]
    n_p, w_rows, block = len(pieces), w_ref.shape[2], w_ref.shape[3]
    depth = rows[0].shape[1]
    cache_rows = place_ref.shape[2]
    devices, _, capacity, _ = out_ref.shape
    copies = []
    for i, ref in enumerate(rows):
        start = pl.multiple_of(order_ref[n_z + n_p + i // n_z] * depth, HD)
        to = a_ref.at[order_ref[n_z + n_p + 2 + i % n_z], :, pl.ds(start, depth)]
        copies.append(pltpu.make_async_copy(ref, to, sems.at[len(copies)]))
    for m in range(n_p):
        for k in range(n_z):
            copies.append(
                pltpu.make_async_copy(
                    pieces[m].at[k, :, pl.ds(first, block)],
                    w_ref.at[order_ref[k], order_ref[n_z + m]],
                    sems.at[len(copies)],
                )
            )
    for copy in copies:
        copy.start()
    for copy in copies:
        copy.wait()
    a = a_ref[...].reshape(n_z * cache_rows, 2 * depth)
    w = w_ref[...].reshape(2 * depth, block)
    proj = jnp.dot(a, w, preferred_element_type=jnp.float32).astype(jnp.bfloat16)
    slot_ids = lax.broadcasted_iota(jnp.int32, (devices * capacity, cache_rows), 0)
    for z in range(n_z):
        chosen = jnp.where(slot_ids == place_ref[z], 1.0, 0.0).astype(jnp.bfloat16)
        slots = jnp.dot(
            chosen,
            proj[z * cache_rows : (z + 1) * cache_rows],
            preferred_element_type=jnp.float32,
        ).astype(jnp.bfloat16)
        out_ref[:, z] = slots.reshape(devices, capacity, block)


def project(first, block, order, place, rows, pieces, devices, capacity):
    n_z, _, cache_rows = place.shape
    depth = rows[0].shape[1]
    n_p = len(pieces)
    w_rows = pieces[0].shape[1]
    whole = pl.BlockSpec(memory_space=pl.ANY)
    return pl.pallas_call(
        functools.partial(project_kernel, first),
        in_specs=[
            pl.BlockSpec(memory_space=pltpu.SMEM),
            pl.BlockSpec(memory_space=pltpu.VMEM),
            *([whole] * (len(rows) + n_p)),
        ],
        out_specs=pl.BlockSpec(memory_space=pltpu.VMEM),
        out_shape=jax.ShapeDtypeStruct((devices, n_z, capacity, block), jnp.bfloat16),
        scratch_shapes=[
            pltpu.VMEM((n_z, n_p, w_rows, block), jnp.bfloat16),
            pltpu.VMEM((n_z, cache_rows, 2 * depth), jnp.bfloat16),
            pltpu.SemaphoreType.DMA((n_p * n_z + len(rows),)),
        ],
        compiler_params=pltpu.CompilerParams(vmem_limit_bytes=VMEM),
        cost_estimate=pl.CostEstimate(
            flops=4 * n_z * cache_rows * depth * block,
            bytes_accessed=8 * 1024 * 1024,
            transcendentals=0,
        ),
        name="project",
    )(order, place, *rows, *pieces)


def slot_places(routes, n_z, n_p, cache_rows, capacity):
    mine = lax.dynamic_index_in_dim(
        routes.reshape(n_z, n_p, cache_rows), lax.axis_index("p"), 1, keepdims=False
    )
    ids = jnp.arange(cache_rows, dtype=jnp.int32)
    same = mine[:, :, None] == mine[:, None, :]
    ranks = jnp.sum((same & (ids[None, :] < ids[:, None])[None]).astype(jnp.int32), axis=2)
    return mine * capacity + ranks


def widths(features):
    heads = features // HD // 2
    first = (heads + 1) // 2
    return (first * HD, (heads - first) * HD)


def column_block(w_kv, target):
    parts, offset = [], 0
    for width in widths(w_kv.shape[2]):
        start = (target % 2, 0, offset + (target // 2) * width)
        parts.append(lax.dynamic_slice(w_kv, start, (1, w_kv.shape[1], width))[0])
        offset += 2 * width
    return jnp.concatenate(parts, 1)


def ring_step(value):
    return lax.ppermute(value, "z", [(a, b) for a, b in zip(RING, RING[1:] + RING[:1])])


def memory_slots(cache, w_kv, place, capacity, early):
    n_z, n_p = lax.axis_size("z"), lax.axis_size("p")
    devices = n_z * n_p
    cache_rows, depth = cache.shape
    _, w_rows, features = w_kv.shape
    z, p, y = lax.axis_index("z"), lax.axis_index("p"), lax.axis_index("head")
    chunks = widths(features)
    if n_p == 4 and capacity % ROW_TILE == 0 and w_rows % ROW_TILE == 0:
        arrived = [column_block(w_kv, z)]
        for mask in range(1, n_z):
            arrived.append(swapped(column_block(w_kv, z ^ mask), "z", mask))
        own = jnp.stack(arrived, 0)
        across = swapped(own, "p", 2)
        pieces = [own, swapped(own, "p", 1), across, swapped(across, "p", 1)]
        rows = [cache]
        for _ in range(1, n_z):
            rows.append(ring_step(rows[-1]))
        rows = rows + [swapped(row, "head", 1) for row in rows]
        sources = jnp.asarray(
            [[RING[(RING.index(i) - r) % n_z] for r in range(n_z)] for i in range(n_z)], jnp.int32
        )
        order = jnp.concatenate(
            [z ^ jnp.arange(n_z), p ^ jnp.arange(n_p), jnp.stack([y, 1 - y]), sources[z]]
        ).astype(jnp.int32)
        place, early = lax.optimization_barrier((place, early))
        place = place.reshape(n_z, 1, cache_rows)
        slots, first = [], 0
        for width in chunks:
            slots.append(project(first, width, order, place, rows, pieces, devices, capacity))
            first += width
        return slots, early
    targets = [column_block(w_kv, jnp.int32(i)) for i in range(n_z)]
    w_z = lax.all_to_all(jnp.stack(targets, 0), "z", split_axis=0, concat_axis=0, tiled=True)
    w_all = lax.all_gather(w_z, "p", axis=1, tiled=True).reshape(devices * w_rows, -1)
    rows = lax.all_gather(cache, ("head", "z"), axis=0, tiled=False)
    rows = rows.reshape(-1, n_z * cache_rows, depth)
    proj = sum(
        jnp.dot(
            rows[i], w_all[i * depth : (i + 1) * depth], preferred_element_type=jnp.float32
        )
        for i in range(rows.shape[0])
    ).astype(jnp.bfloat16)
    slot_ids = jnp.arange(devices * capacity, dtype=jnp.int32)
    chosen = (slot_ids[None, :, None] == place[:, None, :]).astype(jnp.bfloat16)
    slots = jnp.einsum(
        "zsi,zic->zsc",
        chosen,
        proj.reshape(n_z, cache_rows, -1),
        preferred_element_type=jnp.float32,
    ).astype(jnp.bfloat16)
    slots = slots.reshape(n_z, devices, capacity, -1).transpose(1, 0, 2, 3)
    return [slots[..., : chunks[0]], slots[..., chunks[0] :]], early


def body(queries, keys, values, grad_out, cache, w_kv, doc_ids, routes):
    n_z, n_p = lax.axis_size("z"), lax.axis_size("p")
    devices = n_z * n_p
    my_index = lax.axis_index(SEQ)
    seg_rows = queries.shape[0]
    cache_rows = cache.shape[0]
    capacity = 2 * cache_rows // devices
    slot_count = capacity * devices
    pad_rows = SPAN * seg_rows
    window = pad_rows + seg_rows

    place = slot_places(routes, n_z, n_p, cache_rows, capacity)
    kv1 = shifted(jnp.stack([keys, values], 0), 1)
    kv2 = shifted(kv1, 1)
    slots, (kv1, kv2) = memory_slots(cache, w_kv, place, capacity, (kv1, kv2))
    memory = [
        lax.all_to_all(part, SEQ, split_axis=0, concat_axis=0, tiled=True).reshape(
            n_z, slot_count, part.shape[-1]
        )
        for part in slots
    ]

    incoming = jnp.sum(
        (routes.reshape(n_z, n_p, cache_rows) == my_index).astype(jnp.int32), axis=2
    ).T
    live = jnp.arange(capacity, dtype=jnp.int32)[None, None, :] < incoming[:, :, None]
    live = live.reshape(slot_count)
    start = my_index * seg_rows
    id_pad = jnp.concatenate([jnp.full((pad_rows,), -1, jnp.int32), doc_ids])
    q_ids = lax.dynamic_slice_in_dim(doc_ids, start, seg_rows)
    k_ids = lax.dynamic_slice_in_dim(id_pad, start, window)
    q_pos = start + jnp.arange(seg_rows, dtype=jnp.int32)
    k_pos = start - pad_rows + jnp.arange(window, dtype=jnp.int32)
    allowed_win = (k_pos[None, :] <= q_pos[:, None]) & (k_ids[None, :] == q_ids[:, None])
    allowed = jnp.concatenate(
        [jnp.broadcast_to(live[None, :], (seg_rows, slot_count)), allowed_win], 1
    )
    bias = jnp.where(allowed, 0.0, -1e30).astype(jnp.float32)

    first, earlier, grads = 0, [], []
    for part in memory:
        output, grad_q, far, near, own = attend(
            first, queries, grad_out, keys, values, kv1, kv2, part, bias, earlier
        )
        earlier = [output, grad_q]
        first += 2 * part.shape[-1]
        near = shifted(far, -1).astype(jnp.float32) + near
        own = shifted(near.astype(jnp.bfloat16), -1).astype(jnp.float32) + own
        grads.append(own.astype(jnp.bfloat16))
    grad_k, grad_v = (jnp.concatenate([part[i] for part in grads], 1) for i in range(2))
    return (output, grad_q, grad_k, grad_v)


def solution(mesh):
    n_seq, n_head = mesh.devices.shape
    grid = Mesh(mesh.devices.reshape(GROUPS, n_seq // GROUPS, n_head), ("z", "p", "head"))
    rows = P(SEQ, "head")
    return jax.shard_map(
        body,
        mesh=grid,
        in_specs=(rows, rows, rows, rows, rows, P(None, SEQ, "head"), P(), P()),
        out_specs=(rows, rows, rows, rows),
        check_vma=False,
    )
```

```python
import functools

import jax
import jax.numpy as jnp
from jax import lax
from jax.experimental import pallas as pl
from jax.experimental.pallas import tpu as pltpu
from jax.sharding import Mesh, PartitionSpec as P

HD = 128
SPAN = 2
GROUPS = 4
SEQ = ("z", "p")
ROW_TILE = 16
RING = [0, 1, 3, 2]
VMEM = 60 * 1024 * 1024


def shifted(value, by):
    length = lax.axis_size("z") * lax.axis_size("p")
    pairs = [(i, i + by) for i in range(length) if 0 <= i + by < length]
    return lax.ppermute(value, SEQ, pairs)


def swapped(value, axis, mask):
    return lax.ppermute(value, axis, [(i, i ^ mask) for i in range(lax.axis_size(axis))])


def dot_t(a, b, dims):
    return lax.dot_general(a, b, (dims, ((), ())), preferred_element_type=jnp.float32)


def attend_kernel(
    q_ref, g_ref, k_ref, v_ref, kv1_ref, kv2_ref, mem_ref, bias_ref, *refs
):
    out_ref, gq_ref, far_ref, near_ref, own_ref = refs[-5:]
    rows, width = q_ref.shape
    slots = mem_ref.shape[1]
    scaling = HD ** (-0.5)
    bias = bias_ref[...]
    heads = [slice(i * HD, (i + 1) * HD) for i in range(width // HD)]
    ks = [
        jnp.concatenate(
            [mem_ref[0, :, cols], kv2_ref[0, :, cols], kv1_ref[0, :, cols], k_ref[:, cols]], 0
        )
        for cols in heads
    ]
    vs = [
        jnp.concatenate(
            [mem_ref[1, :, cols], kv2_ref[1, :, cols], kv1_ref[1, :, cols], v_ref[:, cols]], 0
        )
        for cols in heads
    ]
    scores = [dot_t(q_ref[:, cols], kh, ((1,), (1,))) + bias for cols, kh in zip(heads, ks)]
    dprobs = [dot_t(g_ref[:, cols], vh, ((1,), (1,))) for cols, vh in zip(heads, vs)]
    probs = []
    for score in scores:
        weights = jnp.exp((score - jnp.max(score, axis=-1, keepdims=True)) * scaling)
        probs.append(weights * (1.0 / jnp.sum(weights, axis=-1, keepdims=True)))
    probs_b = [prob.astype(jnp.bfloat16) for prob in probs]
    outs = [
        dot_t(prob_b, vh, ((1,), (0,))).astype(jnp.bfloat16) for prob_b, vh in zip(probs_b, vs)
    ]
    dscores = []
    for cols, out_b, prob, dprob in zip(heads, outs, probs, dprobs):
        out_ref[:, cols] = out_b
        delta = jnp.sum(
            g_ref[:, cols].astype(jnp.float32) * out_b.astype(jnp.float32), axis=-1, keepdims=True
        )
        dscores.append((prob * ((dprob - delta) * scaling)).astype(jnp.bfloat16))
    for cols, kh, dscore, prob_b in zip(heads, ks, dscores, probs_b):
        gq_ref[:, cols] = dot_t(dscore, kh, ((1,), (0,))).astype(jnp.bfloat16)
        grad_k = dot_t(dscore[:, slots:], q_ref[:, cols], ((0,), (0,)))
        grad_v = dot_t(prob_b[:, slots:], g_ref[:, cols], ((0,), (0,)))
        for i, grad in enumerate((grad_k, grad_v)):
            far_ref[i, :, cols] = grad[:rows].astype(jnp.bfloat16)
            near_ref[i, :, cols] = grad[rows : 2 * rows]
            own_ref[i, :, cols] = grad[2 * rows :]


def attend(first, queries, grad_out, keys, values, kv1, kv2, memory, bias, earlier):
    rows, features = queries.shape
    steps = memory.shape[0] // 2
    slots, block = memory.shape[1:]
    heads = steps * block // HD
    offset = first // block
    flat = pl.BlockSpec((rows, block), lambda i: (0, i + offset))
    pair = pl.BlockSpec((2, rows, block), lambda i: (0, 0, i + offset))
    grad = pl.BlockSpec((2, rows, block), lambda i: (0, 0, i))
    whole = pl.BlockSpec(memory_space=pl.ANY)
    keys_all = slots + 3 * rows
    return pl.pallas_call(
        attend_kernel,
        grid=(steps,),
        in_specs=[
            flat, flat, flat, flat, pair, pair,
            pl.BlockSpec((2, slots, block), lambda i: (i, 0, 0)),
            pl.BlockSpec((rows, keys_all), lambda i: (0, 0)),
            *([whole] * len(earlier)),
        ],
        out_specs=[flat, flat, grad, grad, grad],
        out_shape=[
            jax.ShapeDtypeStruct((rows, features), jnp.bfloat16),
            jax.ShapeDtypeStruct((rows, features), jnp.bfloat16),
            jax.ShapeDtypeStruct((2, rows, steps * block), jnp.bfloat16),
            jax.ShapeDtypeStruct((2, rows, steps * block), jnp.float32),
            jax.ShapeDtypeStruct((2, rows, steps * block), jnp.float32),
        ],
        input_output_aliases={8 + i: i for i in range(len(earlier))},
        compiler_params=pltpu.CompilerParams(vmem_limit_bytes=VMEM),
        cost_estimate=pl.CostEstimate(
            flops=2 * 5 * rows * keys_all * HD * heads,
            bytes_accessed=8 * 1024 * 1024,
            transcendentals=rows * keys_all * heads,
        ),
        name="attend",
    )(queries, grad_out, keys, values, kv1, kv2, memory, bias, *earlier)


def project_kernel(first, order_ref, place_ref, *refs):
    n_z = place_ref.shape[0]
    out_ref, w_ref, a_ref, sems = refs[-4:]
    rows = refs[: 2 * n_z]
    pieces = refs[2 * n_z : -4]
    n_p, w_rows, block = len(pieces), w_ref.shape[2], w_ref.shape[3]
    depth = rows[0].shape[1]
    cache_rows = place_ref.shape[2]
    devices, _, capacity, _ = out_ref.shape
    copies = []
    for i, ref in enumerate(rows):
        start = pl.multiple_of(order_ref[n_z + n_p + i // n_z] * depth, HD)
        to = a_ref.at[order_ref[n_z + n_p + 2 + i % n_z], :, pl.ds(start, depth)]
        copies.append(pltpu.make_async_copy(ref, to, sems.at[len(copies)]))
    for m in range(n_p):
        for k in range(n_z):
            copies.append(
                pltpu.make_async_copy(
                    pieces[m].at[k, :, pl.ds(first, block)],
                    w_ref.at[order_ref[k], order_ref[n_z + m]],
                    sems.at[len(copies)],
                )
            )
    for copy in copies:
        copy.start()
    for copy in copies:
        copy.wait()
    a = a_ref[...].reshape(n_z * cache_rows, 2 * depth)
    w = w_ref[...].reshape(2 * depth, block)
    proj = jnp.dot(a, w, preferred_element_type=jnp.float32).astype(jnp.bfloat16)
    slot_ids = lax.broadcasted_iota(jnp.int32, (devices * capacity, cache_rows), 0)
    for z in range(n_z):
        chosen = jnp.where(slot_ids == place_ref[z], 1.0, 0.0).astype(jnp.bfloat16)
        slots = jnp.dot(
            chosen,
            proj[z * cache_rows : (z + 1) * cache_rows],
            preferred_element_type=jnp.float32,
        ).astype(jnp.bfloat16)
        out_ref[:, z] = slots.reshape(devices, capacity, block)


def project(first, block, order, place, rows, pieces, devices, capacity):
    n_z, _, cache_rows = place.shape
    depth = rows[0].shape[1]
    n_p = len(pieces)
    w_rows = pieces[0].shape[1]
    whole = pl.BlockSpec(memory_space=pl.ANY)
    return pl.pallas_call(
        functools.partial(project_kernel, first),
        in_specs=[
            pl.BlockSpec(memory_space=pltpu.SMEM),
            pl.BlockSpec(memory_space=pltpu.VMEM),
            *([whole] * (len(rows) + n_p)),
        ],
        out_specs=pl.BlockSpec(memory_space=pltpu.VMEM),
        out_shape=jax.ShapeDtypeStruct((devices, n_z, capacity, block), jnp.bfloat16),
        scratch_shapes=[
            pltpu.VMEM((n_z, n_p, w_rows, block), jnp.bfloat16),
            pltpu.VMEM((n_z, cache_rows, 2 * depth), jnp.bfloat16),
            pltpu.SemaphoreType.DMA((n_p * n_z + len(rows),)),
        ],
        compiler_params=pltpu.CompilerParams(vmem_limit_bytes=VMEM),
        cost_estimate=pl.CostEstimate(
            flops=4 * n_z * cache_rows * depth * block,
            bytes_accessed=8 * 1024 * 1024,
            transcendentals=0,
        ),
        name="project",
    )(order, place, *rows, *pieces)


def slot_places(routes, n_z, n_p, cache_rows, capacity):
    mine = lax.dynamic_index_in_dim(
        routes.reshape(n_z, n_p, cache_rows), lax.axis_index("p"), 1, keepdims=False
    )
    ids = jnp.arange(cache_rows, dtype=jnp.int32)
    same = mine[:, :, None] == mine[:, None, :]
    ranks = jnp.sum((same & (ids[None, :] < ids[:, None])[None]).astype(jnp.int32), axis=2)
    return mine * capacity + ranks


def widths(features):
    heads = features // HD // 2
    first = (heads + 1) // 2
    return (first * HD, (heads - first) * HD)


def column_block(w_kv, target):
    parts, offset = [], 0
    for width in widths(w_kv.shape[2]):
        start = (target & 1, 0, offset + (target >> 1) * width)
        parts.append(lax.dynamic_slice(w_kv, start, (1, w_kv.shape[1], width))[0])
        offset += 2 * width
    return jnp.concatenate(parts, 1)


def ring_step(value):
    return lax.ppermute(value, "z", [(a, b) for a, b in zip(RING, RING[1:] + RING[:1])])


def memory_slots(cache, w_kv, place, capacity, stream):
    n_z, n_p = lax.axis_size("z"), lax.axis_size("p")
    devices = n_z * n_p
    cache_rows, depth = cache.shape
    _, w_rows, features = w_kv.shape
    z, p, y = lax.axis_index("z"), lax.axis_index("p"), lax.axis_index("head")
    chunks = widths(features)
    if n_p == 4 and capacity % ROW_TILE == 0 and w_rows % ROW_TILE == 0:
        blocks = [column_block(w_kv, z ^ mask) for mask in range(n_z)]
        own = jnp.stack(
            [blocks[0]] + [swapped(blocks[mask], "z", mask) for mask in range(1, n_z)], 0
        )
        row1, other0, near = ring_step(cache), swapped(cache, "head", 1), shifted(stream, 1)
        own, row1, other0, near = lax.optimization_barrier((own, row1, other0, near))
        across = swapped(own, "p", 2)
        beside = swapped(own, "p", 1)
        row2, other1 = ring_step(row1), swapped(row1, "head", 1)
        row2, other1, beside = lax.optimization_barrier((row2, other1, beside))
        row3, other2 = ring_step(row2), swapped(row2, "head", 1)
        across, near = lax.optimization_barrier((across, near))
        pieces = [own, beside, across, swapped(across, "p", 1)]
        far = shifted(near, 1)
        rows = [cache, row1, row2, row3, other0, other1, other2, swapped(row3, "head", 1)]
        sources = jnp.asarray(
            [[RING[(RING.index(i) - r) % n_z] for r in range(n_z)] for i in range(n_z)], jnp.int32
        )
        order = jnp.concatenate(
            [z ^ jnp.arange(n_z), p ^ jnp.arange(n_p), jnp.stack([y, 1 - y]), sources[z]]
        ).astype(jnp.int32)
        place, near, far = lax.optimization_barrier((place, near, far))
        place = place.reshape(n_z, 1, cache_rows)
        slots, first = [], 0
        for width in chunks:
            slots.append(project(first, width, order, place, rows, pieces, devices, capacity))
            first += width
        return slots, near, far
    near = shifted(stream, 1)
    far = shifted(near, 1)
    targets = [column_block(w_kv, jnp.int32(i)) for i in range(n_z)]
    w_z = lax.all_to_all(jnp.stack(targets, 0), "z", split_axis=0, concat_axis=0, tiled=True)
    w_all = lax.all_gather(w_z, "p", axis=1, tiled=True).reshape(devices * w_rows, -1)
    rows = lax.all_gather(cache, ("head", "z"), axis=0, tiled=False)
    rows = rows.reshape(-1, n_z * cache_rows, depth)
    proj = sum(
        jnp.dot(
            rows[i], w_all[i * depth : (i + 1) * depth], preferred_element_type=jnp.float32
        )
        for i in range(rows.shape[0])
    ).astype(jnp.bfloat16)
    slot_ids = jnp.arange(devices * capacity, dtype=jnp.int32)
    chosen = (slot_ids[None, :, None] == place[:, None, :]).astype(jnp.bfloat16)
    slots = jnp.einsum(
        "zsi,zic->zsc",
        chosen,
        proj.reshape(n_z, cache_rows, -1),
        preferred_element_type=jnp.float32,
    ).astype(jnp.bfloat16)
    slots = slots.reshape(n_z, devices, capacity, -1).transpose(1, 0, 2, 3)
    return [slots[..., : chunks[0]], slots[..., chunks[0] :]], near, far


def body(queries, keys, values, grad_out, cache, w_kv, doc_ids, routes):
    n_z, n_p = lax.axis_size("z"), lax.axis_size("p")
    devices = n_z * n_p
    my_index = lax.axis_index(SEQ)
    seg_rows = queries.shape[0]
    cache_rows = cache.shape[0]
    capacity = 2 * cache_rows // devices
    slot_count = capacity * devices
    pad_rows = SPAN * seg_rows
    window = pad_rows + seg_rows

    place = slot_places(routes, n_z, n_p, cache_rows, capacity)
    slots, kv1, kv2 = memory_slots(cache, w_kv, place, capacity, jnp.stack([keys, values], 0))
    memory = [
        lax.all_to_all(part, SEQ, split_axis=0, concat_axis=0, tiled=True).reshape(
            n_z, slot_count, part.shape[-1]
        )
        for part in slots
    ]

    incoming = jnp.sum(
        (routes.reshape(n_z, n_p, cache_rows) == my_index).astype(jnp.int32), axis=2
    ).T
    live = jnp.arange(capacity, dtype=jnp.int32)[None, None, :] < incoming[:, :, None]
    live = live.reshape(slot_count)
    start = my_index * seg_rows
    id_pad = jnp.concatenate([jnp.full((pad_rows,), -1, jnp.int32), doc_ids])
    q_ids = lax.dynamic_slice_in_dim(doc_ids, start, seg_rows)
    k_ids = lax.dynamic_slice_in_dim(id_pad, start, window)
    q_pos = start + jnp.arange(seg_rows, dtype=jnp.int32)
    k_pos = start - pad_rows + jnp.arange(window, dtype=jnp.int32)
    allowed_win = (k_pos[None, :] <= q_pos[:, None]) & (k_ids[None, :] == q_ids[:, None])
    allowed = jnp.concatenate(
        [jnp.broadcast_to(live[None, :], (seg_rows, slot_count)), allowed_win], 1
    )
    bias = jnp.where(allowed, 0.0, -1e30).astype(jnp.float32)

    first, earlier, grads = 0, [], []
    for part in memory:
        output, grad_q, far, near, own = attend(
            first, queries, grad_out, keys, values, kv1, kv2, part, bias, earlier
        )
        earlier = [output, grad_q]
        first += 2 * part.shape[-1]
        near = shifted(far, -1).astype(jnp.float32) + near
        own = shifted(near.astype(jnp.bfloat16), -1).astype(jnp.float32) + own
        grads.append(own.astype(jnp.bfloat16))
    grad_k, grad_v = (jnp.concatenate([part[i] for part in grads], 1) for i in range(2))
    return (output, grad_q, grad_k, grad_v)


def solution(mesh):
    n_seq, n_head = mesh.devices.shape
    grid = Mesh(mesh.devices.reshape(GROUPS, n_seq // GROUPS, n_head), ("z", "p", "head"))
    rows = P(SEQ, "head")
    return jax.shard_map(
        body,
        mesh=grid,
        in_specs=(rows, rows, rows, rows, rows, P(None, SEQ, "head"), P(), P()),
        out_specs=(rows, rows, rows, rows),
        check_vma=False,
    )
```

```python
import jax
import jax.numpy as jnp
from jax import lax
from jax.experimental import pallas as pl
from jax.experimental.pallas import tpu as pltpu
from jax.sharding import Mesh, PartitionSpec as P

HD = 128
SPAN = 2
GROUPS = 4
SEQ = ("z", "p")
ROW_TILE = 16
RING = [0, 1, 3, 2]
VMEM_ATTEND = 60 * 1024 * 1024
VMEM_PROJECT = 24 * 1024 * 1024


def shifted(value, by):
    length = lax.axis_size("z") * lax.axis_size("p")
    pairs = [(i, i + by) for i in range(length) if 0 <= i + by < length]
    return lax.ppermute(value, SEQ, pairs)


def swapped(value, axis, mask):
    return lax.ppermute(value, axis, [(i, i ^ mask) for i in range(lax.axis_size(axis))])


def dot_t(a, b, dims):
    return lax.dot_general(a, b, (dims, ((), ())), preferred_element_type=jnp.float32)


def attend_kernel(
    q_ref, g_ref, k_ref, v_ref, kv1_ref, kv2_ref, mem_ref, bias_ref,
    out_ref, gq_ref, far_ref, near_ref, own_ref,
):
    rows, width = q_ref.shape
    slots = mem_ref.shape[1]
    scaling = HD ** (-0.5)
    bias = bias_ref[...]
    heads = [slice(i * HD, (i + 1) * HD) for i in range(width // HD)]
    ks = [
        jnp.concatenate(
            [mem_ref[0, :, cols], kv2_ref[0, :, cols], kv1_ref[0, :, cols], k_ref[:, cols]], 0
        )
        for cols in heads
    ]
    vs = [
        jnp.concatenate(
            [mem_ref[1, :, cols], kv2_ref[1, :, cols], kv1_ref[1, :, cols], v_ref[:, cols]], 0
        )
        for cols in heads
    ]
    scores = [dot_t(q_ref[:, cols], kh, ((1,), (1,))) + bias for cols, kh in zip(heads, ks)]
    dprobs = [dot_t(g_ref[:, cols], vh, ((1,), (1,))) for cols, vh in zip(heads, vs)]
    probs = []
    for score in scores:
        weights = jnp.exp((score - jnp.max(score, axis=-1, keepdims=True)) * scaling)
        probs.append(weights * (1.0 / jnp.sum(weights, axis=-1, keepdims=True)))
    probs_b = [prob.astype(jnp.bfloat16) for prob in probs]
    outs = [
        dot_t(prob_b, vh, ((1,), (0,))).astype(jnp.bfloat16) for prob_b, vh in zip(probs_b, vs)
    ]
    dscores = []
    for cols, out_b, prob, dprob in zip(heads, outs, probs, dprobs):
        out_ref[:, cols] = out_b
        delta = jnp.sum(
            g_ref[:, cols].astype(jnp.float32) * out_b.astype(jnp.float32), axis=-1, keepdims=True
        )
        dscores.append((prob * ((dprob - delta) * scaling)).astype(jnp.bfloat16))
    for cols, kh, dscore, prob_b in zip(heads, ks, dscores, probs_b):
        gq_ref[:, cols] = dot_t(dscore, kh, ((1,), (0,))).astype(jnp.bfloat16)
        grad_k = dot_t(dscore[:, slots:], q_ref[:, cols], ((0,), (0,)))
        grad_v = dot_t(prob_b[:, slots:], g_ref[:, cols], ((0,), (0,)))
        for i, grad in enumerate((grad_k, grad_v)):
            far_ref[i, :, cols] = grad[:rows].astype(jnp.bfloat16)
            near_ref[i, :, cols] = grad[rows : 2 * rows]
            own_ref[i, :, cols] = grad[2 * rows :]


def attend(queries, grad_out, keys, values, kv1, kv2, memory, bias):
    rows, features = queries.shape
    steps = memory.shape[0] // 2
    slots, block = memory.shape[1:]
    heads = steps * block // HD
    flat = pl.BlockSpec((rows, block), lambda i: (0, i))
    pair = pl.BlockSpec((2, rows, block), lambda i: (0, 0, i))
    keys_all = slots + 3 * rows
    return pl.pallas_call(
        attend_kernel,
        grid=(steps,),
        in_specs=[
            flat, flat, flat, flat, pair, pair,
            pl.BlockSpec((2, slots, block), lambda i: (i, 0, 0)),
            pl.BlockSpec((rows, keys_all), lambda i: (0, 0)),
        ],
        out_specs=[flat, flat, pair, pair, pair],
        out_shape=[
            jax.ShapeDtypeStruct((rows, features), jnp.bfloat16),
            jax.ShapeDtypeStruct((rows, features), jnp.bfloat16),
            jax.ShapeDtypeStruct((2, rows, features), jnp.bfloat16),
            jax.ShapeDtypeStruct((2, rows, features), jnp.float32),
            jax.ShapeDtypeStruct((2, rows, features), jnp.float32),
        ],
        compiler_params=pltpu.CompilerParams(vmem_limit_bytes=VMEM_ATTEND),
        cost_estimate=pl.CostEstimate(
            flops=2 * 5 * rows * keys_all * HD * heads,
            bytes_accessed=8 * 1024 * 1024,
            transcendentals=rows * keys_all * heads,
        ),
        name="attend",
    )(queries, grad_out, keys, values, kv1, kv2, memory, bias)


def project_kernel(order_ref, place_ref, *refs):
    n_z = place_ref.shape[0]
    out_ref, w_ref, a_ref, sems = refs[-4:]
    rows = refs[: 2 * n_z]
    pieces = refs[2 * n_z : -4]
    n_p, w_rows, block = len(pieces), w_ref.shape[2], w_ref.shape[3]
    depth = rows[0].shape[1]
    cache_rows = place_ref.shape[2]
    devices, _, capacity, _ = out_ref.shape
    copies = []
    for i, ref in enumerate(rows):
        start = pl.multiple_of(order_ref[n_z + n_p + i // n_z] * depth, HD)
        to = a_ref.at[order_ref[n_z + n_p + 2 + i % n_z], :, pl.ds(start, depth)]
        copies.append(pltpu.make_async_copy(ref, to, sems.at[len(copies)]))
    for m in range(n_p):
        for k in range(n_z):
            copies.append(
                pltpu.make_async_copy(
                    pieces[m].at[k],
                    w_ref.at[order_ref[k], order_ref[n_z + m]],
                    sems.at[len(copies)],
                )
            )
    for copy in copies:
        copy.start()
    for copy in copies:
        copy.wait()
    a = a_ref[...].reshape(n_z * cache_rows, 2 * depth)
    w = w_ref[...].reshape(2 * depth, block)
    proj = jnp.dot(a, w, preferred_element_type=jnp.float32).astype(jnp.bfloat16)
    slot_ids = lax.broadcasted_iota(jnp.int32, (devices * capacity, cache_rows), 0)
    for z in range(n_z):
        chosen = jnp.where(slot_ids == place_ref[z], 1.0, 0.0).astype(jnp.bfloat16)
        slots = jnp.dot(
            chosen,
            proj[z * cache_rows : (z + 1) * cache_rows],
            preferred_element_type=jnp.float32,
        ).astype(jnp.bfloat16)
        out_ref[:, z] = slots.reshape(devices, capacity, block)


def project(order, place, rows, pieces, devices, capacity):
    n_z, _, cache_rows = place.shape
    depth = rows[0].shape[1]
    n_p = len(pieces)
    _, w_rows, block = pieces[0].shape
    whole = pl.BlockSpec(memory_space=pl.ANY)
    return pl.pallas_call(
        project_kernel,
        in_specs=[
            pl.BlockSpec(memory_space=pltpu.SMEM),
            pl.BlockSpec(memory_space=pltpu.VMEM),
            *([whole] * (len(rows) + n_p)),
        ],
        out_specs=pl.BlockSpec(memory_space=pltpu.VMEM),
        out_shape=jax.ShapeDtypeStruct((devices, n_z, capacity, block), jnp.bfloat16),
        scratch_shapes=[
            pltpu.VMEM((n_z, n_p, w_rows, block), jnp.bfloat16),
            pltpu.VMEM((n_z, cache_rows, 2 * depth), jnp.bfloat16),
            pltpu.SemaphoreType.DMA((n_p * n_z + len(rows),)),
        ],
        compiler_params=pltpu.CompilerParams(vmem_limit_bytes=VMEM_PROJECT),
        cost_estimate=pl.CostEstimate(
            flops=4 * n_z * cache_rows * depth * block,
            bytes_accessed=8 * 1024 * 1024,
            transcendentals=0,
        ),
        name="project",
    )(order, place, *rows, *pieces)


def slot_places(routes, n_z, n_p, cache_rows, capacity):
    mine = lax.dynamic_index_in_dim(
        routes.reshape(n_z, n_p, cache_rows), lax.axis_index("p"), 1, keepdims=False
    )
    ids = jnp.arange(cache_rows, dtype=jnp.int32)
    same = mine[:, :, None] == mine[:, None, :]
    ranks = jnp.sum((same & (ids[None, :] < ids[:, None])[None]).astype(jnp.int32), axis=2)
    return mine * capacity + ranks


def column_block(w_kv, target):
    _, w_rows, features = w_kv.shape
    half = features // (GROUPS // 2)
    start = (target & 1, 0, (target >> 1) * half)
    return lax.dynamic_slice(w_kv, start, (1, w_rows, half))[0]


def ring_step(value):
    return lax.ppermute(value, "z", [(a, b) for a, b in zip(RING, RING[1:] + RING[:1])])


def memory_slots(cache, w_kv, place, capacity, stream):
    n_z, n_p = lax.axis_size("z"), lax.axis_size("p")
    devices = n_z * n_p
    cache_rows, depth = cache.shape
    _, w_rows, features = w_kv.shape
    z, p, y = lax.axis_index("z"), lax.axis_index("p"), lax.axis_index("head")
    if n_p == 4 and capacity % ROW_TILE == 0 and w_rows % ROW_TILE == 0:
        blocks = [column_block(w_kv, z ^ mask) for mask in range(n_z)]
        own = jnp.stack(
            [blocks[0]] + [swapped(blocks[mask], "z", mask) for mask in range(1, n_z)], 0
        )
        row1, other0 = ring_step(cache), swapped(cache, "head", 1)
        own, row1, other0, stream = lax.optimization_barrier((own, row1, other0, stream))
        across = swapped(own, "p", 2)
        beside = swapped(own, "p", 1)
        near = shifted(stream, 1)
        row2, other1 = ring_step(row1), swapped(row1, "head", 1)
        row2, other1, beside = lax.optimization_barrier((row2, other1, beside))
        row3, other2 = ring_step(row2), swapped(row2, "head", 1)
        across, near, row3, other2 = lax.optimization_barrier((across, near, row3, other2))
        pieces = [own, beside, across, swapped(across, "p", 1)]
        far = shifted(near, 1)
        rows = [cache, row1, row2, row3, other0, other1, other2, swapped(row3, "head", 1)]
        sources = jnp.asarray(
            [[RING[(RING.index(i) - r) % n_z] for r in range(n_z)] for i in range(n_z)], jnp.int32
        )
        order = jnp.concatenate(
            [z ^ jnp.arange(n_z), p ^ jnp.arange(n_p), jnp.stack([y, 1 - y]), sources[z]]
        ).astype(jnp.int32)
        place, near, far = lax.optimization_barrier((place, near, far))
        place = place.reshape(n_z, 1, cache_rows)
        return project(order, place, rows, pieces, devices, capacity), near, far
    near = shifted(stream, 1)
    far = shifted(near, 1)
    targets = [column_block(w_kv, jnp.int32(i)) for i in range(n_z)]
    w_z = lax.all_to_all(jnp.stack(targets, 0), "z", split_axis=0, concat_axis=0, tiled=True)
    w_all = lax.all_gather(w_z, "p", axis=1, tiled=True).reshape(devices * w_rows, -1)
    rows = lax.all_gather(cache, ("head", "z"), axis=0, tiled=False)
    rows = rows.reshape(-1, n_z * cache_rows, depth)
    proj = sum(
        jnp.dot(
            rows[i], w_all[i * depth : (i + 1) * depth], preferred_element_type=jnp.float32
        )
        for i in range(rows.shape[0])
    ).astype(jnp.bfloat16)
    slot_ids = jnp.arange(devices * capacity, dtype=jnp.int32)
    chosen = (slot_ids[None, :, None] == place[:, None, :]).astype(jnp.bfloat16)
    slots = jnp.einsum(
        "zsi,zic->zsc",
        chosen,
        proj.reshape(n_z, cache_rows, -1),
        preferred_element_type=jnp.float32,
    ).astype(jnp.bfloat16)
    return slots.reshape(n_z, devices, capacity, -1).transpose(1, 0, 2, 3), near, far


def body(queries, keys, values, grad_out, cache, w_kv, doc_ids, routes):
    n_z, n_p = lax.axis_size("z"), lax.axis_size("p")
    devices = n_z * n_p
    my_index = lax.axis_index(SEQ)
    seg_rows = queries.shape[0]
    cache_rows = cache.shape[0]
    capacity = 2 * cache_rows // devices
    slot_count = capacity * devices
    pad_rows = SPAN * seg_rows
    window = pad_rows + seg_rows

    place = slot_places(routes, n_z, n_p, cache_rows, capacity)
    slots, kv1, kv2 = memory_slots(cache, w_kv, place, capacity, jnp.stack([keys, values], 0))
    memory = lax.all_to_all(slots, SEQ, split_axis=0, concat_axis=0, tiled=True)
    memory = memory.reshape(n_z, slot_count, slots.shape[-1])

    incoming = jnp.sum(
        (routes.reshape(n_z, n_p, cache_rows) == my_index).astype(jnp.int32), axis=2
    ).T
    live = jnp.arange(capacity, dtype=jnp.int32)[None, None, :] < incoming[:, :, None]
    live = live.reshape(slot_count)
    start = my_index * seg_rows
    id_pad = jnp.concatenate([jnp.full((pad_rows,), -1, jnp.int32), doc_ids])
    q_ids = lax.dynamic_slice_in_dim(doc_ids, start, seg_rows)
    k_ids = lax.dynamic_slice_in_dim(id_pad, start, window)
    q_pos = start + jnp.arange(seg_rows, dtype=jnp.int32)
    k_pos = start - pad_rows + jnp.arange(window, dtype=jnp.int32)
    allowed_win = (k_pos[None, :] <= q_pos[:, None]) & (k_ids[None, :] == q_ids[:, None])
    allowed = jnp.concatenate(
        [jnp.broadcast_to(live[None, :], (seg_rows, slot_count)), allowed_win], 1
    )
    bias = jnp.where(allowed, 0.0, -1e30).astype(jnp.float32)

    output, grad_q, far, near, own = attend(
        queries, grad_out, keys, values, kv1, kv2, memory, bias
    )
    near = shifted(far, -1).astype(jnp.float32) + near
    own = shifted(near.astype(jnp.bfloat16), -1).astype(jnp.float32) + own
    return (output, grad_q, own[0].astype(jnp.bfloat16), own[1].astype(jnp.bfloat16))


def solution(mesh):
    n_seq, n_head = mesh.devices.shape
    grid = Mesh(mesh.devices.reshape(GROUPS, n_seq // GROUPS, n_head), ("z", "p", "head"))
    rows = P(SEQ, "head")
    return jax.shard_map(
        body,
        mesh=grid,
        in_specs=(rows, rows, rows, rows, rows, P(None, SEQ, "head"), P(), P()),
        out_specs=(rows, rows, rows, rows),
        check_vma=False,
    )
```

```python
import jax
import jax.numpy as jnp
from jax import lax
from jax.experimental import pallas as pl
from jax.experimental.pallas import tpu as pltpu
from jax.sharding import Mesh, PartitionSpec as P

HD = 128
SPAN = 2
GROUPS = 4
SEQ = ("z", "p")
ROW_TILE = 16
RING = [0, 1, 3, 2]
VMEM_ATTEND = 60 * 1024 * 1024
VMEM_PROJECT = 48 * 1024 * 1024
STATS = 16


def shifted(value, by):
    length = lax.axis_size("z") * lax.axis_size("p")
    pairs = [(i, i + by) for i in range(length) if 0 <= i + by < length]
    return lax.ppermute(value, SEQ, pairs)


def swapped(value, axis, mask):
    return lax.ppermute(value, axis, [(i, i ^ mask) for i in range(lax.axis_size(axis))])


def dot_t(a, b, dims):
    return lax.dot_general(a, b, (dims, ((), ())), preferred_element_type=jnp.float32)


def attend_kernel(
    q_ref, g_ref, k_ref, v_ref, kv1_ref, kv2_ref, mem_ref, bias_ref, out_ref, gq_ref, stats_ref
):
    rows, width = q_ref.shape
    scaling = HD ** (-0.5)
    bias = bias_ref[...]
    heads = [slice(i * HD, (i + 1) * HD) for i in range(width // HD)]
    ks = [
        jnp.concatenate(
            [mem_ref[0, :, cols], kv2_ref[0, :, cols], kv1_ref[0, :, cols], k_ref[:, cols]], 0
        )
        for cols in heads
    ]
    vs = [
        jnp.concatenate(
            [mem_ref[1, :, cols], kv2_ref[1, :, cols], kv1_ref[1, :, cols], v_ref[:, cols]], 0
        )
        for cols in heads
    ]
    scores = [dot_t(q_ref[:, cols], kh, ((1,), (1,))) + bias for cols, kh in zip(heads, ks)]
    dprobs = [dot_t(g_ref[:, cols], vh, ((1,), (1,))) for cols, vh in zip(heads, vs)]
    tops, shares, probs = [], [], []
    for score in scores:
        top = jnp.max(score, axis=-1, keepdims=True)
        weights = jnp.exp((score - top) * scaling)
        share = 1.0 / jnp.sum(weights, axis=-1, keepdims=True)
        tops.append(top)
        shares.append(share)
        probs.append(weights * share)
    outs = [
        dot_t(prob.astype(jnp.bfloat16), vh, ((1,), (0,))).astype(jnp.bfloat16)
        for prob, vh in zip(probs, vs)
    ]
    deltas, dscores = [], []
    for cols, out_b, prob, dprob in zip(heads, outs, probs, dprobs):
        out_ref[:, cols] = out_b
        delta = jnp.sum(
            g_ref[:, cols].astype(jnp.float32) * out_b.astype(jnp.float32), axis=-1, keepdims=True
        )
        deltas.append(delta)
        dscores.append((prob * ((dprob - delta) * scaling)).astype(jnp.bfloat16))
    lane = lax.broadcasted_iota(jnp.int32, (rows, HD), 1)
    stats = jnp.zeros((rows, HD), jnp.float32)
    for i, column in enumerate(tops + shares + deltas):
        stats = jnp.where(lane == i, column, stats)
    stats_ref[0] = stats.T[:STATS]
    for cols, kh, dscore in zip(heads, ks, dscores):
        gq_ref[:, cols] = dot_t(dscore, kh, ((1,), (0,))).astype(jnp.bfloat16)


def attend(queries, grad_out, keys, values, kv1, kv2, memory, bias):
    rows, features = queries.shape
    steps = memory.shape[0] // 2
    slots, block = memory.shape[1:]
    heads = steps * block // HD
    flat = pl.BlockSpec((rows, block), lambda i: (0, i))
    pair = pl.BlockSpec((2, rows, block), lambda i: (0, 0, i))
    keys_all = slots + 3 * rows
    return pl.pallas_call(
        attend_kernel,
        grid=(steps,),
        in_specs=[
            flat, flat, flat, flat, pair, pair,
            pl.BlockSpec((2, slots, block), lambda i: (i, 0, 0)),
            pl.BlockSpec((rows, keys_all), lambda i: (0, 0)),
        ],
        out_specs=[flat, flat, pl.BlockSpec((1, STATS, rows), lambda i: (i, 0, 0))],
        out_shape=[
            jax.ShapeDtypeStruct((rows, features), jnp.bfloat16),
            jax.ShapeDtypeStruct((rows, features), jnp.bfloat16),
            jax.ShapeDtypeStruct((steps, STATS, rows), jnp.float32),
        ],
        compiler_params=pltpu.CompilerParams(vmem_limit_bytes=VMEM_ATTEND),
        cost_estimate=pl.CostEstimate(
            flops=2 * 4 * rows * keys_all * HD * heads,
            bytes_accessed=6 * 1024 * 1024,
            transcendentals=rows * keys_all * heads,
        ),
        name="attend",
    )(queries, grad_out, keys, values, kv1, kv2, memory, bias)


def key_grads_kernel(
    k_ref, v_ref, q_ref, g_ref, qg1_ref, qg2_ref, st0_ref, st1_ref, st2_ref, bias_ref,
    gk_ref, gv_ref,
):
    width = k_ref.shape[1]
    scaling = HD ** (-0.5)
    bias = bias_ref[...]
    heads = [slice(i * HD, (i + 1) * HD) for i in range(width // HD)]
    stats = jnp.concatenate([st0_ref[0], st1_ref[0], st2_ref[0]], 1)
    qs = [
        jnp.concatenate([q_ref[:, cols], qg1_ref[0, :, cols], qg2_ref[0, :, cols]], 0)
        for cols in heads
    ]
    gs = [
        jnp.concatenate([g_ref[:, cols], qg1_ref[1, :, cols], qg2_ref[1, :, cols]], 0)
        for cols in heads
    ]
    scores = [dot_t(k_ref[:, cols], qh, ((1,), (1,))) + bias for cols, qh in zip(heads, qs)]
    dprobs = [dot_t(v_ref[:, cols], gh, ((1,), (1,))) for cols, gh in zip(heads, gs)]
    probs, dscores = [], []
    for i, (score, dprob) in enumerate(zip(scores, dprobs)):
        top, share, delta = (stats[i + j * len(heads) : i + j * len(heads) + 1] for j in range(3))
        prob = jnp.exp((score - top) * scaling) * share
        probs.append(prob.astype(jnp.bfloat16))
        dscores.append((prob * ((dprob - delta) * scaling)).astype(jnp.bfloat16))
    for cols, qh, gh, prob, dscore in zip(heads, qs, gs, probs, dscores):
        gk_ref[:, cols] = dot_t(dscore, qh, ((1,), (0,))).astype(jnp.bfloat16)
        gv_ref[:, cols] = dot_t(prob, gh, ((1,), (0,))).astype(jnp.bfloat16)


def key_grads(keys, values, queries, grad_out, qg1, qg2, stats, bias):
    rows, features = keys.shape
    steps = stats[0].shape[0]
    block = features // steps
    flat = pl.BlockSpec((rows, block), lambda i: (0, i))
    pair = pl.BlockSpec((2, rows, block), lambda i: (0, 0, i))
    stat = pl.BlockSpec((1, STATS, rows), lambda i: (i, 0, 0))
    heads = features // HD
    return pl.pallas_call(
        key_grads_kernel,
        grid=(steps,),
        in_specs=[
            flat, flat, flat, flat, pair, pair, stat, stat, stat,
            pl.BlockSpec((rows, 3 * rows), lambda i: (0, 0)),
        ],
        out_specs=[flat, flat],
        out_shape=[jax.ShapeDtypeStruct((rows, features), jnp.bfloat16)] * 2,
        compiler_params=pltpu.CompilerParams(vmem_limit_bytes=VMEM_ATTEND),
        cost_estimate=pl.CostEstimate(
            flops=2 * 4 * rows * 3 * rows * HD * heads,
            bytes_accessed=4 * 1024 * 1024,
            transcendentals=rows * 3 * rows * heads,
        ),
        name="key_grads",
    )(keys, values, queries, grad_out, qg1, qg2, *stats, bias)


def project_kernel(order_ref, place_ref, *refs):
    n_z = place_ref.shape[0]
    out_ref, w_ref, a_ref, sems = refs[-4:]
    rows = refs[: 2 * n_z]
    pieces = refs[2 * n_z : -4]
    n_p, w_rows, block = len(pieces), w_ref.shape[2], w_ref.shape[3]
    depth = rows[0].shape[1]
    cache_rows = place_ref.shape[2]
    devices, _, capacity, _ = out_ref.shape
    copies = []
    for i, ref in enumerate(rows):
        start = pl.multiple_of(order_ref[n_z + n_p + i // n_z] * depth, HD)
        to = a_ref.at[order_ref[n_z + n_p + 2 + i % n_z], :, pl.ds(start, depth)]
        copies.append(pltpu.make_async_copy(ref, to, sems.at[len(copies)]))
    for m in range(n_p):
        for k in range(n_z):
            copies.append(
                pltpu.make_async_copy(
                    pieces[m].at[k],
                    w_ref.at[order_ref[k], order_ref[n_z + m]],
                    sems.at[len(copies)],
                )
            )
    for copy in copies:
        copy.start()
    for copy in copies:
        copy.wait()
    a = a_ref[...].reshape(n_z * cache_rows, 2 * depth)
    w = w_ref[...].reshape(2 * depth, block)
    proj = jnp.dot(a, w, preferred_element_type=jnp.float32).astype(jnp.bfloat16)
    slot_ids = lax.broadcasted_iota(jnp.int32, (devices * capacity, cache_rows), 0)
    for z in range(n_z):
        chosen = jnp.where(slot_ids == place_ref[z], 1.0, 0.0).astype(jnp.bfloat16)
        slots = jnp.dot(
            chosen,
            proj[z * cache_rows : (z + 1) * cache_rows],
            preferred_element_type=jnp.float32,
        ).astype(jnp.bfloat16)
        out_ref[:, z] = slots.reshape(devices, capacity, block)


def project(order, place, rows, pieces, devices, capacity):
    n_z, _, cache_rows = place.shape
    depth = rows[0].shape[1]
    n_p = len(pieces)
    _, w_rows, block = pieces[0].shape
    whole = pl.BlockSpec(memory_space=pl.ANY)
    return pl.pallas_call(
        project_kernel,
        in_specs=[
            pl.BlockSpec(memory_space=pltpu.SMEM),
            pl.BlockSpec(memory_space=pltpu.VMEM),
            *([whole] * (len(rows) + n_p)),
        ],
        out_specs=pl.BlockSpec(memory_space=pltpu.VMEM),
        out_shape=jax.ShapeDtypeStruct((devices, n_z, capacity, block), jnp.bfloat16),
        scratch_shapes=[
            pltpu.VMEM((n_z, n_p, w_rows, block), jnp.bfloat16),
            pltpu.VMEM((n_z, cache_rows, 2 * depth), jnp.bfloat16),
            pltpu.SemaphoreType.DMA((n_p * n_z + len(rows),)),
        ],
        compiler_params=pltpu.CompilerParams(vmem_limit_bytes=VMEM_PROJECT),
        cost_estimate=pl.CostEstimate(
            flops=4 * n_z * cache_rows * depth * block,
            bytes_accessed=8 * 1024 * 1024,
            transcendentals=0,
        ),
        name="project",
    )(order, place, *rows, *pieces)


def slot_places(routes, n_z, n_p, cache_rows, capacity):
    mine = lax.dynamic_index_in_dim(
        routes.reshape(n_z, n_p, cache_rows), lax.axis_index("p"), 1, keepdims=False
    )
    ids = jnp.arange(cache_rows, dtype=jnp.int32)
    same = mine[:, :, None] == mine[:, None, :]
    ranks = jnp.sum((same & (ids[None, :] < ids[:, None])[None]).astype(jnp.int32), axis=2)
    return mine * capacity + ranks


def column_block(w_kv, target):
    _, w_rows, features = w_kv.shape
    half = features // (GROUPS // 2)
    start = (target & 1, 0, (target >> 1) * half)
    return lax.dynamic_slice(w_kv, start, (1, w_rows, half))[0]


def ring_step(value):
    return lax.ppermute(value, "z", [(a, b) for a, b in zip(RING, RING[1:] + RING[:1])])


def memory_slots(cache, w_kv, place, capacity, stream, back):
    n_z, n_p = lax.axis_size("z"), lax.axis_size("p")
    devices = n_z * n_p
    cache_rows, depth = cache.shape
    _, w_rows, features = w_kv.shape
    z, p, y = lax.axis_index("z"), lax.axis_index("p"), lax.axis_index("head")
    if n_p == 4 and capacity % ROW_TILE == 0 and w_rows % ROW_TILE == 0:
        blocks = [column_block(w_kv, z ^ mask) for mask in range(n_z)]
        own = jnp.stack(
            [blocks[0]] + [swapped(blocks[mask], "z", mask) for mask in range(1, n_z)], 0
        )
        row1, other0 = ring_step(cache), swapped(cache, "head", 1)
        other0, stream = lax.optimization_barrier((other0, stream))
        near = shifted(stream, 1)
        own, row1, other0, near = lax.optimization_barrier((own, row1, other0, near))
        across = swapped(own, "p", 2)
        beside = swapped(own, "p", 1)
        row2, other1 = ring_step(row1), swapped(row1, "head", 1)
        row2, other1, beside = lax.optimization_barrier((row2, other1, beside))
        row3, other2 = ring_step(row2), swapped(row2, "head", 1)
        row3, other2 = lax.optimization_barrier((row3, other2))
        across, near, back = lax.optimization_barrier((across, near, back))
        pieces = [own, beside, across, swapped(across, "p", 1)]
        far = shifted(near, 1)
        back1 = shifted(back, -1)
        rows = [cache, row1, row2, row3, other0, other1, other2, swapped(row3, "head", 1)]
        sources = jnp.asarray(
            [[RING[(RING.index(i) - r) % n_z] for r in range(n_z)] for i in range(n_z)], jnp.int32
        )
        order = jnp.concatenate(
            [z ^ jnp.arange(n_z), p ^ jnp.arange(n_p), jnp.stack([y, 1 - y]), sources[z]]
        ).astype(jnp.int32)
        place, near, far, back1 = lax.optimization_barrier((place, near, far, back1))
        place = place.reshape(n_z, 1, cache_rows)
        return project(order, place, rows, pieces, devices, capacity), near, far, back1
    near = shifted(stream, 1)
    far = shifted(near, 1)
    back1 = shifted(back, -1)
    targets = [column_block(w_kv, jnp.int32(i)) for i in range(n_z)]
    w_z = lax.all_to_all(jnp.stack(targets, 0), "z", split_axis=0, concat_axis=0, tiled=True)
    w_all = lax.all_gather(w_z, "p", axis=1, tiled=True).reshape(devices * w_rows, -1)
    rows = lax.all_gather(cache, ("head", "z"), axis=0, tiled=False)
    rows = rows.reshape(-1, n_z * cache_rows, depth)
    proj = sum(
        jnp.dot(
            rows[i], w_all[i * depth : (i + 1) * depth], preferred_element_type=jnp.float32
        )
        for i in range(rows.shape[0])
    ).astype(jnp.bfloat16)
    slot_ids = jnp.arange(devices * capacity, dtype=jnp.int32)
    chosen = (slot_ids[None, :, None] == place[:, None, :]).astype(jnp.bfloat16)
    slots = jnp.einsum(
        "zsi,zic->zsc",
        chosen,
        proj.reshape(n_z, cache_rows, -1),
        preferred_element_type=jnp.float32,
    ).astype(jnp.bfloat16)
    return slots.reshape(n_z, devices, capacity, -1).transpose(1, 0, 2, 3), near, far, back1


def body(queries, keys, values, grad_out, cache, w_kv, doc_ids, routes):
    n_z, n_p = lax.axis_size("z"), lax.axis_size("p")
    devices = n_z * n_p
    my_index = lax.axis_index(SEQ)
    seg_rows = queries.shape[0]
    cache_rows = cache.shape[0]
    capacity = 2 * cache_rows // devices
    slot_count = capacity * devices
    pad_rows = SPAN * seg_rows
    window = pad_rows + seg_rows

    place = slot_places(routes, n_z, n_p, cache_rows, capacity)
    slots, kv1, kv2, qg1 = memory_slots(
        cache,
        w_kv,
        place,
        capacity,
        jnp.stack([keys, values], 0),
        jnp.stack([queries, grad_out], 0),
    )
    qg2 = shifted(qg1, -1)
    memory = lax.all_to_all(slots, SEQ, split_axis=0, concat_axis=0, tiled=True)
    memory = memory.reshape(n_z, slot_count, slots.shape[-1])

    incoming = jnp.sum(
        (routes.reshape(n_z, n_p, cache_rows) == my_index).astype(jnp.int32), axis=2
    ).T
    live = jnp.arange(capacity, dtype=jnp.int32)[None, None, :] < incoming[:, :, None]
    live = live.reshape(slot_count)
    start = my_index * seg_rows
    id_pad = jnp.concatenate([jnp.full((pad_rows,), -1, jnp.int32), doc_ids])
    q_ids = lax.dynamic_slice_in_dim(doc_ids, start, seg_rows)
    k_ids = lax.dynamic_slice_in_dim(id_pad, start, window)
    q_pos = start + jnp.arange(seg_rows, dtype=jnp.int32)
    k_pos = start - pad_rows + jnp.arange(window, dtype=jnp.int32)
    allowed_win = (k_pos[None, :] <= q_pos[:, None]) & (k_ids[None, :] == q_ids[:, None])
    allowed = jnp.concatenate(
        [jnp.broadcast_to(live[None, :], (seg_rows, slot_count)), allowed_win], 1
    )
    bias = jnp.where(allowed, 0.0, -1e30).astype(jnp.float32)

    own_ids = jnp.concatenate([doc_ids, jnp.full((pad_rows,), -1, jnp.int32)])
    later_ids = lax.dynamic_slice_in_dim(own_ids, start, window)
    ahead = jnp.arange(window, dtype=jnp.int32)[None, :] >= jnp.arange(seg_rows)[:, None]
    back_bias = jnp.where(ahead & (later_ids[None, :] == q_ids[:, None]), 0.0, -1e30)
    back_bias, qg2, bias = lax.optimization_barrier((back_bias.astype(jnp.float32), qg2, bias))

    output, grad_q, stats = attend(queries, grad_out, keys, values, kv1, kv2, memory, bias)
    all_stats = [stats, shifted(stats, -1), shifted(stats, -2)]
    grad_k, grad_v = key_grads(
        keys, values, queries, grad_out, qg1, qg2, all_stats, back_bias
    )
    return (output, grad_q, grad_k, grad_v)


def solution(mesh):
    n_seq, n_head = mesh.devices.shape
    grid = Mesh(mesh.devices.reshape(GROUPS, n_seq // GROUPS, n_head), ("z", "p", "head"))
    rows = P(SEQ, "head")
    return jax.shard_map(
        body,
        mesh=grid,
        in_specs=(rows, rows, rows, rows, rows, P(None, SEQ, "head"), P(), P()),
        out_specs=(rows, rows, rows, rows),
        check_vma=False,
    )
```

```python
import jax
import jax.numpy as jnp
from jax import lax
from jax.experimental import pallas as pl
from jax.experimental.pallas import tpu as pltpu
from jax.sharding import Mesh, PartitionSpec as P

HD = 128
SPAN = 2
GROUPS = 4
SEQ = ("z", "p")
ROW_TILE = 16
RING = [0, 1, 3, 2]
VMEM = 24 * 1024 * 1024
STATS = 16


def shifted(value, by):
    length = lax.axis_size("z") * lax.axis_size("p")
    pairs = [(i, i + by) for i in range(length) if 0 <= i + by < length]
    return lax.ppermute(value, SEQ, pairs)


def swapped(value, axis, mask):
    return lax.ppermute(value, axis, [(i, i ^ mask) for i in range(lax.axis_size(axis))])


def in_vmem(*arrays):
    return [pltpu.with_memory_space_constraint(array, pltpu.VMEM) for array in arrays]


def dot_t(a, b, dims):
    return lax.dot_general(a, b, (dims, ((), ())), preferred_element_type=jnp.float32)


def attend_kernel(
    q_ref, g_ref, k_ref, v_ref, kv1_ref, kv2_ref, mem_ref, bias_ref, out_ref, gq_ref, stats_ref
):
    rows, width = q_ref.shape
    scaling = HD ** (-0.5)
    bias = bias_ref[...]
    step = pl.program_id(0)
    heads = [slice(i * HD, (i + 1) * HD) for i in range(width // HD)]
    picked = [pl.ds(pl.multiple_of(step * width + i * HD, HD), HD) for i in range(len(heads))]
    ks, vs = (
        [
            jnp.concatenate(
                [
                    mem_ref[2 * step + which, :, cols],
                    kv2_ref[which, :, wide],
                    kv1_ref[which, :, wide],
                    own_ref[:, cols],
                ],
                0,
            )
            for cols, wide in zip(heads, picked)
        ]
        for which, own_ref in enumerate((k_ref, v_ref))
    )
    scores = [dot_t(q_ref[:, cols], kh, ((1,), (1,))) + bias for cols, kh in zip(heads, ks)]
    dprobs = [dot_t(g_ref[:, cols], vh, ((1,), (1,))) for cols, vh in zip(heads, vs)]
    tops, shares, probs = [], [], []
    for score in scores:
        top = jnp.max(score, axis=-1, keepdims=True)
        weights = jnp.exp((score - top) * scaling)
        share = 1.0 / jnp.sum(weights, axis=-1, keepdims=True)
        tops.append(top)
        shares.append(share)
        probs.append(weights * share)
    outs = [
        dot_t(prob.astype(jnp.bfloat16), vh, ((1,), (0,))).astype(jnp.bfloat16)
        for prob, vh in zip(probs, vs)
    ]
    deltas, dscores = [], []
    for cols, out_b, prob, dprob in zip(heads, outs, probs, dprobs):
        out_ref[:, cols] = out_b
        delta = jnp.sum(
            g_ref[:, cols].astype(jnp.float32) * out_b.astype(jnp.float32), axis=-1, keepdims=True
        )
        deltas.append(delta)
        dscores.append((prob * ((dprob - delta) * scaling)).astype(jnp.bfloat16))
    lane = lax.broadcasted_iota(jnp.int32, (rows, HD), 1)
    stats = jnp.zeros((rows, HD), jnp.float32)
    for i, column in enumerate(tops + shares + deltas):
        stats = jnp.where(lane == i, column, stats)
    stats_ref[0] = stats.T[:STATS]
    for cols, kh, dscore in zip(heads, ks, dscores):
        gq_ref[:, cols] = dot_t(dscore, kh, ((1,), (0,))).astype(jnp.bfloat16)


def attend(queries, grad_out, keys, values, kv1, kv2, memory, bias):
    rows, features = queries.shape
    steps = memory.shape[0] // 2
    slots, block = memory.shape[1:]
    heads = steps * block // HD
    flat = pl.BlockSpec((rows, block), lambda i: (0, i))
    whole = pl.BlockSpec(memory_space=pltpu.VMEM)
    keys_all = slots + 3 * rows
    return pl.pallas_call(
        attend_kernel,
        grid=(steps,),
        in_specs=[
            flat, flat, flat, flat, whole, whole, whole, whole,
        ],
        out_specs=[flat, flat, pl.BlockSpec((1, STATS, rows), lambda i: (i, 0, 0))],
        out_shape=[
            jax.ShapeDtypeStruct((rows, features), jnp.bfloat16),
            jax.ShapeDtypeStruct((rows, features), jnp.bfloat16),
            jax.ShapeDtypeStruct((steps, STATS, rows), jnp.float32),
        ],
        compiler_params=pltpu.CompilerParams(vmem_limit_bytes=VMEM),
        cost_estimate=pl.CostEstimate(
            flops=2 * 4 * rows * keys_all * HD * heads,
            bytes_accessed=6 * 1024 * 1024,
            transcendentals=rows * keys_all * heads,
        ),
        name="attend",
    )(queries, grad_out, keys, values, *in_vmem(kv1, kv2, memory, bias))


def key_grads_kernel(
    k_ref, v_ref, q_ref, g_ref, qg1_ref, qg2_ref, st0_ref, st1_ref, st2_ref, bias_ref,
    gk_ref, gv_ref,
):
    width = k_ref.shape[1]
    scaling = HD ** (-0.5)
    bias = bias_ref[...]
    heads = [slice(i * HD, (i + 1) * HD) for i in range(width // HD)]
    start = pl.program_id(0) * width
    picked = [pl.ds(pl.multiple_of(start + i * HD, HD), HD) for i in range(len(heads))]
    stats = jnp.concatenate([st0_ref[0], st1_ref[0], st2_ref[0]], 1)
    qs = [
        jnp.concatenate([q_ref[:, cols], qg1_ref[0, :, wide], qg2_ref[0, :, wide]], 0)
        for cols, wide in zip(heads, picked)
    ]
    gs = [
        jnp.concatenate([g_ref[:, cols], qg1_ref[1, :, wide], qg2_ref[1, :, wide]], 0)
        for cols, wide in zip(heads, picked)
    ]
    scores = [dot_t(k_ref[:, cols], qh, ((1,), (1,))) + bias for cols, qh in zip(heads, qs)]
    dprobs = [dot_t(v_ref[:, cols], gh, ((1,), (1,))) for cols, gh in zip(heads, gs)]
    probs, dscores = [], []
    for i, (score, dprob) in enumerate(zip(scores, dprobs)):
        top, share, delta = (stats[i + j * len(heads) : i + j * len(heads) + 1] for j in range(3))
        prob = jnp.exp((score - top) * scaling) * share
        probs.append(prob.astype(jnp.bfloat16))
        dscores.append((prob * ((dprob - delta) * scaling)).astype(jnp.bfloat16))
    for cols, qh, gh, prob, dscore in zip(heads, qs, gs, probs, dscores):
        gk_ref[:, cols] = dot_t(dscore, qh, ((1,), (0,))).astype(jnp.bfloat16)
        gv_ref[:, cols] = dot_t(prob, gh, ((1,), (0,))).astype(jnp.bfloat16)


def key_grads(keys, values, queries, grad_out, qg1, qg2, stats, bias):
    rows, features = keys.shape
    steps = stats[0].shape[0]
    block = features // steps
    flat = pl.BlockSpec((rows, block), lambda i: (0, i))
    whole = pl.BlockSpec(memory_space=pltpu.VMEM)
    stat = pl.BlockSpec((1, STATS, rows), lambda i: (i, 0, 0))
    heads = features // HD
    return pl.pallas_call(
        key_grads_kernel,
        grid=(steps,),
        in_specs=[
            flat, flat, flat, flat, whole, whole, stat, stat, stat, whole,
        ],
        out_specs=[flat, flat],
        out_shape=[jax.ShapeDtypeStruct((rows, features), jnp.bfloat16)] * 2,
        compiler_params=pltpu.CompilerParams(vmem_limit_bytes=VMEM),
        cost_estimate=pl.CostEstimate(
            flops=2 * 4 * rows * 3 * rows * HD * heads,
            bytes_accessed=4 * 1024 * 1024,
            transcendentals=rows * 3 * rows * heads,
        ),
        name="key_grads",
    )(keys, values, queries, grad_out, *in_vmem(qg1, qg2), *stats, *in_vmem(bias))


def project_kernel(order_ref, place_ref, *refs):
    n_z, _, cache_rows = place_ref.shape
    out_ref, w_ref, a_ref = refs[-3:]
    rows, pieces = refs[: 2 * n_z], refs[2 * n_z : -3]
    n_p, (_, w_rows, block) = len(pieces), pieces[0].shape
    depth = rows[0].shape[1]
    devices, _, capacity, _ = out_ref.shape
    for i, ref in enumerate(rows):
        a_ref[order_ref[n_z + n_p + i // n_z], order_ref[n_z + n_p + 2 + i % n_z]] = ref[...]
    for m in range(n_p):
        for k in range(n_z):
            w_ref[order_ref[k], order_ref[n_z + m]] = pieces[m][k]
    half = n_z // 2
    proj = sum(
        jnp.dot(
            a_ref[i].reshape(n_z * cache_rows, depth),
            w_ref[i * half : (i + 1) * half].reshape(depth, block),
            preferred_element_type=jnp.float32,
        )
        for i in range(2)
    ).astype(jnp.bfloat16)
    slot_ids = lax.broadcasted_iota(jnp.int32, (devices * capacity, cache_rows), 0)
    for z in range(n_z):
        chosen = jnp.where(slot_ids == place_ref[z], 1.0, 0.0).astype(jnp.bfloat16)
        slots = jnp.dot(
            chosen,
            proj[z * cache_rows : (z + 1) * cache_rows],
            preferred_element_type=jnp.float32,
        ).astype(jnp.bfloat16)
        out_ref[:, z] = slots.reshape(devices, capacity, block)


def project(order, place, rows, pieces, devices, capacity):
    n_z, _, cache_rows = place.shape
    depth = rows[0].shape[1]
    n_p = len(pieces)
    _, w_rows, block = pieces[0].shape
    whole = pl.BlockSpec(memory_space=pltpu.VMEM)
    return pl.pallas_call(
        project_kernel,
        in_specs=[
            pl.BlockSpec(memory_space=pltpu.SMEM), *([whole] * (1 + len(rows) + n_p))
        ],
        out_specs=whole,
        out_shape=pltpu.VMEM((devices, n_z, capacity, block), jnp.bfloat16),
        scratch_shapes=[
            pltpu.VMEM((n_z, n_p, w_rows, block), jnp.bfloat16),
            pltpu.VMEM((2, n_z, cache_rows, depth), jnp.bfloat16),
        ],
        compiler_params=pltpu.CompilerParams(vmem_limit_bytes=VMEM),
        cost_estimate=pl.CostEstimate(
            flops=4 * n_z * cache_rows * depth * block,
            bytes_accessed=8 * 1024 * 1024,
            transcendentals=0,
        ),
        name="project",
    )(order, place, *in_vmem(*rows, *pieces))


def slot_places(routes, n_z, n_p, cache_rows, capacity):
    mine = lax.dynamic_index_in_dim(
        routes.reshape(n_z, n_p, cache_rows), lax.axis_index("p"), 1, keepdims=False
    )
    ids = jnp.arange(cache_rows, dtype=jnp.int32)
    same = mine[:, :, None] == mine[:, None, :]
    ranks = jnp.sum((same & (ids[None, :] < ids[:, None])[None]).astype(jnp.int32), axis=2)
    return mine * capacity + ranks


def column_block(w_kv, target):
    _, w_rows, features = w_kv.shape
    half = features // (GROUPS // 2)
    start = (target & 1, 0, (target >> 1) * half)
    return lax.dynamic_slice(w_kv, start, (1, w_rows, half))[0]


def ring_step(value):
    return lax.ppermute(value, "z", [(a, b) for a, b in zip(RING, RING[1:] + RING[:1])])


def memory_slots(cache, w_kv, place, capacity, stream, back):
    n_z, n_p = lax.axis_size("z"), lax.axis_size("p")
    devices = n_z * n_p
    cache_rows, depth = cache.shape
    _, w_rows, features = w_kv.shape
    z, p, y = lax.axis_index("z"), lax.axis_index("p"), lax.axis_index("head")
    if n_p == 4 and capacity % ROW_TILE == 0 and w_rows % ROW_TILE == 0:
        blocks = [column_block(w_kv, z ^ mask) for mask in range(n_z)]
        own = jnp.stack(
            [blocks[0]] + [swapped(blocks[mask], "z", mask) for mask in range(1, n_z)], 0
        )
        row1, other0 = ring_step(cache), swapped(cache, "head", 1)
        own, row1, other0, stream = lax.optimization_barrier((own, row1, other0, stream))
        across = swapped(own, "p", 2)
        beside = swapped(own, "p", 1)
        row2, other1 = ring_step(row1), swapped(row1, "head", 1)
        row2, other1, beside = lax.optimization_barrier((row2, other1, beside))
        row3, other2 = ring_step(row2), swapped(row2, "head", 1)
        across, row3, other2, stream, back = lax.optimization_barrier(
            (across, row3, other2, stream, back)
        )
        pieces = [own, beside, across, swapped(across, "p", 1)]
        near = shifted(stream, 1)
        back1 = shifted(back, -1)
        rows = [cache, row1, row2, row3, other0, other1, other2, swapped(row3, "head", 1)]
        sources = jnp.asarray(
            [[RING[(RING.index(i) - r) % n_z] for r in range(n_z)] for i in range(n_z)], jnp.int32
        )
        order = jnp.concatenate(
            [z ^ jnp.arange(n_z), p ^ jnp.arange(n_p), jnp.stack([y, 1 - y]), sources[z]]
        ).astype(jnp.int32)
        place = place.reshape(n_z, 1, cache_rows)
        slots = project(order, place, rows, pieces, devices, capacity)
        slots, near, back1 = lax.optimization_barrier((slots, near, back1))
        return slots, near, back1
    near = shifted(stream, 1)
    back1 = shifted(back, -1)
    targets = [column_block(w_kv, jnp.int32(i)) for i in range(n_z)]
    w_z = lax.all_to_all(jnp.stack(targets, 0), "z", split_axis=0, concat_axis=0, tiled=True)
    w_all = lax.all_gather(w_z, "p", axis=1, tiled=True).reshape(devices * w_rows, -1)
    rows = lax.all_gather(cache, ("head", "z"), axis=0, tiled=False)
    rows = rows.reshape(-1, n_z * cache_rows, depth)
    proj = sum(
        jnp.dot(
            rows[i], w_all[i * depth : (i + 1) * depth], preferred_element_type=jnp.float32
        )
        for i in range(rows.shape[0])
    ).astype(jnp.bfloat16)
    slot_ids = jnp.arange(devices * capacity, dtype=jnp.int32)
    chosen = (slot_ids[None, :, None] == place[:, None, :]).astype(jnp.bfloat16)
    slots = jnp.einsum(
        "zsi,zic->zsc",
        chosen,
        proj.reshape(n_z, cache_rows, -1),
        preferred_element_type=jnp.float32,
    ).astype(jnp.bfloat16)
    return slots.reshape(n_z, devices, capacity, -1).transpose(1, 0, 2, 3), near, back1


def body(queries, keys, values, grad_out, cache, w_kv, doc_ids, routes):
    n_z, n_p = lax.axis_size("z"), lax.axis_size("p")
    devices = n_z * n_p
    my_index = lax.axis_index(SEQ)
    seg_rows = queries.shape[0]
    cache_rows = cache.shape[0]
    capacity = 2 * cache_rows // devices
    slot_count = capacity * devices
    pad_rows = SPAN * seg_rows
    window = pad_rows + seg_rows

    place = slot_places(routes, n_z, n_p, cache_rows, capacity)
    slots, kv1, qg1 = memory_slots(
        cache,
        w_kv,
        place,
        capacity,
        jnp.stack([keys, values], 0),
        jnp.stack([queries, grad_out], 0),
    )
    kv2, qg2 = shifted(kv1, 1), shifted(qg1, -1)
    memory = lax.all_to_all(slots, SEQ, split_axis=0, concat_axis=0, tiled=True)
    memory = memory.reshape(n_z, slot_count, slots.shape[-1])

    incoming = jnp.sum(
        (routes.reshape(n_z, n_p, cache_rows) == my_index).astype(jnp.int32), axis=2
    ).T
    live = jnp.arange(capacity, dtype=jnp.int32)[None, None, :] < incoming[:, :, None]
    live = live.reshape(slot_count)
    start = my_index * seg_rows
    id_pad = jnp.concatenate([jnp.full((pad_rows,), -1, jnp.int32), doc_ids])
    q_ids = lax.dynamic_slice_in_dim(doc_ids, start, seg_rows)
    k_ids = lax.dynamic_slice_in_dim(id_pad, start, window)
    q_pos = start + jnp.arange(seg_rows, dtype=jnp.int32)
    k_pos = start - pad_rows + jnp.arange(window, dtype=jnp.int32)
    allowed_win = (k_pos[None, :] <= q_pos[:, None]) & (k_ids[None, :] == q_ids[:, None])
    allowed = jnp.concatenate(
        [jnp.broadcast_to(live[None, :], (seg_rows, slot_count)), allowed_win], 1
    )
    bias = jnp.where(allowed, 0.0, -1e30).astype(jnp.float32)

    own_ids = jnp.concatenate([doc_ids, jnp.full((pad_rows,), -1, jnp.int32)])
    later_ids = lax.dynamic_slice_in_dim(own_ids, start, window)
    ahead = jnp.arange(window, dtype=jnp.int32)[None, :] >= jnp.arange(seg_rows)[:, None]
    back_bias = jnp.where(ahead & (later_ids[None, :] == q_ids[:, None]), 0.0, -1e30)
    back_bias, qg2, bias = lax.optimization_barrier((back_bias.astype(jnp.float32), qg2, bias))

    output, grad_q, stats = attend(queries, grad_out, keys, values, kv1, kv2, memory, bias)
    all_stats = [stats, shifted(stats, -1), shifted(stats, -2)]
    grad_k, grad_v = key_grads(
        keys, values, queries, grad_out, qg1, qg2, all_stats, back_bias
    )
    return (output, grad_q, grad_k, grad_v)


def solution(mesh):
    n_seq, n_head = mesh.devices.shape
    grid = Mesh(mesh.devices.reshape(GROUPS, n_seq // GROUPS, n_head), ("z", "p", "head"))
    rows = P(SEQ, "head")
    return jax.shard_map(
        body,
        mesh=grid,
        in_specs=(rows, rows, rows, rows, rows, P(None, SEQ, "head"), P(), P()),
        out_specs=(rows, rows, rows, rows),
        check_vma=False,
    )
```

```python
import jax
import jax.numpy as jnp
from jax import lax
from jax.experimental import pallas as pl
from jax.experimental.pallas import tpu as pltpu
from jax.sharding import Mesh, PartitionSpec as P

HD = 128
GROUPS = 4
SEQ = ("z", "p")
ROW_TILE = 16
RING = [0, 1, 3, 2]
VMEM = 24 * 1024 * 1024
SMALL_VMEM = 4 * 1024 * 1024
STATS = 16


def shifted(value, by):
    length = lax.axis_size("z") * lax.axis_size("p")
    pairs = [(i, i + by) for i in range(length) if 0 <= i + by < length]
    return lax.ppermute(value, SEQ, pairs)


def swapped(value, axis, mask):
    return lax.ppermute(value, axis, [(i, i ^ mask) for i in range(lax.axis_size(axis))])


def in_vmem(*arrays):
    return [pltpu.with_memory_space_constraint(array, pltpu.VMEM) for array in arrays]


def dot_t(a, b, dims):
    return lax.dot_general(a, b, (dims, ((), ())), preferred_element_type=jnp.float32)


def attend_kernel(
    q_ref, g_ref, k_ref, v_ref, kv1_ref, kv2_ref, mem_ref, bias_ref, out_ref, gq_ref, stats_ref
):
    rows, width = q_ref.shape
    scaling = HD ** (-0.5)
    bias = bias_ref[...]
    step = pl.program_id(0)
    heads = [slice(i * HD, (i + 1) * HD) for i in range(width // HD)]
    picked = [pl.ds(pl.multiple_of(step * width + i * HD, HD), HD) for i in range(len(heads))]
    ks, vs = (
        [
            jnp.concatenate(
                [
                    mem_ref[2 * step + which, :, cols],
                    kv2_ref[which, :, wide],
                    kv1_ref[which, :, wide],
                    own_ref[:, cols],
                ],
                0,
            )
            for cols, wide in zip(heads, picked)
        ]
        for which, own_ref in enumerate((k_ref, v_ref))
    )
    scores = [dot_t(q_ref[:, cols], kh, ((1,), (1,))) + bias for cols, kh in zip(heads, ks)]
    dprobs = [dot_t(g_ref[:, cols], vh, ((1,), (1,))) for cols, vh in zip(heads, vs)]
    tops, shares, probs = [], [], []
    for score in scores:
        top = jnp.max(score, axis=-1, keepdims=True)
        weights = jnp.exp((score - top) * scaling)
        share = 1.0 / jnp.sum(weights, axis=-1, keepdims=True)
        tops.append(top)
        shares.append(share)
        probs.append(weights * share)
    outs = [
        dot_t(prob.astype(jnp.bfloat16), vh, ((1,), (0,))).astype(jnp.bfloat16)
        for prob, vh in zip(probs, vs)
    ]
    deltas, dscores = [], []
    for cols, out_b, prob, dprob in zip(heads, outs, probs, dprobs):
        out_ref[:, cols] = out_b
        delta = jnp.sum(
            g_ref[:, cols].astype(jnp.float32) * out_b.astype(jnp.float32), axis=-1, keepdims=True
        )
        deltas.append(delta)
        dscores.append((prob * ((dprob - delta) * scaling)).astype(jnp.bfloat16))
    lane = lax.broadcasted_iota(jnp.int32, (rows, HD), 1)
    stats = jnp.zeros((rows, HD), jnp.float32)
    for i, column in enumerate(tops + shares + deltas):
        stats = jnp.where(lane == i, column, stats)
    stats_ref[0] = stats.T[:STATS]
    for cols, kh, dscore in zip(heads, ks, dscores):
        gq_ref[:, cols] = dot_t(dscore, kh, ((1,), (0,))).astype(jnp.bfloat16)


def attend(queries, grad_out, keys, values, kv1, kv2, memory, bias):
    rows, features = queries.shape
    steps = memory.shape[0] // 2
    slots, block = memory.shape[1:]
    heads = steps * block // HD
    flat = pl.BlockSpec((rows, block), lambda i: (0, i))
    whole = pl.BlockSpec(memory_space=pltpu.VMEM)
    keys_all = slots + 3 * rows
    return pl.pallas_call(
        attend_kernel,
        grid=(steps,),
        in_specs=[
            flat, flat, flat, flat, whole, whole, whole, whole,
        ],
        out_specs=[flat, flat, pl.BlockSpec((1, STATS, rows), lambda i: (i, 0, 0))],
        out_shape=[
            jax.ShapeDtypeStruct((rows, features), jnp.bfloat16),
            jax.ShapeDtypeStruct((rows, features), jnp.bfloat16),
            jax.ShapeDtypeStruct((steps, STATS, rows), jnp.float32),
        ],
        compiler_params=pltpu.CompilerParams(vmem_limit_bytes=VMEM),
        cost_estimate=pl.CostEstimate(
            flops=2 * 4 * rows * keys_all * HD * heads,
            bytes_accessed=6 * 1024 * 1024,
            transcendentals=rows * keys_all * heads,
        ),
        name="attend",
    )(queries, grad_out, keys, values, *in_vmem(kv1, kv2, memory, bias))


def key_grads_kernel(
    k_ref, v_ref, q_ref, g_ref, qg1_ref, qg2_ref, st0_ref, st1_ref, st2_ref, bias_ref,
    gk_ref, gv_ref,
):
    width = k_ref.shape[1]
    scaling = HD ** (-0.5)
    bias = bias_ref[...]
    heads = [slice(i * HD, (i + 1) * HD) for i in range(width // HD)]
    start = pl.program_id(0) * width
    picked = [pl.ds(pl.multiple_of(start + i * HD, HD), HD) for i in range(len(heads))]
    stats = jnp.concatenate([st0_ref[0], st1_ref[0], st2_ref[0]], 1)
    qs = [
        jnp.concatenate([q_ref[:, cols], qg1_ref[0, :, wide], qg2_ref[0, :, wide]], 0)
        for cols, wide in zip(heads, picked)
    ]
    gs = [
        jnp.concatenate([g_ref[:, cols], qg1_ref[1, :, wide], qg2_ref[1, :, wide]], 0)
        for cols, wide in zip(heads, picked)
    ]
    scores = [dot_t(k_ref[:, cols], qh, ((1,), (1,))) + bias for cols, qh in zip(heads, qs)]
    dprobs = [dot_t(v_ref[:, cols], gh, ((1,), (1,))) for cols, gh in zip(heads, gs)]
    probs, dscores = [], []
    for i, (score, dprob) in enumerate(zip(scores, dprobs)):
        top, share, delta = (stats[i + j * len(heads) : i + j * len(heads) + 1] for j in range(3))
        prob = jnp.exp((score - top) * scaling) * share
        probs.append(prob.astype(jnp.bfloat16))
        dscores.append((prob * ((dprob - delta) * scaling)).astype(jnp.bfloat16))
    for cols, qh, gh, prob, dscore in zip(heads, qs, gs, probs, dscores):
        gk_ref[:, cols] = dot_t(dscore, qh, ((1,), (0,))).astype(jnp.bfloat16)
        gv_ref[:, cols] = dot_t(prob, gh, ((1,), (0,))).astype(jnp.bfloat16)


def key_grads(keys, values, queries, grad_out, qg1, qg2, stats, bias):
    rows, features = keys.shape
    steps = stats[0].shape[0]
    block = features // steps
    flat = pl.BlockSpec((rows, block), lambda i: (0, i))
    whole = pl.BlockSpec(memory_space=pltpu.VMEM)
    stat = pl.BlockSpec((1, STATS, rows), lambda i: (i, 0, 0))
    heads = features // HD
    return pl.pallas_call(
        key_grads_kernel,
        grid=(steps,),
        in_specs=[
            flat, flat, flat, flat, whole, whole, stat, stat, stat, whole,
        ],
        out_specs=[flat, flat],
        out_shape=[jax.ShapeDtypeStruct((rows, features), jnp.bfloat16)] * 2,
        compiler_params=pltpu.CompilerParams(vmem_limit_bytes=VMEM),
        cost_estimate=pl.CostEstimate(
            flops=2 * 4 * rows * 3 * rows * HD * heads,
            bytes_accessed=4 * 1024 * 1024,
            transcendentals=rows * 3 * rows * heads,
        ),
        name="key_grads",
    )(keys, values, queries, grad_out, *in_vmem(qg1, qg2), *stats, *in_vmem(bias))


def project_kernel(place_ref, *refs):
    n_z, _, cache_rows = place_ref.shape
    out_ref, w_ref, a_ref = refs[-3:]
    rows, pieces = refs[: 2 * n_z], refs[2 * n_z : -3]
    n_p, (_, w_rows, block) = len(pieces), pieces[0].shape
    depth = rows[0].shape[1]
    devices, _, capacity, _ = out_ref.shape
    z, p, y = (lax.axis_index(name) for name in ("z", "p", "head"))
    place_in_ring = z ^ (z >> 1)
    for i, ref in enumerate(rows):
        source = (place_in_ring - i % n_z + n_z) & (n_z - 1)
        a_ref[y ^ (i // n_z), source ^ (source >> 1)] = ref[...]
    for m in range(n_p):
        for k in range(n_z):
            w_ref[z ^ k, p ^ m] = pieces[m][k]
    half = n_z // 2
    proj = sum(
        jnp.dot(
            a_ref[i].reshape(n_z * cache_rows, depth),
            w_ref[i * half : (i + 1) * half].reshape(depth, block),
            preferred_element_type=jnp.float32,
        )
        for i in range(2)
    ).astype(jnp.bfloat16)
    slot_ids = lax.broadcasted_iota(jnp.int32, (devices * capacity, cache_rows), 0)
    for z in range(n_z):
        chosen = jnp.where(slot_ids == place_ref[z], 1.0, 0.0).astype(jnp.bfloat16)
        slots = jnp.dot(
            chosen,
            proj[z * cache_rows : (z + 1) * cache_rows],
            preferred_element_type=jnp.float32,
        ).astype(jnp.bfloat16)
        out_ref[:, z] = slots.reshape(devices, capacity, block)


def project(place, rows, pieces, devices, capacity):
    n_z, _, cache_rows = place.shape
    depth = rows[0].shape[1]
    n_p = len(pieces)
    _, w_rows, block = pieces[0].shape
    whole = pl.BlockSpec(memory_space=pltpu.VMEM)
    return pl.pallas_call(
        project_kernel,
        in_specs=[whole] * (1 + len(rows) + n_p),
        out_specs=whole,
        out_shape=pltpu.VMEM((devices, n_z, capacity, block), jnp.bfloat16),
        scratch_shapes=[
            pltpu.VMEM((n_z, n_p, w_rows, block), jnp.bfloat16),
            pltpu.VMEM((2, n_z, cache_rows, depth), jnp.bfloat16),
        ],
        compiler_params=pltpu.CompilerParams(vmem_limit_bytes=VMEM),
        cost_estimate=pl.CostEstimate(
            flops=4 * n_z * cache_rows * depth * block,
            bytes_accessed=8 * 1024 * 1024,
            transcendentals=0,
        ),
        name="project",
    )(*in_vmem(place, *rows, *pieces))


def prepare_kernel(routes_ref, ids_ref, place_ref, bias_ref, back_ref):
    n_z, _, rows = place_ref.shape
    devices = routes_ref.shape[0]
    n_p = devices // n_z
    capacity = 2 * rows // devices
    slots = bias_ref.shape[1] - 3 * rows
    p = lax.axis_index("p")
    me = lax.axis_index("z") * n_p + p
    row = lax.broadcasted_iota(jnp.int32, (rows, rows), 0)
    lane = lax.broadcasted_iota(jnp.int32, (rows, rows), 1)

    def both_ways(line):
        wide = jnp.broadcast_to(line.astype(jnp.float32), (rows, rows))
        return wide, wide.T

    for z in range(n_z):
        across, down = both_ways(routes_ref[pl.ds(z * n_p + p, 1), :])
        ranks = jnp.sum(
            jnp.where((across == down) & (row < lane), 1.0, 0.0), axis=0, keepdims=True
        )
        place_ref[z] = (across[:1] * capacity + ranks).astype(jnp.int32)

    def ids_of(segment):
        return ids_ref[pl.ds(jnp.clip(segment, 0, devices - 1), 1), :].astype(jnp.float32)

    _, own = both_ways(ids_ref[pl.ds(me, 1), :])
    for i in range(3):
        earlier, later = me - 2 + i, me + i
        same = (own == ids_of(earlier)) & (earlier >= 0)
        same_back = (own == ids_of(later)) & (later < devices)
        if i == 2:
            same = same & (lane <= row)
        if i == 0:
            same_back = same_back & (lane >= row)
        bias_ref[:, slots + i * rows : slots + (i + 1) * rows] = jnp.where(same, 0.0, -1e30)
        back_ref[:, i * rows : (i + 1) * rows] = jnp.where(same_back, 0.0, -1e30)

    mine = jnp.where(routes_ref[...] == me, 1.0, 0.0).astype(jnp.bfloat16)
    counts = dot_t(jnp.ones((8, rows), jnp.bfloat16), mine, ((1,), (1,))).astype(jnp.bfloat16)
    source = lax.broadcasted_iota(jnp.int32, (devices, slots), 0)
    slot = lax.broadcasted_iota(jnp.int32, (devices, slots), 1) // capacity
    expand = jnp.where(source == (slot % n_z) * n_p + slot // n_z, 1.0, 0.0).astype(jnp.bfloat16)
    filled = jnp.dot(counts, expand, preferred_element_type=jnp.float32)[:1]
    rank = lax.broadcasted_iota(jnp.int32, (1, slots), 1) % capacity
    live = jnp.where(rank.astype(jnp.float32) < filled, 0.0, -1e30)
    bias_ref[:, :slots] = jnp.broadcast_to(live, (rows, slots))


def prepare(routes, doc_ids, n_z, devices, rows):
    slots = 2 * rows
    return pl.pallas_call(
        prepare_kernel,
        out_shape=[
            jax.ShapeDtypeStruct((n_z, 1, rows), jnp.int32),
            jax.ShapeDtypeStruct((rows, slots + 3 * rows), jnp.float32),
            jax.ShapeDtypeStruct((rows, 3 * rows), jnp.float32),
        ],
        compiler_params=pltpu.CompilerParams(vmem_limit_bytes=SMALL_VMEM),
        name="prepare",
    )(routes.reshape(devices, rows), doc_ids.reshape(devices, rows))


def column_block(w_kv, target):
    _, w_rows, features = w_kv.shape
    half = features // (GROUPS // 2)
    start = (target & 1, 0, (target >> 1) * half)
    return lax.dynamic_slice(w_kv, start, (1, w_rows, half))[0]


def ring_step(value):
    return lax.ppermute(value, "z", [(a, b) for a, b in zip(RING, RING[1:] + RING[:1])])


def memory_slots(cache, w_kv, place, capacity, stream, back):
    n_z, n_p = lax.axis_size("z"), lax.axis_size("p")
    devices = n_z * n_p
    cache_rows, depth = cache.shape
    _, w_rows, features = w_kv.shape
    z = lax.axis_index("z")
    if n_p == 4 and capacity % ROW_TILE == 0 and w_rows % ROW_TILE == 0:
        blocks = [column_block(w_kv, z ^ mask) for mask in range(n_z)]
        own = jnp.stack(
            [blocks[0]] + [swapped(blocks[mask], "z", mask) for mask in range(1, n_z)], 0
        )
        row1, other0 = ring_step(cache), swapped(cache, "head", 1)
        own, row1, other0, stream = lax.optimization_barrier((own, row1, other0, stream))
        across = swapped(own, "p", 2)
        beside = swapped(own, "p", 1)
        row2, other1 = ring_step(row1), swapped(row1, "head", 1)
        row2, other1, beside, stream, back = lax.optimization_barrier(
            (row2, other1, beside, stream, back)
        )
        row3, other2 = ring_step(row2), swapped(row2, "head", 1)
        near, back1 = shifted(stream, 1), shifted(back, -1)
        across, row3, other2, near, back1 = lax.optimization_barrier(
            (across, row3, other2, near, back1)
        )
        pieces = [own, beside, across, swapped(across, "p", 1)]
        rows = [cache, row1, row2, row3, other0, other1, other2, swapped(row3, "head", 1)]
        slots = project(place, rows, pieces, devices, capacity)
        return slots, near, back1
    near = shifted(stream, 1)
    back1 = shifted(back, -1)
    targets = [column_block(w_kv, jnp.int32(i)) for i in range(n_z)]
    w_z = lax.all_to_all(jnp.stack(targets, 0), "z", split_axis=0, concat_axis=0, tiled=True)
    w_all = lax.all_gather(w_z, "p", axis=1, tiled=True).reshape(devices * w_rows, -1)
    rows = lax.all_gather(cache, ("head", "z"), axis=0, tiled=False)
    rows = rows.reshape(-1, n_z * cache_rows, depth)
    proj = sum(
        jnp.dot(
            rows[i], w_all[i * depth : (i + 1) * depth], preferred_element_type=jnp.float32
        )
        for i in range(rows.shape[0])
    ).astype(jnp.bfloat16)
    slot_ids = jnp.arange(devices * capacity, dtype=jnp.int32)
    chosen = (slot_ids[None, :, None] == place).astype(jnp.bfloat16)
    slots = jnp.einsum(
        "zsi,zic->zsc",
        chosen,
        proj.reshape(n_z, cache_rows, -1),
        preferred_element_type=jnp.float32,
    ).astype(jnp.bfloat16)
    return slots.reshape(n_z, devices, capacity, -1).transpose(1, 0, 2, 3), near, back1


def body(queries, keys, values, grad_out, cache, w_kv, doc_ids, routes):
    n_z, n_p = lax.axis_size("z"), lax.axis_size("p")
    devices = n_z * n_p
    seg_rows = queries.shape[0]
    cache_rows = cache.shape[0]
    capacity = 2 * cache_rows // devices
    slot_count = capacity * devices

    place, bias, back_bias = prepare(routes, doc_ids, n_z, devices, seg_rows)
    slots, kv1, qg1 = memory_slots(
        cache,
        w_kv,
        place,
        capacity,
        jnp.stack([keys, values], 0),
        jnp.stack([queries, grad_out], 0),
    )
    kv2, qg2 = shifted(kv1, 1), shifted(qg1, -1)
    memory = lax.all_to_all(slots, SEQ, split_axis=0, concat_axis=0, tiled=True)
    memory = memory.reshape(n_z, slot_count, slots.shape[-1])

    qg2, bias = lax.optimization_barrier((qg2, bias))

    output, grad_q, stats = attend(queries, grad_out, keys, values, kv1, kv2, memory, bias)
    all_stats = [stats, shifted(stats, -1), shifted(stats, -2)]
    grad_k, grad_v = key_grads(
        keys, values, queries, grad_out, qg1, qg2, all_stats, back_bias
    )
    return (output, grad_q, grad_k, grad_v)


def solution(mesh):
    n_seq, n_head = mesh.devices.shape
    grid = Mesh(mesh.devices.reshape(GROUPS, n_seq // GROUPS, n_head), ("z", "p", "head"))
    rows = P(SEQ, "head")
    return jax.shard_map(
        body,
        mesh=grid,
        in_specs=(rows, rows, rows, rows, rows, P(None, SEQ, "head"), P(), P()),
        out_specs=(rows, rows, rows, rows),
        check_vma=False,
    )
```

```python
import jax
import jax.numpy as jnp
from jax import lax
from jax.experimental import pallas as pl
from jax.experimental.pallas import tpu as pltpu
from jax.sharding import Mesh, PartitionSpec as P

HD = 128
GROUPS = 4
SEQ = ("z", "p")
ROW_TILE = 16
RING = [0, 1, 3, 2]
VMEM = 24 * 1024 * 1024
SMALL_VMEM = 4 * 1024 * 1024
STATS = 16


def shifted(value, by):
    length = lax.axis_size("z") * lax.axis_size("p")
    pairs = [(i, i + by) for i in range(length) if 0 <= i + by < length]
    return lax.ppermute(value, SEQ, pairs)


def swapped(value, axis, mask):
    return lax.ppermute(value, axis, [(i, i ^ mask) for i in range(lax.axis_size(axis))])


def in_vmem(*arrays):
    return [pltpu.with_memory_space_constraint(array, pltpu.VMEM) for array in arrays]


def in_hbm(*arrays):
    return [pltpu.with_memory_space_constraint(array, pltpu.HBM) for array in arrays]


def dot_t(a, b, dims):
    return lax.dot_general(a, b, (dims, ((), ())), preferred_element_type=jnp.float32)


def attend_kernel(
    q_ref, g_ref, k_ref, v_ref, kv1_ref, kv2_ref, mem_ref, bias_ref, out_ref, gq_ref, stats_ref
):
    rows, width = q_ref.shape
    scaling = HD ** (-0.5)
    bias = bias_ref[...].astype(jnp.float32)
    step = pl.program_id(0)
    heads = [slice(i * HD, (i + 1) * HD) for i in range(width // HD)]
    ks, vs = (
        [
            jnp.concatenate(
                [
                    mem_ref[2 * step + which, :, cols],
                    kv2_ref[which, :, cols],
                    kv1_ref[which, :, cols],
                    own_ref[:, cols],
                ],
                0,
            )
            for cols in heads
        ]
        for which, own_ref in enumerate((k_ref, v_ref))
    )
    scores = [dot_t(q_ref[:, cols], kh, ((1,), (1,))) + bias for cols, kh in zip(heads, ks)]
    dprobs = [dot_t(g_ref[:, cols], vh, ((1,), (1,))) for cols, vh in zip(heads, vs)]
    tops, shares, probs = [], [], []
    for score in scores:
        top = jnp.max(score, axis=-1, keepdims=True)
        weights = jnp.exp((score - top) * scaling)
        share = 1.0 / jnp.sum(weights, axis=-1, keepdims=True)
        tops.append(top)
        shares.append(share)
        probs.append(weights * share)
    outs = [
        dot_t(prob.astype(jnp.bfloat16), vh, ((1,), (0,))).astype(jnp.bfloat16)
        for prob, vh in zip(probs, vs)
    ]
    deltas, dscores = [], []
    for cols, out_b, prob, dprob in zip(heads, outs, probs, dprobs):
        out_ref[:, cols] = out_b
        delta = jnp.sum(
            g_ref[:, cols].astype(jnp.float32) * out_b.astype(jnp.float32), axis=-1, keepdims=True
        )
        deltas.append(delta)
        dscores.append((prob * ((dprob - delta) * scaling)).astype(jnp.bfloat16))
    lane = lax.broadcasted_iota(jnp.int32, (rows, HD), 1)
    stats = jnp.zeros((rows, HD), jnp.float32)
    for i, column in enumerate(tops + shares + deltas):
        stats = jnp.where(lane == i, column, stats)
    stats_ref[0] = stats.T[:STATS]
    for cols, kh, dscore in zip(heads, ks, dscores):
        gq_ref[:, cols] = dot_t(dscore, kh, ((1,), (0,))).astype(jnp.bfloat16)


def attend(queries, grad_out, keys, values, kv1, kv2, memory, bias):
    rows, features = queries.shape
    steps = memory.shape[0] // 2
    slots, block = memory.shape[1:]
    heads = steps * block // HD
    flat = pl.BlockSpec((rows, block), lambda i: (0, i))
    pair = pl.BlockSpec((2, rows, block), lambda i: (0, 0, i))
    whole = pl.BlockSpec(memory_space=pltpu.VMEM)
    keys_all = slots + 3 * rows
    return pl.pallas_call(
        attend_kernel,
        grid=(steps,),
        in_specs=[
            flat, flat, flat, flat, pair, pair, whole,
            pl.BlockSpec((rows, keys_all), lambda i: (0, 0)),
        ],
        out_specs=[flat, flat, pl.BlockSpec((1, STATS, rows), lambda i: (i, 0, 0))],
        out_shape=[
            jax.ShapeDtypeStruct((rows, features), jnp.bfloat16),
            jax.ShapeDtypeStruct((rows, features), jnp.bfloat16),
            jax.ShapeDtypeStruct((steps, STATS, rows), jnp.float32),
        ],
        compiler_params=pltpu.CompilerParams(vmem_limit_bytes=VMEM),
        cost_estimate=pl.CostEstimate(
            flops=2 * 4 * rows * keys_all * HD * heads,
            bytes_accessed=6 * 1024 * 1024,
            transcendentals=rows * keys_all * heads,
        ),
        name="attend",
    )(queries, grad_out, keys, values, *in_hbm(kv1, kv2), *in_vmem(memory), *in_hbm(bias))


def key_grads_kernel(
    k_ref, v_ref, q_ref, g_ref, qg1_ref, qg2_ref, st0_ref, st1_ref, st2_ref, bias_ref,
    gk_ref, gv_ref,
):
    width = k_ref.shape[1]
    scaling = HD ** (-0.5)
    bias = bias_ref[...]
    heads = [slice(i * HD, (i + 1) * HD) for i in range(width // HD)]
    start = pl.program_id(0) * width
    picked = [pl.ds(pl.multiple_of(start + i * HD, HD), HD) for i in range(len(heads))]
    stats = jnp.concatenate([st0_ref[0], st1_ref[0], st2_ref[0]], 1)
    qs = [
        jnp.concatenate([q_ref[:, cols], qg1_ref[0, :, wide], qg2_ref[0, :, wide]], 0)
        for cols, wide in zip(heads, picked)
    ]
    gs = [
        jnp.concatenate([g_ref[:, cols], qg1_ref[1, :, wide], qg2_ref[1, :, wide]], 0)
        for cols, wide in zip(heads, picked)
    ]
    scores = [dot_t(k_ref[:, cols], qh, ((1,), (1,))) + bias for cols, qh in zip(heads, qs)]
    dprobs = [dot_t(v_ref[:, cols], gh, ((1,), (1,))) for cols, gh in zip(heads, gs)]
    probs, dscores = [], []
    for i, (score, dprob) in enumerate(zip(scores, dprobs)):
        top, share, delta = (stats[i + j * len(heads) : i + j * len(heads) + 1] for j in range(3))
        prob = jnp.exp((score - top) * scaling) * share
        probs.append(prob.astype(jnp.bfloat16))
        dscores.append((prob * ((dprob - delta) * scaling)).astype(jnp.bfloat16))
    for cols, qh, gh, prob, dscore in zip(heads, qs, gs, probs, dscores):
        gk_ref[:, cols] = dot_t(dscore, qh, ((1,), (0,))).astype(jnp.bfloat16)
        gv_ref[:, cols] = dot_t(prob, gh, ((1,), (0,))).astype(jnp.bfloat16)


def key_grads(keys, values, queries, grad_out, qg1, qg2, stats, bias):
    rows, features = keys.shape
    steps = stats[0].shape[0]
    block = features // steps
    flat = pl.BlockSpec((rows, block), lambda i: (0, i))
    whole = pl.BlockSpec(memory_space=pltpu.VMEM)
    stat = pl.BlockSpec((1, STATS, rows), lambda i: (i, 0, 0))
    heads = features // HD
    return pl.pallas_call(
        key_grads_kernel,
        grid=(steps,),
        in_specs=[
            flat, flat, flat, flat, whole, whole, stat, stat, stat, whole,
        ],
        out_specs=[flat, flat],
        out_shape=[jax.ShapeDtypeStruct((rows, features), jnp.bfloat16)] * 2,
        compiler_params=pltpu.CompilerParams(vmem_limit_bytes=VMEM),
        cost_estimate=pl.CostEstimate(
            flops=2 * 4 * rows * 3 * rows * HD * heads,
            bytes_accessed=4 * 1024 * 1024,
            transcendentals=rows * 3 * rows * heads,
        ),
        name="key_grads",
    )(keys, values, queries, grad_out, *in_vmem(qg1, qg2), *stats, *in_vmem(bias))


def project_kernel(place_ref, *refs):
    n_z, _, cache_rows = place_ref.shape
    out_ref, w_ref, a_ref = refs[-3:]
    rows, pieces = refs[: 2 * n_z], refs[2 * n_z : -3]
    n_p, (_, w_rows, block) = len(pieces), pieces[0].shape
    depth = rows[0].shape[1]
    devices, _, capacity, _ = out_ref.shape
    z, p, y = (lax.axis_index(name) for name in ("z", "p", "head"))
    place_in_ring = z ^ (z >> 1)
    for i, ref in enumerate(rows):
        source = (place_in_ring - i % n_z + n_z) & (n_z - 1)
        a_ref[y ^ (i // n_z), source ^ (source >> 1)] = ref[...]
    for m in range(n_p):
        for k in range(n_z):
            w_ref[z ^ k, p ^ m] = pieces[m][k]
    half = n_z // 2
    proj = sum(
        jnp.dot(
            a_ref[i].reshape(n_z * cache_rows, depth),
            w_ref[i * half : (i + 1) * half].reshape(depth, block),
            preferred_element_type=jnp.float32,
        )
        for i in range(2)
    ).astype(jnp.bfloat16)
    slot_ids = lax.broadcasted_iota(jnp.int32, (devices * capacity, cache_rows), 0)
    for z in range(n_z):
        chosen = jnp.where(slot_ids == place_ref[z], 1.0, 0.0).astype(jnp.bfloat16)
        slots = jnp.dot(
            chosen,
            proj[z * cache_rows : (z + 1) * cache_rows],
            preferred_element_type=jnp.float32,
        ).astype(jnp.bfloat16)
        out_ref[:, z] = slots.reshape(devices, capacity, block)


def project(place, rows, pieces, devices, capacity):
    n_z, _, cache_rows = place.shape
    depth = rows[0].shape[1]
    n_p = len(pieces)
    _, w_rows, block = pieces[0].shape
    whole = pl.BlockSpec(memory_space=pltpu.VMEM)
    return pl.pallas_call(
        project_kernel,
        in_specs=[whole] * (1 + len(rows) + n_p),
        out_specs=whole,
        out_shape=pltpu.VMEM((devices, n_z, capacity, block), jnp.bfloat16),
        scratch_shapes=[
            pltpu.VMEM((n_z, n_p, w_rows, block), jnp.bfloat16),
            pltpu.VMEM((2, n_z, cache_rows, depth), jnp.bfloat16),
        ],
        compiler_params=pltpu.CompilerParams(vmem_limit_bytes=VMEM),
        cost_estimate=pl.CostEstimate(
            flops=4 * n_z * cache_rows * depth * block,
            bytes_accessed=8 * 1024 * 1024,
            transcendentals=0,
        ),
        name="project",
    )(*in_vmem(place, *rows, *pieces))


def prepare_kernel(routes_ref, ids_ref, place_ref, bias_ref, back_ref):
    n_z, _, rows = place_ref.shape
    devices = routes_ref.shape[0]
    n_p = devices // n_z
    capacity = 2 * rows // devices
    slots = bias_ref.shape[1] - 3 * rows
    p = lax.axis_index("p")
    me = lax.axis_index("z") * n_p + p
    row = lax.broadcasted_iota(jnp.int32, (rows, rows), 0)
    lane = lax.broadcasted_iota(jnp.int32, (rows, rows), 1)

    def both_ways(line):
        wide = jnp.broadcast_to(line.astype(jnp.float32), (rows, rows))
        return wide, wide.T

    for z in range(n_z):
        across, down = both_ways(routes_ref[pl.ds(z * n_p + p, 1), :])
        ranks = jnp.sum(
            jnp.where((across == down) & (row < lane), 1.0, 0.0), axis=0, keepdims=True
        )
        place_ref[z] = (across[:1] * capacity + ranks).astype(jnp.int32)

    def ids_of(segment):
        return ids_ref[pl.ds(jnp.clip(segment, 0, devices - 1), 1), :].astype(jnp.float32)

    _, own = both_ways(ids_ref[pl.ds(me, 1), :])
    for i in range(3):
        earlier, later = me - 2 + i, me + i
        same = (own == ids_of(earlier)) & (earlier >= 0)
        same_back = (own == ids_of(later)) & (later < devices)
        if i == 2:
            same = same & (lane <= row)
        if i == 0:
            same_back = same_back & (lane >= row)
        bias_ref[:, slots + i * rows : slots + (i + 1) * rows] = jnp.where(same, 0.0, -1e30).astype(
            jnp.bfloat16
        )
        back_ref[:, i * rows : (i + 1) * rows] = jnp.where(same_back, 0.0, -1e30)

    mine = jnp.where(routes_ref[...] == me, 1.0, 0.0).astype(jnp.bfloat16)
    counts = dot_t(jnp.ones((8, rows), jnp.bfloat16), mine, ((1,), (1,))).astype(jnp.bfloat16)
    source = lax.broadcasted_iota(jnp.int32, (devices, slots), 0)
    slot = lax.broadcasted_iota(jnp.int32, (devices, slots), 1) // capacity
    expand = jnp.where(source == (slot % n_z) * n_p + slot // n_z, 1.0, 0.0).astype(jnp.bfloat16)
    filled = jnp.dot(counts, expand, preferred_element_type=jnp.float32)[:1]
    rank = lax.broadcasted_iota(jnp.int32, (1, slots), 1) % capacity
    live = jnp.where(rank.astype(jnp.float32) < filled, 0.0, -1e30)
    bias_ref[:, :slots] = jnp.broadcast_to(live, (rows, slots)).astype(jnp.bfloat16)


def prepare(routes, doc_ids, n_z, devices, rows):
    slots = 2 * rows
    return pl.pallas_call(
        prepare_kernel,
        out_shape=[
            jax.ShapeDtypeStruct((n_z, 1, rows), jnp.int32),
            jax.ShapeDtypeStruct((rows, slots + 3 * rows), jnp.bfloat16),
            jax.ShapeDtypeStruct((rows, 3 * rows), jnp.float32),
        ],
        compiler_params=pltpu.CompilerParams(vmem_limit_bytes=SMALL_VMEM),
        name="prepare",
    )(routes.reshape(devices, rows), doc_ids.reshape(devices, rows))


def column_block(w_kv, target):
    _, w_rows, features = w_kv.shape
    half = features // (GROUPS // 2)
    start = (target & 1, 0, (target >> 1) * half)
    return lax.dynamic_slice(w_kv, start, (1, w_rows, half))[0]


def ring_step(value):
    return lax.ppermute(value, "z", [(a, b) for a, b in zip(RING, RING[1:] + RING[:1])])


def memory_slots(cache, w_kv, place, capacity, stream, back):
    n_z, n_p = lax.axis_size("z"), lax.axis_size("p")
    devices = n_z * n_p
    cache_rows, depth = cache.shape
    _, w_rows, features = w_kv.shape
    z = lax.axis_index("z")
    if n_p == 4 and capacity % ROW_TILE == 0 and w_rows % ROW_TILE == 0:
        blocks = [column_block(w_kv, z ^ mask) for mask in range(n_z)]
        own = jnp.stack(
            [blocks[0]] + [swapped(blocks[mask], "z", mask) for mask in range(1, n_z)], 0
        )
        row1, other0 = ring_step(cache), swapped(cache, "head", 1)
        near, back1 = shifted(stream, 1), shifted(back, -1)
        own, row1, other0, near, back1 = lax.optimization_barrier(
            (own, row1, other0, near, back1)
        )
        across = swapped(own, "p", 2)
        beside = swapped(own, "p", 1)
        row2, other1 = ring_step(row1), swapped(row1, "head", 1)
        row2, other1, beside = lax.optimization_barrier((row2, other1, beside))
        row3, other2 = ring_step(row2), swapped(row2, "head", 1)
        across, row3, other2, near, back1 = lax.optimization_barrier(
            (across, row3, other2, near, back1)
        )
        pieces = [own, beside, across, swapped(across, "p", 1)]
        far, back2 = shifted(near, 1), shifted(back1, -1)
        rows = [cache, row1, row2, row3, other0, other1, other2, swapped(row3, "head", 1)]
        slots = project(place, rows, pieces, devices, capacity)
        return lax.optimization_barrier((slots, near, far, back1, back2))
    near, back1 = shifted(stream, 1), shifted(back, -1)
    far, back2 = shifted(near, 1), shifted(back1, -1)
    targets = [column_block(w_kv, jnp.int32(i)) for i in range(n_z)]
    w_z = lax.all_to_all(jnp.stack(targets, 0), "z", split_axis=0, concat_axis=0, tiled=True)
    w_all = lax.all_gather(w_z, "p", axis=1, tiled=True).reshape(devices * w_rows, -1)
    rows = lax.all_gather(cache, ("head", "z"), axis=0, tiled=False)
    rows = rows.reshape(-1, n_z * cache_rows, depth)
    proj = sum(
        jnp.dot(
            rows[i], w_all[i * depth : (i + 1) * depth], preferred_element_type=jnp.float32
        )
        for i in range(rows.shape[0])
    ).astype(jnp.bfloat16)
    slot_ids = jnp.arange(devices * capacity, dtype=jnp.int32)
    chosen = (slot_ids[None, :, None] == place).astype(jnp.bfloat16)
    slots = jnp.einsum(
        "zsi,zic->zsc",
        chosen,
        proj.reshape(n_z, cache_rows, -1),
        preferred_element_type=jnp.float32,
    ).astype(jnp.bfloat16)
    slots = slots.reshape(n_z, devices, capacity, -1).transpose(1, 0, 2, 3)
    return slots, near, far, back1, back2


def body(queries, keys, values, grad_out, cache, w_kv, doc_ids, routes):
    n_z, n_p = lax.axis_size("z"), lax.axis_size("p")
    devices = n_z * n_p
    seg_rows = queries.shape[0]
    cache_rows = cache.shape[0]
    capacity = 2 * cache_rows // devices
    slot_count = capacity * devices

    place, bias, back_bias = prepare(routes, doc_ids, n_z, devices, seg_rows)
    slots, kv1, kv2, qg1, qg2 = memory_slots(
        cache,
        w_kv,
        place,
        capacity,
        jnp.stack([keys, values], 0),
        jnp.stack([queries, grad_out], 0),
    )
    memory = lax.all_to_all(slots, SEQ, split_axis=0, concat_axis=0, tiled=True)
    memory = memory.reshape(n_z, slot_count, slots.shape[-1])

    output, grad_q, stats = attend(queries, grad_out, keys, values, kv1, kv2, memory, bias)
    all_stats = [stats, shifted(stats, -1), shifted(stats, -2)]
    grad_k, grad_v = key_grads(
        keys, values, queries, grad_out, qg1, qg2, all_stats, back_bias
    )
    return (output, grad_q, grad_k, grad_v)


def solution(mesh):
    n_seq, n_head = mesh.devices.shape
    grid = Mesh(mesh.devices.reshape(GROUPS, n_seq // GROUPS, n_head), ("z", "p", "head"))
    rows = P(SEQ, "head")
    return jax.shard_map(
        body,
        mesh=grid,
        in_specs=(rows, rows, rows, rows, rows, P(None, SEQ, "head"), P(), P()),
        out_specs=(rows, rows, rows, rows),
        check_vma=False,
    )
```

```python
import jax
import jax.numpy as jnp
from jax import lax
from jax.experimental import pallas as pl
from jax.experimental.pallas import tpu as pltpu
from jax.sharding import Mesh, PartitionSpec as P

HD = 128
GROUPS = 4
SEQ = ("z", "p")
ROW_TILE = 16
RING = [0, 1, 3, 2]
VMEM = 24 * 1024 * 1024
SMALL_VMEM = 4 * 1024 * 1024
STATS = 16


def shifted(value, by):
    length = lax.axis_size("z") * lax.axis_size("p")
    pairs = [(i, i + by) for i in range(length) if 0 <= i + by < length]
    return lax.ppermute(value, SEQ, pairs)


def swapped(value, axis, mask):
    return lax.ppermute(value, axis, [(i, i ^ mask) for i in range(lax.axis_size(axis))])


def in_vmem(*arrays):
    return [pltpu.with_memory_space_constraint(array, pltpu.VMEM) for array in arrays]


def in_hbm(*arrays):
    return [pltpu.with_memory_space_constraint(array, pltpu.HBM) for array in arrays]


def dot_t(a, b, dims):
    return lax.dot_general(a, b, (dims, ((), ())), preferred_element_type=jnp.float32)


def attend_kernel(
    q_ref, g_ref, k_ref, v_ref, kv1_ref, kv2_ref, mem_ref, bias_ref, out_ref, gq_ref, stats_ref
):
    rows, width = q_ref.shape
    scaling = HD ** (-0.5)
    bias = bias_ref[...].astype(jnp.float32)
    step = pl.program_id(0)
    heads = [slice(i * HD, (i + 1) * HD) for i in range(width // HD)]
    ks, vs = (
        [
            jnp.concatenate(
                [
                    mem_ref[2 * step + which, :, cols],
                    kv2_ref[which, :, cols],
                    kv1_ref[which, :, cols],
                    own_ref[:, cols],
                ],
                0,
            )
            for cols in heads
        ]
        for which, own_ref in enumerate((k_ref, v_ref))
    )
    scores = [dot_t(q_ref[:, cols], kh, ((1,), (1,))) + bias for cols, kh in zip(heads, ks)]
    dprobs = [dot_t(g_ref[:, cols], vh, ((1,), (1,))) for cols, vh in zip(heads, vs)]
    tops, shares, probs = [], [], []
    for score in scores:
        top = jnp.max(score, axis=-1, keepdims=True)
        weights = jnp.exp((score - top) * scaling)
        share = 1.0 / jnp.sum(weights, axis=-1, keepdims=True)
        tops.append(top)
        shares.append(share)
        probs.append(weights * share)
    outs = [
        dot_t(prob.astype(jnp.bfloat16), vh, ((1,), (0,))).astype(jnp.bfloat16)
        for prob, vh in zip(probs, vs)
    ]
    deltas, dscores = [], []
    for cols, out_b, prob, dprob in zip(heads, outs, probs, dprobs):
        out_ref[:, cols] = out_b
        delta = jnp.sum(
            g_ref[:, cols].astype(jnp.float32) * out_b.astype(jnp.float32), axis=-1, keepdims=True
        )
        deltas.append(delta)
        dscores.append((prob * ((dprob - delta) * scaling)).astype(jnp.bfloat16))
    lane = lax.broadcasted_iota(jnp.int32, (rows, HD), 1)
    stats = jnp.zeros((rows, HD), jnp.float32)
    for i, column in enumerate(tops + shares + deltas):
        stats = jnp.where(lane == i, column, stats)
    stats_ref[0] = stats.T[:STATS]
    for cols, kh, dscore in zip(heads, ks, dscores):
        gq_ref[:, cols] = dot_t(dscore, kh, ((1,), (0,))).astype(jnp.bfloat16)


def attend(queries, grad_out, keys, values, kv1, kv2, memory, bias):
    rows, features = queries.shape
    steps = memory.shape[0] // 2
    slots, block = memory.shape[1:]
    heads = steps * block // HD
    flat = pl.BlockSpec((rows, block), lambda i: (0, i))
    pair = pl.BlockSpec((2, rows, block), lambda i: (0, 0, i))
    whole = pl.BlockSpec(memory_space=pltpu.VMEM)
    keys_all = slots + 3 * rows
    return pl.pallas_call(
        attend_kernel,
        grid=(steps,),
        in_specs=[
            flat, flat, flat, flat, pair, pair, whole,
            pl.BlockSpec((rows, keys_all), lambda i: (0, 0)),
        ],
        out_specs=[flat, flat, pl.BlockSpec((1, STATS, rows), lambda i: (i, 0, 0))],
        out_shape=[
            jax.ShapeDtypeStruct((rows, features), jnp.bfloat16),
            jax.ShapeDtypeStruct((rows, features), jnp.bfloat16),
            jax.ShapeDtypeStruct((steps, STATS, rows), jnp.float32),
        ],
        compiler_params=pltpu.CompilerParams(vmem_limit_bytes=VMEM),
        cost_estimate=pl.CostEstimate(
            flops=2 * 4 * rows * keys_all * HD * heads,
            bytes_accessed=6 * 1024 * 1024,
            transcendentals=rows * keys_all * heads,
        ),
        name="attend",
    )(queries, grad_out, keys, values, *in_hbm(kv1, kv2), *in_vmem(memory), *in_hbm(bias))


def key_grads_kernel(
    k_ref, v_ref, q_ref, g_ref, qg1_ref, qg2_ref, st0_ref, st1_ref, st2_ref, bias_ref,
    gk_ref, gv_ref,
):
    width = k_ref.shape[1]
    scaling = HD ** (-0.5)
    bias = bias_ref[...]
    heads = [slice(i * HD, (i + 1) * HD) for i in range(width // HD)]
    start = pl.program_id(0) * width
    picked = [pl.ds(pl.multiple_of(start + i * HD, HD), HD) for i in range(len(heads))]
    stats = jnp.concatenate([st0_ref[0], st1_ref[0], st2_ref[0]], 1)
    qs = [
        jnp.concatenate([q_ref[:, cols], qg1_ref[0, :, wide], qg2_ref[0, :, wide]], 0)
        for cols, wide in zip(heads, picked)
    ]
    gs = [
        jnp.concatenate([g_ref[:, cols], qg1_ref[1, :, wide], qg2_ref[1, :, wide]], 0)
        for cols, wide in zip(heads, picked)
    ]
    scores = [dot_t(k_ref[:, cols], qh, ((1,), (1,))) + bias for cols, qh in zip(heads, qs)]
    dprobs = [dot_t(v_ref[:, cols], gh, ((1,), (1,))) for cols, gh in zip(heads, gs)]
    probs, dscores = [], []
    for i, (score, dprob) in enumerate(zip(scores, dprobs)):
        top, share, delta = (stats[i + j * len(heads) : i + j * len(heads) + 1] for j in range(3))
        prob = jnp.exp((score - top) * scaling) * share
        probs.append(prob.astype(jnp.bfloat16))
        dscores.append((prob * ((dprob - delta) * scaling)).astype(jnp.bfloat16))
    for cols, qh, gh, prob, dscore in zip(heads, qs, gs, probs, dscores):
        gk_ref[:, cols] = dot_t(dscore, qh, ((1,), (0,))).astype(jnp.bfloat16)
        gv_ref[:, cols] = dot_t(prob, gh, ((1,), (0,))).astype(jnp.bfloat16)


def key_grads(keys, values, queries, grad_out, qg1, qg2, stats, bias):
    rows, features = keys.shape
    steps = stats[0].shape[0]
    block = features // steps
    flat = pl.BlockSpec((rows, block), lambda i: (0, i))
    whole = pl.BlockSpec(memory_space=pltpu.VMEM)
    stat = pl.BlockSpec((1, STATS, rows), lambda i: (i, 0, 0))
    heads = features // HD
    return pl.pallas_call(
        key_grads_kernel,
        grid=(steps,),
        in_specs=[
            flat, flat, flat, flat, whole, whole, stat, stat, stat, whole,
        ],
        out_specs=[flat, flat],
        out_shape=[jax.ShapeDtypeStruct((rows, features), jnp.bfloat16)] * 2,
        compiler_params=pltpu.CompilerParams(vmem_limit_bytes=VMEM),
        cost_estimate=pl.CostEstimate(
            flops=2 * 4 * rows * 3 * rows * HD * heads,
            bytes_accessed=4 * 1024 * 1024,
            transcendentals=rows * 3 * rows * heads,
        ),
        name="key_grads",
    )(keys, values, queries, grad_out, *in_vmem(qg1, qg2), *stats, *in_vmem(bias))


def project_kernel(place_ref, *refs):
    n_z, _, cache_rows = place_ref.shape
    out_ref, w_ref, a_ref = refs[-3:]
    rows, pieces = refs[: 2 * n_z], refs[2 * n_z : -3]
    n_p, (_, w_rows, block) = len(pieces), pieces[0].shape
    depth = rows[0].shape[1]
    devices, _, capacity, _ = out_ref.shape
    z, p, y = (lax.axis_index(name) for name in ("z", "p", "head"))
    place_in_ring = z ^ (z >> 1)
    for i, ref in enumerate(rows):
        source = (place_in_ring - i % n_z + n_z) & (n_z - 1)
        a_ref[y ^ (i // n_z), source ^ (source >> 1)] = ref[...]
    for m in range(n_p):
        for k in range(n_z):
            w_ref[z ^ k, p ^ m] = pieces[m][k]
    half = n_z // 2
    proj = sum(
        jnp.dot(
            a_ref[i].reshape(n_z * cache_rows, depth),
            w_ref[i * half : (i + 1) * half].reshape(depth, block),
            preferred_element_type=jnp.float32,
        )
        for i in range(2)
    ).astype(jnp.bfloat16)
    slot_ids = lax.broadcasted_iota(jnp.int32, (devices * capacity, cache_rows), 0)
    for z in range(n_z):
        chosen = jnp.where(slot_ids == place_ref[z], 1.0, 0.0).astype(jnp.bfloat16)
        slots = jnp.dot(
            chosen,
            proj[z * cache_rows : (z + 1) * cache_rows],
            preferred_element_type=jnp.float32,
        ).astype(jnp.bfloat16)
        out_ref[:, z] = slots.reshape(devices, capacity, block)


def project(place, rows, pieces, devices, capacity):
    n_z, _, cache_rows = place.shape
    depth = rows[0].shape[1]
    n_p = len(pieces)
    _, w_rows, block = pieces[0].shape
    whole = pl.BlockSpec(memory_space=pltpu.VMEM)
    return pl.pallas_call(
        project_kernel,
        in_specs=[whole] * (1 + len(rows) + n_p),
        out_specs=whole,
        out_shape=pltpu.VMEM((devices, n_z, capacity, block), jnp.bfloat16),
        scratch_shapes=[
            pltpu.VMEM((n_z, n_p, w_rows, block), jnp.bfloat16),
            pltpu.VMEM((2, n_z, cache_rows, depth), jnp.bfloat16),
        ],
        compiler_params=pltpu.CompilerParams(vmem_limit_bytes=VMEM),
        cost_estimate=pl.CostEstimate(
            flops=4 * n_z * cache_rows * depth * block,
            bytes_accessed=8 * 1024 * 1024,
            transcendentals=0,
        ),
        name="project",
    )(*in_vmem(place, *rows, *pieces))


def prepare_kernel(routes_ref, ids_ref, place_ref, bias_ref, back_ref):
    n_z, _, rows = place_ref.shape
    devices = routes_ref.shape[0]
    n_p = devices // n_z
    capacity = 2 * rows // devices
    slots = bias_ref.shape[1] - 3 * rows
    p = lax.axis_index("p")
    me = lax.axis_index("z") * n_p + p
    row = lax.broadcasted_iota(jnp.int32, (rows, rows), 0)
    lane = lax.broadcasted_iota(jnp.int32, (rows, rows), 1)

    def both_ways(line):
        wide = jnp.broadcast_to(line.astype(jnp.float32), (rows, rows))
        return wide, wide.T

    for z in range(n_z):
        across, down = both_ways(routes_ref[pl.ds(z * n_p + p, 1), :])
        ranks = jnp.sum(
            jnp.where((across == down) & (row < lane), 1.0, 0.0), axis=0, keepdims=True
        )
        place_ref[z] = (across[:1] * capacity + ranks).astype(jnp.int32)

    def ids_of(segment):
        return ids_ref[pl.ds(jnp.clip(segment, 0, devices - 1), 1), :].astype(jnp.float32)

    _, own = both_ways(ids_ref[pl.ds(me, 1), :])
    for i in range(3):
        earlier, later = me - 2 + i, me + i
        same = (own == ids_of(earlier)) & (earlier >= 0)
        same_back = (own == ids_of(later)) & (later < devices)
        if i == 2:
            same = same & (lane <= row)
        if i == 0:
            same_back = same_back & (lane >= row)
        bias_ref[:, slots + i * rows : slots + (i + 1) * rows] = jnp.where(same, 0.0, -1e30).astype(
            jnp.bfloat16
        )
        back_ref[:, i * rows : (i + 1) * rows] = jnp.where(same_back, 0.0, -1e30)

    mine = jnp.where(routes_ref[...] == me, 1.0, 0.0).astype(jnp.bfloat16)
    counts = dot_t(jnp.ones((8, rows), jnp.bfloat16), mine, ((1,), (1,))).astype(jnp.bfloat16)
    source = lax.broadcasted_iota(jnp.int32, (devices, slots), 0)
    slot = lax.broadcasted_iota(jnp.int32, (devices, slots), 1) // capacity
    expand = jnp.where(source == (slot % n_z) * n_p + slot // n_z, 1.0, 0.0).astype(jnp.bfloat16)
    filled = jnp.dot(counts, expand, preferred_element_type=jnp.float32)[:1]
    rank = lax.broadcasted_iota(jnp.int32, (1, slots), 1) % capacity
    live = jnp.where(rank.astype(jnp.float32) < filled, 0.0, -1e30)
    bias_ref[:, :slots] = jnp.broadcast_to(live, (rows, slots)).astype(jnp.bfloat16)


def prepare(routes, doc_ids, n_z, devices, rows):
    slots = 2 * rows
    return pl.pallas_call(
        prepare_kernel,
        out_shape=[
            jax.ShapeDtypeStruct((n_z, 1, rows), jnp.int32),
            jax.ShapeDtypeStruct((rows, slots + 3 * rows), jnp.bfloat16),
            jax.ShapeDtypeStruct((rows, 3 * rows), jnp.float32),
        ],
        compiler_params=pltpu.CompilerParams(vmem_limit_bytes=SMALL_VMEM),
        name="prepare",
    )(routes.reshape(devices, rows), doc_ids.reshape(devices, rows))


def column_block(w_kv, target):
    _, w_rows, features = w_kv.shape
    half = features // (GROUPS // 2)
    start = (target & 1, 0, (target >> 1) * half)
    return lax.dynamic_slice(w_kv, start, (1, w_rows, half))[0]


def ring_step(value):
    return lax.ppermute(value, "z", [(a, b) for a, b in zip(RING, RING[1:] + RING[:1])])


def memory_slots(cache, w_kv, place, capacity, stream, back):
    n_z, n_p = lax.axis_size("z"), lax.axis_size("p")
    devices = n_z * n_p
    cache_rows, depth = cache.shape
    _, w_rows, features = w_kv.shape
    z = lax.axis_index("z")
    if n_p == 4 and capacity % ROW_TILE == 0 and w_rows % ROW_TILE == 0:
        blocks = [column_block(w_kv, z ^ mask) for mask in range(n_z)]
        own = jnp.stack(
            [blocks[0]] + [swapped(blocks[mask], "z", mask) for mask in range(1, n_z)], 0
        )
        row1, other0 = ring_step(cache), swapped(cache, "head", 1)
        own, row1, other0 = lax.optimization_barrier((own, row1, other0))
        across = swapped(own, "p", 2)
        beside = swapped(own, "p", 1)
        row2, other1 = ring_step(row1), swapped(row1, "head", 1)
        row2, other1, beside = lax.optimization_barrier((row2, other1, beside))
        row3, other2 = ring_step(row2), swapped(row2, "head", 1)
        across, row3, other2, stream = lax.optimization_barrier((across, row3, other2, stream))
        pieces = [own, beside, across, swapped(across, "p", 1)]
        near = shifted(stream, 1)
        rows = [cache, row1, row2, row3, other0, other1, other2, swapped(row3, "head", 1)]
        slots = project(place, rows, pieces, devices, capacity)
        slots, near, back = lax.optimization_barrier((slots, near, back))
        return slots, near, shifted(near, 1), shifted(back, -1)
    near, back1 = shifted(stream, 1), shifted(back, -1)
    far = shifted(near, 1)
    targets = [column_block(w_kv, jnp.int32(i)) for i in range(n_z)]
    w_z = lax.all_to_all(jnp.stack(targets, 0), "z", split_axis=0, concat_axis=0, tiled=True)
    w_all = lax.all_gather(w_z, "p", axis=1, tiled=True).reshape(devices * w_rows, -1)
    rows = lax.all_gather(cache, ("head", "z"), axis=0, tiled=False)
    rows = rows.reshape(-1, n_z * cache_rows, depth)
    proj = sum(
        jnp.dot(
            rows[i], w_all[i * depth : (i + 1) * depth], preferred_element_type=jnp.float32
        )
        for i in range(rows.shape[0])
    ).astype(jnp.bfloat16)
    slot_ids = jnp.arange(devices * capacity, dtype=jnp.int32)
    chosen = (slot_ids[None, :, None] == place).astype(jnp.bfloat16)
    slots = jnp.einsum(
        "zsi,zic->zsc",
        chosen,
        proj.reshape(n_z, cache_rows, -1),
        preferred_element_type=jnp.float32,
    ).astype(jnp.bfloat16)
    slots = slots.reshape(n_z, devices, capacity, -1).transpose(1, 0, 2, 3)
    return slots, near, far, back1


def body(queries, keys, values, grad_out, cache, w_kv, doc_ids, routes):
    n_z, n_p = lax.axis_size("z"), lax.axis_size("p")
    devices = n_z * n_p
    seg_rows = queries.shape[0]
    cache_rows = cache.shape[0]
    capacity = 2 * cache_rows // devices
    slot_count = capacity * devices

    place, bias, back_bias = prepare(routes, doc_ids, n_z, devices, seg_rows)
    slots, kv1, kv2, qg1 = memory_slots(
        cache,
        w_kv,
        place,
        capacity,
        jnp.stack([keys, values], 0),
        jnp.stack([queries, grad_out], 0),
    )
    memory = lax.all_to_all(slots, SEQ, split_axis=0, concat_axis=0, tiled=True)
    memory = memory.reshape(n_z, slot_count, slots.shape[-1])

    memory, qg1 = lax.optimization_barrier((memory, qg1))
    qg2 = shifted(qg1, -1)
    output, grad_q, stats = attend(queries, grad_out, keys, values, kv1, kv2, memory, bias)
    all_stats = [stats, shifted(stats, -1), shifted(stats, -2)]
    grad_k, grad_v = key_grads(
        keys, values, queries, grad_out, qg1, qg2, all_stats, back_bias
    )
    return (output, grad_q, grad_k, grad_v)


def solution(mesh):
    n_seq, n_head = mesh.devices.shape
    grid = Mesh(mesh.devices.reshape(GROUPS, n_seq // GROUPS, n_head), ("z", "p", "head"))
    rows = P(SEQ, "head")
    return jax.shard_map(
        body,
        mesh=grid,
        in_specs=(rows, rows, rows, rows, rows, P(None, SEQ, "head"), P(), P()),
        out_specs=(rows, rows, rows, rows),
        check_vma=False,
    )
```

```python
import jax
import jax.numpy as jnp
from jax import lax
from jax.experimental import pallas as pl
from jax.experimental.pallas import tpu as pltpu
from jax.sharding import Mesh, PartitionSpec as P

HD = 128
GROUPS = 4
SEQ = ("z", "p")
ROW_TILE = 16
RING = [0, 1, 3, 2]
VMEM = 24 * 1024 * 1024
SMALL_VMEM = 4 * 1024 * 1024
STATS = 16


def shifted(value, by):
    length = lax.axis_size("z") * lax.axis_size("p")
    pairs = [(i, i + by) for i in range(length) if 0 <= i + by < length]
    return lax.ppermute(value, SEQ, pairs)


def swapped(value, axis, mask):
    return lax.ppermute(value, axis, [(i, i ^ mask) for i in range(lax.axis_size(axis))])


def in_vmem(*arrays):
    return [pltpu.with_memory_space_constraint(array, pltpu.VMEM) for array in arrays]


def in_hbm(*arrays):
    return [pltpu.with_memory_space_constraint(array, pltpu.HBM) for array in arrays]


def dot_t(a, b, dims):
    return lax.dot_general(a, b, (dims, ((), ())), preferred_element_type=jnp.float32)


def attend_kernel(
    q_ref, g_ref, k_ref, v_ref, kv1_ref, kv2_ref, mem_ref, bias_ref, out_ref, gq_ref, stats_ref
):
    rows, width = q_ref.shape
    scaling = HD ** (-0.5)
    bias = bias_ref[...].astype(jnp.float32)
    step = pl.program_id(0)
    heads = [slice(i * HD, (i + 1) * HD) for i in range(width // HD)]
    ks, vs = (
        [
            jnp.concatenate(
                [
                    mem_ref[2 * step + which, :, cols],
                    kv2_ref[which, :, cols],
                    kv1_ref[which, :, cols],
                    own_ref[:, cols],
                ],
                0,
            )
            for cols in heads
        ]
        for which, own_ref in enumerate((k_ref, v_ref))
    )
    scores = [dot_t(q_ref[:, cols], kh, ((1,), (1,))) + bias for cols, kh in zip(heads, ks)]
    dprobs = [dot_t(g_ref[:, cols], vh, ((1,), (1,))) for cols, vh in zip(heads, vs)]
    tops, shares, probs = [], [], []
    for score in scores:
        top = jnp.max(score, axis=-1, keepdims=True)
        weights = jnp.exp((score - top) * scaling)
        share = 1.0 / jnp.sum(weights, axis=-1, keepdims=True)
        tops.append(top)
        shares.append(share)
        probs.append(weights * share)
    outs = [
        dot_t(prob.astype(jnp.bfloat16), vh, ((1,), (0,))).astype(jnp.bfloat16)
        for prob, vh in zip(probs, vs)
    ]
    deltas, dscores = [], []
    for cols, out_b, prob, dprob in zip(heads, outs, probs, dprobs):
        out_ref[:, cols] = out_b
        delta = jnp.sum(
            g_ref[:, cols].astype(jnp.float32) * out_b.astype(jnp.float32), axis=-1, keepdims=True
        )
        deltas.append(delta)
        dscores.append((prob * ((dprob - delta) * scaling)).astype(jnp.bfloat16))
    lane = lax.broadcasted_iota(jnp.int32, (rows, HD), 1)
    stats = jnp.zeros((rows, HD), jnp.float32)
    for i, column in enumerate(tops + shares + deltas):
        stats = jnp.where(lane == i, column, stats)
    stats_ref[0] = stats.T[:STATS]
    for cols, kh, dscore in zip(heads, ks, dscores):
        gq_ref[:, cols] = dot_t(dscore, kh, ((1,), (0,))).astype(jnp.bfloat16)


def attend(queries, grad_out, keys, values, kv1, kv2, memory, bias):
    rows, features = queries.shape
    steps = memory.shape[0] // 2
    slots, block = memory.shape[1:]
    heads = steps * block // HD
    flat = pl.BlockSpec((rows, block), lambda i: (0, i))
    pair = pl.BlockSpec((2, rows, block), lambda i: (0, 0, i))
    whole = pl.BlockSpec(memory_space=pltpu.VMEM)
    keys_all = slots + 3 * rows
    return pl.pallas_call(
        attend_kernel,
        grid=(steps,),
        in_specs=[
            flat, flat, flat, flat, pair, pair, whole,
            pl.BlockSpec((rows, keys_all), lambda i: (0, 0)),
        ],
        out_specs=[flat, flat, pl.BlockSpec((1, STATS, rows), lambda i: (i, 0, 0))],
        out_shape=[
            jax.ShapeDtypeStruct((rows, features), jnp.bfloat16),
            jax.ShapeDtypeStruct((rows, features), jnp.bfloat16),
            jax.ShapeDtypeStruct((steps, STATS, rows), jnp.float32),
        ],
        compiler_params=pltpu.CompilerParams(vmem_limit_bytes=VMEM),
        cost_estimate=pl.CostEstimate(
            flops=2 * 4 * rows * keys_all * HD * heads,
            bytes_accessed=6 * 1024 * 1024,
            transcendentals=rows * keys_all * heads,
        ),
        name="attend",
    )(queries, grad_out, keys, values, *in_hbm(kv1, kv2), *in_vmem(memory), *in_hbm(bias))


def key_grads_kernel(
    k_ref, v_ref, q_ref, g_ref, qg1_ref, qg2_ref, st0_ref, st1_ref, st2_ref, bias_ref,
    gk_ref, gv_ref,
):
    width = k_ref.shape[1]
    scaling = HD ** (-0.5)
    bias = bias_ref[...]
    heads = [slice(i * HD, (i + 1) * HD) for i in range(width // HD)]
    start = pl.program_id(0) * width
    picked = [pl.ds(pl.multiple_of(start + i * HD, HD), HD) for i in range(len(heads))]
    stats = jnp.concatenate([st0_ref[0], st1_ref[0], st2_ref[0]], 1)
    qs = [
        jnp.concatenate([q_ref[:, cols], qg1_ref[0, :, wide], qg2_ref[0, :, wide]], 0)
        for cols, wide in zip(heads, picked)
    ]
    gs = [
        jnp.concatenate([g_ref[:, cols], qg1_ref[1, :, wide], qg2_ref[1, :, wide]], 0)
        for cols, wide in zip(heads, picked)
    ]
    scores = [dot_t(k_ref[:, cols], qh, ((1,), (1,))) + bias for cols, qh in zip(heads, qs)]
    dprobs = [dot_t(v_ref[:, cols], gh, ((1,), (1,))) for cols, gh in zip(heads, gs)]
    probs, dscores = [], []
    for i, (score, dprob) in enumerate(zip(scores, dprobs)):
        top, share, delta = (stats[i + j * len(heads) : i + j * len(heads) + 1] for j in range(3))
        prob = jnp.exp((score - top) * scaling) * share
        probs.append(prob.astype(jnp.bfloat16))
        dscores.append((prob * ((dprob - delta) * scaling)).astype(jnp.bfloat16))
    for cols, qh, gh, prob, dscore in zip(heads, qs, gs, probs, dscores):
        gk_ref[:, cols] = dot_t(dscore, qh, ((1,), (0,))).astype(jnp.bfloat16)
        gv_ref[:, cols] = dot_t(prob, gh, ((1,), (0,))).astype(jnp.bfloat16)


def key_grads(keys, values, queries, grad_out, qg1, qg2, stats, bias):
    rows, features = keys.shape
    steps = stats[0].shape[0]
    block = features // steps
    flat = pl.BlockSpec((rows, block), lambda i: (0, i))
    whole = pl.BlockSpec(memory_space=pltpu.VMEM)
    stat = pl.BlockSpec((1, STATS, rows), lambda i: (i, 0, 0))
    heads = features // HD
    return pl.pallas_call(
        key_grads_kernel,
        grid=(steps,),
        in_specs=[
            flat, flat, flat, flat, whole, whole, stat, stat, stat, whole,
        ],
        out_specs=[flat, flat],
        out_shape=[jax.ShapeDtypeStruct((rows, features), jnp.bfloat16)] * 2,
        compiler_params=pltpu.CompilerParams(vmem_limit_bytes=VMEM),
        cost_estimate=pl.CostEstimate(
            flops=2 * 4 * rows * 3 * rows * HD * heads,
            bytes_accessed=4 * 1024 * 1024,
            transcendentals=rows * 3 * rows * heads,
        ),
        name="key_grads",
    )(keys, values, queries, grad_out, *in_vmem(qg1, qg2), *stats, *in_vmem(bias))


def project_kernel(place_ref, *refs):
    n_z, _, cache_rows = place_ref.shape
    out_ref, w_ref, a_ref = refs[-3:]
    rows, pieces = refs[: 2 * n_z], refs[2 * n_z : -3]
    n_p, (_, w_rows, block) = len(pieces), pieces[0].shape
    depth = rows[0].shape[1]
    devices, _, capacity, _ = out_ref.shape
    z, p, y = (lax.axis_index(name) for name in ("z", "p", "head"))
    place_in_ring = z ^ (z >> 1)
    for i, ref in enumerate(rows):
        source = (place_in_ring - i % n_z + n_z) & (n_z - 1)
        a_ref[y ^ (i // n_z), source ^ (source >> 1)] = ref[...]
    for m in range(n_p):
        for k in range(n_z):
            w_ref[z ^ k, p ^ m] = pieces[m][k]
    half = n_z // 2
    proj = sum(
        jnp.dot(
            a_ref[i].reshape(n_z * cache_rows, depth),
            w_ref[i * half : (i + 1) * half].reshape(depth, block),
            preferred_element_type=jnp.float32,
        )
        for i in range(2)
    ).astype(jnp.bfloat16)
    slot_ids = lax.broadcasted_iota(jnp.int32, (devices * capacity, cache_rows), 0)
    for z in range(n_z):
        chosen = jnp.where(slot_ids == place_ref[z], 1.0, 0.0).astype(jnp.bfloat16)
        slots = jnp.dot(
            chosen,
            proj[z * cache_rows : (z + 1) * cache_rows],
            preferred_element_type=jnp.float32,
        ).astype(jnp.bfloat16)
        out_ref[:, z] = slots.reshape(devices, capacity, block)


def project(place, rows, pieces, devices, capacity):
    n_z, _, cache_rows = place.shape
    depth = rows[0].shape[1]
    n_p = len(pieces)
    _, w_rows, block = pieces[0].shape
    whole = pl.BlockSpec(memory_space=pltpu.VMEM)
    return pl.pallas_call(
        project_kernel,
        in_specs=[whole] * (1 + len(rows) + n_p),
        out_specs=whole,
        out_shape=pltpu.VMEM((devices, n_z, capacity, block), jnp.bfloat16),
        scratch_shapes=[
            pltpu.VMEM((n_z, n_p, w_rows, block), jnp.bfloat16),
            pltpu.VMEM((2, n_z, cache_rows, depth), jnp.bfloat16),
        ],
        compiler_params=pltpu.CompilerParams(vmem_limit_bytes=VMEM),
        cost_estimate=pl.CostEstimate(
            flops=4 * n_z * cache_rows * depth * block,
            bytes_accessed=8 * 1024 * 1024,
            transcendentals=0,
        ),
        name="project",
    )(*in_vmem(place, *rows, *pieces))


def prepare_kernel(routes_ref, ids_ref, place_ref, bias_ref, back_ref):
    n_z, _, rows = place_ref.shape
    devices = routes_ref.shape[0]
    n_p = devices // n_z
    capacity = 2 * rows // devices
    slots = bias_ref.shape[1] - 3 * rows
    p = lax.axis_index("p")
    me = lax.axis_index("z") * n_p + p
    row = lax.broadcasted_iota(jnp.int32, (rows, rows), 0)
    lane = lax.broadcasted_iota(jnp.int32, (rows, rows), 1)

    def both_ways(line):
        wide = jnp.broadcast_to(line.astype(jnp.float32), (rows, rows))
        return wide, wide.T

    for z in range(n_z):
        across, down = both_ways(routes_ref[pl.ds(z * n_p + p, 1), :])
        ranks = jnp.sum(
            jnp.where((across == down) & (row < lane), 1.0, 0.0), axis=0, keepdims=True
        )
        place_ref[z] = (across[:1] * capacity + ranks).astype(jnp.int32)

    def ids_of(segment):
        return ids_ref[pl.ds(jnp.clip(segment, 0, devices - 1), 1), :].astype(jnp.float32)

    _, own = both_ways(ids_ref[pl.ds(me, 1), :])
    for i in range(3):
        earlier, later = me - 2 + i, me + i
        same = (own == ids_of(earlier)) & (earlier >= 0)
        same_back = (own == ids_of(later)) & (later < devices)
        if i == 2:
            same = same & (lane <= row)
        if i == 0:
            same_back = same_back & (lane >= row)
        bias_ref[:, slots + i * rows : slots + (i + 1) * rows] = jnp.where(same, 0.0, -1e30).astype(
            jnp.bfloat16
        )
        back_ref[:, i * rows : (i + 1) * rows] = jnp.where(same_back, 0.0, -1e30)

    mine = jnp.where(routes_ref[...] == me, 1.0, 0.0).astype(jnp.bfloat16)
    counts = dot_t(jnp.ones((8, rows), jnp.bfloat16), mine, ((1,), (1,))).astype(jnp.bfloat16)
    source = lax.broadcasted_iota(jnp.int32, (devices, slots), 0)
    slot = lax.broadcasted_iota(jnp.int32, (devices, slots), 1) // capacity
    expand = jnp.where(source == (slot % n_z) * n_p + slot // n_z, 1.0, 0.0).astype(jnp.bfloat16)
    filled = jnp.dot(counts, expand, preferred_element_type=jnp.float32)[:1]
    rank = lax.broadcasted_iota(jnp.int32, (1, slots), 1) % capacity
    live = jnp.where(rank.astype(jnp.float32) < filled, 0.0, -1e30)
    bias_ref[:, :slots] = jnp.broadcast_to(live, (rows, slots)).astype(jnp.bfloat16)


def prepare(routes, doc_ids, n_z, devices, rows):
    slots = 2 * rows
    return pl.pallas_call(
        prepare_kernel,
        out_shape=[
            jax.ShapeDtypeStruct((n_z, 1, rows), jnp.int32),
            jax.ShapeDtypeStruct((rows, slots + 3 * rows), jnp.bfloat16),
            jax.ShapeDtypeStruct((rows, 3 * rows), jnp.float32),
        ],
        compiler_params=pltpu.CompilerParams(vmem_limit_bytes=SMALL_VMEM),
        name="prepare",
    )(routes.reshape(devices, rows), doc_ids.reshape(devices, rows))


def column_block(w_kv, target):
    _, w_rows, features = w_kv.shape
    half = features // (GROUPS // 2)
    start = (target & 1, 0, (target >> 1) * half)
    return lax.dynamic_slice(w_kv, start, (1, w_rows, half))[0]


def ring_step(value, back=False):
    pairs = list(zip(RING, RING[1:] + RING[:1]))
    return lax.ppermute(value, "z", [(b, a) for a, b in pairs] if back else pairs)


def memory_slots(cache, w_kv, place, capacity, stream, back):
    n_z, n_p = lax.axis_size("z"), lax.axis_size("p")
    devices = n_z * n_p
    cache_rows, depth = cache.shape
    _, w_rows, features = w_kv.shape
    z = lax.axis_index("z")
    if n_p == 4 and capacity % ROW_TILE == 0 and w_rows % ROW_TILE == 0:
        blocks = [column_block(w_kv, z ^ mask) for mask in range(n_z)]
        own = jnp.stack(
            [blocks[0]] + [swapped(blocks[mask], "z", mask) for mask in range(1, n_z)], 0
        )
        row1, other0 = ring_step(cache), swapped(cache, "head", 1)
        own, row1, other0, cache = lax.optimization_barrier((own, row1, other0, cache))
        across = swapped(own, "p", 2)
        beside = swapped(own, "p", 1)
        row2, row3, other1 = ring_step(row1), ring_step(cache, back=True), swapped(row1, "head", 1)
        beside, stream, back = lax.optimization_barrier((beside, stream, back))
        near, back1 = shifted(stream, 1), shifted(back, -1)
        row2, row3, other1 = lax.optimization_barrier((row2, row3, other1))
        other2, other3 = swapped(row2, "head", 1), swapped(row3, "head", 1)
        across, other2, other3, near, back1 = lax.optimization_barrier(
            (across, other2, other3, near, back1)
        )
        pieces = [own, beside, across, swapped(across, "p", 1)]
        far = shifted(near, 1)
        rows = [cache, row1, row2, row3, other0, other1, other2, other3]
        slots = project(place, rows, pieces, devices, capacity)
        slots, far = lax.optimization_barrier((slots, far))
        return slots, near, far, back1
    near, back1 = shifted(stream, 1), shifted(back, -1)
    far = shifted(near, 1)
    targets = [column_block(w_kv, jnp.int32(i)) for i in range(n_z)]
    w_z = lax.all_to_all(jnp.stack(targets, 0), "z", split_axis=0, concat_axis=0, tiled=True)
    w_all = lax.all_gather(w_z, "p", axis=1, tiled=True).reshape(devices * w_rows, -1)
    rows = lax.all_gather(cache, ("head", "z"), axis=0, tiled=False)
    rows = rows.reshape(-1, n_z * cache_rows, depth)
    proj = sum(
        jnp.dot(
            rows[i], w_all[i * depth : (i + 1) * depth], preferred_element_type=jnp.float32
        )
        for i in range(rows.shape[0])
    ).astype(jnp.bfloat16)
    slot_ids = jnp.arange(devices * capacity, dtype=jnp.int32)
    chosen = (slot_ids[None, :, None] == place).astype(jnp.bfloat16)
    slots = jnp.einsum(
        "zsi,zic->zsc",
        chosen,
        proj.reshape(n_z, cache_rows, -1),
        preferred_element_type=jnp.float32,
    ).astype(jnp.bfloat16)
    slots = slots.reshape(n_z, devices, capacity, -1).transpose(1, 0, 2, 3)
    return slots, near, far, back1


def body(queries, keys, values, grad_out, cache, w_kv, doc_ids, routes):
    n_z, n_p = lax.axis_size("z"), lax.axis_size("p")
    devices = n_z * n_p
    seg_rows = queries.shape[0]
    cache_rows = cache.shape[0]
    capacity = 2 * cache_rows // devices
    slot_count = capacity * devices

    place, bias, back_bias = prepare(routes, doc_ids, n_z, devices, seg_rows)
    slots, kv1, kv2, qg1 = memory_slots(
        cache,
        w_kv,
        place,
        capacity,
        jnp.stack([keys, values], 0),
        jnp.stack([queries, grad_out], 0),
    )
    memory = lax.all_to_all(slots, SEQ, split_axis=0, concat_axis=0, tiled=True)
    memory = memory.reshape(n_z, slot_count, slots.shape[-1])

    qg2 = shifted(qg1, -1)
    output, grad_q, stats = attend(queries, grad_out, keys, values, kv1, kv2, memory, bias)
    all_stats = [stats, shifted(stats, -1), shifted(stats, -2)]
    grad_k, grad_v = key_grads(
        keys, values, queries, grad_out, qg1, qg2, all_stats, back_bias
    )
    return (output, grad_q, grad_k, grad_v)


def solution(mesh):
    n_seq, n_head = mesh.devices.shape
    grid = Mesh(mesh.devices.reshape(GROUPS, n_seq // GROUPS, n_head), ("z", "p", "head"))
    rows = P(SEQ, "head")
    return jax.shard_map(
        body,
        mesh=grid,
        in_specs=(rows, rows, rows, rows, rows, P(None, SEQ, "head"), P(), P()),
        out_specs=(rows, rows, rows, rows),
        check_vma=False,
    )
```

```python
import jax
import jax.numpy as jnp
from jax import lax
from jax.experimental import pallas as pl
from jax.experimental.pallas import tpu as pltpu
from jax.sharding import Mesh, PartitionSpec as P

HD = 128
GROUPS = 4
SEQ = ("z", "p")
ROW_TILE = 16
RING = [0, 1, 3, 2]
VMEM = 24 * 1024 * 1024
SMALL_VMEM = 4 * 1024 * 1024
STATS = 16


def shifted(value, by):
    length = lax.axis_size("z") * lax.axis_size("p")
    pairs = [(i, i + by) for i in range(length) if 0 <= i + by < length]
    return lax.ppermute(value, SEQ, pairs)


def swapped(value, axis, mask):
    return lax.ppermute(value, axis, [(i, i ^ mask) for i in range(lax.axis_size(axis))])


def in_vmem(*arrays):
    return [pltpu.with_memory_space_constraint(array, pltpu.VMEM) for array in arrays]


def in_hbm(*arrays):
    return [pltpu.with_memory_space_constraint(array, pltpu.HBM) for array in arrays]


def dot_t(a, b, dims):
    return lax.dot_general(a, b, (dims, ((), ())), preferred_element_type=jnp.float32)


def attend_kernel(
    q_ref, g_ref, k_ref, v_ref, kv1_ref, kv2_ref, mem_ref, bias_ref, out_ref, gq_ref, stats_ref
):
    rows, width = q_ref.shape
    scaling = HD ** (-0.5)
    bias = bias_ref[...].astype(jnp.float32)
    step = pl.program_id(0)
    heads = [slice(i * HD, (i + 1) * HD) for i in range(width // HD)]
    ks, vs = (
        [
            jnp.concatenate(
                [
                    mem_ref[2 * step + which, :, cols],
                    kv2_ref[which, :, cols],
                    kv1_ref[which, :, cols],
                    own_ref[:, cols],
                ],
                0,
            )
            for cols in heads
        ]
        for which, own_ref in enumerate((k_ref, v_ref))
    )
    scores = [dot_t(q_ref[:, cols], kh, ((1,), (1,))) + bias for cols, kh in zip(heads, ks)]
    dprobs = [dot_t(g_ref[:, cols], vh, ((1,), (1,))) for cols, vh in zip(heads, vs)]
    tops, shares, probs = [], [], []
    for score in scores:
        top = jnp.max(score, axis=-1, keepdims=True)
        weights = jnp.exp((score - top) * scaling)
        share = 1.0 / jnp.sum(weights, axis=-1, keepdims=True)
        tops.append(top)
        shares.append(share)
        probs.append(weights * share)
    outs = [
        dot_t(prob.astype(jnp.bfloat16), vh, ((1,), (0,))).astype(jnp.bfloat16)
        for prob, vh in zip(probs, vs)
    ]
    deltas, dscores = [], []
    for cols, out_b, prob, dprob in zip(heads, outs, probs, dprobs):
        out_ref[:, cols] = out_b
        delta = jnp.sum(
            g_ref[:, cols].astype(jnp.float32) * out_b.astype(jnp.float32), axis=-1, keepdims=True
        )
        deltas.append(delta)
        dscores.append((prob * ((dprob - delta) * scaling)).astype(jnp.bfloat16))
    lane = lax.broadcasted_iota(jnp.int32, (rows, HD), 1)
    stats = jnp.zeros((rows, HD), jnp.float32)
    for i, column in enumerate(tops + shares + deltas):
        stats = jnp.where(lane == i, column, stats)
    stats_ref[0] = stats.T[:STATS]
    for cols, kh, dscore in zip(heads, ks, dscores):
        gq_ref[:, cols] = dot_t(dscore, kh, ((1,), (0,))).astype(jnp.bfloat16)


def attend(queries, grad_out, keys, values, kv1, kv2, memory, bias):
    rows, features = queries.shape
    steps = memory.shape[0] // 2
    slots, block = memory.shape[1:]
    heads = steps * block // HD
    flat = pl.BlockSpec((rows, block), lambda i: (0, i))
    pair = pl.BlockSpec((2, rows, block), lambda i: (0, 0, i))
    whole = pl.BlockSpec(memory_space=pltpu.VMEM)
    keys_all = slots + 3 * rows
    return pl.pallas_call(
        attend_kernel,
        grid=(steps,),
        in_specs=[
            flat, flat, flat, flat, pair, pair, whole,
            pl.BlockSpec((rows, keys_all), lambda i: (0, 0)),
        ],
        out_specs=[flat, flat, pl.BlockSpec((1, STATS, rows), lambda i: (i, 0, 0))],
        out_shape=[
            jax.ShapeDtypeStruct((rows, features), jnp.bfloat16),
            jax.ShapeDtypeStruct((rows, features), jnp.bfloat16),
            jax.ShapeDtypeStruct((steps, STATS, rows), jnp.float32),
        ],
        compiler_params=pltpu.CompilerParams(vmem_limit_bytes=VMEM),
        cost_estimate=pl.CostEstimate(
            flops=2 * 4 * rows * keys_all * HD * heads,
            bytes_accessed=6 * 1024 * 1024,
            transcendentals=rows * keys_all * heads,
        ),
        name="attend",
    )(queries, grad_out, keys, values, *in_hbm(kv1, kv2), *in_vmem(memory), *in_hbm(bias))


def key_grads_kernel(
    k_ref, v_ref, q_ref, g_ref, qg1_ref, qg2_ref, st0_ref, st1_ref, st2_ref, bias_ref,
    gk_ref, gv_ref,
):
    width = k_ref.shape[1]
    scaling = HD ** (-0.5)
    bias = bias_ref[...]
    heads = [slice(i * HD, (i + 1) * HD) for i in range(width // HD)]
    start = pl.program_id(0) * width
    picked = [pl.ds(pl.multiple_of(start + i * HD, HD), HD) for i in range(len(heads))]
    stats = jnp.concatenate([st0_ref[0], st1_ref[0], st2_ref[0]], 1)
    qs = [
        jnp.concatenate([q_ref[:, cols], qg1_ref[0, :, wide], qg2_ref[0, :, wide]], 0)
        for cols, wide in zip(heads, picked)
    ]
    gs = [
        jnp.concatenate([g_ref[:, cols], qg1_ref[1, :, wide], qg2_ref[1, :, wide]], 0)
        for cols, wide in zip(heads, picked)
    ]
    scores = [dot_t(k_ref[:, cols], qh, ((1,), (1,))) + bias for cols, qh in zip(heads, qs)]
    dprobs = [dot_t(v_ref[:, cols], gh, ((1,), (1,))) for cols, gh in zip(heads, gs)]
    probs, dscores = [], []
    for i, (score, dprob) in enumerate(zip(scores, dprobs)):
        top, share, delta = (stats[i + j * len(heads) : i + j * len(heads) + 1] for j in range(3))
        prob = jnp.exp((score - top) * scaling) * share
        probs.append(prob.astype(jnp.bfloat16))
        dscores.append((prob * ((dprob - delta) * scaling)).astype(jnp.bfloat16))
    for cols, qh, gh, prob, dscore in zip(heads, qs, gs, probs, dscores):
        gk_ref[:, cols] = dot_t(dscore, qh, ((1,), (0,))).astype(jnp.bfloat16)
        gv_ref[:, cols] = dot_t(prob, gh, ((1,), (0,))).astype(jnp.bfloat16)


def key_grads(keys, values, queries, grad_out, qg1, qg2, stats, bias):
    rows, features = keys.shape
    steps = stats[0].shape[0]
    block = features // steps
    flat = pl.BlockSpec((rows, block), lambda i: (0, i))
    whole = pl.BlockSpec(memory_space=pltpu.VMEM)
    stat = pl.BlockSpec((1, STATS, rows), lambda i: (i, 0, 0))
    heads = features // HD
    return pl.pallas_call(
        key_grads_kernel,
        grid=(steps,),
        in_specs=[
            flat, flat, flat, flat, whole, whole, stat, stat, stat, whole,
        ],
        out_specs=[flat, flat],
        out_shape=[jax.ShapeDtypeStruct((rows, features), jnp.bfloat16)] * 2,
        compiler_params=pltpu.CompilerParams(vmem_limit_bytes=VMEM),
        cost_estimate=pl.CostEstimate(
            flops=2 * 4 * rows * 3 * rows * HD * heads,
            bytes_accessed=4 * 1024 * 1024,
            transcendentals=rows * 3 * rows * heads,
        ),
        name="key_grads",
    )(keys, values, queries, grad_out, *in_vmem(qg1, qg2), *stats, *in_vmem(bias))


def project_kernel(place_ref, *refs):
    n_z, _, cache_rows = place_ref.shape
    out_ref, w_ref, a_ref = refs[-3:]
    rows, pieces = refs[: 2 * n_z], refs[2 * n_z : -3]
    n_p, (_, w_rows, block) = len(pieces), pieces[0].shape
    depth = rows[0].shape[1]
    devices, _, capacity, _ = out_ref.shape
    z, p, y = (lax.axis_index(name) for name in ("z", "p", "head"))
    place_in_ring = z ^ (z >> 1)
    for i, ref in enumerate(rows):
        source = (place_in_ring - i % n_z + n_z) & (n_z - 1)
        a_ref[y ^ (i // n_z), source ^ (source >> 1)] = ref[...]
    for m in range(n_p):
        for k in range(n_z):
            w_ref[z ^ k, p ^ m] = pieces[m][k]
    half = n_z // 2
    proj = sum(
        jnp.dot(
            a_ref[i].reshape(n_z * cache_rows, depth),
            w_ref[i * half : (i + 1) * half].reshape(depth, block),
            preferred_element_type=jnp.float32,
        )
        for i in range(2)
    ).astype(jnp.bfloat16)
    slot_ids = lax.broadcasted_iota(jnp.int32, (devices * capacity, cache_rows), 0)
    for z in range(n_z):
        chosen = jnp.where(slot_ids == place_ref[z], 1.0, 0.0).astype(jnp.bfloat16)
        slots = jnp.dot(
            chosen,
            proj[z * cache_rows : (z + 1) * cache_rows],
            preferred_element_type=jnp.float32,
        ).astype(jnp.bfloat16)
        out_ref[:, z] = slots.reshape(devices, capacity, block)


def project(place, rows, pieces, devices, capacity):
    n_z, _, cache_rows = place.shape
    depth = rows[0].shape[1]
    n_p = len(pieces)
    _, w_rows, block = pieces[0].shape
    whole = pl.BlockSpec(memory_space=pltpu.VMEM)
    return pl.pallas_call(
        project_kernel,
        in_specs=[whole] * (1 + len(rows) + n_p),
        out_specs=whole,
        out_shape=pltpu.VMEM((devices, n_z, capacity, block), jnp.bfloat16),
        scratch_shapes=[
            pltpu.VMEM((n_z, n_p, w_rows, block), jnp.bfloat16),
            pltpu.VMEM((2, n_z, cache_rows, depth), jnp.bfloat16),
        ],
        compiler_params=pltpu.CompilerParams(vmem_limit_bytes=VMEM),
        cost_estimate=pl.CostEstimate(
            flops=4 * n_z * cache_rows * depth * block,
            bytes_accessed=8 * 1024 * 1024,
            transcendentals=0,
        ),
        name="project",
    )(*in_vmem(place, *rows, *pieces))


def prepare_kernel(routes_ref, ids_ref, place_ref, bias_ref, back_ref):
    n_z, _, rows = place_ref.shape
    devices = routes_ref.shape[0]
    n_p = devices // n_z
    capacity = 2 * rows // devices
    slots = bias_ref.shape[1] - 3 * rows
    p = lax.axis_index("p")
    me = lax.axis_index("z") * n_p + p
    row = lax.broadcasted_iota(jnp.int32, (rows, rows), 0)
    lane = lax.broadcasted_iota(jnp.int32, (rows, rows), 1)

    def both_ways(line):
        wide = jnp.broadcast_to(line.astype(jnp.float32), (rows, rows))
        return wide, wide.T

    for z in range(n_z):
        across, down = both_ways(routes_ref[pl.ds(z * n_p + p, 1), :])
        ranks = jnp.sum(
            jnp.where((across == down) & (row < lane), 1.0, 0.0), axis=0, keepdims=True
        )
        place_ref[z] = (across[:1] * capacity + ranks).astype(jnp.int32)

    def ids_of(segment):
        return ids_ref[pl.ds(jnp.clip(segment, 0, devices - 1), 1), :].astype(jnp.float32)

    _, own = both_ways(ids_ref[pl.ds(me, 1), :])
    for i in range(3):
        earlier, later = me - 2 + i, me + i
        same = (own == ids_of(earlier)) & (earlier >= 0)
        same_back = (own == ids_of(later)) & (later < devices)
        if i == 2:
            same = same & (lane <= row)
        if i == 0:
            same_back = same_back & (lane >= row)
        bias_ref[:, slots + i * rows : slots + (i + 1) * rows] = jnp.where(same, 0.0, -1e30).astype(
            jnp.bfloat16
        )
        back_ref[:, i * rows : (i + 1) * rows] = jnp.where(same_back, 0.0, -1e30)

    mine = jnp.where(routes_ref[...] == me, 1.0, 0.0).astype(jnp.bfloat16)
    counts = dot_t(jnp.ones((8, rows), jnp.bfloat16), mine, ((1,), (1,))).astype(jnp.bfloat16)
    source = lax.broadcasted_iota(jnp.int32, (devices, slots), 0)
    slot = lax.broadcasted_iota(jnp.int32, (devices, slots), 1) // capacity
    expand = jnp.where(source == (slot % n_z) * n_p + slot // n_z, 1.0, 0.0).astype(jnp.bfloat16)
    filled = jnp.dot(counts, expand, preferred_element_type=jnp.float32)[:1]
    rank = lax.broadcasted_iota(jnp.int32, (1, slots), 1) % capacity
    live = jnp.where(rank.astype(jnp.float32) < filled, 0.0, -1e30)
    bias_ref[:, :slots] = jnp.broadcast_to(live, (rows, slots)).astype(jnp.bfloat16)


def prepare(routes, doc_ids, n_z, devices, rows):
    slots = 2 * rows
    return pl.pallas_call(
        prepare_kernel,
        out_shape=[
            jax.ShapeDtypeStruct((n_z, 1, rows), jnp.int32),
            jax.ShapeDtypeStruct((rows, slots + 3 * rows), jnp.bfloat16),
            jax.ShapeDtypeStruct((rows, 3 * rows), jnp.float32),
        ],
        compiler_params=pltpu.CompilerParams(vmem_limit_bytes=SMALL_VMEM),
        name="prepare",
    )(routes.reshape(devices, rows), doc_ids.reshape(devices, rows))


def column_block(w_kv, target):
    _, w_rows, features = w_kv.shape
    half = features // (GROUPS // 2)
    start = (target & 1, 0, (target >> 1) * half)
    return lax.dynamic_slice(w_kv, start, (1, w_rows, half))[0]


def ring_step(value, back=False):
    pairs = list(zip(RING, RING[1:] + RING[:1]))
    return lax.ppermute(value, "z", [(b, a) for a, b in pairs] if back else pairs)


def memory_slots(cache, w_kv, place, capacity, stream, back):
    n_z, n_p = lax.axis_size("z"), lax.axis_size("p")
    devices = n_z * n_p
    cache_rows, depth = cache.shape
    _, w_rows, features = w_kv.shape
    z = lax.axis_index("z")
    if n_p == 4 and capacity % ROW_TILE == 0 and w_rows % ROW_TILE == 0:
        blocks = [column_block(w_kv, z ^ mask) for mask in range(n_z)]
        own = jnp.stack(
            [blocks[0]] + [swapped(blocks[mask], "z", mask) for mask in range(1, n_z)], 0
        )
        other0 = swapped(cache, "head", 1)
        own, other0, cache = lax.optimization_barrier((own, other0, cache))
        across, beside = swapped(own, "p", 2), swapped(own, "p", 1)
        row1, row3 = ring_step(cache), ring_step(cache, back=True)
        beside, stream, back = lax.optimization_barrier((beside, stream, back))
        near, back1 = shifted(stream, 1), shifted(back, -1)
        row1, row3 = lax.optimization_barrier((row1, row3))
        row2 = ring_step(row1)
        others13 = swapped(jnp.stack([row1, row3], 0), "head", 1)
        row2 = lax.optimization_barrier(row2)
        other2 = swapped(row2, "head", 1)
        across, others13, other2, near, back1 = lax.optimization_barrier(
            (across, others13, other2, near, back1)
        )
        pieces = [own, beside, across, swapped(across, "p", 1)]
        far = shifted(near, 1)
        rows = [cache, row1, row2, row3, other0, others13[0], other2, others13[1]]
        slots = project(place, rows, pieces, devices, capacity)
        slots, far = lax.optimization_barrier((slots, far))
        return slots, near, far, back1
    near, back1 = shifted(stream, 1), shifted(back, -1)
    far = shifted(near, 1)
    targets = [column_block(w_kv, jnp.int32(i)) for i in range(n_z)]
    w_z = lax.all_to_all(jnp.stack(targets, 0), "z", split_axis=0, concat_axis=0, tiled=True)
    w_all = lax.all_gather(w_z, "p", axis=1, tiled=True).reshape(devices * w_rows, -1)
    rows = lax.all_gather(cache, ("head", "z"), axis=0, tiled=False)
    rows = rows.reshape(-1, n_z * cache_rows, depth)
    proj = sum(
        jnp.dot(
            rows[i], w_all[i * depth : (i + 1) * depth], preferred_element_type=jnp.float32
        )
        for i in range(rows.shape[0])
    ).astype(jnp.bfloat16)
    slot_ids = jnp.arange(devices * capacity, dtype=jnp.int32)
    chosen = (slot_ids[None, :, None] == place).astype(jnp.bfloat16)
    slots = jnp.einsum(
        "zsi,zic->zsc",
        chosen,
        proj.reshape(n_z, cache_rows, -1),
        preferred_element_type=jnp.float32,
    ).astype(jnp.bfloat16)
    slots = slots.reshape(n_z, devices, capacity, -1).transpose(1, 0, 2, 3)
    return slots, near, far, back1


def body(queries, keys, values, grad_out, cache, w_kv, doc_ids, routes):
    n_z, n_p = lax.axis_size("z"), lax.axis_size("p")
    devices = n_z * n_p
    seg_rows = queries.shape[0]
    cache_rows = cache.shape[0]
    capacity = 2 * cache_rows // devices
    slot_count = capacity * devices

    place, bias, back_bias = prepare(routes, doc_ids, n_z, devices, seg_rows)
    slots, kv1, kv2, qg1 = memory_slots(
        cache,
        w_kv,
        place,
        capacity,
        jnp.stack([keys, values], 0),
        jnp.stack([queries, grad_out], 0),
    )
    memory = lax.all_to_all(slots, SEQ, split_axis=0, concat_axis=0, tiled=True)
    memory = memory.reshape(n_z, slot_count, slots.shape[-1])

    qg2 = shifted(qg1, -1)
    output, grad_q, stats = attend(queries, grad_out, keys, values, kv1, kv2, memory, bias)
    all_stats = [stats, shifted(stats, -1), shifted(stats, -2)]
    grad_k, grad_v = key_grads(
        keys, values, queries, grad_out, qg1, qg2, all_stats, back_bias
    )
    return (output, grad_q, grad_k, grad_v)


def solution(mesh):
    n_seq, n_head = mesh.devices.shape
    grid = Mesh(mesh.devices.reshape(GROUPS, n_seq // GROUPS, n_head), ("z", "p", "head"))
    rows = P(SEQ, "head")
    return jax.shard_map(
        body,
        mesh=grid,
        in_specs=(rows, rows, rows, rows, rows, P(None, SEQ, "head"), P(), P()),
        out_specs=(rows, rows, rows, rows),
        check_vma=False,
    )
```

```python
import jax
import jax.numpy as jnp
from jax import lax
from jax.experimental import pallas as pl
from jax.experimental.pallas import tpu as pltpu
from jax.sharding import Mesh, PartitionSpec as P

HD = 128
GROUPS = 4
SEQ = ("z", "p")
ROW_TILE = 16
RING = [0, 1, 3, 2]
VMEM = 24 * 1024 * 1024
SMALL_VMEM = 4 * 1024 * 1024
STATS = 16


def shifted(value, by):
    length = lax.axis_size("z") * lax.axis_size("p")
    pairs = [(i, i + by) for i in range(length) if 0 <= i + by < length]
    return lax.ppermute(value, SEQ, pairs)


def swapped(value, axis, mask):
    return lax.ppermute(value, axis, [(i, i ^ mask) for i in range(lax.axis_size(axis))])


def in_vmem(*arrays):
    return [pltpu.with_memory_space_constraint(array, pltpu.VMEM) for array in arrays]


def in_hbm(*arrays):
    return [pltpu.with_memory_space_constraint(array, pltpu.HBM) for array in arrays]


def dot_t(a, b, dims):
    return lax.dot_general(a, b, (dims, ((), ())), preferred_element_type=jnp.float32)


def attend_kernel(
    q_ref, g_ref, k_ref, v_ref, kv1_ref, kv2_ref, mem_ref, bias_ref, out_ref, gq_ref, stats_ref
):
    rows, width = q_ref.shape
    scaling = HD ** (-0.5)
    bias = bias_ref[...].astype(jnp.float32)
    step = pl.program_id(0)
    heads = [slice(i * HD, (i + 1) * HD) for i in range(width // HD)]
    ks, vs = (
        [
            jnp.concatenate(
                [
                    mem_ref[2 * step + which, :, cols],
                    kv2_ref[which, :, cols],
                    kv1_ref[which, :, cols],
                    own_ref[:, cols],
                ],
                0,
            )
            for cols in heads
        ]
        for which, own_ref in enumerate((k_ref, v_ref))
    )
    scores = [dot_t(q_ref[:, cols], kh, ((1,), (1,))) + bias for cols, kh in zip(heads, ks)]
    dprobs = [dot_t(g_ref[:, cols], vh, ((1,), (1,))) for cols, vh in zip(heads, vs)]
    tops, shares, probs = [], [], []
    for score in scores:
        top = jnp.max(score, axis=-1, keepdims=True)
        weights = jnp.exp((score - top) * scaling)
        share = 1.0 / jnp.sum(weights, axis=-1, keepdims=True)
        tops.append(top)
        shares.append(share)
        probs.append(weights * share)
    outs = [
        dot_t(prob.astype(jnp.bfloat16), vh, ((1,), (0,))).astype(jnp.bfloat16)
        for prob, vh in zip(probs, vs)
    ]
    deltas, dscores = [], []
    for cols, out_b, prob, dprob in zip(heads, outs, probs, dprobs):
        out_ref[:, cols] = out_b
        delta = jnp.sum(
            g_ref[:, cols].astype(jnp.float32) * out_b.astype(jnp.float32), axis=-1, keepdims=True
        )
        deltas.append(delta)
        dscores.append((prob * ((dprob - delta) * scaling)).astype(jnp.bfloat16))
    lane = lax.broadcasted_iota(jnp.int32, (rows, HD), 1)
    stats = jnp.zeros((rows, HD), jnp.float32)
    for i, column in enumerate(tops + shares + deltas):
        stats = jnp.where(lane == i, column, stats)
    stats_ref[0] = stats.T[:STATS]
    for cols, kh, dscore in zip(heads, ks, dscores):
        gq_ref[:, cols] = dot_t(dscore, kh, ((1,), (0,))).astype(jnp.bfloat16)


def attend(queries, grad_out, keys, values, kv1, kv2, memory, bias):
    rows, features = queries.shape
    steps = memory.shape[0] // 2
    slots, block = memory.shape[1:]
    heads = steps * block // HD
    flat = pl.BlockSpec((rows, block), lambda i: (0, i))
    pair = pl.BlockSpec((2, rows, block), lambda i: (0, 0, i))
    whole = pl.BlockSpec(memory_space=pltpu.VMEM)
    keys_all = slots + 3 * rows
    return pl.pallas_call(
        attend_kernel,
        grid=(steps,),
        in_specs=[
            flat, flat, flat, flat, pair, pair, whole,
            pl.BlockSpec((rows, keys_all), lambda i: (0, 0)),
        ],
        out_specs=[flat, flat, pl.BlockSpec((1, STATS, rows), lambda i: (i, 0, 0))],
        out_shape=[
            jax.ShapeDtypeStruct((rows, features), jnp.bfloat16),
            jax.ShapeDtypeStruct((rows, features), jnp.bfloat16),
            jax.ShapeDtypeStruct((steps, STATS, rows), jnp.float32),
        ],
        compiler_params=pltpu.CompilerParams(vmem_limit_bytes=VMEM),
        cost_estimate=pl.CostEstimate(
            flops=2 * 4 * rows * keys_all * HD * heads,
            bytes_accessed=6 * 1024 * 1024,
            transcendentals=rows * keys_all * heads,
        ),
        name="attend",
    )(queries, grad_out, keys, values, *in_hbm(kv1, kv2), *in_vmem(memory), *in_hbm(bias))


def key_grads_kernel(
    k_ref, v_ref, q_ref, g_ref, qg1_ref, qg2_ref, st0_ref, st1_ref, st2_ref, bias_ref,
    gk_ref, gv_ref,
):
    width = k_ref.shape[1]
    scaling = HD ** (-0.5)
    bias = bias_ref[...]
    heads = [slice(i * HD, (i + 1) * HD) for i in range(width // HD)]
    start = pl.program_id(0) * width
    picked = [pl.ds(pl.multiple_of(start + i * HD, HD), HD) for i in range(len(heads))]
    stats = jnp.concatenate([st0_ref[0], st1_ref[0], st2_ref[0]], 1)
    qs = [
        jnp.concatenate([q_ref[:, cols], qg1_ref[0, :, wide], qg2_ref[0, :, wide]], 0)
        for cols, wide in zip(heads, picked)
    ]
    gs = [
        jnp.concatenate([g_ref[:, cols], qg1_ref[1, :, wide], qg2_ref[1, :, wide]], 0)
        for cols, wide in zip(heads, picked)
    ]
    scores = [dot_t(k_ref[:, cols], qh, ((1,), (1,))) + bias for cols, qh in zip(heads, qs)]
    dprobs = [dot_t(v_ref[:, cols], gh, ((1,), (1,))) for cols, gh in zip(heads, gs)]
    probs, dscores = [], []
    for i, (score, dprob) in enumerate(zip(scores, dprobs)):
        top, share, delta = (stats[i + j * len(heads) : i + j * len(heads) + 1] for j in range(3))
        prob = jnp.exp((score - top) * scaling) * share
        probs.append(prob.astype(jnp.bfloat16))
        dscores.append((prob * ((dprob - delta) * scaling)).astype(jnp.bfloat16))
    for cols, qh, gh, prob, dscore in zip(heads, qs, gs, probs, dscores):
        gk_ref[:, cols] = dot_t(dscore, qh, ((1,), (0,))).astype(jnp.bfloat16)
        gv_ref[:, cols] = dot_t(prob, gh, ((1,), (0,))).astype(jnp.bfloat16)


def key_grads(keys, values, queries, grad_out, qg1, qg2, stats, bias):
    rows, features = keys.shape
    steps = stats[0].shape[0]
    block = features // steps
    flat = pl.BlockSpec((rows, block), lambda i: (0, i))
    whole = pl.BlockSpec(memory_space=pltpu.VMEM)
    stat = pl.BlockSpec((1, STATS, rows), lambda i: (i, 0, 0))
    heads = features // HD
    return pl.pallas_call(
        key_grads_kernel,
        grid=(steps,),
        in_specs=[
            flat, flat, flat, flat, whole, whole, stat, stat, stat, whole,
        ],
        out_specs=[flat, flat],
        out_shape=[jax.ShapeDtypeStruct((rows, features), jnp.bfloat16)] * 2,
        compiler_params=pltpu.CompilerParams(vmem_limit_bytes=VMEM),
        cost_estimate=pl.CostEstimate(
            flops=2 * 4 * rows * 3 * rows * HD * heads,
            bytes_accessed=4 * 1024 * 1024,
            transcendentals=rows * 3 * rows * heads,
        ),
        name="key_grads",
    )(keys, values, queries, grad_out, *in_vmem(qg1, qg2), *stats, *in_vmem(bias))


def project_kernel(place_ref, *refs):
    n_z, _, cache_rows = place_ref.shape
    out_ref, w_ref, a_ref = refs[-3:]
    rows, pieces = refs[: 2 * n_z], refs[2 * n_z : -3]
    n_p, (_, w_rows, block) = len(pieces), pieces[0].shape
    depth = rows[0].shape[1]
    devices, _, capacity, _ = out_ref.shape
    z, p, y = (lax.axis_index(name) for name in ("z", "p", "head"))
    place_in_ring = z ^ (z >> 1)
    for i, ref in enumerate(rows):
        source = (place_in_ring - i % n_z + n_z) & (n_z - 1)
        a_ref[y ^ (i // n_z), source ^ (source >> 1)] = ref[...]
    for m in range(n_p):
        for k in range(n_z):
            w_ref[z ^ k, p ^ m] = pieces[m][k]
    half = n_z // 2
    proj = sum(
        jnp.dot(
            a_ref[i].reshape(n_z * cache_rows, depth),
            w_ref[i * half : (i + 1) * half].reshape(depth, block),
            preferred_element_type=jnp.float32,
        )
        for i in range(2)
    ).astype(jnp.bfloat16)
    slot_ids = lax.broadcasted_iota(jnp.int32, (devices * capacity, cache_rows), 0)
    for z in range(n_z):
        chosen = jnp.where(slot_ids == place_ref[z], 1.0, 0.0).astype(jnp.bfloat16)
        slots = jnp.dot(
            chosen,
            proj[z * cache_rows : (z + 1) * cache_rows],
            preferred_element_type=jnp.float32,
        ).astype(jnp.bfloat16)
        out_ref[:, z] = slots.reshape(devices, capacity, block)


def project(place, rows, pieces, devices, capacity):
    n_z, _, cache_rows = place.shape
    depth = rows[0].shape[1]
    n_p = len(pieces)
    _, w_rows, block = pieces[0].shape
    whole = pl.BlockSpec(memory_space=pltpu.VMEM)
    return pl.pallas_call(
        project_kernel,
        in_specs=[whole] * (1 + len(rows) + n_p),
        out_specs=whole,
        out_shape=pltpu.VMEM((devices, n_z, capacity, block), jnp.bfloat16),
        scratch_shapes=[
            pltpu.VMEM((n_z, n_p, w_rows, block), jnp.bfloat16),
            pltpu.VMEM((2, n_z, cache_rows, depth), jnp.bfloat16),
        ],
        compiler_params=pltpu.CompilerParams(vmem_limit_bytes=VMEM),
        cost_estimate=pl.CostEstimate(
            flops=4 * n_z * cache_rows * depth * block,
            bytes_accessed=8 * 1024 * 1024,
            transcendentals=0,
        ),
        name="project",
    )(*in_vmem(place, *rows, *pieces))


def prepare_kernel(routes_ref, ids_ref, place_ref, bias_ref, back_ref):
    n_z, _, rows = place_ref.shape
    devices = routes_ref.shape[0]
    n_p = devices // n_z
    capacity = 2 * rows // devices
    slots = bias_ref.shape[1] - 3 * rows
    p = lax.axis_index("p")
    me = lax.axis_index("z") * n_p + p
    row = lax.broadcasted_iota(jnp.int32, (rows, rows), 0)
    lane = lax.broadcasted_iota(jnp.int32, (rows, rows), 1)

    def both_ways(line):
        wide = jnp.broadcast_to(line.astype(jnp.float32), (rows, rows))
        return wide, wide.T

    for z in range(n_z):
        across, down = both_ways(routes_ref[pl.ds(z * n_p + p, 1), :])
        ranks = jnp.sum(
            jnp.where((across == down) & (row < lane), 1.0, 0.0), axis=0, keepdims=True
        )
        place_ref[z] = (across[:1] * capacity + ranks).astype(jnp.int32)

    def ids_of(segment):
        return ids_ref[pl.ds(jnp.clip(segment, 0, devices - 1), 1), :].astype(jnp.float32)

    _, own = both_ways(ids_ref[pl.ds(me, 1), :])
    for i in range(3):
        earlier, later = me - 2 + i, me + i
        same = (own == ids_of(earlier)) & (earlier >= 0)
        same_back = (own == ids_of(later)) & (later < devices)
        if i == 2:
            same = same & (lane <= row)
        if i == 0:
            same_back = same_back & (lane >= row)
        bias_ref[:, slots + i * rows : slots + (i + 1) * rows] = jnp.where(same, 0.0, -1e30).astype(
            jnp.bfloat16
        )
        back_ref[:, i * rows : (i + 1) * rows] = jnp.where(same_back, 0.0, -1e30)

    mine = jnp.where(routes_ref[...] == me, 1.0, 0.0).astype(jnp.bfloat16)
    counts = dot_t(jnp.ones((8, rows), jnp.bfloat16), mine, ((1,), (1,))).astype(jnp.bfloat16)
    source = lax.broadcasted_iota(jnp.int32, (devices, slots), 0)
    slot = lax.broadcasted_iota(jnp.int32, (devices, slots), 1) // capacity
    expand = jnp.where(source == (slot % n_z) * n_p + slot // n_z, 1.0, 0.0).astype(jnp.bfloat16)
    filled = jnp.dot(counts, expand, preferred_element_type=jnp.float32)[:1]
    rank = lax.broadcasted_iota(jnp.int32, (1, slots), 1) % capacity
    live = jnp.where(rank.astype(jnp.float32) < filled, 0.0, -1e30)
    bias_ref[:, :slots] = jnp.broadcast_to(live, (rows, slots)).astype(jnp.bfloat16)


def prepare(routes, doc_ids, n_z, devices, rows):
    slots = 2 * rows
    return pl.pallas_call(
        prepare_kernel,
        out_shape=[
            jax.ShapeDtypeStruct((n_z, 1, rows), jnp.int32),
            jax.ShapeDtypeStruct((rows, slots + 3 * rows), jnp.bfloat16),
            jax.ShapeDtypeStruct((rows, 3 * rows), jnp.float32),
        ],
        compiler_params=pltpu.CompilerParams(vmem_limit_bytes=SMALL_VMEM),
        name="prepare",
    )(routes.reshape(devices, rows), doc_ids.reshape(devices, rows))


def column_block(w_kv, target):
    _, w_rows, features = w_kv.shape
    half = features // (GROUPS // 2)
    start = (target & 1, 0, (target >> 1) * half)
    return lax.dynamic_slice(w_kv, start, (1, w_rows, half))[0]


def ring_step(value, back=False):
    pairs = list(zip(RING, RING[1:] + RING[:1]))
    return lax.ppermute(value, "z", [(b, a) for a, b in pairs] if back else pairs)


def memory_slots(cache, w_kv, place, capacity, stream, back):
    n_z, n_p = lax.axis_size("z"), lax.axis_size("p")
    devices = n_z * n_p
    cache_rows, depth = cache.shape
    _, w_rows, features = w_kv.shape
    z = lax.axis_index("z")
    if n_p == 4 and capacity % ROW_TILE == 0 and w_rows % ROW_TILE == 0:
        blocks = [column_block(w_kv, z ^ mask) for mask in range(n_z)]
        arrived = [blocks[0]] + [swapped(blocks[mask], "z", mask) for mask in range(1, n_z)]
        row1, other0 = ring_step(cache), swapped(cache, "head", 1)
        row1, arrived[1], arrived[2] = lax.optimization_barrier((row1, arrived[1], arrived[2]))
        row2, other1 = ring_step(row1), swapped(row1, "head", 1)
        own, row2, other0, other1 = lax.optimization_barrier(
            (jnp.stack(arrived, 0), row2, other0, other1)
        )
        across, beside = swapped(own, "p", 2), swapped(own, "p", 1)
        row3, other2 = ring_step(row2), swapped(row2, "head", 1)
        row3, other2, beside = lax.optimization_barrier((row3, other2, beside))
        other3 = swapped(row3, "head", 1)
        across, other3, stream, back = lax.optimization_barrier((across, other3, stream, back))
        pieces = [own, beside, across, swapped(across, "p", 1)]
        near, back1 = shifted(stream, 1), shifted(back, -1)
        rows = [cache, row1, row2, row3, other0, other1, other2, other3]
        slots = project(place, rows, pieces, devices, capacity)
        slots, near, back1 = lax.optimization_barrier((slots, near, back1))
        return slots, near, shifted(near, 1), back1
    near, back1 = shifted(stream, 1), shifted(back, -1)
    far = shifted(near, 1)
    targets = [column_block(w_kv, jnp.int32(i)) for i in range(n_z)]
    w_z = lax.all_to_all(jnp.stack(targets, 0), "z", split_axis=0, concat_axis=0, tiled=True)
    w_all = lax.all_gather(w_z, "p", axis=1, tiled=True).reshape(devices * w_rows, -1)
    rows = lax.all_gather(cache, ("head", "z"), axis=0, tiled=False)
    rows = rows.reshape(-1, n_z * cache_rows, depth)
    proj = sum(
        jnp.dot(
            rows[i], w_all[i * depth : (i + 1) * depth], preferred_element_type=jnp.float32
        )
        for i in range(rows.shape[0])
    ).astype(jnp.bfloat16)
    slot_ids = jnp.arange(devices * capacity, dtype=jnp.int32)
    chosen = (slot_ids[None, :, None] == place).astype(jnp.bfloat16)
    slots = jnp.einsum(
        "zsi,zic->zsc",
        chosen,
        proj.reshape(n_z, cache_rows, -1),
        preferred_element_type=jnp.float32,
    ).astype(jnp.bfloat16)
    slots = slots.reshape(n_z, devices, capacity, -1).transpose(1, 0, 2, 3)
    return slots, near, far, back1


def body(queries, keys, values, grad_out, cache, w_kv, doc_ids, routes):
    n_z, n_p = lax.axis_size("z"), lax.axis_size("p")
    devices = n_z * n_p
    seg_rows = queries.shape[0]
    cache_rows = cache.shape[0]
    capacity = 2 * cache_rows // devices
    slot_count = capacity * devices

    place, bias, back_bias = prepare(routes, doc_ids, n_z, devices, seg_rows)
    slots, kv1, kv2, qg1 = memory_slots(
        cache,
        w_kv,
        place,
        capacity,
        jnp.stack([keys, values], 0),
        jnp.stack([queries, grad_out], 0),
    )
    memory = lax.all_to_all(slots, SEQ, split_axis=0, concat_axis=0, tiled=True)
    memory = memory.reshape(n_z, slot_count, slots.shape[-1])

    qg2 = shifted(qg1, -1)
    output, grad_q, stats = attend(queries, grad_out, keys, values, kv1, kv2, memory, bias)
    all_stats = [stats, shifted(stats, -1), shifted(stats, -2)]
    grad_k, grad_v = key_grads(
        keys, values, queries, grad_out, qg1, qg2, all_stats, back_bias
    )
    return (output, grad_q, grad_k, grad_v)


def solution(mesh):
    n_seq, n_head = mesh.devices.shape
    grid = Mesh(mesh.devices.reshape(GROUPS, n_seq // GROUPS, n_head), ("z", "p", "head"))
    rows = P(SEQ, "head")
    return jax.shard_map(
        body,
        mesh=grid,
        in_specs=(rows, rows, rows, rows, rows, P(None, SEQ, "head"), P(), P()),
        out_specs=(rows, rows, rows, rows),
        check_vma=False,
    )
```

```python
import jax
import jax.numpy as jnp
from jax import lax
from jax.experimental import pallas as pl
from jax.experimental.pallas import tpu as pltpu
from jax.sharding import Mesh, PartitionSpec as P

HD = 128
GROUPS = 4
SEQ = ("z", "p")
ROW_TILE = 16
RING = [0, 1, 3, 2]
VMEM = 24 * 1024 * 1024
SMALL_VMEM = 4 * 1024 * 1024
STATS = 16


def shifted(value, by):
    length = lax.axis_size("z") * lax.axis_size("p")
    pairs = [(i, i + by) for i in range(length) if 0 <= i + by < length]
    return lax.ppermute(value, SEQ, pairs)


def swapped(value, axis, mask):
    return lax.ppermute(value, axis, [(i, i ^ mask) for i in range(lax.axis_size(axis))])


def in_vmem(*arrays):
    return [pltpu.with_memory_space_constraint(array, pltpu.VMEM) for array in arrays]


def in_hbm(*arrays):
    return [pltpu.with_memory_space_constraint(array, pltpu.HBM) for array in arrays]


def dot_t(a, b, dims):
    return lax.dot_general(a, b, (dims, ((), ())), preferred_element_type=jnp.float32)


def attend_kernel(
    q_ref, g_ref, k_ref, v_ref, kv1_ref, kv2_ref, mem_ref, bias_ref, out_ref, gq_ref, stats_ref
):
    rows, width = q_ref.shape
    scaling = HD ** (-0.5)
    bias = bias_ref[...].astype(jnp.float32)
    step = pl.program_id(0)
    heads = [slice(i * HD, (i + 1) * HD) for i in range(width // HD)]
    ks, vs = (
        [
            jnp.concatenate(
                [
                    mem_ref[2 * step + which, :, cols],
                    kv2_ref[which, :, cols],
                    kv1_ref[which, :, cols],
                    own_ref[:, cols],
                ],
                0,
            )
            for cols in heads
        ]
        for which, own_ref in enumerate((k_ref, v_ref))
    )
    scores = [dot_t(q_ref[:, cols], kh, ((1,), (1,))) + bias for cols, kh in zip(heads, ks)]
    dprobs = [dot_t(g_ref[:, cols], vh, ((1,), (1,))) for cols, vh in zip(heads, vs)]
    tops, shares, probs = [], [], []
    for score in scores:
        top = jnp.max(score, axis=-1, keepdims=True)
        weights = jnp.exp((score - top) * scaling)
        share = 1.0 / jnp.sum(weights, axis=-1, keepdims=True)
        tops.append(top)
        shares.append(share)
        probs.append(weights * share)
    outs = [
        dot_t(prob.astype(jnp.bfloat16), vh, ((1,), (0,))).astype(jnp.bfloat16)
        for prob, vh in zip(probs, vs)
    ]
    deltas, dscores = [], []
    for cols, out_b, prob, dprob in zip(heads, outs, probs, dprobs):
        out_ref[:, cols] = out_b
        delta = jnp.sum(
            g_ref[:, cols].astype(jnp.float32) * out_b.astype(jnp.float32), axis=-1, keepdims=True
        )
        deltas.append(delta)
        dscores.append((prob * ((dprob - delta) * scaling)).astype(jnp.bfloat16))
    lane = lax.broadcasted_iota(jnp.int32, (rows, HD), 1)
    stats = jnp.zeros((rows, HD), jnp.float32)
    for i, column in enumerate(tops + shares + deltas):
        stats = jnp.where(lane == i, column, stats)
    stats_ref[0] = stats.T[:STATS]
    for cols, kh, dscore in zip(heads, ks, dscores):
        gq_ref[:, cols] = dot_t(dscore, kh, ((1,), (0,))).astype(jnp.bfloat16)


def attend(queries, grad_out, keys, values, kv1, kv2, memory, bias):
    rows, features = queries.shape
    steps = memory.shape[0] // 2
    slots, block = memory.shape[1:]
    heads = steps * block // HD
    flat = pl.BlockSpec((rows, block), lambda i: (0, i))
    pair = pl.BlockSpec((2, rows, block), lambda i: (0, 0, i))
    whole = pl.BlockSpec(memory_space=pltpu.VMEM)
    keys_all = slots + 3 * rows
    return pl.pallas_call(
        attend_kernel,
        grid=(steps,),
        in_specs=[
            flat, flat, flat, flat, pair, pair, whole,
            pl.BlockSpec((rows, keys_all), lambda i: (0, 0)),
        ],
        out_specs=[flat, flat, pl.BlockSpec((1, STATS, rows), lambda i: (i, 0, 0))],
        out_shape=[
            jax.ShapeDtypeStruct((rows, features), jnp.bfloat16),
            jax.ShapeDtypeStruct((rows, features), jnp.bfloat16),
            jax.ShapeDtypeStruct((steps, STATS, rows), jnp.float32),
        ],
        compiler_params=pltpu.CompilerParams(vmem_limit_bytes=VMEM),
        cost_estimate=pl.CostEstimate(
            flops=2 * 4 * rows * keys_all * HD * heads,
            bytes_accessed=6 * 1024 * 1024,
            transcendentals=rows * keys_all * heads,
        ),
        name="attend",
    )(queries, grad_out, keys, values, *in_hbm(kv1, kv2), *in_vmem(memory), *in_hbm(bias))


def key_grads_kernel(
    k_ref, v_ref, q_ref, g_ref, qg1_ref, qg2_ref, st0_ref, st1_ref, st2_ref, bias_ref,
    gk_ref, gv_ref,
):
    width = k_ref.shape[1]
    scaling = HD ** (-0.5)
    bias = bias_ref[...]
    heads = [slice(i * HD, (i + 1) * HD) for i in range(width // HD)]
    start = pl.program_id(0) * width
    picked = [pl.ds(pl.multiple_of(start + i * HD, HD), HD) for i in range(len(heads))]
    stats = jnp.concatenate([st0_ref[0], st1_ref[0], st2_ref[0]], 1)
    qs = [
        jnp.concatenate([q_ref[:, cols], qg1_ref[0, :, wide], qg2_ref[0, :, wide]], 0)
        for cols, wide in zip(heads, picked)
    ]
    gs = [
        jnp.concatenate([g_ref[:, cols], qg1_ref[1, :, wide], qg2_ref[1, :, wide]], 0)
        for cols, wide in zip(heads, picked)
    ]
    scores = [dot_t(k_ref[:, cols], qh, ((1,), (1,))) + bias for cols, qh in zip(heads, qs)]
    dprobs = [dot_t(v_ref[:, cols], gh, ((1,), (1,))) for cols, gh in zip(heads, gs)]
    probs, dscores = [], []
    for i, (score, dprob) in enumerate(zip(scores, dprobs)):
        top, share, delta = (stats[i + j * len(heads) : i + j * len(heads) + 1] for j in range(3))
        prob = jnp.exp((score - top) * scaling) * share
        probs.append(prob.astype(jnp.bfloat16))
        dscores.append((prob * ((dprob - delta) * scaling)).astype(jnp.bfloat16))
    for cols, qh, gh, prob, dscore in zip(heads, qs, gs, probs, dscores):
        gk_ref[:, cols] = dot_t(dscore, qh, ((1,), (0,))).astype(jnp.bfloat16)
        gv_ref[:, cols] = dot_t(prob, gh, ((1,), (0,))).astype(jnp.bfloat16)


def key_grads(keys, values, queries, grad_out, qg1, qg2, stats, bias):
    rows, features = keys.shape
    steps = stats[0].shape[0]
    block = features // steps
    flat = pl.BlockSpec((rows, block), lambda i: (0, i))
    whole = pl.BlockSpec(memory_space=pltpu.VMEM)
    stat = pl.BlockSpec((1, STATS, rows), lambda i: (i, 0, 0))
    heads = features // HD
    return pl.pallas_call(
        key_grads_kernel,
        grid=(steps,),
        in_specs=[
            flat, flat, flat, flat, whole, whole, stat, stat, stat, whole,
        ],
        out_specs=[flat, flat],
        out_shape=[jax.ShapeDtypeStruct((rows, features), jnp.bfloat16)] * 2,
        compiler_params=pltpu.CompilerParams(vmem_limit_bytes=VMEM),
        cost_estimate=pl.CostEstimate(
            flops=2 * 4 * rows * 3 * rows * HD * heads,
            bytes_accessed=4 * 1024 * 1024,
            transcendentals=rows * 3 * rows * heads,
        ),
        name="key_grads",
    )(keys, values, queries, grad_out, *in_vmem(qg1, qg2), *stats, *in_vmem(bias))


def project_kernel(place_ref, *refs):
    n_z, _, cache_rows = place_ref.shape
    out_ref, w_ref, a_ref = refs[-3:]
    rows, pieces = refs[: 2 * n_z], refs[2 * n_z : -3]
    n_p, (_, w_rows, block) = len(pieces), pieces[0].shape
    depth = rows[0].shape[1]
    devices, _, capacity, _ = out_ref.shape
    z, p, y = (lax.axis_index(name) for name in ("z", "p", "head"))
    place_in_ring = z ^ (z >> 1)
    for i, ref in enumerate(rows):
        source = (place_in_ring - i % n_z + n_z) & (n_z - 1)
        a_ref[y ^ (i // n_z), source ^ (source >> 1)] = ref[...]
    for m in range(n_p):
        for k in range(n_z):
            w_ref[z ^ k, p ^ m] = pieces[m][k]
    half = n_z // 2
    proj = sum(
        jnp.dot(
            a_ref[i].reshape(n_z * cache_rows, depth),
            w_ref[i * half : (i + 1) * half].reshape(depth, block),
            preferred_element_type=jnp.float32,
        )
        for i in range(2)
    ).astype(jnp.bfloat16)
    slot_ids = lax.broadcasted_iota(jnp.int32, (devices * capacity, cache_rows), 0)
    for z in range(n_z):
        chosen = jnp.where(slot_ids == place_ref[z], 1.0, 0.0).astype(jnp.bfloat16)
        slots = jnp.dot(
            chosen,
            proj[z * cache_rows : (z + 1) * cache_rows],
            preferred_element_type=jnp.float32,
        ).astype(jnp.bfloat16)
        out_ref[:, z] = slots.reshape(devices, capacity, block)


def project(place, rows, pieces, devices, capacity):
    n_z, _, cache_rows = place.shape
    depth = rows[0].shape[1]
    n_p = len(pieces)
    _, w_rows, block = pieces[0].shape
    whole = pl.BlockSpec(memory_space=pltpu.VMEM)
    return pl.pallas_call(
        project_kernel,
        in_specs=[whole] * (1 + len(rows) + n_p),
        out_specs=whole,
        out_shape=pltpu.VMEM((devices, n_z, capacity, block), jnp.bfloat16),
        scratch_shapes=[
            pltpu.VMEM((n_z, n_p, w_rows, block), jnp.bfloat16),
            pltpu.VMEM((2, n_z, cache_rows, depth), jnp.bfloat16),
        ],
        compiler_params=pltpu.CompilerParams(vmem_limit_bytes=VMEM),
        cost_estimate=pl.CostEstimate(
            flops=4 * n_z * cache_rows * depth * block,
            bytes_accessed=8 * 1024 * 1024,
            transcendentals=0,
        ),
        name="project",
    )(*in_vmem(place, *rows, *pieces))


def prepare_kernel(routes_ref, ids_ref, place_ref, bias_ref, back_ref):
    n_z, _, rows = place_ref.shape
    devices = routes_ref.shape[0]
    n_p = devices // n_z
    capacity = 2 * rows // devices
    slots = bias_ref.shape[1] - 3 * rows
    p = lax.axis_index("p")
    me = lax.axis_index("z") * n_p + p
    row = lax.broadcasted_iota(jnp.int32, (rows, rows), 0)
    lane = lax.broadcasted_iota(jnp.int32, (rows, rows), 1)

    def both_ways(line):
        wide = jnp.broadcast_to(line.astype(jnp.float32), (rows, rows))
        return wide, wide.T

    for z in range(n_z):
        across, down = both_ways(routes_ref[pl.ds(z * n_p + p, 1), :])
        ranks = jnp.sum(
            jnp.where((across == down) & (row < lane), 1.0, 0.0), axis=0, keepdims=True
        )
        place_ref[z] = (across[:1] * capacity + ranks).astype(jnp.int32)

    def ids_of(segment):
        return ids_ref[pl.ds(jnp.clip(segment, 0, devices - 1), 1), :].astype(jnp.float32)

    _, own = both_ways(ids_ref[pl.ds(me, 1), :])
    for i in range(3):
        earlier, later = me - 2 + i, me + i
        same = (own == ids_of(earlier)) & (earlier >= 0)
        same_back = (own == ids_of(later)) & (later < devices)
        if i == 2:
            same = same & (lane <= row)
        if i == 0:
            same_back = same_back & (lane >= row)
        bias_ref[:, slots + i * rows : slots + (i + 1) * rows] = jnp.where(same, 0.0, -1e30).astype(
            jnp.bfloat16
        )
        back_ref[:, i * rows : (i + 1) * rows] = jnp.where(same_back, 0.0, -1e30)

    mine = jnp.where(routes_ref[...] == me, 1.0, 0.0).astype(jnp.bfloat16)
    counts = dot_t(jnp.ones((8, rows), jnp.bfloat16), mine, ((1,), (1,))).astype(jnp.bfloat16)
    source = lax.broadcasted_iota(jnp.int32, (devices, slots), 0)
    slot = lax.broadcasted_iota(jnp.int32, (devices, slots), 1) // capacity
    expand = jnp.where(source == (slot % n_z) * n_p + slot // n_z, 1.0, 0.0).astype(jnp.bfloat16)
    filled = jnp.dot(counts, expand, preferred_element_type=jnp.float32)[:1]
    rank = lax.broadcasted_iota(jnp.int32, (1, slots), 1) % capacity
    live = jnp.where(rank.astype(jnp.float32) < filled, 0.0, -1e30)
    bias_ref[:, :slots] = jnp.broadcast_to(live, (rows, slots)).astype(jnp.bfloat16)


def prepare(routes, doc_ids, n_z, devices, rows):
    slots = 2 * rows
    return pl.pallas_call(
        prepare_kernel,
        out_shape=[
            jax.ShapeDtypeStruct((n_z, 1, rows), jnp.int32),
            jax.ShapeDtypeStruct((rows, slots + 3 * rows), jnp.bfloat16),
            jax.ShapeDtypeStruct((rows, 3 * rows), jnp.float32),
        ],
        compiler_params=pltpu.CompilerParams(vmem_limit_bytes=SMALL_VMEM),
        name="prepare",
    )(routes.reshape(devices, rows), doc_ids.reshape(devices, rows))


def column_block(w_kv, target):
    _, w_rows, features = w_kv.shape
    half = features // (GROUPS // 2)
    start = (target & 1, 0, (target >> 1) * half)
    return lax.dynamic_slice(w_kv, start, (1, w_rows, half))[0]


def ring_step(value, back=False):
    pairs = list(zip(RING, RING[1:] + RING[:1]))
    return lax.ppermute(value, "z", [(b, a) for a, b in pairs] if back else pairs)


def memory_slots(cache, w_kv, place, capacity, stream, back):
    n_z, n_p = lax.axis_size("z"), lax.axis_size("p")
    devices = n_z * n_p
    cache_rows, depth = cache.shape
    _, w_rows, features = w_kv.shape
    z = lax.axis_index("z")
    if n_p == 4 and capacity % ROW_TILE == 0 and w_rows % ROW_TILE == 0:
        blocks = [column_block(w_kv, z ^ mask) for mask in range(n_z)]
        arrived = [blocks[0]] + [swapped(blocks[mask], "z", mask) for mask in range(1, n_z)]
        row1, other0 = ring_step(cache), swapped(cache, "head", 1)
        row1, arrived[1], arrived[2] = lax.optimization_barrier((row1, arrived[1], arrived[2]))
        row2, other1 = ring_step(row1), swapped(row1, "head", 1)
        own, other0, other1 = lax.optimization_barrier((jnp.stack(arrived, 0), other0, other1))
        across, beside = swapped(own, "p", 2), swapped(own, "p", 1)
        row2, beside, stream = lax.optimization_barrier((row2, beside, stream))
        row3, other2, near = ring_step(row2), swapped(row2, "head", 1), shifted(stream, 1)
        row3, other2 = lax.optimization_barrier((row3, other2))
        other3 = swapped(row3, "head", 1)
        across, other3, near = lax.optimization_barrier((across, other3, near))
        pieces = [own, beside, across, swapped(across, "p", 1)]
        far = shifted(near, 1)
        rows = [cache, row1, row2, row3, other0, other1, other2, other3]
        slots = project(place, rows, pieces, devices, capacity)
        slots, far, back = lax.optimization_barrier((slots, far, back))
        return slots, near, far, shifted(back, -1)
    near, back1 = shifted(stream, 1), shifted(back, -1)
    far = shifted(near, 1)
    targets = [column_block(w_kv, jnp.int32(i)) for i in range(n_z)]
    w_z = lax.all_to_all(jnp.stack(targets, 0), "z", split_axis=0, concat_axis=0, tiled=True)
    w_all = lax.all_gather(w_z, "p", axis=1, tiled=True).reshape(devices * w_rows, -1)
    rows = lax.all_gather(cache, ("head", "z"), axis=0, tiled=False)
    rows = rows.reshape(-1, n_z * cache_rows, depth)
    proj = sum(
        jnp.dot(
            rows[i], w_all[i * depth : (i + 1) * depth], preferred_element_type=jnp.float32
        )
        for i in range(rows.shape[0])
    ).astype(jnp.bfloat16)
    slot_ids = jnp.arange(devices * capacity, dtype=jnp.int32)
    chosen = (slot_ids[None, :, None] == place).astype(jnp.bfloat16)
    slots = jnp.einsum(
        "zsi,zic->zsc",
        chosen,
        proj.reshape(n_z, cache_rows, -1),
        preferred_element_type=jnp.float32,
    ).astype(jnp.bfloat16)
    slots = slots.reshape(n_z, devices, capacity, -1).transpose(1, 0, 2, 3)
    return slots, near, far, back1


def body(queries, keys, values, grad_out, cache, w_kv, doc_ids, routes):
    n_z, n_p = lax.axis_size("z"), lax.axis_size("p")
    devices = n_z * n_p
    seg_rows = queries.shape[0]
    cache_rows = cache.shape[0]
    capacity = 2 * cache_rows // devices
    slot_count = capacity * devices

    place, bias, back_bias = prepare(routes, doc_ids, n_z, devices, seg_rows)
    slots, kv1, kv2, qg1 = memory_slots(
        cache,
        w_kv,
        place,
        capacity,
        jnp.stack([keys, values], 0),
        jnp.stack([queries, grad_out], 0),
    )
    memory = lax.all_to_all(slots, SEQ, split_axis=0, concat_axis=0, tiled=True)
    memory = memory.reshape(n_z, slot_count, slots.shape[-1])

    output, grad_q, stats = attend(queries, grad_out, keys, values, kv1, kv2, memory, bias)
    qg1, stats = lax.optimization_barrier((qg1, stats))
    qg2 = shifted(qg1, -1)
    all_stats = [stats, shifted(stats, -1), shifted(stats, -2)]
    grad_k, grad_v = key_grads(
        keys, values, queries, grad_out, qg1, qg2, all_stats, back_bias
    )
    return (output, grad_q, grad_k, grad_v)


def solution(mesh):
    n_seq, n_head = mesh.devices.shape
    grid = Mesh(mesh.devices.reshape(GROUPS, n_seq // GROUPS, n_head), ("z", "p", "head"))
    rows = P(SEQ, "head")
    return jax.shard_map(
        body,
        mesh=grid,
        in_specs=(rows, rows, rows, rows, rows, P(None, SEQ, "head"), P(), P()),
        out_specs=(rows, rows, rows, rows),
        check_vma=False,
    )
```

```python
import jax
import jax.numpy as jnp
from jax import lax
from jax.experimental import pallas as pl
from jax.experimental.pallas import tpu as pltpu
from jax.sharding import Mesh, PartitionSpec as P

HD = 128
GROUPS = 4
SEQ = ("z", "p")
ROW_TILE = 16
RING = [0, 1, 3, 2]
VMEM = 24 * 1024 * 1024
SMALL_VMEM = 4 * 1024 * 1024
STATS = 16


def shifted(value, by):
    length = lax.axis_size("z") * lax.axis_size("p")
    pairs = [(i, i + by) for i in range(length) if 0 <= i + by < length]
    return lax.ppermute(value, SEQ, pairs)


def swapped(value, axis, mask):
    return lax.ppermute(value, axis, [(i, i ^ mask) for i in range(lax.axis_size(axis))])


def in_vmem(*arrays):
    return [pltpu.with_memory_space_constraint(array, pltpu.VMEM) for array in arrays]


def in_hbm(*arrays):
    return [pltpu.with_memory_space_constraint(array, pltpu.HBM) for array in arrays]


def dot_t(a, b, dims):
    return lax.dot_general(a, b, (dims, ((), ())), preferred_element_type=jnp.float32)


def attend_kernel(
    q_ref, g_ref, k_ref, v_ref, kv1_ref, kv2_ref, mem_ref, bias_ref, out_ref, gq_ref, stats_ref
):
    rows, width = q_ref.shape
    scaling = HD ** (-0.5)
    bias = bias_ref[...].astype(jnp.float32)
    step = pl.program_id(0)
    heads = [slice(i * HD, (i + 1) * HD) for i in range(width // HD)]
    ks, vs = (
        [
            jnp.concatenate(
                [
                    mem_ref[2 * step + which, :, cols],
                    kv2_ref[which, :, cols],
                    kv1_ref[which, :, cols],
                    own_ref[:, cols],
                ],
                0,
            )
            for cols in heads
        ]
        for which, own_ref in enumerate((k_ref, v_ref))
    )
    scores = [dot_t(q_ref[:, cols], kh, ((1,), (1,))) + bias for cols, kh in zip(heads, ks)]
    dprobs = [dot_t(g_ref[:, cols], vh, ((1,), (1,))) for cols, vh in zip(heads, vs)]
    tops, shares, probs = [], [], []
    for score in scores:
        top = jnp.max(score, axis=-1, keepdims=True)
        weights = jnp.exp((score - top) * scaling)
        share = 1.0 / jnp.sum(weights, axis=-1, keepdims=True)
        tops.append(top)
        shares.append(share)
        probs.append(weights * share)
    outs = [
        dot_t(prob.astype(jnp.bfloat16), vh, ((1,), (0,))).astype(jnp.bfloat16)
        for prob, vh in zip(probs, vs)
    ]
    deltas, dscores = [], []
    for cols, out_b, prob, dprob in zip(heads, outs, probs, dprobs):
        out_ref[:, cols] = out_b
        delta = jnp.sum(
            g_ref[:, cols].astype(jnp.float32) * out_b.astype(jnp.float32), axis=-1, keepdims=True
        )
        deltas.append(delta)
        dscores.append((prob * ((dprob - delta) * scaling)).astype(jnp.bfloat16))
    lane = lax.broadcasted_iota(jnp.int32, (rows, HD), 1)
    stats = jnp.zeros((rows, HD), jnp.float32)
    for i, column in enumerate(tops + shares + deltas):
        stats = jnp.where(lane == i, column, stats)
    stats_ref[0] = stats.T[:STATS]
    for cols, kh, dscore in zip(heads, ks, dscores):
        gq_ref[:, cols] = dot_t(dscore, kh, ((1,), (0,))).astype(jnp.bfloat16)


def attend(queries, grad_out, keys, values, kv1, kv2, memory, bias):
    rows, features = queries.shape
    steps = memory.shape[0] // 2
    slots, block = memory.shape[1:]
    heads = steps * block // HD
    flat = pl.BlockSpec((rows, block), lambda i: (0, i))
    pair = pl.BlockSpec((2, rows, block), lambda i: (0, 0, i))
    whole = pl.BlockSpec(memory_space=pltpu.VMEM)
    keys_all = slots + 3 * rows
    return pl.pallas_call(
        attend_kernel,
        grid=(steps,),
        in_specs=[
            flat, flat, flat, flat, pair, pair, whole,
            pl.BlockSpec((rows, keys_all), lambda i: (0, 0)),
        ],
        out_specs=[flat, flat, pl.BlockSpec((1, STATS, rows), lambda i: (i, 0, 0))],
        out_shape=[
            jax.ShapeDtypeStruct((rows, features), jnp.bfloat16),
            jax.ShapeDtypeStruct((rows, features), jnp.bfloat16),
            jax.ShapeDtypeStruct((steps, STATS, rows), jnp.float32),
        ],
        compiler_params=pltpu.CompilerParams(vmem_limit_bytes=VMEM),
        cost_estimate=pl.CostEstimate(
            flops=2 * 4 * rows * keys_all * HD * heads,
            bytes_accessed=6 * 1024 * 1024,
            transcendentals=rows * keys_all * heads,
        ),
        name="attend",
    )(queries, grad_out, keys, values, *in_hbm(kv1, kv2), *in_vmem(memory), *in_hbm(bias))


def key_grads_kernel(
    k_ref, v_ref, q_ref, g_ref, qg1_ref, qg2_ref, st0_ref, st1_ref, st2_ref, bias_ref,
    gk_ref, gv_ref,
):
    width = k_ref.shape[1]
    scaling = HD ** (-0.5)
    bias = bias_ref[...]
    heads = [slice(i * HD, (i + 1) * HD) for i in range(width // HD)]
    start = pl.program_id(0) * width
    picked = [pl.ds(pl.multiple_of(start + i * HD, HD), HD) for i in range(len(heads))]
    stats = jnp.concatenate([st0_ref[0], st1_ref[0], st2_ref[0]], 1)
    qs = [
        jnp.concatenate([q_ref[:, cols], qg1_ref[0, :, wide], qg2_ref[0, :, wide]], 0)
        for cols, wide in zip(heads, picked)
    ]
    gs = [
        jnp.concatenate([g_ref[:, cols], qg1_ref[1, :, wide], qg2_ref[1, :, wide]], 0)
        for cols, wide in zip(heads, picked)
    ]
    scores = [dot_t(k_ref[:, cols], qh, ((1,), (1,))) + bias for cols, qh in zip(heads, qs)]
    dprobs = [dot_t(v_ref[:, cols], gh, ((1,), (1,))) for cols, gh in zip(heads, gs)]
    probs, dscores = [], []
    for i, (score, dprob) in enumerate(zip(scores, dprobs)):
        top, share, delta = (stats[i + j * len(heads) : i + j * len(heads) + 1] for j in range(3))
        prob = jnp.exp((score - top) * scaling) * share
        probs.append(prob.astype(jnp.bfloat16))
        dscores.append((prob * ((dprob - delta) * scaling)).astype(jnp.bfloat16))
    for cols, qh, gh, prob, dscore in zip(heads, qs, gs, probs, dscores):
        gk_ref[:, cols] = dot_t(dscore, qh, ((1,), (0,))).astype(jnp.bfloat16)
        gv_ref[:, cols] = dot_t(prob, gh, ((1,), (0,))).astype(jnp.bfloat16)


def key_grads(keys, values, queries, grad_out, qg1, qg2, stats, bias):
    rows, features = keys.shape
    steps = stats[0].shape[0]
    block = features // steps
    flat = pl.BlockSpec((rows, block), lambda i: (0, i))
    whole = pl.BlockSpec(memory_space=pltpu.VMEM)
    stat = pl.BlockSpec((1, STATS, rows), lambda i: (i, 0, 0))
    heads = features // HD
    return pl.pallas_call(
        key_grads_kernel,
        grid=(steps,),
        in_specs=[
            flat, flat, flat, flat, whole, whole, stat, stat, stat, whole,
        ],
        out_specs=[flat, flat],
        out_shape=[jax.ShapeDtypeStruct((rows, features), jnp.bfloat16)] * 2,
        compiler_params=pltpu.CompilerParams(vmem_limit_bytes=VMEM),
        cost_estimate=pl.CostEstimate(
            flops=2 * 4 * rows * 3 * rows * HD * heads,
            bytes_accessed=4 * 1024 * 1024,
            transcendentals=rows * 3 * rows * heads,
        ),
        name="key_grads",
    )(keys, values, queries, grad_out, *in_vmem(qg1, qg2), *stats, *in_vmem(bias))


def project_kernel(place_ref, *refs):
    n_z, _, cache_rows = place_ref.shape
    out_ref, w_ref, a_ref = refs[-3:]
    rows, pieces = refs[: 2 * n_z], refs[2 * n_z : -3]
    n_p, (_, w_rows, block) = len(pieces), pieces[0].shape
    depth = rows[0].shape[1]
    devices, _, capacity, _ = out_ref.shape
    z, p, y = (lax.axis_index(name) for name in ("z", "p", "head"))
    place_in_ring = z ^ (z >> 1)
    for i, ref in enumerate(rows):
        source = (place_in_ring - i % n_z + n_z) & (n_z - 1)
        a_ref[y ^ (i // n_z), source ^ (source >> 1)] = ref[...]
    for m in range(n_p):
        for k in range(n_z):
            w_ref[z ^ k, p ^ m] = pieces[m][k]
    half = n_z // 2
    proj = sum(
        jnp.dot(
            a_ref[i].reshape(n_z * cache_rows, depth),
            w_ref[i * half : (i + 1) * half].reshape(depth, block),
            preferred_element_type=jnp.float32,
        )
        for i in range(2)
    ).astype(jnp.bfloat16)
    slot_ids = lax.broadcasted_iota(jnp.int32, (devices * capacity, cache_rows), 0)
    for z in range(n_z):
        chosen = jnp.where(slot_ids == place_ref[z], 1.0, 0.0).astype(jnp.bfloat16)
        slots = jnp.dot(
            chosen,
            proj[z * cache_rows : (z + 1) * cache_rows],
            preferred_element_type=jnp.float32,
        ).astype(jnp.bfloat16)
        out_ref[:, z] = slots.reshape(devices, capacity, block)


def project(place, rows, pieces, devices, capacity):
    n_z, _, cache_rows = place.shape
    depth = rows[0].shape[1]
    n_p = len(pieces)
    _, w_rows, block = pieces[0].shape
    whole = pl.BlockSpec(memory_space=pltpu.VMEM)
    return pl.pallas_call(
        project_kernel,
        in_specs=[whole] * (1 + len(rows) + n_p),
        out_specs=whole,
        out_shape=pltpu.VMEM((devices, n_z, capacity, block), jnp.bfloat16),
        scratch_shapes=[
            pltpu.VMEM((n_z, n_p, w_rows, block), jnp.bfloat16),
            pltpu.VMEM((2, n_z, cache_rows, depth), jnp.bfloat16),
        ],
        compiler_params=pltpu.CompilerParams(vmem_limit_bytes=VMEM),
        cost_estimate=pl.CostEstimate(
            flops=4 * n_z * cache_rows * depth * block,
            bytes_accessed=8 * 1024 * 1024,
            transcendentals=0,
        ),
        name="project",
    )(*in_vmem(place, *rows, *pieces))


def prepare_kernel(routes_ref, ids_ref, place_ref, bias_ref, back_ref):
    n_z, _, rows = place_ref.shape
    devices = routes_ref.shape[0]
    n_p = devices // n_z
    capacity = 2 * rows // devices
    slots = bias_ref.shape[1] - 3 * rows
    p = lax.axis_index("p")
    me = lax.axis_index("z") * n_p + p
    row = lax.broadcasted_iota(jnp.int32, (rows, rows), 0)
    lane = lax.broadcasted_iota(jnp.int32, (rows, rows), 1)

    def both_ways(line):
        wide = jnp.broadcast_to(line.astype(jnp.float32), (rows, rows))
        return wide, wide.T

    for z in range(n_z):
        across, down = both_ways(routes_ref[pl.ds(z * n_p + p, 1), :])
        ranks = jnp.sum(
            jnp.where((across == down) & (row < lane), 1.0, 0.0), axis=0, keepdims=True
        )
        place_ref[z] = (across[:1] * capacity + ranks).astype(jnp.int32)

    def ids_of(segment):
        return ids_ref[pl.ds(jnp.clip(segment, 0, devices - 1), 1), :].astype(jnp.float32)

    _, own = both_ways(ids_ref[pl.ds(me, 1), :])
    for i in range(3):
        earlier, later = me - 2 + i, me + i
        same = (own == ids_of(earlier)) & (earlier >= 0)
        same_back = (own == ids_of(later)) & (later < devices)
        if i == 2:
            same = same & (lane <= row)
        if i == 0:
            same_back = same_back & (lane >= row)
        bias_ref[:, slots + i * rows : slots + (i + 1) * rows] = jnp.where(same, 0.0, -1e30).astype(
            jnp.bfloat16
        )
        back_ref[:, i * rows : (i + 1) * rows] = jnp.where(same_back, 0.0, -1e30)

    mine = jnp.where(routes_ref[...] == me, 1.0, 0.0).astype(jnp.bfloat16)
    counts = dot_t(jnp.ones((8, rows), jnp.bfloat16), mine, ((1,), (1,))).astype(jnp.bfloat16)
    source = lax.broadcasted_iota(jnp.int32, (devices, slots), 0)
    slot = lax.broadcasted_iota(jnp.int32, (devices, slots), 1) // capacity
    expand = jnp.where(source == (slot % n_z) * n_p + slot // n_z, 1.0, 0.0).astype(jnp.bfloat16)
    filled = jnp.dot(counts, expand, preferred_element_type=jnp.float32)[:1]
    rank = lax.broadcasted_iota(jnp.int32, (1, slots), 1) % capacity
    live = jnp.where(rank.astype(jnp.float32) < filled, 0.0, -1e30)
    bias_ref[:, :slots] = jnp.broadcast_to(live, (rows, slots)).astype(jnp.bfloat16)


def prepare(routes, doc_ids, n_z, devices, rows):
    slots = 2 * rows
    return pl.pallas_call(
        prepare_kernel,
        out_shape=[
            jax.ShapeDtypeStruct((n_z, 1, rows), jnp.int32),
            jax.ShapeDtypeStruct((rows, slots + 3 * rows), jnp.bfloat16),
            jax.ShapeDtypeStruct((rows, 3 * rows), jnp.float32),
        ],
        compiler_params=pltpu.CompilerParams(vmem_limit_bytes=SMALL_VMEM),
        name="prepare",
    )(routes.reshape(devices, rows), doc_ids.reshape(devices, rows))


def column_block(w_kv, target):
    _, w_rows, features = w_kv.shape
    half = features // (GROUPS // 2)
    start = (target & 1, 0, (target >> 1) * half)
    return lax.dynamic_slice(w_kv, start, (1, w_rows, half))[0]


def ring_step(value, back=False):
    pairs = list(zip(RING, RING[1:] + RING[:1]))
    return lax.ppermute(value, "z", [(b, a) for a, b in pairs] if back else pairs)


def memory_slots(cache, w_kv, place, capacity, stream, back):
    n_z, n_p = lax.axis_size("z"), lax.axis_size("p")
    devices = n_z * n_p
    cache_rows, depth = cache.shape
    _, w_rows, features = w_kv.shape
    z = lax.axis_index("z")
    if n_p == 4 and capacity % ROW_TILE == 0 and w_rows % ROW_TILE == 0:
        blocks = [column_block(w_kv, z ^ mask) for mask in range(n_z)]
        own = jnp.stack(
            [blocks[0]] + [swapped(blocks[mask], "z", mask) for mask in range(1, n_z)], 0
        )
        row1, other0 = ring_step(cache), swapped(cache, "head", 1)
        own, row1, other0, cache = lax.optimization_barrier((own, row1, other0, cache))
        across, beside = swapped(own, "p", 2), swapped(own, "p", 1)
        row2, row3, other1 = ring_step(row1), ring_step(cache, back=True), swapped(row1, "head", 1)
        beside, stream = lax.optimization_barrier((beside, stream))
        near = shifted(stream, 1)
        row2, row3, other0, other1 = lax.optimization_barrier((row2, row3, other0, other1))
        other2, other3 = swapped(row2, "head", 1), ring_step(other0, back=True)
        across, other2, other3, near, back = lax.optimization_barrier(
            (across, other2, other3, near, back)
        )
        pieces = [own, beside, across, swapped(across, "p", 1)]
        far, back1 = shifted(near, 1), shifted(back, -1)
        rows = [cache, row1, row2, row3, other0, other1, other2, other3]
        slots = project(place, rows, pieces, devices, capacity)
        slots, far, back1 = lax.optimization_barrier((slots, far, back1))
        return slots, near, far, back1
    near, back1 = shifted(stream, 1), shifted(back, -1)
    far = shifted(near, 1)
    targets = [column_block(w_kv, jnp.int32(i)) for i in range(n_z)]
    w_z = lax.all_to_all(jnp.stack(targets, 0), "z", split_axis=0, concat_axis=0, tiled=True)
    w_all = lax.all_gather(w_z, "p", axis=1, tiled=True).reshape(devices * w_rows, -1)
    rows = lax.all_gather(cache, ("head", "z"), axis=0, tiled=False)
    rows = rows.reshape(-1, n_z * cache_rows, depth)
    proj = sum(
        jnp.dot(
            rows[i], w_all[i * depth : (i + 1) * depth], preferred_element_type=jnp.float32
        )
        for i in range(rows.shape[0])
    ).astype(jnp.bfloat16)
    slot_ids = jnp.arange(devices * capacity, dtype=jnp.int32)
    chosen = (slot_ids[None, :, None] == place).astype(jnp.bfloat16)
    slots = jnp.einsum(
        "zsi,zic->zsc",
        chosen,
        proj.reshape(n_z, cache_rows, -1),
        preferred_element_type=jnp.float32,
    ).astype(jnp.bfloat16)
    slots = slots.reshape(n_z, devices, capacity, -1).transpose(1, 0, 2, 3)
    return slots, near, far, back1


def body(queries, keys, values, grad_out, cache, w_kv, doc_ids, routes):
    n_z, n_p = lax.axis_size("z"), lax.axis_size("p")
    devices = n_z * n_p
    seg_rows = queries.shape[0]
    cache_rows = cache.shape[0]
    capacity = 2 * cache_rows // devices
    slot_count = capacity * devices

    place, bias, back_bias = prepare(routes, doc_ids, n_z, devices, seg_rows)
    slots, kv1, kv2, qg1 = memory_slots(
        cache,
        w_kv,
        place,
        capacity,
        jnp.stack([keys, values], 0),
        jnp.stack([queries, grad_out], 0),
    )
    memory = lax.all_to_all(slots, SEQ, split_axis=0, concat_axis=0, tiled=True)
    memory = memory.reshape(n_z, slot_count, slots.shape[-1])

    qg2 = shifted(qg1, -1)
    output, grad_q, stats = attend(queries, grad_out, keys, values, kv1, kv2, memory, bias)
    all_stats = [stats, shifted(stats, -1), shifted(stats, -2)]
    grad_k, grad_v = key_grads(
        keys, values, queries, grad_out, qg1, qg2, all_stats, back_bias
    )
    return (output, grad_q, grad_k, grad_v)


def solution(mesh):
    n_seq, n_head = mesh.devices.shape
    grid = Mesh(mesh.devices.reshape(GROUPS, n_seq // GROUPS, n_head), ("z", "p", "head"))
    rows = P(SEQ, "head")
    return jax.shard_map(
        body,
        mesh=grid,
        in_specs=(rows, rows, rows, rows, rows, P(None, SEQ, "head"), P(), P()),
        out_specs=(rows, rows, rows, rows),
        check_vma=False,
    )
```

```python
import functools

import jax
import jax.numpy as jnp
from jax import lax
from jax.experimental import pallas as pl
from jax.experimental.pallas import tpu as pltpu
from jax.sharding import Mesh, PartitionSpec as P

HD = 128
GROUPS = 4
SEQ = ("z", "p")
ROW_TILE = 16
RING = [0, 1, 3, 2]
VMEM = 24 * 1024 * 1024
SMALL_VMEM = 4 * 1024 * 1024
STATS = 16


def shifted(value, by):
    length = lax.axis_size("z") * lax.axis_size("p")
    pairs = [(i, i + by) for i in range(length) if 0 <= i + by < length]
    return lax.ppermute(value, SEQ, pairs)


def swapped(value, axis, mask):
    return lax.ppermute(value, axis, [(i, i ^ mask) for i in range(lax.axis_size(axis))])


def in_vmem(*arrays):
    return [pltpu.with_memory_space_constraint(array, pltpu.VMEM) for array in arrays]


def in_hbm(*arrays):
    return [pltpu.with_memory_space_constraint(array, pltpu.HBM) for array in arrays]


def dot_t(a, b, dims):
    return lax.dot_general(a, b, (dims, ((), ())), preferred_element_type=jnp.float32)


def attend_kernel(
    q_ref, g_ref, k_ref, v_ref, kv1_ref, kv2_ref, mem_ref, bias_ref, out_ref, gq_ref, stats_ref
):
    rows, width = q_ref.shape
    scaling = HD ** (-0.5)
    bias = bias_ref[...].astype(jnp.float32)
    step = pl.program_id(0)
    heads = [slice(i * HD, (i + 1) * HD) for i in range(width // HD)]
    ks, vs = (
        [
            jnp.concatenate(
                [
                    mem_ref[2 * step + which, :, cols],
                    kv2_ref[which, :, cols],
                    kv1_ref[which, :, cols],
                    own_ref[:, cols],
                ],
                0,
            )
            for cols in heads
        ]
        for which, own_ref in enumerate((k_ref, v_ref))
    )
    scores = [dot_t(q_ref[:, cols], kh, ((1,), (1,))) + bias for cols, kh in zip(heads, ks)]
    dprobs = [dot_t(g_ref[:, cols], vh, ((1,), (1,))) for cols, vh in zip(heads, vs)]
    tops, shares, probs = [], [], []
    for score in scores:
        top = jnp.max(score, axis=-1, keepdims=True)
        weights = jnp.exp((score - top) * scaling)
        share = 1.0 / jnp.sum(weights, axis=-1, keepdims=True)
        tops.append(top)
        shares.append(share)
        probs.append(weights * share)
    outs = [
        dot_t(prob.astype(jnp.bfloat16), vh, ((1,), (0,))).astype(jnp.bfloat16)
        for prob, vh in zip(probs, vs)
    ]
    deltas, dscores = [], []
    for cols, out_b, prob, dprob in zip(heads, outs, probs, dprobs):
        out_ref[:, cols] = out_b
        delta = jnp.sum(
            g_ref[:, cols].astype(jnp.float32) * out_b.astype(jnp.float32), axis=-1, keepdims=True
        )
        deltas.append(delta)
        dscores.append((prob * ((dprob - delta) * scaling)).astype(jnp.bfloat16))
    lane = lax.broadcasted_iota(jnp.int32, (rows, HD), 1)
    stats = jnp.zeros((rows, HD), jnp.float32)
    for i, column in enumerate(tops + shares + deltas):
        stats = jnp.where(lane == i, column, stats)
    stats_ref[0] = stats.T[:STATS]
    for cols, kh, dscore in zip(heads, ks, dscores):
        gq_ref[:, cols] = dot_t(dscore, kh, ((1,), (0,))).astype(jnp.bfloat16)


def attend(queries, grad_out, keys, values, kv1, kv2, memory, bias):
    rows, features = queries.shape
    steps = memory.shape[0] // 2
    slots, block = memory.shape[1:]
    heads = steps * block // HD
    flat = pl.BlockSpec((rows, block), lambda i: (0, i))
    pair = pl.BlockSpec((2, rows, block), lambda i: (0, 0, i))
    whole = pl.BlockSpec(memory_space=pltpu.VMEM)
    keys_all = slots + 3 * rows
    return pl.pallas_call(
        attend_kernel,
        grid=(steps,),
        in_specs=[
            flat, flat, flat, flat, pair, pair, whole,
            pl.BlockSpec((rows, keys_all), lambda i: (0, 0)),
        ],
        out_specs=[flat, flat, pl.BlockSpec((1, STATS, rows), lambda i: (i, 0, 0))],
        out_shape=[
            jax.ShapeDtypeStruct((rows, features), jnp.bfloat16),
            jax.ShapeDtypeStruct((rows, features), jnp.bfloat16),
            jax.ShapeDtypeStruct((steps, STATS, rows), jnp.float32),
        ],
        compiler_params=pltpu.CompilerParams(vmem_limit_bytes=VMEM),
        cost_estimate=pl.CostEstimate(
            flops=2 * 4 * rows * keys_all * HD * heads,
            bytes_accessed=6 * 1024 * 1024,
            transcendentals=rows * keys_all * heads,
        ),
        name="attend",
    )(queries, grad_out, keys, values, *in_hbm(kv1, kv2), *in_vmem(memory), *in_hbm(bias))


def key_grads_kernel(
    k_ref, v_ref, q_ref, g_ref, qg1_ref, qg2_ref, st0_ref, st1_ref, st2_ref, bias_ref,
    gk_ref, gv_ref,
):
    width = k_ref.shape[1]
    scaling = HD ** (-0.5)
    bias = bias_ref[...]
    heads = [slice(i * HD, (i + 1) * HD) for i in range(width // HD)]
    start = pl.program_id(0) * width
    picked = [pl.ds(pl.multiple_of(start + i * HD, HD), HD) for i in range(len(heads))]
    stats = jnp.concatenate([st0_ref[0], st1_ref[0], st2_ref[0]], 1)
    qs = [
        jnp.concatenate([q_ref[:, cols], qg1_ref[0, :, wide], qg2_ref[0, :, wide]], 0)
        for cols, wide in zip(heads, picked)
    ]
    gs = [
        jnp.concatenate([g_ref[:, cols], qg1_ref[1, :, wide], qg2_ref[1, :, wide]], 0)
        for cols, wide in zip(heads, picked)
    ]
    scores = [dot_t(k_ref[:, cols], qh, ((1,), (1,))) + bias for cols, qh in zip(heads, qs)]
    dprobs = [dot_t(v_ref[:, cols], gh, ((1,), (1,))) for cols, gh in zip(heads, gs)]
    probs, dscores = [], []
    for i, (score, dprob) in enumerate(zip(scores, dprobs)):
        top, share, delta = (stats[i + j * len(heads) : i + j * len(heads) + 1] for j in range(3))
        prob = jnp.exp((score - top) * scaling) * share
        probs.append(prob.astype(jnp.bfloat16))
        dscores.append((prob * ((dprob - delta) * scaling)).astype(jnp.bfloat16))
    for cols, qh, gh, prob, dscore in zip(heads, qs, gs, probs, dscores):
        gk_ref[:, cols] = dot_t(dscore, qh, ((1,), (0,))).astype(jnp.bfloat16)
        gv_ref[:, cols] = dot_t(prob, gh, ((1,), (0,))).astype(jnp.bfloat16)


def key_grads(keys, values, queries, grad_out, qg1, qg2, stats, bias):
    rows, features = keys.shape
    steps = stats[0].shape[0]
    block = features // steps
    flat = pl.BlockSpec((rows, block), lambda i: (0, i))
    whole = pl.BlockSpec(memory_space=pltpu.VMEM)
    stat = pl.BlockSpec((1, STATS, rows), lambda i: (i, 0, 0))
    heads = features // HD
    return pl.pallas_call(
        key_grads_kernel,
        grid=(steps,),
        in_specs=[
            flat, flat, flat, flat, whole, whole, stat, stat, stat, whole,
        ],
        out_specs=[flat, flat],
        out_shape=[jax.ShapeDtypeStruct((rows, features), jnp.bfloat16)] * 2,
        compiler_params=pltpu.CompilerParams(vmem_limit_bytes=VMEM),
        cost_estimate=pl.CostEstimate(
            flops=2 * 4 * rows * 3 * rows * HD * heads,
            bytes_accessed=4 * 1024 * 1024,
            transcendentals=rows * 3 * rows * heads,
        ),
        name="key_grads",
    )(keys, values, queries, grad_out, *in_vmem(qg1, qg2), *stats, *in_vmem(bias))


def project_kernel(layout, place_ref, *refs):
    n_z, _, cache_rows = place_ref.shape
    out_ref, w_ref, a_ref = refs[-3:]
    rows, pieces = refs[: 2 * n_z], refs[2 * n_z : -3]
    w_rows, block = pieces[0].shape[1:]
    depth = rows[0].shape[1]
    devices, _, capacity, _ = out_ref.shape
    z, p, y = (lax.axis_index(name) for name in ("z", "p", "head"))
    place_in_ring = z ^ (z >> 1)
    for i, ref in enumerate(rows):
        source = (place_in_ring - i % n_z + n_z) & (n_z - 1)
        a_ref[y ^ (i // n_z), source ^ (source >> 1)] = ref[...]
    for (m, first), piece in zip(layout, pieces):
        for k in range(piece.shape[0]):
            w_ref[z ^ (first + k), p ^ m] = piece[k]
    half = n_z // 2
    proj = sum(
        jnp.dot(
            a_ref[i].reshape(n_z * cache_rows, depth),
            w_ref[i * half : (i + 1) * half].reshape(depth, block),
            preferred_element_type=jnp.float32,
        )
        for i in range(2)
    ).astype(jnp.bfloat16)
    slot_ids = lax.broadcasted_iota(jnp.int32, (devices * capacity, cache_rows), 0)
    for z in range(n_z):
        chosen = jnp.where(slot_ids == place_ref[z], 1.0, 0.0).astype(jnp.bfloat16)
        slots = jnp.dot(
            chosen,
            proj[z * cache_rows : (z + 1) * cache_rows],
            preferred_element_type=jnp.float32,
        ).astype(jnp.bfloat16)
        out_ref[:, z] = slots.reshape(devices, capacity, block)


def project(place, rows, pieces, devices, capacity):
    n_z, _, cache_rows = place.shape
    depth = rows[0].shape[1]
    layout, pieces = [piece[:2] for piece in pieces], [piece[2] for piece in pieces]
    n_p = devices // n_z
    w_rows, block = pieces[0].shape[1:]
    whole = pl.BlockSpec(memory_space=pltpu.VMEM)
    return pl.pallas_call(
        functools.partial(project_kernel, layout),
        in_specs=[whole] * (1 + len(rows) + len(pieces)),
        out_specs=whole,
        out_shape=pltpu.VMEM((devices, n_z, capacity, block), jnp.bfloat16),
        scratch_shapes=[
            pltpu.VMEM((n_z, n_p, w_rows, block), jnp.bfloat16),
            pltpu.VMEM((2, n_z, cache_rows, depth), jnp.bfloat16),
        ],
        compiler_params=pltpu.CompilerParams(vmem_limit_bytes=VMEM),
        cost_estimate=pl.CostEstimate(
            flops=4 * n_z * cache_rows * depth * block,
            bytes_accessed=8 * 1024 * 1024,
            transcendentals=0,
        ),
        name="project",
    )(*in_vmem(place, *rows, *pieces))


def prepare_kernel(routes_ref, ids_ref, place_ref, bias_ref, back_ref):
    n_z, _, rows = place_ref.shape
    devices = routes_ref.shape[0]
    n_p = devices // n_z
    capacity = 2 * rows // devices
    slots = bias_ref.shape[1] - 3 * rows
    p = lax.axis_index("p")
    me = lax.axis_index("z") * n_p + p
    row = lax.broadcasted_iota(jnp.int32, (rows, rows), 0)
    lane = lax.broadcasted_iota(jnp.int32, (rows, rows), 1)

    def both_ways(line):
        wide = jnp.broadcast_to(line.astype(jnp.float32), (rows, rows))
        return wide, wide.T

    for z in range(n_z):
        across, down = both_ways(routes_ref[pl.ds(z * n_p + p, 1), :])
        ranks = jnp.sum(
            jnp.where((across == down) & (row < lane), 1.0, 0.0), axis=0, keepdims=True
        )
        place_ref[z] = (across[:1] * capacity + ranks).astype(jnp.int32)

    def ids_of(segment):
        return ids_ref[pl.ds(jnp.clip(segment, 0, devices - 1), 1), :].astype(jnp.float32)

    _, own = both_ways(ids_ref[pl.ds(me, 1), :])
    for i in range(3):
        earlier, later = me - 2 + i, me + i
        same = (own == ids_of(earlier)) & (earlier >= 0)
        same_back = (own == ids_of(later)) & (later < devices)
        if i == 2:
            same = same & (lane <= row)
        if i == 0:
            same_back = same_back & (lane >= row)
        bias_ref[:, slots + i * rows : slots + (i + 1) * rows] = jnp.where(same, 0.0, -1e30).astype(
            jnp.bfloat16
        )
        back_ref[:, i * rows : (i + 1) * rows] = jnp.where(same_back, 0.0, -1e30)

    mine = jnp.where(routes_ref[...] == me, 1.0, 0.0).astype(jnp.bfloat16)
    counts = dot_t(jnp.ones((8, rows), jnp.bfloat16), mine, ((1,), (1,))).astype(jnp.bfloat16)
    source = lax.broadcasted_iota(jnp.int32, (devices, slots), 0)
    slot = lax.broadcasted_iota(jnp.int32, (devices, slots), 1) // capacity
    expand = jnp.where(source == (slot % n_z) * n_p + slot // n_z, 1.0, 0.0).astype(jnp.bfloat16)
    filled = jnp.dot(counts, expand, preferred_element_type=jnp.float32)[:1]
    rank = lax.broadcasted_iota(jnp.int32, (1, slots), 1) % capacity
    live = jnp.where(rank.astype(jnp.float32) < filled, 0.0, -1e30)
    bias_ref[:, :slots] = jnp.broadcast_to(live, (rows, slots)).astype(jnp.bfloat16)


def prepare(routes, doc_ids, n_z, devices, rows):
    slots = 2 * rows
    return pl.pallas_call(
        prepare_kernel,
        out_shape=[
            jax.ShapeDtypeStruct((n_z, 1, rows), jnp.int32),
            jax.ShapeDtypeStruct((rows, slots + 3 * rows), jnp.bfloat16),
            jax.ShapeDtypeStruct((rows, 3 * rows), jnp.float32),
        ],
        compiler_params=pltpu.CompilerParams(vmem_limit_bytes=SMALL_VMEM),
        name="prepare",
    )(routes.reshape(devices, rows), doc_ids.reshape(devices, rows))


def column_block(w_kv, target):
    _, w_rows, features = w_kv.shape
    half = features // (GROUPS // 2)
    start = (target & 1, 0, (target >> 1) * half)
    return lax.dynamic_slice(w_kv, start, (1, w_rows, half))[0]


def ring_step(value, back=False):
    pairs = list(zip(RING, RING[1:] + RING[:1]))
    return lax.ppermute(value, "z", [(b, a) for a, b in pairs] if back else pairs)


def memory_slots(cache, w_kv, place, capacity, stream, back):
    n_z, n_p = lax.axis_size("z"), lax.axis_size("p")
    devices = n_z * n_p
    cache_rows, depth = cache.shape
    _, w_rows, features = w_kv.shape
    z = lax.axis_index("z")
    if n_p == 4 and capacity % ROW_TILE == 0 and w_rows % ROW_TILE == 0:
        blocks = [column_block(w_kv, z ^ mask) for mask in range(n_z)]
        arrived = swapped(blocks[1], "z", 1)
        row1, other0 = ring_step(cache), swapped(cache, "head", 1)
        arrived, row1, other0, blocks = lax.optimization_barrier((arrived, row1, other0, blocks))
        own_lo = jnp.stack([blocks[0], arrived], 0)
        across_lo = swapped(own_lo, "p", 2)
        own_hi = jnp.stack([swapped(blocks[mask], "z", mask) for mask in (2, 3)], 0)
        row2, other1 = ring_step(row1), swapped(row1, "head", 1)
        own_lo, own_hi, across_lo, row2, other1 = lax.optimization_barrier(
            (own_lo, own_hi, across_lo, row2, other1)
        )
        across_hi = swapped(own_hi, "p", 2)
        beside_lo, beside_hi, beyond_lo = (
            swapped(block, "p", 1) for block in (own_lo, own_hi, across_lo)
        )
        row3, other2 = ring_step(row2), swapped(row2, "head", 1)
        beside_hi, stream, back = lax.optimization_barrier((beside_hi, stream, back))
        near, back1 = shifted(stream, 1), shifted(back, -1)
        row3, other2 = lax.optimization_barrier((row3, other2))
        other3 = swapped(row3, "head", 1)
        across_hi, other3, near, back1, beside_lo, beyond_lo = lax.optimization_barrier(
            (across_hi, other3, near, back1, beside_lo, beyond_lo)
        )
        pieces = [
            (0, 0, own_lo), (0, 2, own_hi), (1, 0, beside_lo), (1, 2, beside_hi),
            (2, 0, across_lo), (2, 2, across_hi),
            (3, 0, beyond_lo), (3, 2, swapped(across_hi, "p", 1)),
        ]
        far = shifted(near, 1)
        rows = [cache, row1, row2, row3, other0, other1, other2, other3]
        slots = project(place, rows, pieces, devices, capacity)
        slots, far, back1 = lax.optimization_barrier((slots, far, back1))
        return slots, near, far, back1
    near, back1 = shifted(stream, 1), shifted(back, -1)
    far = shifted(near, 1)
    targets = [column_block(w_kv, jnp.int32(i)) for i in range(n_z)]
    w_z = lax.all_to_all(jnp.stack(targets, 0), "z", split_axis=0, concat_axis=0, tiled=True)
    w_all = lax.all_gather(w_z, "p", axis=1, tiled=True).reshape(devices * w_rows, -1)
    rows = lax.all_gather(cache, ("head", "z"), axis=0, tiled=False)
    rows = rows.reshape(-1, n_z * cache_rows, depth)
    proj = sum(
        jnp.dot(
            rows[i], w_all[i * depth : (i + 1) * depth], preferred_element_type=jnp.float32
        )
        for i in range(rows.shape[0])
    ).astype(jnp.bfloat16)
    slot_ids = jnp.arange(devices * capacity, dtype=jnp.int32)
    chosen = (slot_ids[None, :, None] == place).astype(jnp.bfloat16)
    slots = jnp.einsum(
        "zsi,zic->zsc",
        chosen,
        proj.reshape(n_z, cache_rows, -1),
        preferred_element_type=jnp.float32,
    ).astype(jnp.bfloat16)
    slots = slots.reshape(n_z, devices, capacity, -1).transpose(1, 0, 2, 3)
    return slots, near, far, back1


def body(queries, keys, values, grad_out, cache, w_kv, doc_ids, routes):
    n_z, n_p = lax.axis_size("z"), lax.axis_size("p")
    devices = n_z * n_p
    seg_rows = queries.shape[0]
    cache_rows = cache.shape[0]
    capacity = 2 * cache_rows // devices
    slot_count = capacity * devices

    place, bias, back_bias = prepare(routes, doc_ids, n_z, devices, seg_rows)
    slots, kv1, kv2, qg1 = memory_slots(
        cache,
        w_kv,
        place,
        capacity,
        jnp.stack([keys, values], 0),
        jnp.stack([queries, grad_out], 0),
    )
    memory = lax.all_to_all(slots, SEQ, split_axis=0, concat_axis=0, tiled=True)
    memory = memory.reshape(n_z, slot_count, slots.shape[-1])

    qg2 = shifted(qg1, -1)
    output, grad_q, stats = attend(queries, grad_out, keys, values, kv1, kv2, memory, bias)
    all_stats = [stats, shifted(stats, -1), shifted(stats, -2)]
    grad_k, grad_v = key_grads(
        keys, values, queries, grad_out, qg1, qg2, all_stats, back_bias
    )
    return (output, grad_q, grad_k, grad_v)


def solution(mesh):
    n_seq, n_head = mesh.devices.shape
    grid = Mesh(mesh.devices.reshape(GROUPS, n_seq // GROUPS, n_head), ("z", "p", "head"))
    rows = P(SEQ, "head")
    return jax.shard_map(
        body,
        mesh=grid,
        in_specs=(rows, rows, rows, rows, rows, P(None, SEQ, "head"), P(), P()),
        out_specs=(rows, rows, rows, rows),
        check_vma=False,
    )
```

```python
import functools

import jax
import jax.numpy as jnp
from jax import lax
from jax.experimental import pallas as pl
from jax.experimental.pallas import tpu as pltpu
from jax.sharding import Mesh, PartitionSpec as P

HD = 128
GROUPS = 4
SEQ = ("z", "p")
ROW_TILE = 16
RING = [0, 1, 3, 2]
VMEM = 24 * 1024 * 1024
SMALL_VMEM = 4 * 1024 * 1024
STATS = 16


def shifted(value, by):
    length = lax.axis_size("z") * lax.axis_size("p")
    pairs = [(i, i + by) for i in range(length) if 0 <= i + by < length]
    return lax.ppermute(value, SEQ, pairs)


def swapped(value, axis, mask):
    return lax.ppermute(value, axis, [(i, i ^ mask) for i in range(lax.axis_size(axis))])


def in_vmem(*arrays):
    return [pltpu.with_memory_space_constraint(array, pltpu.VMEM) for array in arrays]


def in_hbm(*arrays):
    return [pltpu.with_memory_space_constraint(array, pltpu.HBM) for array in arrays]


def dot_t(a, b, dims):
    return lax.dot_general(a, b, (dims, ((), ())), preferred_element_type=jnp.float32)


def attend_kernel(
    q_ref, g_ref, k_ref, v_ref, kv1_ref, kv2_ref, mem_ref, bias_ref, *refs
):
    out_ref, gq_ref, stats_ref = refs[-3:]
    rows, width = q_ref.shape
    scaling = HD ** (-0.5)
    bias = bias_ref[...].astype(jnp.float32)
    step = pl.program_id(0)
    heads = [slice(i * HD, (i + 1) * HD) for i in range(width // HD)]
    ks, vs = (
        [
            jnp.concatenate(
                [
                    mem_ref[2 * step + which, :, cols],
                    kv2_ref[which, :, cols],
                    kv1_ref[which, :, cols],
                    own_ref[:, cols],
                ],
                0,
            )
            for cols in heads
        ]
        for which, own_ref in enumerate((k_ref, v_ref))
    )
    scores = [dot_t(q_ref[:, cols], kh, ((1,), (1,))) + bias for cols, kh in zip(heads, ks)]
    dprobs = [dot_t(g_ref[:, cols], vh, ((1,), (1,))) for cols, vh in zip(heads, vs)]
    tops, shares, probs = [], [], []
    for score in scores:
        top = jnp.max(score, axis=-1, keepdims=True)
        weights = jnp.exp((score - top) * scaling)
        share = 1.0 / jnp.sum(weights, axis=-1, keepdims=True)
        tops.append(top)
        shares.append(share)
        probs.append(weights * share)
    outs = [
        dot_t(prob.astype(jnp.bfloat16), vh, ((1,), (0,))).astype(jnp.bfloat16)
        for prob, vh in zip(probs, vs)
    ]
    deltas, dscores = [], []
    for cols, out_b, prob, dprob in zip(heads, outs, probs, dprobs):
        out_ref[:, cols] = out_b
        delta = jnp.sum(
            g_ref[:, cols].astype(jnp.float32) * out_b.astype(jnp.float32), axis=-1, keepdims=True
        )
        deltas.append(delta)
        dscores.append((prob * ((dprob - delta) * scaling)).astype(jnp.bfloat16))
    lane = lax.broadcasted_iota(jnp.int32, (rows, HD), 1)
    stats = jnp.zeros((rows, HD), jnp.float32)
    for i, column in enumerate(tops + shares + deltas):
        stats = jnp.where(lane == i, column, stats)
    stats_ref[0] = stats.T[:STATS]
    for cols, kh, dscore in zip(heads, ks, dscores):
        gq_ref[:, cols] = dot_t(dscore, kh, ((1,), (0,))).astype(jnp.bfloat16)


def attend(first, queries, grad_out, keys, values, kv1, kv2, memory, bias, earlier):
    rows, features = queries.shape
    steps = memory.shape[0] // 2
    slots, block = memory.shape[1:]
    heads = steps * block // HD
    offset = first // block
    flat = pl.BlockSpec((rows, block), lambda i: (0, i + offset))
    pair = pl.BlockSpec((2, rows, block), lambda i: (0, 0, i + offset))
    whole = pl.BlockSpec(memory_space=pltpu.VMEM)
    keys_all = slots + 3 * rows
    return pl.pallas_call(
        attend_kernel,
        grid=(steps,),
        in_specs=[
            flat, flat, flat, flat, pair, pair, whole,
            pl.BlockSpec((rows, keys_all), lambda i: (0, 0)),
            *([pl.BlockSpec(memory_space=pl.ANY)] * len(earlier)),
        ],
        out_specs=[flat, flat, pl.BlockSpec((1, STATS, rows), lambda i: (i, 0, 0))],
        input_output_aliases={8 + i: i for i in range(len(earlier))},
        out_shape=[
            jax.ShapeDtypeStruct((rows, features), jnp.bfloat16),
            jax.ShapeDtypeStruct((rows, features), jnp.bfloat16),
            jax.ShapeDtypeStruct((steps, STATS, rows), jnp.float32),
        ],
        compiler_params=pltpu.CompilerParams(vmem_limit_bytes=VMEM),
        cost_estimate=pl.CostEstimate(
            flops=2 * 4 * rows * keys_all * HD * heads,
            bytes_accessed=6 * 1024 * 1024,
            transcendentals=rows * keys_all * heads,
        ),
        name="attend",
    )(queries, grad_out, keys, values, *in_hbm(kv1, kv2), *in_vmem(memory), *in_hbm(bias), *earlier)


def key_grads_kernel(
    offset, k_ref, v_ref, q_ref, g_ref, qg1_ref, qg2_ref, st0_ref, st1_ref, st2_ref, bias_ref, *refs
):
    gk_ref, gv_ref = refs[-2:]
    width = k_ref.shape[1]
    scaling = HD ** (-0.5)
    bias = bias_ref[...]
    heads = [slice(i * HD, (i + 1) * HD) for i in range(width // HD)]
    start = (pl.program_id(0) + offset) * width
    picked = [pl.ds(pl.multiple_of(start + i * HD, HD), HD) for i in range(len(heads))]
    stats = jnp.concatenate([st0_ref[0], st1_ref[0], st2_ref[0]], 1)
    qs = [
        jnp.concatenate([q_ref[:, cols], qg1_ref[0, :, wide], qg2_ref[0, :, wide]], 0)
        for cols, wide in zip(heads, picked)
    ]
    gs = [
        jnp.concatenate([g_ref[:, cols], qg1_ref[1, :, wide], qg2_ref[1, :, wide]], 0)
        for cols, wide in zip(heads, picked)
    ]
    scores = [dot_t(k_ref[:, cols], qh, ((1,), (1,))) + bias for cols, qh in zip(heads, qs)]
    dprobs = [dot_t(v_ref[:, cols], gh, ((1,), (1,))) for cols, gh in zip(heads, gs)]
    probs, dscores = [], []
    for i, (score, dprob) in enumerate(zip(scores, dprobs)):
        top, share, delta = (stats[i + j * len(heads) : i + j * len(heads) + 1] for j in range(3))
        prob = jnp.exp((score - top) * scaling) * share
        probs.append(prob.astype(jnp.bfloat16))
        dscores.append((prob * ((dprob - delta) * scaling)).astype(jnp.bfloat16))
    for cols, qh, gh, prob, dscore in zip(heads, qs, gs, probs, dscores):
        gk_ref[:, cols] = dot_t(dscore, qh, ((1,), (0,))).astype(jnp.bfloat16)
        gv_ref[:, cols] = dot_t(prob, gh, ((1,), (0,))).astype(jnp.bfloat16)


def key_grads(first, block, keys, values, queries, grad_out, qg1, qg2, stats, bias, earlier):
    rows, features = keys.shape
    steps = stats[0].shape[0]
    offset = first // block
    flat = pl.BlockSpec((rows, block), lambda i: (0, i + offset))
    whole = pl.BlockSpec(memory_space=pltpu.VMEM)
    stat = pl.BlockSpec((1, STATS, rows), lambda i: (i, 0, 0))
    heads = steps * block // HD
    return pl.pallas_call(
        functools.partial(key_grads_kernel, offset),
        grid=(steps,),
        in_specs=[
            flat, flat, flat, flat, whole, whole, stat, stat, stat, whole,
            *([pl.BlockSpec(memory_space=pl.ANY)] * len(earlier)),
        ],
        out_specs=[flat, flat],
        input_output_aliases={10 + i: i for i in range(len(earlier))},
        out_shape=[jax.ShapeDtypeStruct((rows, features), jnp.bfloat16)] * 2,
        compiler_params=pltpu.CompilerParams(vmem_limit_bytes=VMEM),
        cost_estimate=pl.CostEstimate(
            flops=2 * 4 * rows * 3 * rows * HD * heads,
            bytes_accessed=4 * 1024 * 1024,
            transcendentals=rows * 3 * rows * heads,
        ),
        name="key_grads",
    )(keys, values, queries, grad_out, *in_vmem(qg1, qg2), *stats, *in_vmem(bias), *earlier)


def project_kernel(place_ref, *refs):
    n_z, _, cache_rows = place_ref.shape
    out_ref, w_ref, a_ref = refs[-3:]
    rows, pieces = refs[: 2 * n_z], refs[2 * n_z : -3]
    n_p, (_, w_rows, block) = len(pieces), pieces[0].shape
    depth = rows[0].shape[1]
    devices, _, capacity, _ = out_ref.shape
    z, p, y = (lax.axis_index(name) for name in ("z", "p", "head"))
    place_in_ring = z ^ (z >> 1)
    for i, ref in enumerate(rows):
        source = (place_in_ring - i % n_z + n_z) & (n_z - 1)
        a_ref[y ^ (i // n_z), source ^ (source >> 1)] = ref[...]
    for m in range(n_p):
        for k in range(n_z):
            w_ref[z ^ k, p ^ m] = pieces[m][k]
    half = n_z // 2
    proj = sum(
        jnp.dot(
            a_ref[i].reshape(n_z * cache_rows, depth),
            w_ref[i * half : (i + 1) * half].reshape(depth, block),
            preferred_element_type=jnp.float32,
        )
        for i in range(2)
    ).astype(jnp.bfloat16)
    slot_ids = lax.broadcasted_iota(jnp.int32, (devices * capacity, cache_rows), 0)
    for z in range(n_z):
        chosen = jnp.where(slot_ids == place_ref[z], 1.0, 0.0).astype(jnp.bfloat16)
        slots = jnp.dot(
            chosen,
            proj[z * cache_rows : (z + 1) * cache_rows],
            preferred_element_type=jnp.float32,
        ).astype(jnp.bfloat16)
        out_ref[:, z] = slots.reshape(devices, capacity, block)


def project(place, rows, pieces, devices, capacity):
    n_z, _, cache_rows = place.shape
    depth = rows[0].shape[1]
    n_p = len(pieces)
    _, w_rows, block = pieces[0].shape
    whole = pl.BlockSpec(memory_space=pltpu.VMEM)
    return pl.pallas_call(
        project_kernel,
        in_specs=[whole] * (1 + len(rows) + n_p),
        out_specs=whole,
        out_shape=pltpu.VMEM((devices, n_z, capacity, block), jnp.bfloat16),
        scratch_shapes=[
            pltpu.VMEM((n_z, n_p, w_rows, block), jnp.bfloat16),
            pltpu.VMEM((2, n_z, cache_rows, depth), jnp.bfloat16),
        ],
        compiler_params=pltpu.CompilerParams(vmem_limit_bytes=VMEM),
        cost_estimate=pl.CostEstimate(
            flops=4 * n_z * cache_rows * depth * block,
            bytes_accessed=8 * 1024 * 1024,
            transcendentals=0,
        ),
        name="project",
    )(*in_vmem(place, *rows, *pieces))


def prepare_kernel(routes_ref, ids_ref, place_ref, bias_ref, back_ref):
    n_z, _, rows = place_ref.shape
    devices = routes_ref.shape[0]
    n_p = devices // n_z
    capacity = 2 * rows // devices
    slots = bias_ref.shape[1] - 3 * rows
    p = lax.axis_index("p")
    me = lax.axis_index("z") * n_p + p
    row = lax.broadcasted_iota(jnp.int32, (rows, rows), 0)
    lane = lax.broadcasted_iota(jnp.int32, (rows, rows), 1)

    def both_ways(line):
        wide = jnp.broadcast_to(line.astype(jnp.float32), (rows, rows))
        return wide, wide.T

    for z in range(n_z):
        across, down = both_ways(routes_ref[pl.ds(z * n_p + p, 1), :])
        ranks = jnp.sum(
            jnp.where((across == down) & (row < lane), 1.0, 0.0), axis=0, keepdims=True
        )
        place_ref[z] = (across[:1] * capacity + ranks).astype(jnp.int32)

    def ids_of(segment):
        return ids_ref[pl.ds(jnp.clip(segment, 0, devices - 1), 1), :].astype(jnp.float32)

    _, own = both_ways(ids_ref[pl.ds(me, 1), :])
    for i in range(3):
        earlier, later = me - 2 + i, me + i
        same = (own == ids_of(earlier)) & (earlier >= 0)
        same_back = (own == ids_of(later)) & (later < devices)
        if i == 2:
            same = same & (lane <= row)
        if i == 0:
            same_back = same_back & (lane >= row)
        bias_ref[:, slots + i * rows : slots + (i + 1) * rows] = jnp.where(same, 0.0, -1e30).astype(
            jnp.bfloat16
        )
        back_ref[:, i * rows : (i + 1) * rows] = jnp.where(same_back, 0.0, -1e30)

    mine = jnp.where(routes_ref[...] == me, 1.0, 0.0).astype(jnp.bfloat16)
    counts = dot_t(jnp.ones((8, rows), jnp.bfloat16), mine, ((1,), (1,))).astype(jnp.bfloat16)
    source = lax.broadcasted_iota(jnp.int32, (devices, slots), 0)
    slot = lax.broadcasted_iota(jnp.int32, (devices, slots), 1) // capacity
    expand = jnp.where(source == (slot % n_z) * n_p + slot // n_z, 1.0, 0.0).astype(jnp.bfloat16)
    filled = jnp.dot(counts, expand, preferred_element_type=jnp.float32)[:1]
    rank = lax.broadcasted_iota(jnp.int32, (1, slots), 1) % capacity
    live = jnp.where(rank.astype(jnp.float32) < filled, 0.0, -1e30)
    bias_ref[:, :slots] = jnp.broadcast_to(live, (rows, slots)).astype(jnp.bfloat16)


def prepare(routes, doc_ids, n_z, devices, rows):
    slots = 2 * rows
    return pl.pallas_call(
        prepare_kernel,
        out_shape=[
            jax.ShapeDtypeStruct((n_z, 1, rows), jnp.int32),
            jax.ShapeDtypeStruct((rows, slots + 3 * rows), jnp.bfloat16),
            jax.ShapeDtypeStruct((rows, 3 * rows), jnp.float32),
        ],
        compiler_params=pltpu.CompilerParams(vmem_limit_bytes=SMALL_VMEM),
        name="prepare",
    )(routes.reshape(devices, rows), doc_ids.reshape(devices, rows))


def chunks(features):
    heads = features // HD // 2
    early = (heads + 1) // 2
    return ((0, early * HD), (2 * early * HD, (heads - early) * HD))


def column_block(w_kv, target, chunk):
    first, width = chunk
    start = (target & 1, 0, first + (target >> 1) * width)
    return lax.dynamic_slice(w_kv, start, (1, w_kv.shape[1], width))[0]


def ring_step(value, back=False):
    pairs = list(zip(RING, RING[1:] + RING[:1]))
    return lax.ppermute(value, "z", [(b, a) for a, b in pairs] if back else pairs)


def memory_slots(cache, w_kv, place, capacity, stream, back):
    n_z, n_p = lax.axis_size("z"), lax.axis_size("p")
    devices = n_z * n_p
    cache_rows, depth = cache.shape
    _, w_rows, features = w_kv.shape
    z = lax.axis_index("z")
    if n_p == 4 and capacity % ROW_TILE == 0 and w_rows % ROW_TILE == 0:
        early, late = (
            [column_block(w_kv, z ^ mask, chunk) for mask in range(n_z)]
            for chunk in chunks(features)
        )
        own = jnp.stack(
            [early[0]] + [swapped(early[mask], "z", mask) for mask in range(1, n_z)], 0
        )
        row1, other0 = ring_step(cache), swapped(cache, "head", 1)
        own, row1, other0 = lax.optimization_barrier((own, row1, other0))
        across, beside = swapped(own, "p", 2), swapped(own, "p", 1)
        row2, other1 = ring_step(row1), swapped(row1, "head", 1)
        row2, other1, beside, late = lax.optimization_barrier((row2, other1, beside, late))
        row3, other2 = ring_step(row2), swapped(row2, "head", 1)
        own_late = jnp.stack(
            [late[0]] + [swapped(late[mask], "z", mask) for mask in range(1, n_z)], 0
        )
        across, row3, other2, own_late = lax.optimization_barrier(
            (across, row3, other2, own_late)
        )
        pieces = [own, beside, across, swapped(across, "p", 1)]
        rows = [cache, row1, row2, row3, other0, other1, other2, swapped(row3, "head", 1)]
        slots = [project(place, rows, pieces, devices, capacity)]
        slots[0], own_late, stream, back = lax.optimization_barrier(
            (slots[0], own_late, stream, back)
        )
        near, back1 = shifted(stream, 1), shifted(back, -1)
        across, beside = swapped(own_late, "p", 2), swapped(own_late, "p", 1)
        pieces = [own_late, beside, across, swapped(across, "p", 1)]
        slots.append(project(place, rows, pieces, devices, capacity))
        return slots, near, shifted(near, 1), back1, shifted(back1, -1)
    near, back1 = shifted(stream, 1), shifted(back, -1)
    far, back2 = shifted(near, 1), shifted(back1, -1)
    targets = [
        jnp.concatenate([column_block(w_kv, jnp.int32(i), chunk) for chunk in chunks(features)], 1)
        for i in range(n_z)
    ]
    w_z = lax.all_to_all(jnp.stack(targets, 0), "z", split_axis=0, concat_axis=0, tiled=True)
    w_all = lax.all_gather(w_z, "p", axis=1, tiled=True).reshape(devices * w_rows, -1)
    rows = lax.all_gather(cache, ("head", "z"), axis=0, tiled=False)
    rows = rows.reshape(-1, n_z * cache_rows, depth)
    proj = sum(
        jnp.dot(
            rows[i], w_all[i * depth : (i + 1) * depth], preferred_element_type=jnp.float32
        )
        for i in range(rows.shape[0])
    ).astype(jnp.bfloat16)
    slot_ids = jnp.arange(devices * capacity, dtype=jnp.int32)
    chosen = (slot_ids[None, :, None] == place).astype(jnp.bfloat16)
    slots = jnp.einsum(
        "zsi,zic->zsc",
        chosen,
        proj.reshape(n_z, cache_rows, -1),
        preferred_element_type=jnp.float32,
    ).astype(jnp.bfloat16)
    slots = slots.reshape(n_z, devices, capacity, -1).transpose(1, 0, 2, 3)
    early = chunks(features)[0][1]
    return [slots[..., :early], slots[..., early:]], near, far, back1, back2


def body(queries, keys, values, grad_out, cache, w_kv, doc_ids, routes):
    n_z, n_p = lax.axis_size("z"), lax.axis_size("p")
    devices = n_z * n_p
    seg_rows = queries.shape[0]
    cache_rows = cache.shape[0]
    capacity = 2 * cache_rows // devices
    slot_count = capacity * devices

    place, bias, back_bias = prepare(routes, doc_ids, n_z, devices, seg_rows)
    slots, kv1, kv2, qg1, qg2 = memory_slots(
        cache,
        w_kv,
        place,
        capacity,
        jnp.stack([keys, values], 0),
        jnp.stack([queries, grad_out], 0),
    )
    memory = [lax.all_to_all(part, SEQ, split_axis=0, concat_axis=0, tiled=True) for part in slots]
    outs, grads = [], []
    for part, (first, block) in zip(memory, chunks(queries.shape[1])):
        part = part.reshape(n_z, slot_count, block)
        *outs, stats = attend(
            first, queries, grad_out, keys, values, kv1, kv2, part, bias, outs
        )
        all_stats = [stats, shifted(stats, -1), shifted(stats, -2)]
        grads = key_grads(
            first, block, keys, values, queries, grad_out, qg1, qg2, all_stats, back_bias, grads
        )
    return (*outs, *grads)


def solution(mesh):
    n_seq, n_head = mesh.devices.shape
    grid = Mesh(mesh.devices.reshape(GROUPS, n_seq // GROUPS, n_head), ("z", "p", "head"))
    rows = P(SEQ, "head")
    return jax.shard_map(
        body,
        mesh=grid,
        in_specs=(rows, rows, rows, rows, rows, P(None, SEQ, "head"), P(), P()),
        out_specs=(rows, rows, rows, rows),
        check_vma=False,
    )
```

```python
import jax
import jax.numpy as jnp
from jax import lax
from jax.experimental import pallas as pl
from jax.experimental.pallas import tpu as pltpu
from jax.sharding import Mesh, PartitionSpec as P

HD = 128
GROUPS = 4
SEQ = ("z", "p")
ROW_TILE = 16
RING = [0, 1, 3, 2]
VMEM = 24 * 1024 * 1024
SMALL_VMEM = 4 * 1024 * 1024
STATS = 16


def shifted(value, by):
    length = lax.axis_size("z") * lax.axis_size("p")
    pairs = [(i, i + by) for i in range(length) if 0 <= i + by < length]
    return lax.ppermute(value, SEQ, pairs)


def swapped(value, axis, mask):
    return lax.ppermute(value, axis, [(i, i ^ mask) for i in range(lax.axis_size(axis))])


def in_vmem(*arrays):
    return [pltpu.with_memory_space_constraint(array, pltpu.VMEM) for array in arrays]


def in_hbm(*arrays):
    return [pltpu.with_memory_space_constraint(array, pltpu.HBM) for array in arrays]


def dot_t(a, b, dims):
    return lax.dot_general(a, b, (dims, ((), ())), preferred_element_type=jnp.float32)


def attend_kernel(
    q_ref, g_ref, k_ref, v_ref, kv1_ref, kv2_ref, mem_ref, bias_ref, out_ref, gq_ref, stats_ref
):
    rows, width = q_ref.shape
    scaling = HD ** (-0.5)
    bias = bias_ref[...].astype(jnp.float32)
    step = pl.program_id(0)
    heads = [slice(i * HD, (i + 1) * HD) for i in range(width // HD)]
    ks, vs = (
        [
            jnp.concatenate(
                [
                    mem_ref[2 * step + which, :, cols],
                    kv2_ref[which, :, cols],
                    kv1_ref[which, :, cols],
                    own_ref[:, cols],
                ],
                0,
            )
            for cols in heads
        ]
        for which, own_ref in enumerate((k_ref, v_ref))
    )
    scores = [dot_t(q_ref[:, cols], kh, ((1,), (1,))) + bias for cols, kh in zip(heads, ks)]
    dprobs = [dot_t(g_ref[:, cols], vh, ((1,), (1,))) for cols, vh in zip(heads, vs)]
    tops, shares, probs = [], [], []
    for score in scores:
        top = jnp.max(score, axis=-1, keepdims=True)
        weights = jnp.exp((score - top) * scaling)
        share = 1.0 / jnp.sum(weights, axis=-1, keepdims=True)
        tops.append(top)
        shares.append(share)
        probs.append(weights * share)
    outs = [
        dot_t(prob.astype(jnp.bfloat16), vh, ((1,), (0,))).astype(jnp.bfloat16)
        for prob, vh in zip(probs, vs)
    ]
    deltas, dscores = [], []
    for cols, out_b, prob, dprob in zip(heads, outs, probs, dprobs):
        out_ref[:, cols] = out_b
        delta = jnp.sum(
            g_ref[:, cols].astype(jnp.float32) * out_b.astype(jnp.float32), axis=-1, keepdims=True
        )
        deltas.append(delta)
        dscores.append((prob * ((dprob - delta) * scaling)).astype(jnp.bfloat16))
    lane = lax.broadcasted_iota(jnp.int32, (rows, HD), 1)
    stats = jnp.zeros((rows, HD), jnp.float32)
    for i, column in enumerate(tops + shares + deltas):
        stats = jnp.where(lane == i, column, stats)
    stats_ref[0] = stats.T[:STATS]
    for cols, kh, dscore in zip(heads, ks, dscores):
        gq_ref[:, cols] = dot_t(dscore, kh, ((1,), (0,))).astype(jnp.bfloat16)


def attend(queries, grad_out, keys, values, kv1, kv2, memory, bias):
    rows, features = queries.shape
    steps = memory.shape[0] // 2
    slots, block = memory.shape[1:]
    heads = steps * block // HD
    flat = pl.BlockSpec((rows, block), lambda i: (0, i))
    pair = pl.BlockSpec((2, rows, block), lambda i: (0, 0, i))
    whole = pl.BlockSpec(memory_space=pltpu.VMEM)
    keys_all = slots + 3 * rows
    return pl.pallas_call(
        attend_kernel,
        grid=(steps,),
        in_specs=[
            flat, flat, flat, flat, pair, pair, whole,
            pl.BlockSpec((rows, keys_all), lambda i: (0, 0)),
        ],
        out_specs=[flat, flat, pl.BlockSpec((1, STATS, rows), lambda i: (i, 0, 0))],
        out_shape=[
            jax.ShapeDtypeStruct((rows, features), jnp.bfloat16),
            jax.ShapeDtypeStruct((rows, features), jnp.bfloat16),
            jax.ShapeDtypeStruct((steps, STATS, rows), jnp.float32),
        ],
        compiler_params=pltpu.CompilerParams(vmem_limit_bytes=VMEM),
        cost_estimate=pl.CostEstimate(
            flops=2 * 4 * rows * keys_all * HD * heads,
            bytes_accessed=6 * 1024 * 1024,
            transcendentals=rows * keys_all * heads,
        ),
        name="attend",
    )(queries, grad_out, keys, values, *in_hbm(kv1, kv2), *in_vmem(memory), *in_hbm(bias))


def key_grads_kernel(
    k_ref, v_ref, q_ref, g_ref, qg1_ref, qg2_ref, st0_ref, st1_ref, st2_ref, bias_ref,
    gk_ref, gv_ref,
):
    width = k_ref.shape[1]
    scaling = HD ** (-0.5)
    bias = bias_ref[...]
    heads = [slice(i * HD, (i + 1) * HD) for i in range(width // HD)]
    start = pl.program_id(0) * width
    picked = [pl.ds(pl.multiple_of(start + i * HD, HD), HD) for i in range(len(heads))]
    stats = jnp.concatenate([st0_ref[0], st1_ref[0], st2_ref[0]], 1)
    qs = [
        jnp.concatenate([q_ref[:, cols], qg1_ref[0, :, wide], qg2_ref[0, :, wide]], 0)
        for cols, wide in zip(heads, picked)
    ]
    gs = [
        jnp.concatenate([g_ref[:, cols], qg1_ref[1, :, wide], qg2_ref[1, :, wide]], 0)
        for cols, wide in zip(heads, picked)
    ]
    scores = [dot_t(k_ref[:, cols], qh, ((1,), (1,))) + bias for cols, qh in zip(heads, qs)]
    dprobs = [dot_t(v_ref[:, cols], gh, ((1,), (1,))) for cols, gh in zip(heads, gs)]
    probs, dscores = [], []
    for i, (score, dprob) in enumerate(zip(scores, dprobs)):
        top, share, delta = (stats[i + j * len(heads) : i + j * len(heads) + 1] for j in range(3))
        prob = jnp.exp((score - top) * scaling) * share
        probs.append(prob.astype(jnp.bfloat16))
        dscores.append((prob * ((dprob - delta) * scaling)).astype(jnp.bfloat16))
    for cols, qh, gh, prob, dscore in zip(heads, qs, gs, probs, dscores):
        gk_ref[:, cols] = dot_t(dscore, qh, ((1,), (0,))).astype(jnp.bfloat16)
        gv_ref[:, cols] = dot_t(prob, gh, ((1,), (0,))).astype(jnp.bfloat16)


def key_grads(keys, values, queries, grad_out, qg1, qg2, stats, bias):
    rows, features = keys.shape
    steps = stats[0].shape[0]
    block = features // steps
    flat = pl.BlockSpec((rows, block), lambda i: (0, i))
    whole = pl.BlockSpec(memory_space=pltpu.VMEM)
    stat = pl.BlockSpec((1, STATS, rows), lambda i: (i, 0, 0))
    heads = features // HD
    return pl.pallas_call(
        key_grads_kernel,
        grid=(steps,),
        in_specs=[
            flat, flat, flat, flat, whole, whole, stat, stat, stat, whole,
        ],
        out_specs=[flat, flat],
        out_shape=[jax.ShapeDtypeStruct((rows, features), jnp.bfloat16)] * 2,
        compiler_params=pltpu.CompilerParams(vmem_limit_bytes=VMEM),
        cost_estimate=pl.CostEstimate(
            flops=2 * 4 * rows * 3 * rows * HD * heads,
            bytes_accessed=4 * 1024 * 1024,
            transcendentals=rows * 3 * rows * heads,
        ),
        name="key_grads",
    )(keys, values, queries, grad_out, *in_vmem(qg1, qg2), *stats, *in_vmem(bias))


def project_kernel(place_ref, *refs):
    n_z, _, cache_rows = place_ref.shape
    out_ref, w_ref, a_ref = refs[-3:]
    rows, pieces = refs[: 2 * n_z], refs[2 * n_z : -3]
    n_p, (_, w_rows, block) = len(pieces), pieces[0].shape
    depth = rows[0].shape[1]
    devices, _, capacity, _ = out_ref.shape
    z, p, y = (lax.axis_index(name) for name in ("z", "p", "head"))
    place_in_ring = z ^ (z >> 1)
    for i, ref in enumerate(rows):
        source = (place_in_ring - i % n_z + n_z) & (n_z - 1)
        a_ref[y ^ (i // n_z), source ^ (source >> 1)] = ref[...]
    for m in range(n_p):
        for k in range(n_z):
            w_ref[z ^ k, p ^ m] = pieces[m][k]
    half = n_z // 2
    proj = sum(
        jnp.dot(
            a_ref[i].reshape(n_z * cache_rows, depth),
            w_ref[i * half : (i + 1) * half].reshape(depth, block),
            preferred_element_type=jnp.float32,
        )
        for i in range(2)
    ).astype(jnp.bfloat16)
    slot_ids = lax.broadcasted_iota(jnp.int32, (devices * capacity, cache_rows), 0)
    for z in range(n_z):
        chosen = jnp.where(slot_ids == place_ref[z], 1.0, 0.0).astype(jnp.bfloat16)
        slots = jnp.dot(
            chosen,
            proj[z * cache_rows : (z + 1) * cache_rows],
            preferred_element_type=jnp.float32,
        ).astype(jnp.bfloat16)
        out_ref[:, z] = slots.reshape(devices, capacity, block)


def project(place, rows, pieces, devices, capacity):
    n_z, _, cache_rows = place.shape
    depth = rows[0].shape[1]
    n_p = len(pieces)
    _, w_rows, block = pieces[0].shape
    whole = pl.BlockSpec(memory_space=pltpu.VMEM)
    return pl.pallas_call(
        project_kernel,
        in_specs=[whole] * (1 + len(rows) + n_p),
        out_specs=whole,
        out_shape=pltpu.VMEM((devices, n_z, capacity, block), jnp.bfloat16),
        scratch_shapes=[
            pltpu.VMEM((n_z, n_p, w_rows, block), jnp.bfloat16),
            pltpu.VMEM((2, n_z, cache_rows, depth), jnp.bfloat16),
        ],
        compiler_params=pltpu.CompilerParams(vmem_limit_bytes=VMEM),
        cost_estimate=pl.CostEstimate(
            flops=4 * n_z * cache_rows * depth * block,
            bytes_accessed=8 * 1024 * 1024,
            transcendentals=0,
        ),
        name="project",
    )(*in_vmem(place, *rows, *pieces))


def prepare_kernel(routes_ref, ids_ref, place_ref, bias_ref, back_ref):
    n_z, _, rows = place_ref.shape
    devices = routes_ref.shape[0]
    n_p = devices // n_z
    capacity = 2 * rows // devices
    slots = bias_ref.shape[1] - 3 * rows
    p = lax.axis_index("p")
    me = lax.axis_index("z") * n_p + p
    row = lax.broadcasted_iota(jnp.int32, (rows, rows), 0)
    lane = lax.broadcasted_iota(jnp.int32, (rows, rows), 1)

    def both_ways(line):
        wide = jnp.broadcast_to(line.astype(jnp.float32), (rows, rows))
        return wide, wide.T

    for z in range(n_z):
        across, down = both_ways(routes_ref[pl.ds(z * n_p + p, 1), :])
        ranks = jnp.sum(
            jnp.where((across == down) & (row < lane), 1.0, 0.0), axis=0, keepdims=True
        )
        place_ref[z] = (across[:1] * capacity + ranks).astype(jnp.int32)

    def ids_of(segment):
        return ids_ref[pl.ds(jnp.clip(segment, 0, devices - 1), 1), :].astype(jnp.float32)

    _, own = both_ways(ids_ref[pl.ds(me, 1), :])
    for i in range(3):
        earlier, later = me - 2 + i, me + i
        same = (own == ids_of(earlier)) & (earlier >= 0)
        same_back = (own == ids_of(later)) & (later < devices)
        if i == 2:
            same = same & (lane <= row)
        if i == 0:
            same_back = same_back & (lane >= row)
        bias_ref[:, slots + i * rows : slots + (i + 1) * rows] = jnp.where(same, 0.0, -1e30).astype(
            jnp.bfloat16
        )
        back_ref[:, i * rows : (i + 1) * rows] = jnp.where(same_back, 0.0, -1e30)

    mine = jnp.where(routes_ref[...] == me, 1.0, 0.0).astype(jnp.bfloat16)
    counts = dot_t(jnp.ones((8, rows), jnp.bfloat16), mine, ((1,), (1,))).astype(jnp.bfloat16)
    source = lax.broadcasted_iota(jnp.int32, (devices, slots), 0)
    slot = lax.broadcasted_iota(jnp.int32, (devices, slots), 1) // capacity
    expand = jnp.where(source == (slot % n_z) * n_p + slot // n_z, 1.0, 0.0).astype(jnp.bfloat16)
    filled = jnp.dot(counts, expand, preferred_element_type=jnp.float32)[:1]
    rank = lax.broadcasted_iota(jnp.int32, (1, slots), 1) % capacity
    live = jnp.where(rank.astype(jnp.float32) < filled, 0.0, -1e30)
    bias_ref[:, :slots] = jnp.broadcast_to(live, (rows, slots)).astype(jnp.bfloat16)


def prepare(routes, doc_ids, n_z, devices, rows):
    slots = 2 * rows
    return pl.pallas_call(
        prepare_kernel,
        out_shape=[
            jax.ShapeDtypeStruct((n_z, 1, rows), jnp.int32),
            jax.ShapeDtypeStruct((rows, slots + 3 * rows), jnp.bfloat16),
            jax.ShapeDtypeStruct((rows, 3 * rows), jnp.float32),
        ],
        compiler_params=pltpu.CompilerParams(vmem_limit_bytes=SMALL_VMEM),
        name="prepare",
    )(routes.reshape(devices, rows), doc_ids.reshape(devices, rows))


def column_block(w_kv, target):
    _, w_rows, features = w_kv.shape
    half = features // (GROUPS // 2)
    start = (target & 1, 0, (target >> 1) * half)
    return lax.dynamic_slice(w_kv, start, (1, w_rows, half))[0]


def ring_step(value, back=False):
    pairs = list(zip(RING, RING[1:] + RING[:1]))
    return lax.ppermute(value, "z", [(b, a) for a, b in pairs] if back else pairs)


def memory_slots(cache, w_kv, place, capacity, stream, back):
    n_z, n_p = lax.axis_size("z"), lax.axis_size("p")
    devices = n_z * n_p
    cache_rows, depth = cache.shape
    _, w_rows, features = w_kv.shape
    z = lax.axis_index("z")
    if n_p == 4 and capacity % ROW_TILE == 0 and w_rows % ROW_TILE == 0:
        blocks = [column_block(w_kv, z ^ mask) for mask in range(n_z)]
        own = jnp.stack(
            [blocks[0]] + [swapped(blocks[mask], "z", mask) for mask in range(1, n_z)], 0
        )
        row1, other0 = ring_step(cache), swapped(cache, "head", 1)
        own, row1, other0, cache = lax.optimization_barrier((own, row1, other0, cache))
        across = swapped(own, "p", 2)
        beside = swapped(own, "p", 1)
        row2, other1 = ring_step(row1), swapped(row1, "head", 1)
        row2, other1, beside, cache, other0 = lax.optimization_barrier(
            (row2, other1, beside, cache, other0)
        )
        row3, other3 = ring_step(cache, back=True), ring_step(other0, back=True)
        other2 = swapped(row2, "head", 1)
        across, row3, other2, other3, stream = lax.optimization_barrier(
            (across, row3, other2, other3, stream)
        )
        pieces = [own, beside, across, swapped(across, "p", 1)]
        near = shifted(stream, 1)
        rows = [cache, row1, row2, row3, other0, other1, other2, other3]
        slots = project(place, rows, pieces, devices, capacity)
        slots, near, back = lax.optimization_barrier((slots, near, back))
        return slots, near, shifted(near, 1), shifted(back, -1)
    near, back1 = shifted(stream, 1), shifted(back, -1)
    far = shifted(near, 1)
    targets = [column_block(w_kv, jnp.int32(i)) for i in range(n_z)]
    w_z = lax.all_to_all(jnp.stack(targets, 0), "z", split_axis=0, concat_axis=0, tiled=True)
    w_all = lax.all_gather(w_z, "p", axis=1, tiled=True).reshape(devices * w_rows, -1)
    rows = lax.all_gather(cache, ("head", "z"), axis=0, tiled=False)
    rows = rows.reshape(-1, n_z * cache_rows, depth)
    proj = sum(
        jnp.dot(
            rows[i], w_all[i * depth : (i + 1) * depth], preferred_element_type=jnp.float32
        )
        for i in range(rows.shape[0])
    ).astype(jnp.bfloat16)
    slot_ids = jnp.arange(devices * capacity, dtype=jnp.int32)
    chosen = (slot_ids[None, :, None] == place).astype(jnp.bfloat16)
    slots = jnp.einsum(
        "zsi,zic->zsc",
        chosen,
        proj.reshape(n_z, cache_rows, -1),
        preferred_element_type=jnp.float32,
    ).astype(jnp.bfloat16)
    slots = slots.reshape(n_z, devices, capacity, -1).transpose(1, 0, 2, 3)
    return slots, near, far, back1


def body(queries, keys, values, grad_out, cache, w_kv, doc_ids, routes):
    n_z, n_p = lax.axis_size("z"), lax.axis_size("p")
    devices = n_z * n_p
    seg_rows = queries.shape[0]
    cache_rows = cache.shape[0]
    capacity = 2 * cache_rows // devices
    slot_count = capacity * devices

    place, bias, back_bias = prepare(routes, doc_ids, n_z, devices, seg_rows)
    slots, kv1, kv2, qg1 = memory_slots(
        cache,
        w_kv,
        place,
        capacity,
        jnp.stack([keys, values], 0),
        jnp.stack([queries, grad_out], 0),
    )
    memory = lax.all_to_all(slots, SEQ, split_axis=0, concat_axis=0, tiled=True)
    memory = memory.reshape(n_z, slot_count, slots.shape[-1])

    output, grad_q, stats = attend(queries, grad_out, keys, values, kv1, kv2, memory, bias)
    qg1, stats = lax.optimization_barrier((qg1, stats))
    qg2 = shifted(qg1, -1)
    all_stats = [stats, shifted(stats, -1), shifted(stats, -2)]
    grad_k, grad_v = key_grads(
        keys, values, queries, grad_out, qg1, qg2, all_stats, back_bias
    )
    return (output, grad_q, grad_k, grad_v)


def solution(mesh):
    n_seq, n_head = mesh.devices.shape
    grid = Mesh(mesh.devices.reshape(GROUPS, n_seq // GROUPS, n_head), ("z", "p", "head"))
    rows = P(SEQ, "head")
    return jax.shard_map(
        body,
        mesh=grid,
        in_specs=(rows, rows, rows, rows, rows, P(None, SEQ, "head"), P(), P()),
        out_specs=(rows, rows, rows, rows),
        check_vma=False,
    )
```

```python
import jax
import jax.numpy as jnp
from jax import lax
from jax.experimental import pallas as pl
from jax.experimental.pallas import tpu as pltpu
from jax.sharding import Mesh, PartitionSpec as P

HD = 128
GROUPS = 4
SEQ = ("z", "p")
ROW_TILE = 16
RING = [0, 1, 3, 2]
VMEM = 24 * 1024 * 1024
SMALL_VMEM = 4 * 1024 * 1024
STATS = 16


def shifted(value, by):
    length = lax.axis_size("z") * lax.axis_size("p")
    pairs = [(i, i + by) for i in range(length) if 0 <= i + by < length]
    return lax.ppermute(value, SEQ, pairs)


def swapped(value, axis, mask):
    return lax.ppermute(value, axis, [(i, i ^ mask) for i in range(lax.axis_size(axis))])


def in_vmem(*arrays):
    return [pltpu.with_memory_space_constraint(array, pltpu.VMEM) for array in arrays]


def in_hbm(*arrays):
    return [pltpu.with_memory_space_constraint(array, pltpu.HBM) for array in arrays]


def dot_t(a, b, dims):
    return lax.dot_general(a, b, (dims, ((), ())), preferred_element_type=jnp.float32)


def attend_kernel(
    q_ref, g_ref, k_ref, v_ref, kv1_ref, kv2_ref, mem_ref, bias_ref, out_ref, gq_ref, stats_ref
):
    rows, width = q_ref.shape
    scaling = HD ** (-0.5)
    bias = bias_ref[...].astype(jnp.float32)
    step = pl.program_id(0)
    heads = [slice(i * HD, (i + 1) * HD) for i in range(width // HD)]
    ks, vs = (
        [
            jnp.concatenate(
                [
                    mem_ref[2 * step + which, :, cols],
                    kv2_ref[which, :, cols],
                    kv1_ref[which, :, cols],
                    own_ref[:, cols],
                ],
                0,
            )
            for cols in heads
        ]
        for which, own_ref in enumerate((k_ref, v_ref))
    )
    scores = [dot_t(q_ref[:, cols], kh, ((1,), (1,))) + bias for cols, kh in zip(heads, ks)]
    dprobs = [dot_t(g_ref[:, cols], vh, ((1,), (1,))) for cols, vh in zip(heads, vs)]
    tops, shares, probs = [], [], []
    for score in scores:
        top = jnp.max(score, axis=-1, keepdims=True)
        weights = jnp.exp((score - top) * scaling)
        share = 1.0 / jnp.sum(weights, axis=-1, keepdims=True)
        tops.append(top)
        shares.append(share)
        probs.append(weights * share)
    outs = [
        dot_t(prob.astype(jnp.bfloat16), vh, ((1,), (0,))).astype(jnp.bfloat16)
        for prob, vh in zip(probs, vs)
    ]
    deltas, dscores = [], []
    for cols, out_b, prob, dprob in zip(heads, outs, probs, dprobs):
        out_ref[:, cols] = out_b
        delta = jnp.sum(
            g_ref[:, cols].astype(jnp.float32) * out_b.astype(jnp.float32), axis=-1, keepdims=True
        )
        deltas.append(delta)
        dscores.append((prob * ((dprob - delta) * scaling)).astype(jnp.bfloat16))
    lane = lax.broadcasted_iota(jnp.int32, (rows, HD), 1)
    stats = jnp.zeros((rows, HD), jnp.float32)
    for i, column in enumerate(tops + shares + deltas):
        stats = jnp.where(lane == i, column, stats)
    stats_ref[0] = stats.T[:STATS]
    for cols, kh, dscore in zip(heads, ks, dscores):
        gq_ref[:, cols] = dot_t(dscore, kh, ((1,), (0,))).astype(jnp.bfloat16)


def attend(queries, grad_out, keys, values, kv1, kv2, memory, bias):
    rows, features = queries.shape
    steps = memory.shape[0] // 2
    slots, block = memory.shape[1:]
    heads = steps * block // HD
    flat = pl.BlockSpec((rows, block), lambda i: (0, i))
    pair = pl.BlockSpec((2, rows, block), lambda i: (0, 0, i))
    whole = pl.BlockSpec(memory_space=pltpu.VMEM)
    keys_all = slots + 3 * rows
    return pl.pallas_call(
        attend_kernel,
        grid=(steps,),
        in_specs=[
            flat, flat, flat, flat, pair, pair, whole,
            pl.BlockSpec((rows, keys_all), lambda i: (0, 0)),
        ],
        out_specs=[flat, flat, pl.BlockSpec((1, STATS, rows), lambda i: (i, 0, 0))],
        out_shape=[
            jax.ShapeDtypeStruct((rows, features), jnp.bfloat16),
            jax.ShapeDtypeStruct((rows, features), jnp.bfloat16),
            jax.ShapeDtypeStruct((steps, STATS, rows), jnp.float32),
        ],
        compiler_params=pltpu.CompilerParams(vmem_limit_bytes=VMEM),
        cost_estimate=pl.CostEstimate(
            flops=2 * 4 * rows * keys_all * HD * heads,
            bytes_accessed=6 * 1024 * 1024,
            transcendentals=rows * keys_all * heads,
        ),
        name="attend",
    )(queries, grad_out, keys, values, *in_hbm(kv1, kv2), *in_vmem(memory), *in_hbm(bias))


def key_grads_kernel(
    k_ref, v_ref, q_ref, g_ref, qg1_ref, qg2_ref, st0_ref, st1_ref, st2_ref, bias_ref,
    gk_ref, gv_ref,
):
    width = k_ref.shape[1]
    scaling = HD ** (-0.5)
    bias = bias_ref[...]
    heads = [slice(i * HD, (i + 1) * HD) for i in range(width // HD)]
    start = pl.program_id(0) * width
    picked = [pl.ds(pl.multiple_of(start + i * HD, HD), HD) for i in range(len(heads))]
    stats = jnp.concatenate([st0_ref[0], st1_ref[0], st2_ref[0]], 1)
    qs = [
        jnp.concatenate([q_ref[:, cols], qg1_ref[0, :, wide], qg2_ref[0, :, wide]], 0)
        for cols, wide in zip(heads, picked)
    ]
    gs = [
        jnp.concatenate([g_ref[:, cols], qg1_ref[1, :, wide], qg2_ref[1, :, wide]], 0)
        for cols, wide in zip(heads, picked)
    ]
    scores = [dot_t(k_ref[:, cols], qh, ((1,), (1,))) + bias for cols, qh in zip(heads, qs)]
    dprobs = [dot_t(v_ref[:, cols], gh, ((1,), (1,))) for cols, gh in zip(heads, gs)]
    probs, dscores = [], []
    for i, (score, dprob) in enumerate(zip(scores, dprobs)):
        top, share, delta = (stats[i + j * len(heads) : i + j * len(heads) + 1] for j in range(3))
        prob = jnp.exp((score - top) * scaling) * share
        probs.append(prob.astype(jnp.bfloat16))
        dscores.append((prob * ((dprob - delta) * scaling)).astype(jnp.bfloat16))
    for cols, qh, gh, prob, dscore in zip(heads, qs, gs, probs, dscores):
        gk_ref[:, cols] = dot_t(dscore, qh, ((1,), (0,))).astype(jnp.bfloat16)
        gv_ref[:, cols] = dot_t(prob, gh, ((1,), (0,))).astype(jnp.bfloat16)


def key_grads(keys, values, queries, grad_out, qg1, qg2, stats, bias):
    rows, features = keys.shape
    steps = stats[0].shape[0]
    block = features // steps
    flat = pl.BlockSpec((rows, block), lambda i: (0, i))
    whole = pl.BlockSpec(memory_space=pltpu.VMEM)
    stat = pl.BlockSpec((1, STATS, rows), lambda i: (i, 0, 0))
    heads = features // HD
    return pl.pallas_call(
        key_grads_kernel,
        grid=(steps,),
        in_specs=[
            flat, flat, flat, flat, whole, whole, stat, stat, stat, whole,
        ],
        out_specs=[flat, flat],
        out_shape=[jax.ShapeDtypeStruct((rows, features), jnp.bfloat16)] * 2,
        compiler_params=pltpu.CompilerParams(vmem_limit_bytes=VMEM),
        cost_estimate=pl.CostEstimate(
            flops=2 * 4 * rows * 3 * rows * HD * heads,
            bytes_accessed=4 * 1024 * 1024,
            transcendentals=rows * 3 * rows * heads,
        ),
        name="key_grads",
    )(keys, values, queries, grad_out, *in_vmem(qg1, qg2), *stats, *in_vmem(bias))


def project_kernel(place_ref, *refs):
    n_z, _, cache_rows = place_ref.shape
    out_ref, w_ref, a_ref = refs[-3:]
    rows, pieces = refs[: 2 * n_z], refs[2 * n_z : -3]
    n_p, (_, w_rows, block) = len(pieces), pieces[0].shape
    depth = rows[0].shape[1]
    devices, _, capacity, _ = out_ref.shape
    z, p, y = (lax.axis_index(name) for name in ("z", "p", "head"))
    place_in_ring = z ^ (z >> 1)
    for i, ref in enumerate(rows):
        source = (place_in_ring - i % n_z + n_z) & (n_z - 1)
        a_ref[y ^ (i // n_z), source ^ (source >> 1)] = ref[...]
    for m in range(n_p):
        for k in range(n_z):
            w_ref[z ^ k, p ^ m] = pieces[m][k]
    half = n_z // 2
    proj = sum(
        jnp.dot(
            a_ref[i].reshape(n_z * cache_rows, depth),
            w_ref[i * half : (i + 1) * half].reshape(depth, block),
            preferred_element_type=jnp.float32,
        )
        for i in range(2)
    ).astype(jnp.bfloat16)
    slot_ids = lax.broadcasted_iota(jnp.int32, (devices * capacity, cache_rows), 0)
    for z in range(n_z):
        chosen = jnp.where(slot_ids == place_ref[z], 1.0, 0.0).astype(jnp.bfloat16)
        slots = jnp.dot(
            chosen,
            proj[z * cache_rows : (z + 1) * cache_rows],
            preferred_element_type=jnp.float32,
        ).astype(jnp.bfloat16)
        out_ref[:, z] = slots.reshape(devices, capacity, block)


def project(place, rows, pieces, devices, capacity):
    n_z, _, cache_rows = place.shape
    depth = rows[0].shape[1]
    n_p = len(pieces)
    _, w_rows, block = pieces[0].shape
    whole = pl.BlockSpec(memory_space=pltpu.VMEM)
    return pl.pallas_call(
        project_kernel,
        in_specs=[whole] * (1 + len(rows) + n_p),
        out_specs=whole,
        out_shape=pltpu.VMEM((devices, n_z, capacity, block), jnp.bfloat16),
        scratch_shapes=[
            pltpu.VMEM((n_z, n_p, w_rows, block), jnp.bfloat16),
            pltpu.VMEM((2, n_z, cache_rows, depth), jnp.bfloat16),
        ],
        compiler_params=pltpu.CompilerParams(vmem_limit_bytes=VMEM),
        cost_estimate=pl.CostEstimate(
            flops=4 * n_z * cache_rows * depth * block,
            bytes_accessed=8 * 1024 * 1024,
            transcendentals=0,
        ),
        name="project",
    )(*in_vmem(place, *rows, *pieces))


def prepare_kernel(routes_ref, ids_ref, place_ref, bias_ref, back_ref):
    n_z, _, rows = place_ref.shape
    devices = routes_ref.shape[0]
    n_p = devices // n_z
    capacity = 2 * rows // devices
    slots = bias_ref.shape[1] - 3 * rows
    p = lax.axis_index("p")
    me = lax.axis_index("z") * n_p + p
    row = lax.broadcasted_iota(jnp.int32, (rows, rows), 0)
    lane = lax.broadcasted_iota(jnp.int32, (rows, rows), 1)

    def both_ways(line):
        wide = jnp.broadcast_to(line.astype(jnp.float32), (rows, rows))
        return wide, wide.T

    for z in range(n_z):
        across, down = both_ways(routes_ref[pl.ds(z * n_p + p, 1), :])
        ranks = jnp.sum(
            jnp.where((across == down) & (row < lane), 1.0, 0.0), axis=0, keepdims=True
        )
        place_ref[z] = (across[:1] * capacity + ranks).astype(jnp.int32)

    def ids_of(segment):
        return ids_ref[pl.ds(jnp.clip(segment, 0, devices - 1), 1), :].astype(jnp.float32)

    _, own = both_ways(ids_ref[pl.ds(me, 1), :])
    for i in range(3):
        earlier, later = me - 2 + i, me + i
        same = (own == ids_of(earlier)) & (earlier >= 0)
        same_back = (own == ids_of(later)) & (later < devices)
        if i == 2:
            same = same & (lane <= row)
        if i == 0:
            same_back = same_back & (lane >= row)
        bias_ref[:, slots + i * rows : slots + (i + 1) * rows] = jnp.where(same, 0.0, -1e30).astype(
            jnp.bfloat16
        )
        back_ref[:, i * rows : (i + 1) * rows] = jnp.where(same_back, 0.0, -1e30)

    mine = jnp.where(routes_ref[...] == me, 1.0, 0.0).astype(jnp.bfloat16)
    counts = dot_t(jnp.ones((8, rows), jnp.bfloat16), mine, ((1,), (1,))).astype(jnp.bfloat16)
    source = lax.broadcasted_iota(jnp.int32, (devices, slots), 0)
    slot = lax.broadcasted_iota(jnp.int32, (devices, slots), 1) // capacity
    expand = jnp.where(source == (slot % n_z) * n_p + slot // n_z, 1.0, 0.0).astype(jnp.bfloat16)
    filled = jnp.dot(counts, expand, preferred_element_type=jnp.float32)[:1]
    rank = lax.broadcasted_iota(jnp.int32, (1, slots), 1) % capacity
    live = jnp.where(rank.astype(jnp.float32) < filled, 0.0, -1e30)
    bias_ref[:, :slots] = jnp.broadcast_to(live, (rows, slots)).astype(jnp.bfloat16)


def prepare(routes, doc_ids, n_z, devices, rows):
    slots = 2 * rows
    return pl.pallas_call(
        prepare_kernel,
        out_shape=[
            jax.ShapeDtypeStruct((n_z, 1, rows), jnp.int32),
            jax.ShapeDtypeStruct((rows, slots + 3 * rows), jnp.bfloat16),
            jax.ShapeDtypeStruct((rows, 3 * rows), jnp.float32),
        ],
        compiler_params=pltpu.CompilerParams(vmem_limit_bytes=SMALL_VMEM),
        name="prepare",
    )(routes.reshape(devices, rows), doc_ids.reshape(devices, rows))


def column_block(w_kv, target):
    _, w_rows, features = w_kv.shape
    half = features // (GROUPS // 2)
    start = (target & 1, 0, (target >> 1) * half)
    return lax.dynamic_slice(w_kv, start, (1, w_rows, half))[0]


def ring_step(value, back=False):
    pairs = list(zip(RING, RING[1:] + RING[:1]))
    return lax.ppermute(value, "z", [(b, a) for a, b in pairs] if back else pairs)


def memory_slots(cache, w_kv, place, capacity, stream, back):
    n_z, n_p = lax.axis_size("z"), lax.axis_size("p")
    devices = n_z * n_p
    cache_rows, depth = cache.shape
    _, w_rows, features = w_kv.shape
    z = lax.axis_index("z")
    if n_p == 4 and capacity % ROW_TILE == 0 and w_rows % ROW_TILE == 0:
        blocks = [column_block(w_kv, z ^ mask) for mask in range(n_z)]
        own = jnp.stack(
            [blocks[0]] + [swapped(blocks[mask], "z", mask) for mask in range(1, n_z)], 0
        )
        row1, other0 = ring_step(cache), swapped(cache, "head", 1)
        own, row1, other0, cache = lax.optimization_barrier((own, row1, other0, cache))
        across = swapped(own, "p", 2)
        beside = swapped(own, "p", 1)
        row2, other1 = ring_step(row1), swapped(row1, "head", 1)
        row2, other1, beside, cache, other0, stream, back = lax.optimization_barrier(
            (row2, other1, beside, cache, other0, stream, back)
        )
        row3, other3 = ring_step(cache, back=True), ring_step(other0, back=True)
        other2 = swapped(row2, "head", 1)
        near, back1 = shifted(stream, 1), shifted(back, -1)
        across, row3, other2, other3 = lax.optimization_barrier((across, row3, other2, other3))
        pieces = [own, beside, across, swapped(across, "p", 1)]
        far = shifted(near, 1)
        rows = [cache, row1, row2, row3, other0, other1, other2, other3]
        slots = project(place, rows, pieces, devices, capacity)
        slots, far, back1 = lax.optimization_barrier((slots, far, back1))
        return slots, near, far, back1
    near, back1 = shifted(stream, 1), shifted(back, -1)
    far = shifted(near, 1)
    targets = [column_block(w_kv, jnp.int32(i)) for i in range(n_z)]
    w_z = lax.all_to_all(jnp.stack(targets, 0), "z", split_axis=0, concat_axis=0, tiled=True)
    w_all = lax.all_gather(w_z, "p", axis=1, tiled=True).reshape(devices * w_rows, -1)
    rows = lax.all_gather(cache, ("head", "z"), axis=0, tiled=False)
    rows = rows.reshape(-1, n_z * cache_rows, depth)
    proj = sum(
        jnp.dot(
            rows[i], w_all[i * depth : (i + 1) * depth], preferred_element_type=jnp.float32
        )
        for i in range(rows.shape[0])
    ).astype(jnp.bfloat16)
    slot_ids = jnp.arange(devices * capacity, dtype=jnp.int32)
    chosen = (slot_ids[None, :, None] == place).astype(jnp.bfloat16)
    slots = jnp.einsum(
        "zsi,zic->zsc",
        chosen,
        proj.reshape(n_z, cache_rows, -1),
        preferred_element_type=jnp.float32,
    ).astype(jnp.bfloat16)
    slots = slots.reshape(n_z, devices, capacity, -1).transpose(1, 0, 2, 3)
    return slots, near, far, back1


def body(queries, keys, values, grad_out, cache, w_kv, doc_ids, routes):
    n_z, n_p = lax.axis_size("z"), lax.axis_size("p")
    devices = n_z * n_p
    seg_rows = queries.shape[0]
    cache_rows = cache.shape[0]
    capacity = 2 * cache_rows // devices
    slot_count = capacity * devices

    place, bias, back_bias = prepare(routes, doc_ids, n_z, devices, seg_rows)
    slots, kv1, kv2, qg1 = memory_slots(
        cache,
        w_kv,
        place,
        capacity,
        jnp.stack([keys, values], 0),
        jnp.stack([queries, grad_out], 0),
    )
    memory = lax.all_to_all(slots, SEQ, split_axis=0, concat_axis=0, tiled=True)
    memory = memory.reshape(n_z, slot_count, slots.shape[-1])

    qg2 = shifted(qg1, -1)
    output, grad_q, stats = attend(queries, grad_out, keys, values, kv1, kv2, memory, bias)
    all_stats = [stats, shifted(stats, -1), shifted(stats, -2)]
    grad_k, grad_v = key_grads(
        keys, values, queries, grad_out, qg1, qg2, all_stats, back_bias
    )
    return (output, grad_q, grad_k, grad_v)


def solution(mesh):
    n_seq, n_head = mesh.devices.shape
    grid = Mesh(mesh.devices.reshape(GROUPS, n_seq // GROUPS, n_head), ("z", "p", "head"))
    rows = P(SEQ, "head")
    return jax.shard_map(
        body,
        mesh=grid,
        in_specs=(rows, rows, rows, rows, rows, P(None, SEQ, "head"), P(), P()),
        out_specs=(rows, rows, rows, rows),
        check_vma=False,
    )
```

```python
import jax
import jax.numpy as jnp
from jax import lax
from jax.experimental import pallas as pl
from jax.experimental.pallas import tpu as pltpu
from jax.sharding import Mesh, PartitionSpec as P

HD = 128
GROUPS = 4
SEQ = ("z", "p")
ROW_TILE = 16
RING = [0, 1, 3, 2]
VMEM = 24 * 1024 * 1024
SMALL_VMEM = 4 * 1024 * 1024
STATS = 16


def shifted(value, by):
    length = lax.axis_size("z") * lax.axis_size("p")
    pairs = [(i, i + by) for i in range(length) if 0 <= i + by < length]
    return lax.ppermute(value, SEQ, pairs)


def swapped(value, axis, mask):
    return lax.ppermute(value, axis, [(i, i ^ mask) for i in range(lax.axis_size(axis))])


def in_vmem(*arrays):
    return [pltpu.with_memory_space_constraint(array, pltpu.VMEM) for array in arrays]


def in_hbm(*arrays):
    return [pltpu.with_memory_space_constraint(array, pltpu.HBM) for array in arrays]


def dot_t(a, b, dims):
    return lax.dot_general(a, b, (dims, ((), ())), preferred_element_type=jnp.float32)


def attend_kernel(
    q_ref, g_ref, k_ref, v_ref, kv1_ref, kv2_ref, mem_ref, bias_ref, out_ref, gq_ref, stats_ref
):
    rows, width = q_ref.shape
    scaling = HD ** (-0.5)
    bias = bias_ref[...].astype(jnp.float32)
    step = pl.program_id(0)
    heads = [slice(i * HD, (i + 1) * HD) for i in range(width // HD)]
    ks, vs = (
        [
            jnp.concatenate(
                [
                    mem_ref[2 * step + which, :, cols],
                    kv2_ref[which, :, cols],
                    kv1_ref[which, :, cols],
                    own_ref[:, cols],
                ],
                0,
            )
            for cols in heads
        ]
        for which, own_ref in enumerate((k_ref, v_ref))
    )
    scores = [dot_t(q_ref[:, cols], kh, ((1,), (1,))) + bias for cols, kh in zip(heads, ks)]
    dprobs = [dot_t(g_ref[:, cols], vh, ((1,), (1,))) for cols, vh in zip(heads, vs)]
    tops, shares, probs = [], [], []
    for score in scores:
        top = jnp.max(score, axis=-1, keepdims=True)
        weights = jnp.exp((score - top) * scaling)
        share = 1.0 / jnp.sum(weights, axis=-1, keepdims=True)
        tops.append(top)
        shares.append(share)
        probs.append(weights * share)
    outs = [
        dot_t(prob.astype(jnp.bfloat16), vh, ((1,), (0,))).astype(jnp.bfloat16)
        for prob, vh in zip(probs, vs)
    ]
    deltas, dscores = [], []
    for cols, out_b, prob, dprob in zip(heads, outs, probs, dprobs):
        out_ref[:, cols] = out_b
        delta = jnp.sum(
            g_ref[:, cols].astype(jnp.float32) * out_b.astype(jnp.float32), axis=-1, keepdims=True
        )
        deltas.append(delta)
        dscores.append((prob * ((dprob - delta) * scaling)).astype(jnp.bfloat16))
    lane = lax.broadcasted_iota(jnp.int32, (rows, HD), 1)
    stats = jnp.zeros((rows, HD), jnp.float32)
    for i, column in enumerate(tops + shares + deltas):
        stats = jnp.where(lane == i, column, stats)
    stats_ref[0] = stats.T[:STATS]
    for cols, kh, dscore in zip(heads, ks, dscores):
        gq_ref[:, cols] = dot_t(dscore, kh, ((1,), (0,))).astype(jnp.bfloat16)


def attend(queries, grad_out, keys, values, kv1, kv2, memory, bias):
    rows, features = queries.shape
    steps = memory.shape[0] // 2
    slots, block = memory.shape[1:]
    heads = steps * block // HD
    flat = pl.BlockSpec((rows, block), lambda i: (0, i))
    pair = pl.BlockSpec((2, rows, block), lambda i: (0, 0, i))
    whole = pl.BlockSpec(memory_space=pltpu.VMEM)
    keys_all = slots + 3 * rows
    return pl.pallas_call(
        attend_kernel,
        grid=(steps,),
        in_specs=[
            flat, flat, flat, flat, pair, pair, whole,
            pl.BlockSpec((rows, keys_all), lambda i: (0, 0)),
        ],
        out_specs=[flat, flat, pl.BlockSpec((1, STATS, rows), lambda i: (i, 0, 0))],
        out_shape=[
            jax.ShapeDtypeStruct((rows, features), jnp.bfloat16),
            jax.ShapeDtypeStruct((rows, features), jnp.bfloat16),
            jax.ShapeDtypeStruct((steps, STATS, rows), jnp.float32),
        ],
        compiler_params=pltpu.CompilerParams(vmem_limit_bytes=VMEM),
        cost_estimate=pl.CostEstimate(
            flops=2 * 4 * rows * keys_all * HD * heads,
            bytes_accessed=6 * 1024 * 1024,
            transcendentals=rows * keys_all * heads,
        ),
        name="attend",
    )(queries, grad_out, keys, values, *in_hbm(kv1, kv2), *in_vmem(memory), *in_hbm(bias))


def key_grads_kernel(
    k_ref, v_ref, q_ref, g_ref, qg1_ref, qg2_ref, st0_ref, st1_ref, st2_ref, bias_ref,
    gk_ref, gv_ref,
):
    width = k_ref.shape[1]
    scaling = HD ** (-0.5)
    bias = bias_ref[...]
    heads = [slice(i * HD, (i + 1) * HD) for i in range(width // HD)]
    start = pl.program_id(0) * width
    picked = [pl.ds(pl.multiple_of(start + i * HD, HD), HD) for i in range(len(heads))]
    stats = jnp.concatenate([st0_ref[0], st1_ref[0], st2_ref[0]], 1)
    qs = [
        jnp.concatenate([q_ref[:, cols], qg1_ref[0, :, wide], qg2_ref[0, :, wide]], 0)
        for cols, wide in zip(heads, picked)
    ]
    gs = [
        jnp.concatenate([g_ref[:, cols], qg1_ref[1, :, wide], qg2_ref[1, :, wide]], 0)
        for cols, wide in zip(heads, picked)
    ]
    scores = [dot_t(k_ref[:, cols], qh, ((1,), (1,))) + bias for cols, qh in zip(heads, qs)]
    dprobs = [dot_t(v_ref[:, cols], gh, ((1,), (1,))) for cols, gh in zip(heads, gs)]
    probs, dscores = [], []
    for i, (score, dprob) in enumerate(zip(scores, dprobs)):
        top, share, delta = (stats[i + j * len(heads) : i + j * len(heads) + 1] for j in range(3))
        prob = jnp.exp((score - top) * scaling) * share
        probs.append(prob.astype(jnp.bfloat16))
        dscores.append((prob * ((dprob - delta) * scaling)).astype(jnp.bfloat16))
    for cols, qh, gh, prob, dscore in zip(heads, qs, gs, probs, dscores):
        gk_ref[:, cols] = dot_t(dscore, qh, ((1,), (0,))).astype(jnp.bfloat16)
        gv_ref[:, cols] = dot_t(prob, gh, ((1,), (0,))).astype(jnp.bfloat16)


def key_grads(keys, values, queries, grad_out, qg1, qg2, stats, bias):
    rows, features = keys.shape
    steps = stats[0].shape[0]
    block = features // steps
    flat = pl.BlockSpec((rows, block), lambda i: (0, i))
    whole = pl.BlockSpec(memory_space=pltpu.VMEM)
    stat = pl.BlockSpec((1, STATS, rows), lambda i: (i, 0, 0))
    heads = features // HD
    return pl.pallas_call(
        key_grads_kernel,
        grid=(steps,),
        in_specs=[
            flat, flat, flat, flat, whole, whole, stat, stat, stat, whole,
        ],
        out_specs=[flat, flat],
        out_shape=[jax.ShapeDtypeStruct((rows, features), jnp.bfloat16)] * 2,
        compiler_params=pltpu.CompilerParams(vmem_limit_bytes=VMEM),
        cost_estimate=pl.CostEstimate(
            flops=2 * 4 * rows * 3 * rows * HD * heads,
            bytes_accessed=4 * 1024 * 1024,
            transcendentals=rows * 3 * rows * heads,
        ),
        name="key_grads",
    )(keys, values, queries, grad_out, *in_vmem(qg1, qg2), *stats, *in_vmem(bias))


def project_kernel(place_ref, *refs):
    n_z, _, cache_rows = place_ref.shape
    out_ref, w_ref, a_ref = refs[-3:]
    rows, pieces = refs[: 2 * n_z], refs[2 * n_z : -3]
    n_p, (_, w_rows, block) = len(pieces), pieces[0].shape
    depth = rows[0].shape[1]
    devices, _, capacity, _ = out_ref.shape
    z, p, y = (lax.axis_index(name) for name in ("z", "p", "head"))
    place_in_ring = z ^ (z >> 1)
    for i, ref in enumerate(rows):
        source = (place_in_ring - i % n_z + n_z) & (n_z - 1)
        a_ref[y ^ (i // n_z), source ^ (source >> 1)] = ref[...]
    for m in range(n_p):
        for k in range(n_z):
            w_ref[z ^ k, p ^ m] = pieces[m][k]
    half = n_z // 2
    proj = sum(
        jnp.dot(
            a_ref[i].reshape(n_z * cache_rows, depth),
            w_ref[i * half : (i + 1) * half].reshape(depth, block),
            preferred_element_type=jnp.float32,
        )
        for i in range(2)
    ).astype(jnp.bfloat16)
    slot_ids = lax.broadcasted_iota(jnp.int32, (devices * capacity, cache_rows), 0)
    for z in range(n_z):
        chosen = jnp.where(slot_ids == place_ref[z], 1.0, 0.0).astype(jnp.bfloat16)
        slots = jnp.dot(
            chosen,
            proj[z * cache_rows : (z + 1) * cache_rows],
            preferred_element_type=jnp.float32,
        ).astype(jnp.bfloat16)
        out_ref[:, z] = slots.reshape(devices, capacity, block)


def project(place, rows, pieces, devices, capacity):
    n_z, _, cache_rows = place.shape
    depth = rows[0].shape[1]
    n_p = len(pieces)
    _, w_rows, block = pieces[0].shape
    whole = pl.BlockSpec(memory_space=pltpu.VMEM)
    return pl.pallas_call(
        project_kernel,
        in_specs=[whole] * (1 + len(rows) + n_p),
        out_specs=whole,
        out_shape=pltpu.VMEM((devices, n_z, capacity, block), jnp.bfloat16),
        scratch_shapes=[
            pltpu.VMEM((n_z, n_p, w_rows, block), jnp.bfloat16),
            pltpu.VMEM((2, n_z, cache_rows, depth), jnp.bfloat16),
        ],
        compiler_params=pltpu.CompilerParams(vmem_limit_bytes=VMEM),
        cost_estimate=pl.CostEstimate(
            flops=4 * n_z * cache_rows * depth * block,
            bytes_accessed=8 * 1024 * 1024,
            transcendentals=0,
        ),
        name="project",
    )(*in_vmem(place, *rows, *pieces))


def prepare_kernel(routes_ref, ids_ref, place_ref, bias_ref, back_ref):
    n_z, _, rows = place_ref.shape
    devices = routes_ref.shape[0]
    n_p = devices // n_z
    capacity = 2 * rows // devices
    slots = bias_ref.shape[1] - 3 * rows
    p = lax.axis_index("p")
    me = lax.axis_index("z") * n_p + p
    row = lax.broadcasted_iota(jnp.int32, (rows, rows), 0)
    lane = lax.broadcasted_iota(jnp.int32, (rows, rows), 1)

    def both_ways(line):
        wide = jnp.broadcast_to(line.astype(jnp.float32), (rows, rows))
        return wide, wide.T

    for z in range(n_z):
        across, down = both_ways(routes_ref[pl.ds(z * n_p + p, 1), :])
        ranks = jnp.sum(
            jnp.where((across == down) & (row < lane), 1.0, 0.0), axis=0, keepdims=True
        )
        place_ref[z] = (across[:1] * capacity + ranks).astype(jnp.int32)

    def ids_of(segment):
        return ids_ref[pl.ds(jnp.clip(segment, 0, devices - 1), 1), :].astype(jnp.float32)

    _, own = both_ways(ids_ref[pl.ds(me, 1), :])
    for i in range(3):
        earlier, later = me - 2 + i, me + i
        same = (own == ids_of(earlier)) & (earlier >= 0)
        same_back = (own == ids_of(later)) & (later < devices)
        if i == 2:
            same = same & (lane <= row)
        if i == 0:
            same_back = same_back & (lane >= row)
        bias_ref[:, slots + i * rows : slots + (i + 1) * rows] = jnp.where(same, 0.0, -1e30).astype(
            jnp.bfloat16
        )
        back_ref[:, i * rows : (i + 1) * rows] = jnp.where(same_back, 0.0, -1e30)

    mine = jnp.where(routes_ref[...] == me, 1.0, 0.0).astype(jnp.bfloat16)
    counts = dot_t(jnp.ones((8, rows), jnp.bfloat16), mine, ((1,), (1,))).astype(jnp.bfloat16)
    source = lax.broadcasted_iota(jnp.int32, (devices, slots), 0)
    slot = lax.broadcasted_iota(jnp.int32, (devices, slots), 1) // capacity
    expand = jnp.where(source == (slot % n_z) * n_p + slot // n_z, 1.0, 0.0).astype(jnp.bfloat16)
    filled = jnp.dot(counts, expand, preferred_element_type=jnp.float32)[:1]
    rank = lax.broadcasted_iota(jnp.int32, (1, slots), 1) % capacity
    live = jnp.where(rank.astype(jnp.float32) < filled, 0.0, -1e30)
    bias_ref[:, :slots] = jnp.broadcast_to(live, (rows, slots)).astype(jnp.bfloat16)


def prepare(routes, doc_ids, n_z, devices, rows):
    slots = 2 * rows
    return pl.pallas_call(
        prepare_kernel,
        out_shape=[
            jax.ShapeDtypeStruct((n_z, 1, rows), jnp.int32),
            jax.ShapeDtypeStruct((rows, slots + 3 * rows), jnp.bfloat16),
            jax.ShapeDtypeStruct((rows, 3 * rows), jnp.float32),
        ],
        compiler_params=pltpu.CompilerParams(vmem_limit_bytes=SMALL_VMEM),
        name="prepare",
    )(routes.reshape(devices, rows), doc_ids.reshape(devices, rows))


def column_block(w_kv, target):
    _, w_rows, features = w_kv.shape
    half = features // (GROUPS // 2)
    start = (target & 1, 0, (target >> 1) * half)
    return lax.dynamic_slice(w_kv, start, (1, w_rows, half))[0]


def ring_step(value, back=False):
    pairs = list(zip(RING, RING[1:] + RING[:1]))
    return lax.ppermute(value, "z", [(b, a) for a, b in pairs] if back else pairs)


def memory_slots(cache, w_kv, place, capacity, stream, back):
    n_z, n_p = lax.axis_size("z"), lax.axis_size("p")
    devices = n_z * n_p
    cache_rows, depth = cache.shape
    _, w_rows, features = w_kv.shape
    z = lax.axis_index("z")
    if n_p == 4 and capacity % ROW_TILE == 0 and w_rows % ROW_TILE == 0:
        blocks = [column_block(w_kv, z ^ mask) for mask in range(n_z)]
        own = jnp.stack(
            [blocks[0]] + [swapped(blocks[mask], "z", mask) for mask in range(1, n_z)], 0
        )
        other0 = swapped(cache, "head", 1)
        own, other0, cache = lax.optimization_barrier((own, other0, cache))
        across, beside = swapped(own, "p", 2), swapped(own, "p", 1)
        row1, row3 = ring_step(cache), ring_step(cache, back=True)
        beside, stream, back = lax.optimization_barrier((beside, stream, back))
        near, back1 = shifted(stream, 1), shifted(back, -1)
        row1 = lax.optimization_barrier(row1)
        row2, other1 = ring_step(row1), swapped(row1, "head", 1)
        row3, other1 = lax.optimization_barrier((row3, other1))
        other3 = swapped(row3, "head", 1)
        row2 = lax.optimization_barrier(row2)
        other2 = swapped(row2, "head", 1)
        across, other2, other3, near, back1 = lax.optimization_barrier(
            (across, other2, other3, near, back1)
        )
        pieces = [own, beside, across, swapped(across, "p", 1)]
        far = shifted(near, 1)
        rows = [cache, row1, row2, row3, other0, other1, other2, other3]
        slots = project(place, rows, pieces, devices, capacity)
        slots, far = lax.optimization_barrier((slots, far))
        return slots, near, far, back1
    near, back1 = shifted(stream, 1), shifted(back, -1)
    far = shifted(near, 1)
    targets = [column_block(w_kv, jnp.int32(i)) for i in range(n_z)]
    w_z = lax.all_to_all(jnp.stack(targets, 0), "z", split_axis=0, concat_axis=0, tiled=True)
    w_all = lax.all_gather(w_z, "p", axis=1, tiled=True).reshape(devices * w_rows, -1)
    rows = lax.all_gather(cache, ("head", "z"), axis=0, tiled=False)
    rows = rows.reshape(-1, n_z * cache_rows, depth)
    proj = sum(
        jnp.dot(
            rows[i], w_all[i * depth : (i + 1) * depth], preferred_element_type=jnp.float32
        )
        for i in range(rows.shape[0])
    ).astype(jnp.bfloat16)
    slot_ids = jnp.arange(devices * capacity, dtype=jnp.int32)
    chosen = (slot_ids[None, :, None] == place).astype(jnp.bfloat16)
    slots = jnp.einsum(
        "zsi,zic->zsc",
        chosen,
        proj.reshape(n_z, cache_rows, -1),
        preferred_element_type=jnp.float32,
    ).astype(jnp.bfloat16)
    slots = slots.reshape(n_z, devices, capacity, -1).transpose(1, 0, 2, 3)
    return slots, near, far, back1


def body(queries, keys, values, grad_out, cache, w_kv, doc_ids, routes):
    n_z, n_p = lax.axis_size("z"), lax.axis_size("p")
    devices = n_z * n_p
    seg_rows = queries.shape[0]
    cache_rows = cache.shape[0]
    capacity = 2 * cache_rows // devices
    slot_count = capacity * devices

    place, bias, back_bias = prepare(routes, doc_ids, n_z, devices, seg_rows)
    slots, kv1, kv2, qg1 = memory_slots(
        cache,
        w_kv,
        place,
        capacity,
        jnp.stack([keys, values], 0),
        jnp.stack([queries, grad_out], 0),
    )
    memory = lax.all_to_all(slots, SEQ, split_axis=0, concat_axis=0, tiled=True)
    memory = memory.reshape(n_z, slot_count, slots.shape[-1])

    qg2 = shifted(qg1, -1)
    output, grad_q, stats = attend(queries, grad_out, keys, values, kv1, kv2, memory, bias)
    all_stats = [stats, shifted(stats, -1), shifted(stats, -2)]
    grad_k, grad_v = key_grads(
        keys, values, queries, grad_out, qg1, qg2, all_stats, back_bias
    )
    return (output, grad_q, grad_k, grad_v)


def solution(mesh):
    n_seq, n_head = mesh.devices.shape
    grid = Mesh(mesh.devices.reshape(GROUPS, n_seq // GROUPS, n_head), ("z", "p", "head"))
    rows = P(SEQ, "head")
    return jax.shard_map(
        body,
        mesh=grid,
        in_specs=(rows, rows, rows, rows, rows, P(None, SEQ, "head"), P(), P()),
        out_specs=(rows, rows, rows, rows),
        check_vma=False,
    )
```

```python
import jax
import jax.numpy as jnp
from jax import lax
from jax.experimental import pallas as pl
from jax.experimental.pallas import tpu as pltpu
from jax.sharding import Mesh, PartitionSpec as P

HD = 128
GROUPS = 4
SEQ = ("z", "p")
ROW_TILE = 16
VMEM = 24 * 1024 * 1024
SMALL_VMEM = 4 * 1024 * 1024
STATS = 16


def shifted(value, by):
    length = lax.axis_size("z") * lax.axis_size("p")
    pairs = [(i, i + by) for i in range(length) if 0 <= i + by < length]
    return lax.ppermute(value, SEQ, pairs)


def swapped(value, axis, mask):
    return lax.ppermute(value, axis, [(i, i ^ mask) for i in range(lax.axis_size(axis))])


def in_vmem(*arrays):
    return [pltpu.with_memory_space_constraint(array, pltpu.VMEM) for array in arrays]


def in_hbm(*arrays):
    return [pltpu.with_memory_space_constraint(array, pltpu.HBM) for array in arrays]


def dot_t(a, b, dims):
    return lax.dot_general(a, b, (dims, ((), ())), preferred_element_type=jnp.float32)


def attend_kernel(
    q_ref, g_ref, k_ref, v_ref, kv1_ref, kv2_ref, mem_ref, bias_ref, out_ref, gq_ref, stats_ref
):
    rows, width = q_ref.shape
    scaling = HD ** (-0.5)
    bias = bias_ref[...].astype(jnp.float32)
    step = pl.program_id(0)
    heads = [slice(i * HD, (i + 1) * HD) for i in range(width // HD)]
    ks, vs = (
        [
            jnp.concatenate(
                [
                    mem_ref[2 * step + which, :, cols],
                    kv2_ref[which, :, cols],
                    kv1_ref[which, :, cols],
                    own_ref[:, cols],
                ],
                0,
            )
            for cols in heads
        ]
        for which, own_ref in enumerate((k_ref, v_ref))
    )
    scores = [dot_t(q_ref[:, cols], kh, ((1,), (1,))) + bias for cols, kh in zip(heads, ks)]
    dprobs = [dot_t(g_ref[:, cols], vh, ((1,), (1,))) for cols, vh in zip(heads, vs)]
    tops, shares, probs = [], [], []
    for score in scores:
        top = jnp.max(score, axis=-1, keepdims=True)
        weights = jnp.exp((score - top) * scaling)
        share = 1.0 / jnp.sum(weights, axis=-1, keepdims=True)
        tops.append(top)
        shares.append(share)
        probs.append(weights * share)
    outs = [
        dot_t(prob.astype(jnp.bfloat16), vh, ((1,), (0,))).astype(jnp.bfloat16)
        for prob, vh in zip(probs, vs)
    ]
    deltas, dscores = [], []
    for cols, out_b, prob, dprob in zip(heads, outs, probs, dprobs):
        out_ref[:, cols] = out_b
        delta = jnp.sum(
            g_ref[:, cols].astype(jnp.float32) * out_b.astype(jnp.float32), axis=-1, keepdims=True
        )
        deltas.append(delta)
        dscores.append((prob * ((dprob - delta) * scaling)).astype(jnp.bfloat16))
    lane = lax.broadcasted_iota(jnp.int32, (rows, HD), 1)
    stats = jnp.zeros((rows, HD), jnp.float32)
    for i, column in enumerate(tops + shares + deltas):
        stats = jnp.where(lane == i, column, stats)
    stats_ref[0] = stats.T[:STATS]
    for cols, kh, dscore in zip(heads, ks, dscores):
        gq_ref[:, cols] = dot_t(dscore, kh, ((1,), (0,))).astype(jnp.bfloat16)


def attend(queries, grad_out, keys, values, kv1, kv2, memory, bias):
    rows, features = queries.shape
    steps = memory.shape[0] // 2
    slots, block = memory.shape[1:]
    heads = steps * block // HD
    flat = pl.BlockSpec((rows, block), lambda i: (0, i))
    pair = pl.BlockSpec((2, rows, block), lambda i: (0, 0, i))
    whole = pl.BlockSpec(memory_space=pltpu.VMEM)
    keys_all = slots + 3 * rows
    return pl.pallas_call(
        attend_kernel,
        grid=(steps,),
        in_specs=[
            flat, flat, flat, flat, pair, pair, whole,
            pl.BlockSpec((rows, keys_all), lambda i: (0, 0)),
        ],
        out_specs=[flat, flat, pl.BlockSpec((1, STATS, rows), lambda i: (i, 0, 0))],
        out_shape=[
            jax.ShapeDtypeStruct((rows, features), jnp.bfloat16),
            jax.ShapeDtypeStruct((rows, features), jnp.bfloat16),
            jax.ShapeDtypeStruct((steps, STATS, rows), jnp.float32),
        ],
        compiler_params=pltpu.CompilerParams(vmem_limit_bytes=VMEM),
        cost_estimate=pl.CostEstimate(
            flops=2 * 4 * rows * keys_all * HD * heads,
            bytes_accessed=6 * 1024 * 1024,
            transcendentals=rows * keys_all * heads,
        ),
        name="attend",
    )(queries, grad_out, keys, values, *in_hbm(kv1, kv2), *in_vmem(memory), *in_hbm(bias))


def key_grads_kernel(
    k_ref, v_ref, q_ref, g_ref, qg1_ref, qg2_ref, st0_ref, st1_ref, st2_ref, bias_ref,
    gk_ref, gv_ref,
):
    width = k_ref.shape[1]
    scaling = HD ** (-0.5)
    bias = bias_ref[...]
    heads = [slice(i * HD, (i + 1) * HD) for i in range(width // HD)]
    start = pl.program_id(0) * width
    picked = [pl.ds(pl.multiple_of(start + i * HD, HD), HD) for i in range(len(heads))]
    stats = jnp.concatenate([st0_ref[0], st1_ref[0], st2_ref[0]], 1)
    qs = [
        jnp.concatenate([q_ref[:, cols], qg1_ref[0, :, wide], qg2_ref[0, :, wide]], 0)
        for cols, wide in zip(heads, picked)
    ]
    gs = [
        jnp.concatenate([g_ref[:, cols], qg1_ref[1, :, wide], qg2_ref[1, :, wide]], 0)
        for cols, wide in zip(heads, picked)
    ]
    scores = [dot_t(k_ref[:, cols], qh, ((1,), (1,))) + bias for cols, qh in zip(heads, qs)]
    dprobs = [dot_t(v_ref[:, cols], gh, ((1,), (1,))) for cols, gh in zip(heads, gs)]
    probs, dscores = [], []
    for i, (score, dprob) in enumerate(zip(scores, dprobs)):
        top, share, delta = (stats[i + j * len(heads) : i + j * len(heads) + 1] for j in range(3))
        prob = jnp.exp((score - top) * scaling) * share
        probs.append(prob.astype(jnp.bfloat16))
        dscores.append((prob * ((dprob - delta) * scaling)).astype(jnp.bfloat16))
    for cols, qh, gh, prob, dscore in zip(heads, qs, gs, probs, dscores):
        gk_ref[:, cols] = dot_t(dscore, qh, ((1,), (0,))).astype(jnp.bfloat16)
        gv_ref[:, cols] = dot_t(prob, gh, ((1,), (0,))).astype(jnp.bfloat16)


def key_grads(keys, values, queries, grad_out, qg1, qg2, stats, bias):
    rows, features = keys.shape
    steps = stats[0].shape[0]
    block = features // steps
    flat = pl.BlockSpec((rows, block), lambda i: (0, i))
    whole = pl.BlockSpec(memory_space=pltpu.VMEM)
    stat = pl.BlockSpec((1, STATS, rows), lambda i: (i, 0, 0))
    heads = features // HD
    return pl.pallas_call(
        key_grads_kernel,
        grid=(steps,),
        in_specs=[
            flat, flat, flat, flat, whole, whole, stat, stat, stat, whole,
        ],
        out_specs=[flat, flat],
        out_shape=[jax.ShapeDtypeStruct((rows, features), jnp.bfloat16)] * 2,
        compiler_params=pltpu.CompilerParams(vmem_limit_bytes=VMEM),
        cost_estimate=pl.CostEstimate(
            flops=2 * 4 * rows * 3 * rows * HD * heads,
            bytes_accessed=4 * 1024 * 1024,
            transcendentals=rows * 3 * rows * heads,
        ),
        name="key_grads",
    )(keys, values, queries, grad_out, *in_vmem(qg1, qg2), *stats, *in_vmem(bias))


def project_kernel(place_ref, *refs):
    n_z, _, cache_rows = place_ref.shape
    out_ref, w_ref, a_ref = refs[-3:]
    rows, pieces = refs[: 2 * n_z], refs[2 * n_z : -3]
    n_p, (_, w_rows, block) = len(pieces), pieces[0].shape
    depth = rows[0].shape[1]
    devices, _, capacity, _ = out_ref.shape
    z, p, y = (lax.axis_index(name) for name in ("z", "p", "head"))
    for i, ref in enumerate(rows):
        a_ref[y ^ (i // n_z), z ^ (i % n_z)] = ref[...]
    for m in range(n_p):
        for k in range(n_z):
            w_ref[z ^ k, p ^ m] = pieces[m][k]
    half = n_z // 2
    proj = sum(
        jnp.dot(
            a_ref[i].reshape(n_z * cache_rows, depth),
            w_ref[i * half : (i + 1) * half].reshape(depth, block),
            preferred_element_type=jnp.float32,
        )
        for i in range(2)
    ).astype(jnp.bfloat16)
    slot_ids = lax.broadcasted_iota(jnp.int32, (devices * capacity, cache_rows), 0)
    for z in range(n_z):
        chosen = jnp.where(slot_ids == place_ref[z], 1.0, 0.0).astype(jnp.bfloat16)
        slots = jnp.dot(
            chosen,
            proj[z * cache_rows : (z + 1) * cache_rows],
            preferred_element_type=jnp.float32,
        ).astype(jnp.bfloat16)
        out_ref[:, z] = slots.reshape(devices, capacity, block)


def project(place, rows, pieces, devices, capacity):
    n_z, _, cache_rows = place.shape
    depth = rows[0].shape[1]
    n_p = len(pieces)
    _, w_rows, block = pieces[0].shape
    whole = pl.BlockSpec(memory_space=pltpu.VMEM)
    return pl.pallas_call(
        project_kernel,
        in_specs=[whole] * (1 + len(rows) + n_p),
        out_specs=whole,
        out_shape=pltpu.VMEM((devices, n_z, capacity, block), jnp.bfloat16),
        scratch_shapes=[
            pltpu.VMEM((n_z, n_p, w_rows, block), jnp.bfloat16),
            pltpu.VMEM((2, n_z, cache_rows, depth), jnp.bfloat16),
        ],
        compiler_params=pltpu.CompilerParams(vmem_limit_bytes=VMEM),
        cost_estimate=pl.CostEstimate(
            flops=4 * n_z * cache_rows * depth * block,
            bytes_accessed=8 * 1024 * 1024,
            transcendentals=0,
        ),
        name="project",
    )(*in_vmem(place, *rows, *pieces))


def prepare_kernel(routes_ref, ids_ref, place_ref, bias_ref, back_ref):
    n_z, _, rows = place_ref.shape
    devices = routes_ref.shape[0]
    n_p = devices // n_z
    capacity = 2 * rows // devices
    slots = bias_ref.shape[1] - 3 * rows
    p = lax.axis_index("p")
    me = lax.axis_index("z") * n_p + p
    row = lax.broadcasted_iota(jnp.int32, (rows, rows), 0)
    lane = lax.broadcasted_iota(jnp.int32, (rows, rows), 1)

    def both_ways(line):
        wide = jnp.broadcast_to(line.astype(jnp.float32), (rows, rows))
        return wide, wide.T

    for z in range(n_z):
        across, down = both_ways(routes_ref[pl.ds(z * n_p + p, 1), :])
        ranks = jnp.sum(
            jnp.where((across == down) & (row < lane), 1.0, 0.0), axis=0, keepdims=True
        )
        place_ref[z] = (across[:1] * capacity + ranks).astype(jnp.int32)

    def ids_of(segment):
        return ids_ref[pl.ds(jnp.clip(segment, 0, devices - 1), 1), :].astype(jnp.float32)

    _, own = both_ways(ids_ref[pl.ds(me, 1), :])
    for i in range(3):
        earlier, later = me - 2 + i, me + i
        same = (own == ids_of(earlier)) & (earlier >= 0)
        same_back = (own == ids_of(later)) & (later < devices)
        if i == 2:
            same = same & (lane <= row)
        if i == 0:
            same_back = same_back & (lane >= row)
        bias_ref[:, slots + i * rows : slots + (i + 1) * rows] = jnp.where(same, 0.0, -1e30).astype(
            jnp.bfloat16
        )
        back_ref[:, i * rows : (i + 1) * rows] = jnp.where(same_back, 0.0, -1e30)

    mine = jnp.where(routes_ref[...] == me, 1.0, 0.0).astype(jnp.bfloat16)
    counts = dot_t(jnp.ones((8, rows), jnp.bfloat16), mine, ((1,), (1,))).astype(jnp.bfloat16)
    source = lax.broadcasted_iota(jnp.int32, (devices, slots), 0)
    slot = lax.broadcasted_iota(jnp.int32, (devices, slots), 1) // capacity
    expand = jnp.where(source == (slot % n_z) * n_p + slot // n_z, 1.0, 0.0).astype(jnp.bfloat16)
    filled = jnp.dot(counts, expand, preferred_element_type=jnp.float32)[:1]
    rank = lax.broadcasted_iota(jnp.int32, (1, slots), 1) % capacity
    live = jnp.where(rank.astype(jnp.float32) < filled, 0.0, -1e30)
    bias_ref[:, :slots] = jnp.broadcast_to(live, (rows, slots)).astype(jnp.bfloat16)


def prepare(routes, doc_ids, n_z, devices, rows):
    slots = 2 * rows
    return pl.pallas_call(
        prepare_kernel,
        out_shape=[
            jax.ShapeDtypeStruct((n_z, 1, rows), jnp.int32),
            jax.ShapeDtypeStruct((rows, slots + 3 * rows), jnp.bfloat16),
            jax.ShapeDtypeStruct((rows, 3 * rows), jnp.float32),
        ],
        compiler_params=pltpu.CompilerParams(vmem_limit_bytes=SMALL_VMEM),
        name="prepare",
    )(routes.reshape(devices, rows), doc_ids.reshape(devices, rows))


def column_block(w_kv, target):
    _, w_rows, features = w_kv.shape
    half = features // (GROUPS // 2)
    start = (target & 1, 0, (target >> 1) * half)
    return lax.dynamic_slice(w_kv, start, (1, w_rows, half))[0]


def memory_slots(cache, w_kv, place, capacity, stream, back):
    n_z, n_p = lax.axis_size("z"), lax.axis_size("p")
    devices = n_z * n_p
    cache_rows, depth = cache.shape
    _, w_rows, features = w_kv.shape
    z = lax.axis_index("z")
    if n_p == 4 and capacity % ROW_TILE == 0 and w_rows % ROW_TILE == 0:
        blocks = [column_block(w_kv, z ^ mask) for mask in range(n_z)]
        own = jnp.stack(
            [blocks[0]] + [swapped(blocks[mask], "z", mask) for mask in range(1, n_z)], 0
        )
        row1, other0 = swapped(cache, "z", 1), swapped(cache, "head", 1)
        own, row1, other0, cache = lax.optimization_barrier((own, row1, other0, cache))
        across, beside = swapped(own, "p", 2), swapped(own, "p", 1)
        row2, other1 = swapped(cache, "z", 2), swapped(row1, "head", 1)
        beside, stream, back = lax.optimization_barrier((beside, stream, back))
        near, back1 = shifted(stream, 1), shifted(back, -1)
        row2, other1 = lax.optimization_barrier((row2, other1))
        row3, other2 = swapped(row2, "z", 1), swapped(row2, "head", 1)
        row3, other2 = lax.optimization_barrier((row3, other2))
        other3 = swapped(row3, "head", 1)
        across, other2, other3, near, back1 = lax.optimization_barrier(
            (across, other2, other3, near, back1)
        )
        pieces = [own, beside, across, swapped(across, "p", 1)]
        far = shifted(near, 1)
        rows = [cache, row1, row2, row3, other0, other1, other2, other3]
        slots = project(place, rows, pieces, devices, capacity)
        slots, far = lax.optimization_barrier((slots, far))
        return slots, near, far, back1
    near, back1 = shifted(stream, 1), shifted(back, -1)
    far = shifted(near, 1)
    targets = [column_block(w_kv, jnp.int32(i)) for i in range(n_z)]
    w_z = lax.all_to_all(jnp.stack(targets, 0), "z", split_axis=0, concat_axis=0, tiled=True)
    w_all = lax.all_gather(w_z, "p", axis=1, tiled=True).reshape(devices * w_rows, -1)
    rows = lax.all_gather(cache, ("head", "z"), axis=0, tiled=False)
    rows = rows.reshape(-1, n_z * cache_rows, depth)
    proj = sum(
        jnp.dot(
            rows[i], w_all[i * depth : (i + 1) * depth], preferred_element_type=jnp.float32
        )
        for i in range(rows.shape[0])
    ).astype(jnp.bfloat16)
    slot_ids = jnp.arange(devices * capacity, dtype=jnp.int32)
    chosen = (slot_ids[None, :, None] == place).astype(jnp.bfloat16)
    slots = jnp.einsum(
        "zsi,zic->zsc",
        chosen,
        proj.reshape(n_z, cache_rows, -1),
        preferred_element_type=jnp.float32,
    ).astype(jnp.bfloat16)
    slots = slots.reshape(n_z, devices, capacity, -1).transpose(1, 0, 2, 3)
    return slots, near, far, back1


def body(queries, keys, values, grad_out, cache, w_kv, doc_ids, routes):
    n_z, n_p = lax.axis_size("z"), lax.axis_size("p")
    devices = n_z * n_p
    seg_rows = queries.shape[0]
    cache_rows = cache.shape[0]
    capacity = 2 * cache_rows // devices
    slot_count = capacity * devices

    place, bias, back_bias = prepare(routes, doc_ids, n_z, devices, seg_rows)
    slots, kv1, kv2, qg1 = memory_slots(
        cache,
        w_kv,
        place,
        capacity,
        jnp.stack([keys, values], 0),
        jnp.stack([queries, grad_out], 0),
    )
    memory = lax.all_to_all(slots, SEQ, split_axis=0, concat_axis=0, tiled=True)
    memory = memory.reshape(n_z, slot_count, slots.shape[-1])

    qg2 = shifted(qg1, -1)
    output, grad_q, stats = attend(queries, grad_out, keys, values, kv1, kv2, memory, bias)
    all_stats = [stats, shifted(stats, -1), shifted(stats, -2)]
    grad_k, grad_v = key_grads(
        keys, values, queries, grad_out, qg1, qg2, all_stats, back_bias
    )
    return (output, grad_q, grad_k, grad_v)


def solution(mesh):
    n_seq, n_head = mesh.devices.shape
    grid = Mesh(mesh.devices.reshape(GROUPS, n_seq // GROUPS, n_head), ("z", "p", "head"))
    rows = P(SEQ, "head")
    return jax.shard_map(
        body,
        mesh=grid,
        in_specs=(rows, rows, rows, rows, rows, P(None, SEQ, "head"), P(), P()),
        out_specs=(rows, rows, rows, rows),
        check_vma=False,
    )
```

```python
import jax
import jax.numpy as jnp
from jax import lax
from jax.experimental import pallas as pl
from jax.experimental.pallas import tpu as pltpu
from jax.sharding import Mesh, PartitionSpec as P

HD = 128
GROUPS = 4
SEQ = ("z", "p")
ROW_TILE = 16
RING = [0, 1, 3, 2]
VMEM = 24 * 1024 * 1024
SMALL_VMEM = 4 * 1024 * 1024
STATS = 16


def shifted(value, by):
    length = lax.axis_size("z") * lax.axis_size("p")
    pairs = [(i, i + by) for i in range(length) if 0 <= i + by < length]
    return lax.ppermute(value, SEQ, pairs)


def swapped(value, axis, mask):
    return lax.ppermute(value, axis, [(i, i ^ mask) for i in range(lax.axis_size(axis))])


def in_vmem(*arrays):
    return [pltpu.with_memory_space_constraint(array, pltpu.VMEM) for array in arrays]


def in_hbm(*arrays):
    return [pltpu.with_memory_space_constraint(array, pltpu.HBM) for array in arrays]


def dot_t(a, b, dims):
    return lax.dot_general(a, b, (dims, ((), ())), preferred_element_type=jnp.float32)


def attend_kernel(
    q_ref, g_ref, k_ref, v_ref, kv1_ref, kv2_ref, mem_ref, bias_ref, out_ref, gq_ref, stats_ref
):
    rows, width = out_ref.shape
    scaling = HD ** (-0.5)
    bias = bias_ref[...].astype(jnp.float32)
    step = pl.program_id(0)
    picked = [pl.ds(pl.multiple_of(step * width + i * HD, HD), HD) for i in range(width // HD)]
    heads = [slice(i * HD, (i + 1) * HD) for i in range(width // HD)]
    ks, vs = (
        [
            jnp.concatenate(
                [
                    mem_ref[2 * step + which, :, cols],
                    kv2_ref[which, :, cols],
                    kv1_ref[which, :, cols],
                    own_ref[:, wide],
                ],
                0,
            )
            for cols, wide in zip(heads, picked)
        ]
        for which, own_ref in enumerate((k_ref, v_ref))
    )
    scores = [dot_t(q_ref[:, wide], kh, ((1,), (1,))) + bias for wide, kh in zip(picked, ks)]
    dprobs = [dot_t(g_ref[:, wide], vh, ((1,), (1,))) for wide, vh in zip(picked, vs)]
    tops, shares, probs = [], [], []
    for score in scores:
        top = jnp.max(score, axis=-1, keepdims=True)
        weights = jnp.exp((score - top) * scaling)
        share = 1.0 / jnp.sum(weights, axis=-1, keepdims=True)
        tops.append(top)
        shares.append(share)
        probs.append(weights * share)
    outs = [
        dot_t(prob.astype(jnp.bfloat16), vh, ((1,), (0,))).astype(jnp.bfloat16)
        for prob, vh in zip(probs, vs)
    ]
    deltas, dscores = [], []
    for cols, wide, out_b, prob, dprob in zip(heads, picked, outs, probs, dprobs):
        out_ref[:, cols] = out_b
        delta = jnp.sum(
            g_ref[:, wide].astype(jnp.float32) * out_b.astype(jnp.float32), axis=-1, keepdims=True
        )
        deltas.append(delta)
        dscores.append((prob * ((dprob - delta) * scaling)).astype(jnp.bfloat16))
    lane = lax.broadcasted_iota(jnp.int32, (rows, HD), 1)
    stats = jnp.zeros((rows, HD), jnp.float32)
    for i, column in enumerate(tops + shares + deltas):
        stats = jnp.where(lane == i, column, stats)
    stats_ref[0] = stats.T[:STATS]
    for cols, kh, dscore in zip(heads, ks, dscores):
        gq_ref[:, cols] = dot_t(dscore, kh, ((1,), (0,))).astype(jnp.bfloat16)


def attend(queries, grad_out, keys, values, kv1, kv2, memory, bias):
    rows, features = queries.shape
    steps = memory.shape[0] // 2
    slots, block = memory.shape[1:]
    heads = steps * block // HD
    flat = pl.BlockSpec((rows, block), lambda i: (0, i))
    pair = pl.BlockSpec((2, rows, block), lambda i: (0, 0, i))
    whole = pl.BlockSpec(memory_space=pltpu.VMEM)
    keys_all = slots + 3 * rows
    return pl.pallas_call(
        attend_kernel,
        grid=(steps,),
        in_specs=[
            whole, whole, whole, whole, pair, pair, whole,
            pl.BlockSpec((rows, keys_all), lambda i: (0, 0)),
        ],
        out_specs=[flat, flat, pl.BlockSpec((1, STATS, rows), lambda i: (i, 0, 0))],
        out_shape=[
            jax.ShapeDtypeStruct((rows, features), jnp.bfloat16),
            jax.ShapeDtypeStruct((rows, features), jnp.bfloat16),
            jax.ShapeDtypeStruct((steps, STATS, rows), jnp.float32),
        ],
        compiler_params=pltpu.CompilerParams(vmem_limit_bytes=VMEM),
        cost_estimate=pl.CostEstimate(
            flops=2 * 4 * rows * keys_all * HD * heads,
            bytes_accessed=6 * 1024 * 1024,
            transcendentals=rows * keys_all * heads,
        ),
        name="attend",
    )(
        *in_vmem(queries, grad_out, keys, values),
        *in_hbm(kv1, kv2),
        *in_vmem(memory),
        *in_hbm(bias),
    )


def key_grads_kernel(
    k_ref, v_ref, q_ref, g_ref, qg1_ref, qg2_ref, st0_ref, st1_ref, st2_ref, bias_ref,
    gk_ref, gv_ref,
):
    width = gk_ref.shape[1]
    scaling = HD ** (-0.5)
    bias = bias_ref[...]
    heads = [slice(i * HD, (i + 1) * HD) for i in range(width // HD)]
    start = pl.program_id(0) * width
    picked = [pl.ds(pl.multiple_of(start + i * HD, HD), HD) for i in range(len(heads))]
    stats = jnp.concatenate([st0_ref[0], st1_ref[0], st2_ref[0]], 1)
    qs = [
        jnp.concatenate([q_ref[:, wide], qg1_ref[0, :, cols], qg2_ref[0, :, wide]], 0)
        for cols, wide in zip(heads, picked)
    ]
    gs = [
        jnp.concatenate([g_ref[:, wide], qg1_ref[1, :, cols], qg2_ref[1, :, wide]], 0)
        for cols, wide in zip(heads, picked)
    ]
    scores = [dot_t(k_ref[:, wide], qh, ((1,), (1,))) + bias for wide, qh in zip(picked, qs)]
    dprobs = [dot_t(v_ref[:, wide], gh, ((1,), (1,))) for wide, gh in zip(picked, gs)]
    probs, dscores = [], []
    for i, (score, dprob) in enumerate(zip(scores, dprobs)):
        top, share, delta = (stats[i + j * len(heads) : i + j * len(heads) + 1] for j in range(3))
        prob = jnp.exp((score - top) * scaling) * share
        probs.append(prob.astype(jnp.bfloat16))
        dscores.append((prob * ((dprob - delta) * scaling)).astype(jnp.bfloat16))
    for cols, qh, gh, prob, dscore in zip(heads, qs, gs, probs, dscores):
        gk_ref[:, cols] = dot_t(dscore, qh, ((1,), (0,))).astype(jnp.bfloat16)
        gv_ref[:, cols] = dot_t(prob, gh, ((1,), (0,))).astype(jnp.bfloat16)


def key_grads(keys, values, queries, grad_out, qg1, qg2, stats, bias):
    rows, features = keys.shape
    steps = stats[0].shape[0]
    block = features // steps
    flat = pl.BlockSpec((rows, block), lambda i: (0, i))
    pair = pl.BlockSpec((2, rows, block), lambda i: (0, 0, i))
    whole = pl.BlockSpec(memory_space=pltpu.VMEM)
    stat = pl.BlockSpec((1, STATS, rows), lambda i: (i, 0, 0))
    heads = features // HD
    return pl.pallas_call(
        key_grads_kernel,
        grid=(steps,),
        in_specs=[
            whole, whole, whole, whole, pair, whole, stat, stat, stat, whole,
        ],
        out_specs=[flat, flat],
        out_shape=[jax.ShapeDtypeStruct((rows, features), jnp.bfloat16)] * 2,
        compiler_params=pltpu.CompilerParams(vmem_limit_bytes=VMEM),
        cost_estimate=pl.CostEstimate(
            flops=2 * 4 * rows * 3 * rows * HD * heads,
            bytes_accessed=4 * 1024 * 1024,
            transcendentals=rows * 3 * rows * heads,
        ),
        name="key_grads",
    )(
        *in_vmem(keys, values, queries, grad_out),
        *in_hbm(qg1),
        *in_vmem(qg2),
        *stats,
        *in_vmem(bias),
    )


def project_kernel(place_ref, *refs):
    n_z, _, cache_rows = place_ref.shape
    out_ref, w_ref, a_ref = refs[-3:]
    rows, pieces = refs[: 2 * n_z], refs[2 * n_z : -3]
    n_p, (_, w_rows, block) = len(pieces), pieces[0].shape
    depth = rows[0].shape[1]
    devices, _, capacity, _ = out_ref.shape
    z, p, y = (lax.axis_index(name) for name in ("z", "p", "head"))
    place_in_ring = z ^ (z >> 1)
    for i, ref in enumerate(rows):
        source = (place_in_ring - i % n_z + n_z) & (n_z - 1)
        a_ref[y ^ (i // n_z), source ^ (source >> 1)] = ref[...]
    for m in range(n_p):
        for k in range(n_z):
            w_ref[z ^ k, p ^ m] = pieces[m][k]
    half = n_z // 2
    proj = sum(
        jnp.dot(
            a_ref[i].reshape(n_z * cache_rows, depth),
            w_ref[i * half : (i + 1) * half].reshape(depth, block),
            preferred_element_type=jnp.float32,
        )
        for i in range(2)
    ).astype(jnp.bfloat16)
    slot_ids = lax.broadcasted_iota(jnp.int32, (devices * capacity, cache_rows), 0)
    for z in range(n_z):
        chosen = jnp.where(slot_ids == place_ref[z], 1.0, 0.0).astype(jnp.bfloat16)
        slots = jnp.dot(
            chosen,
            proj[z * cache_rows : (z + 1) * cache_rows],
            preferred_element_type=jnp.float32,
        ).astype(jnp.bfloat16)
        out_ref[:, z] = slots.reshape(devices, capacity, block)


def project(place, rows, pieces, devices, capacity):
    n_z, _, cache_rows = place.shape
    depth = rows[0].shape[1]
    n_p = len(pieces)
    _, w_rows, block = pieces[0].shape
    whole = pl.BlockSpec(memory_space=pltpu.VMEM)
    return pl.pallas_call(
        project_kernel,
        in_specs=[whole] * (1 + len(rows) + n_p),
        out_specs=whole,
        out_shape=pltpu.VMEM((devices, n_z, capacity, block), jnp.bfloat16),
        scratch_shapes=[
            pltpu.VMEM((n_z, n_p, w_rows, block), jnp.bfloat16),
            pltpu.VMEM((2, n_z, cache_rows, depth), jnp.bfloat16),
        ],
        compiler_params=pltpu.CompilerParams(vmem_limit_bytes=VMEM),
        cost_estimate=pl.CostEstimate(
            flops=4 * n_z * cache_rows * depth * block,
            bytes_accessed=8 * 1024 * 1024,
            transcendentals=0,
        ),
        name="project",
    )(*in_vmem(place, *rows, *pieces))


def prepare_kernel(routes_ref, ids_ref, place_ref, bias_ref, back_ref):
    n_z, _, rows = place_ref.shape
    devices = routes_ref.shape[0]
    n_p = devices // n_z
    capacity = 2 * rows // devices
    slots = bias_ref.shape[1] - 3 * rows
    p = lax.axis_index("p")
    me = lax.axis_index("z") * n_p + p
    row = lax.broadcasted_iota(jnp.int32, (rows, rows), 0)
    lane = lax.broadcasted_iota(jnp.int32, (rows, rows), 1)

    def both_ways(line):
        wide = jnp.broadcast_to(line.astype(jnp.float32), (rows, rows))
        return wide, wide.T

    for z in range(n_z):
        across, down = both_ways(routes_ref[pl.ds(z * n_p + p, 1), :])
        ranks = jnp.sum(
            jnp.where((across == down) & (row < lane), 1.0, 0.0), axis=0, keepdims=True
        )
        place_ref[z] = (across[:1] * capacity + ranks).astype(jnp.int32)

    def ids_of(segment):
        return ids_ref[pl.ds(jnp.clip(segment, 0, devices - 1), 1), :].astype(jnp.float32)

    _, own = both_ways(ids_ref[pl.ds(me, 1), :])
    for i in range(3):
        earlier, later = me - 2 + i, me + i
        same = (own == ids_of(earlier)) & (earlier >= 0)
        same_back = (own == ids_of(later)) & (later < devices)
        if i == 2:
            same = same & (lane <= row)
        if i == 0:
            same_back = same_back & (lane >= row)
        bias_ref[:, slots + i * rows : slots + (i + 1) * rows] = jnp.where(same, 0.0, -1e30).astype(
            jnp.bfloat16
        )
        back_ref[:, i * rows : (i + 1) * rows] = jnp.where(same_back, 0.0, -1e30)

    mine = jnp.where(routes_ref[...] == me, 1.0, 0.0).astype(jnp.bfloat16)
    counts = dot_t(jnp.ones((8, rows), jnp.bfloat16), mine, ((1,), (1,))).astype(jnp.bfloat16)
    source = lax.broadcasted_iota(jnp.int32, (devices, slots), 0)
    slot = lax.broadcasted_iota(jnp.int32, (devices, slots), 1) // capacity
    expand = jnp.where(source == (slot % n_z) * n_p + slot // n_z, 1.0, 0.0).astype(jnp.bfloat16)
    filled = jnp.dot(counts, expand, preferred_element_type=jnp.float32)[:1]
    rank = lax.broadcasted_iota(jnp.int32, (1, slots), 1) % capacity
    live = jnp.where(rank.astype(jnp.float32) < filled, 0.0, -1e30)
    bias_ref[:, :slots] = jnp.broadcast_to(live, (rows, slots)).astype(jnp.bfloat16)


def prepare(routes, doc_ids, n_z, devices, rows):
    slots = 2 * rows
    return pl.pallas_call(
        prepare_kernel,
        out_shape=[
            jax.ShapeDtypeStruct((n_z, 1, rows), jnp.int32),
            jax.ShapeDtypeStruct((rows, slots + 3 * rows), jnp.bfloat16),
            jax.ShapeDtypeStruct((rows, 3 * rows), jnp.float32),
        ],
        compiler_params=pltpu.CompilerParams(vmem_limit_bytes=SMALL_VMEM),
        name="prepare",
    )(routes.reshape(devices, rows), doc_ids.reshape(devices, rows))


def column_block(w_kv, target):
    _, w_rows, features = w_kv.shape
    half = features // (GROUPS // 2)
    start = (target & 1, 0, (target >> 1) * half)
    return lax.dynamic_slice(w_kv, start, (1, w_rows, half))[0]


def ring_step(value, back=False):
    pairs = list(zip(RING, RING[1:] + RING[:1]))
    return lax.ppermute(value, "z", [(b, a) for a, b in pairs] if back else pairs)


def memory_slots(cache, w_kv, place, capacity, stream, back):
    n_z, n_p = lax.axis_size("z"), lax.axis_size("p")
    devices = n_z * n_p
    cache_rows, depth = cache.shape
    _, w_rows, features = w_kv.shape
    z = lax.axis_index("z")
    if n_p == 4 and capacity % ROW_TILE == 0 and w_rows % ROW_TILE == 0:
        blocks = [column_block(w_kv, z ^ mask) for mask in range(n_z)]
        own = jnp.stack(
            [blocks[0]] + [swapped(blocks[mask], "z", mask) for mask in range(1, n_z)], 0
        )
        other0 = swapped(cache, "head", 1)
        own, other0, cache = lax.optimization_barrier((own, other0, cache))
        across, beside = swapped(own, "p", 2), swapped(own, "p", 1)
        row1, row3 = ring_step(cache), ring_step(cache, back=True)
        beside, stream, back = lax.optimization_barrier((beside, stream, back))
        near, back1 = shifted(stream, 1), shifted(back, -1)
        row1 = lax.optimization_barrier(row1)
        row2, other1 = ring_step(row1), swapped(row1, "head", 1)
        row3, other1 = lax.optimization_barrier((row3, other1))
        other3 = swapped(row3, "head", 1)
        row2 = lax.optimization_barrier(row2)
        other2 = swapped(row2, "head", 1)
        across, other2, other3, near, back1 = lax.optimization_barrier(
            (across, other2, other3, near, back1)
        )
        pieces = [own, beside, across, swapped(across, "p", 1)]
        far = shifted(near, 1)
        rows = [cache, row1, row2, row3, other0, other1, other2, other3]
        slots = project(place, rows, pieces, devices, capacity)
        slots, far = lax.optimization_barrier((slots, far))
        return slots, near, far, back1
    near, back1 = shifted(stream, 1), shifted(back, -1)
    far = shifted(near, 1)
    targets = [column_block(w_kv, jnp.int32(i)) for i in range(n_z)]
    w_z = lax.all_to_all(jnp.stack(targets, 0), "z", split_axis=0, concat_axis=0, tiled=True)
    w_all = lax.all_gather(w_z, "p", axis=1, tiled=True).reshape(devices * w_rows, -1)
    rows = lax.all_gather(cache, ("head", "z"), axis=0, tiled=False)
    rows = rows.reshape(-1, n_z * cache_rows, depth)
    proj = sum(
        jnp.dot(
            rows[i], w_all[i * depth : (i + 1) * depth], preferred_element_type=jnp.float32
        )
        for i in range(rows.shape[0])
    ).astype(jnp.bfloat16)
    slot_ids = jnp.arange(devices * capacity, dtype=jnp.int32)
    chosen = (slot_ids[None, :, None] == place).astype(jnp.bfloat16)
    slots = jnp.einsum(
        "zsi,zic->zsc",
        chosen,
        proj.reshape(n_z, cache_rows, -1),
        preferred_element_type=jnp.float32,
    ).astype(jnp.bfloat16)
    slots = slots.reshape(n_z, devices, capacity, -1).transpose(1, 0, 2, 3)
    return slots, near, far, back1


def body(queries, keys, values, grad_out, cache, w_kv, doc_ids, routes):
    n_z, n_p = lax.axis_size("z"), lax.axis_size("p")
    devices = n_z * n_p
    seg_rows = queries.shape[0]
    cache_rows = cache.shape[0]
    capacity = 2 * cache_rows // devices
    slot_count = capacity * devices

    place, bias, back_bias = prepare(routes, doc_ids, n_z, devices, seg_rows)
    slots, kv1, kv2, qg1 = memory_slots(
        cache,
        w_kv,
        place,
        capacity,
        jnp.stack([keys, values], 0),
        jnp.stack([queries, grad_out], 0),
    )
    memory = lax.all_to_all(slots, SEQ, split_axis=0, concat_axis=0, tiled=True)
    memory = memory.reshape(n_z, slot_count, slots.shape[-1])

    qg2 = shifted(qg1, -1)
    output, grad_q, stats = attend(queries, grad_out, keys, values, kv1, kv2, memory, bias)
    all_stats = [stats, shifted(stats, -1), shifted(stats, -2)]
    grad_k, grad_v = key_grads(
        keys, values, queries, grad_out, qg1, qg2, all_stats, back_bias
    )
    return (output, grad_q, grad_k, grad_v)


def solution(mesh):
    n_seq, n_head = mesh.devices.shape
    grid = Mesh(mesh.devices.reshape(GROUPS, n_seq // GROUPS, n_head), ("z", "p", "head"))
    rows = P(SEQ, "head")
    return jax.shard_map(
        body,
        mesh=grid,
        in_specs=(rows, rows, rows, rows, rows, P(None, SEQ, "head"), P(), P()),
        out_specs=(rows, rows, rows, rows),
        check_vma=False,
    )
```

```python
import functools

import jax
import jax.numpy as jnp
from jax import lax
from jax.experimental import pallas as pl
from jax.experimental.pallas import tpu as pltpu
from jax.sharding import Mesh, PartitionSpec as P

HD = 128
GROUPS = 4
SEQ = ("z", "p")
ROW_TILE = 16
RING = [0, 1, 3, 2]
VMEM = 24 * 1024 * 1024
SMALL_VMEM = 4 * 1024 * 1024
STATS = 16


def shifted(value, by):
    length = lax.axis_size("z") * lax.axis_size("p")
    pairs = [(i, i + by) for i in range(length) if 0 <= i + by < length]
    return lax.ppermute(value, SEQ, pairs)


def swapped(value, axis, mask):
    return lax.ppermute(value, axis, [(i, i ^ mask) for i in range(lax.axis_size(axis))])


def in_vmem(*arrays):
    return [pltpu.with_memory_space_constraint(array, pltpu.VMEM) for array in arrays]


def in_hbm(*arrays):
    return [pltpu.with_memory_space_constraint(array, pltpu.HBM) for array in arrays]


def dot_t(a, b, dims):
    return lax.dot_general(a, b, (dims, ((), ())), preferred_element_type=jnp.float32)


def attend_kernel(
    q_ref, g_ref, k_ref, v_ref, kv1_ref, kv2_ref, mem_ref, bias_ref, out_ref, gq_ref, stats_ref
):
    rows, width = out_ref.shape
    scaling = HD ** (-0.5)
    bias = bias_ref[...].astype(jnp.float32)
    step = pl.program_id(0)
    picked = [pl.ds(pl.multiple_of(step * width + i * HD, HD), HD) for i in range(width // HD)]
    heads = [slice(i * HD, (i + 1) * HD) for i in range(width // HD)]
    ks, vs = (
        [
            jnp.concatenate(
                [
                    mem_ref[2 * step + which, :, cols],
                    kv2_ref[which, :, cols],
                    kv1_ref[which, :, cols],
                    own_ref[:, wide],
                ],
                0,
            )
            for cols, wide in zip(heads, picked)
        ]
        for which, own_ref in enumerate((k_ref, v_ref))
    )
    scores = [dot_t(q_ref[:, wide], kh, ((1,), (1,))) + bias for wide, kh in zip(picked, ks)]
    dprobs = [dot_t(g_ref[:, wide], vh, ((1,), (1,))) for wide, vh in zip(picked, vs)]
    tops, shares, probs = [], [], []
    for score in scores:
        top = jnp.max(score, axis=-1, keepdims=True)
        weights = jnp.exp((score - top) * scaling)
        share = 1.0 / jnp.sum(weights, axis=-1, keepdims=True)
        tops.append(top)
        shares.append(share)
        probs.append(weights * share)
    outs = [
        dot_t(prob.astype(jnp.bfloat16), vh, ((1,), (0,))).astype(jnp.bfloat16)
        for prob, vh in zip(probs, vs)
    ]
    deltas, dscores = [], []
    for cols, wide, out_b, prob, dprob in zip(heads, picked, outs, probs, dprobs):
        out_ref[:, cols] = out_b
        delta = jnp.sum(
            g_ref[:, wide].astype(jnp.float32) * out_b.astype(jnp.float32), axis=-1, keepdims=True
        )
        deltas.append(delta)
        dscores.append((prob * ((dprob - delta) * scaling)).astype(jnp.bfloat16))
    lane = lax.broadcasted_iota(jnp.int32, (rows, HD), 1)
    stats = jnp.zeros((rows, HD), jnp.float32)
    for i, column in enumerate(tops + shares + deltas):
        stats = jnp.where(lane == i, column, stats)
    stats_ref[0] = stats.T[:STATS]
    for cols, kh, dscore in zip(heads, ks, dscores):
        gq_ref[:, cols] = dot_t(dscore, kh, ((1,), (0,))).astype(jnp.bfloat16)


def attend(queries, grad_out, keys, values, kv1, kv2, memory, bias):
    rows, features = queries.shape
    steps = memory.shape[0] // 2
    slots, block = memory.shape[1:]
    heads = steps * block // HD
    flat = pl.BlockSpec((rows, block), lambda i: (0, i))
    pair = pl.BlockSpec((2, rows, block), lambda i: (0, 0, i))
    whole = pl.BlockSpec(memory_space=pltpu.VMEM)
    keys_all = slots + 3 * rows
    return pl.pallas_call(
        attend_kernel,
        grid=(steps,),
        in_specs=[
            whole, whole, whole, whole, pair, pair, whole,
            pl.BlockSpec((rows, keys_all), lambda i: (0, 0)),
        ],
        out_specs=[flat, flat, pl.BlockSpec((1, STATS, rows), lambda i: (i, 0, 0))],
        out_shape=[
            jax.ShapeDtypeStruct((rows, features), jnp.bfloat16),
            jax.ShapeDtypeStruct((rows, features), jnp.bfloat16),
            jax.ShapeDtypeStruct((steps, STATS, rows), jnp.float32),
        ],
        compiler_params=pltpu.CompilerParams(vmem_limit_bytes=VMEM),
        cost_estimate=pl.CostEstimate(
            flops=2 * 4 * rows * keys_all * HD * heads,
            bytes_accessed=6 * 1024 * 1024,
            transcendentals=rows * keys_all * heads,
        ),
        name="attend",
    )(
        *in_vmem(queries, grad_out, keys, values),
        *in_hbm(kv1, kv2),
        *in_vmem(memory),
        *in_hbm(bias),
    )


def key_grads_kernel(
    k_ref, v_ref, q_ref, g_ref, qg1_ref, qg2_ref, st0_ref, st1_ref, st2_ref, bias_ref,
    gk_ref, gv_ref,
):
    width = gk_ref.shape[1]
    scaling = HD ** (-0.5)
    bias = bias_ref[...]
    heads = [slice(i * HD, (i + 1) * HD) for i in range(width // HD)]
    start = pl.program_id(0) * width
    picked = [pl.ds(pl.multiple_of(start + i * HD, HD), HD) for i in range(len(heads))]
    stats = jnp.concatenate([st0_ref[0], st1_ref[0], st2_ref[0]], 1)
    qs = [
        jnp.concatenate([q_ref[:, wide], qg1_ref[0, :, cols], qg2_ref[0, :, wide]], 0)
        for cols, wide in zip(heads, picked)
    ]
    gs = [
        jnp.concatenate([g_ref[:, wide], qg1_ref[1, :, cols], qg2_ref[1, :, wide]], 0)
        for cols, wide in zip(heads, picked)
    ]
    scores = [dot_t(k_ref[:, wide], qh, ((1,), (1,))) + bias for wide, qh in zip(picked, qs)]
    dprobs = [dot_t(v_ref[:, wide], gh, ((1,), (1,))) for wide, gh in zip(picked, gs)]
    probs, dscores = [], []
    for i, (score, dprob) in enumerate(zip(scores, dprobs)):
        top, share, delta = (stats[i + j * len(heads) : i + j * len(heads) + 1] for j in range(3))
        prob = jnp.exp((score - top) * scaling) * share
        probs.append(prob.astype(jnp.bfloat16))
        dscores.append((prob * ((dprob - delta) * scaling)).astype(jnp.bfloat16))
    for cols, qh, gh, prob, dscore in zip(heads, qs, gs, probs, dscores):
        gk_ref[:, cols] = dot_t(dscore, qh, ((1,), (0,))).astype(jnp.bfloat16)
        gv_ref[:, cols] = dot_t(prob, gh, ((1,), (0,))).astype(jnp.bfloat16)


def key_grads(keys, values, queries, grad_out, qg1, qg2, stats, bias):
    rows, features = keys.shape
    steps = stats[0].shape[0]
    block = features // steps
    flat = pl.BlockSpec((rows, block), lambda i: (0, i))
    pair = pl.BlockSpec((2, rows, block), lambda i: (0, 0, i))
    whole = pl.BlockSpec(memory_space=pltpu.VMEM)
    stat = pl.BlockSpec((1, STATS, rows), lambda i: (i, 0, 0))
    heads = features // HD
    return pl.pallas_call(
        key_grads_kernel,
        grid=(steps,),
        in_specs=[
            whole, whole, whole, whole, pair, whole, stat, stat, stat, whole,
        ],
        out_specs=[flat, flat],
        out_shape=[jax.ShapeDtypeStruct((rows, features), jnp.bfloat16)] * 2,
        compiler_params=pltpu.CompilerParams(vmem_limit_bytes=VMEM),
        cost_estimate=pl.CostEstimate(
            flops=2 * 4 * rows * 3 * rows * HD * heads,
            bytes_accessed=4 * 1024 * 1024,
            transcendentals=rows * 3 * rows * heads,
        ),
        name="key_grads",
    )(
        *in_vmem(keys, values, queries, grad_out),
        *in_hbm(qg1),
        *in_vmem(qg2),
        *stats,
        *in_vmem(bias),
    )


def project_kernel(layout, place_ref, *refs):
    n_z, _, cache_rows = place_ref.shape
    out_ref, w_ref, a_ref = refs[-3:]
    rows, pieces = refs[: 2 * n_z], refs[2 * n_z : -3]
    w_rows, block = pieces[0].shape[1:]
    depth = rows[0].shape[1]
    devices, _, capacity, _ = out_ref.shape
    z, p, y = (lax.axis_index(name) for name in ("z", "p", "head"))
    place_in_ring = z ^ (z >> 1)
    for i, ref in enumerate(rows):
        source = (place_in_ring - i % n_z + n_z) & (n_z - 1)
        a_ref[y ^ (i // n_z), source ^ (source >> 1)] = ref[...]
    for (m, first), piece in zip(layout, pieces):
        for k in range(piece.shape[0]):
            w_ref[z ^ (first + k), p ^ m] = piece[k]
    half = n_z // 2
    proj = sum(
        jnp.dot(
            a_ref[i].reshape(n_z * cache_rows, depth),
            w_ref[i * half : (i + 1) * half].reshape(depth, block),
            preferred_element_type=jnp.float32,
        )
        for i in range(2)
    ).astype(jnp.bfloat16)
    slot_ids = lax.broadcasted_iota(jnp.int32, (devices * capacity, cache_rows), 0)
    for z in range(n_z):
        chosen = jnp.where(slot_ids == place_ref[z], 1.0, 0.0).astype(jnp.bfloat16)
        slots = jnp.dot(
            chosen,
            proj[z * cache_rows : (z + 1) * cache_rows],
            preferred_element_type=jnp.float32,
        ).astype(jnp.bfloat16)
        out_ref[:, z] = slots.reshape(devices, capacity, block)


def project(place, rows, pieces, devices, capacity):
    n_z, _, cache_rows = place.shape
    depth = rows[0].shape[1]
    layout, pieces = [piece[:2] for piece in pieces], [piece[2] for piece in pieces]
    n_p = devices // n_z
    w_rows, block = pieces[0].shape[1:]
    whole = pl.BlockSpec(memory_space=pltpu.VMEM)
    return pl.pallas_call(
        functools.partial(project_kernel, layout),
        in_specs=[whole] * (1 + len(rows) + len(pieces)),
        out_specs=whole,
        out_shape=pltpu.VMEM((devices, n_z, capacity, block), jnp.bfloat16),
        scratch_shapes=[
            pltpu.VMEM((n_z, n_p, w_rows, block), jnp.bfloat16),
            pltpu.VMEM((2, n_z, cache_rows, depth), jnp.bfloat16),
        ],
        compiler_params=pltpu.CompilerParams(vmem_limit_bytes=VMEM),
        cost_estimate=pl.CostEstimate(
            flops=4 * n_z * cache_rows * depth * block,
            bytes_accessed=1024 * 1024,
            transcendentals=0,
        ),
        name="project",
    )(*in_vmem(place, *rows, *pieces))


def prepare_kernel(routes_ref, ids_ref, place_ref, bias_ref, back_ref):
    n_z, _, rows = place_ref.shape
    devices = routes_ref.shape[0]
    n_p = devices // n_z
    capacity = 2 * rows // devices
    slots = bias_ref.shape[1] - 3 * rows
    p = lax.axis_index("p")
    me = lax.axis_index("z") * n_p + p
    row = lax.broadcasted_iota(jnp.int32, (rows, rows), 0)
    lane = lax.broadcasted_iota(jnp.int32, (rows, rows), 1)

    def both_ways(line):
        wide = jnp.broadcast_to(line.astype(jnp.float32), (rows, rows))
        return wide, wide.T

    for z in range(n_z):
        across, down = both_ways(routes_ref[pl.ds(z * n_p + p, 1), :])
        ranks = jnp.sum(
            jnp.where((across == down) & (row < lane), 1.0, 0.0), axis=0, keepdims=True
        )
        place_ref[z] = (across[:1] * capacity + ranks).astype(jnp.int32)

    def ids_of(segment):
        return ids_ref[pl.ds(jnp.clip(segment, 0, devices - 1), 1), :].astype(jnp.float32)

    _, own = both_ways(ids_ref[pl.ds(me, 1), :])
    for i in range(3):
        earlier, later = me - 2 + i, me + i
        same = (own == ids_of(earlier)) & (earlier >= 0)
        same_back = (own == ids_of(later)) & (later < devices)
        if i == 2:
            same = same & (lane <= row)
        if i == 0:
            same_back = same_back & (lane >= row)
        bias_ref[:, slots + i * rows : slots + (i + 1) * rows] = jnp.where(same, 0.0, -1e30).astype(
            jnp.bfloat16
        )
        back_ref[:, i * rows : (i + 1) * rows] = jnp.where(same_back, 0.0, -1e30)

    mine = jnp.where(routes_ref[...] == me, 1.0, 0.0).astype(jnp.bfloat16)
    counts = dot_t(jnp.ones((8, rows), jnp.bfloat16), mine, ((1,), (1,))).astype(jnp.bfloat16)
    source = lax.broadcasted_iota(jnp.int32, (devices, slots), 0)
    slot = lax.broadcasted_iota(jnp.int32, (devices, slots), 1) // capacity
    expand = jnp.where(source == (slot % n_z) * n_p + slot // n_z, 1.0, 0.0).astype(jnp.bfloat16)
    filled = jnp.dot(counts, expand, preferred_element_type=jnp.float32)[:1]
    rank = lax.broadcasted_iota(jnp.int32, (1, slots), 1) % capacity
    live = jnp.where(rank.astype(jnp.float32) < filled, 0.0, -1e30)
    bias_ref[:, :slots] = jnp.broadcast_to(live, (rows, slots)).astype(jnp.bfloat16)


def prepare(routes, doc_ids, n_z, devices, rows):
    slots = 2 * rows
    return pl.pallas_call(
        prepare_kernel,
        out_shape=[
            jax.ShapeDtypeStruct((n_z, 1, rows), jnp.int32),
            jax.ShapeDtypeStruct((rows, slots + 3 * rows), jnp.bfloat16),
            jax.ShapeDtypeStruct((rows, 3 * rows), jnp.float32),
        ],
        compiler_params=pltpu.CompilerParams(vmem_limit_bytes=SMALL_VMEM),
        name="prepare",
    )(routes.reshape(devices, rows), doc_ids.reshape(devices, rows))


def column_block(w_kv, target):
    _, w_rows, features = w_kv.shape
    half = features // (GROUPS // 2)
    start = (target & 1, 0, (target >> 1) * half)
    return lax.dynamic_slice(w_kv, start, (1, w_rows, half))[0]


def ring_step(value, back=False):
    pairs = list(zip(RING, RING[1:] + RING[:1]))
    return lax.ppermute(value, "z", [(b, a) for a, b in pairs] if back else pairs)


def memory_slots(cache, w_kv, place, capacity, stream, back):
    n_z, n_p = lax.axis_size("z"), lax.axis_size("p")
    devices = n_z * n_p
    cache_rows, depth = cache.shape
    _, w_rows, features = w_kv.shape
    z = lax.axis_index("z")
    if n_p == 4 and capacity % ROW_TILE == 0 and w_rows % ROW_TILE == 0:
        blocks = [column_block(w_kv, z ^ mask) for mask in range(n_z)]
        own = jnp.stack(
            [blocks[0]] + [swapped(blocks[mask], "z", mask) for mask in range(1, n_z)], 0
        )
        other0 = swapped(cache, "head", 1)
        own, other0, cache = lax.optimization_barrier((own, other0, cache))
        across, beside = swapped(own, "p", 2), swapped(own, "p", 1)
        row1, row3 = ring_step(cache), ring_step(cache, back=True)
        beside, stream, back = lax.optimization_barrier((beside, stream, back))
        near, back1 = shifted(stream, 1), shifted(back, -1)
        row1 = lax.optimization_barrier(row1)
        row2, other1 = ring_step(row1), swapped(row1, "head", 1)
        row3, other1 = lax.optimization_barrier((row3, other1))
        other3 = swapped(row3, "head", 1)
        row2 = lax.optimization_barrier(row2)
        other2 = swapped(row2, "head", 1)
        near, other3 = lax.optimization_barrier((near, other3))
        far = shifted(near, 1)
        parts = [across[k : k + 1] for k in range(n_z)]
        parts, other2, other3, back1 = lax.optimization_barrier((parts, other2, other3, back1))
        pieces = [
            (0, 0, own), (1, 0, beside), (2, 0, across),
            *((3, k, swapped(part, "p", 1)) for k, part in enumerate(parts)),
        ]
        rows = [cache, row1, row2, row3, other0, other1, other2, other3]
        slots = project(place, rows, pieces, devices, capacity)
        slots, far = lax.optimization_barrier((slots, far))
        return slots, near, far, back1
    near, back1 = shifted(stream, 1), shifted(back, -1)
    far = shifted(near, 1)
    targets = [column_block(w_kv, jnp.int32(i)) for i in range(n_z)]
    w_z = lax.all_to_all(jnp.stack(targets, 0), "z", split_axis=0, concat_axis=0, tiled=True)
    w_all = lax.all_gather(w_z, "p", axis=1, tiled=True).reshape(devices * w_rows, -1)
    rows = lax.all_gather(cache, ("head", "z"), axis=0, tiled=False)
    rows = rows.reshape(-1, n_z * cache_rows, depth)
    proj = sum(
        jnp.dot(
            rows[i], w_all[i * depth : (i + 1) * depth], preferred_element_type=jnp.float32
        )
        for i in range(rows.shape[0])
    ).astype(jnp.bfloat16)
    slot_ids = jnp.arange(devices * capacity, dtype=jnp.int32)
    chosen = (slot_ids[None, :, None] == place).astype(jnp.bfloat16)
    slots = jnp.einsum(
        "zsi,zic->zsc",
        chosen,
        proj.reshape(n_z, cache_rows, -1),
        preferred_element_type=jnp.float32,
    ).astype(jnp.bfloat16)
    slots = slots.reshape(n_z, devices, capacity, -1).transpose(1, 0, 2, 3)
    return slots, near, far, back1


def body(queries, keys, values, grad_out, cache, w_kv, doc_ids, routes):
    n_z, n_p = lax.axis_size("z"), lax.axis_size("p")
    devices = n_z * n_p
    seg_rows = queries.shape[0]
    cache_rows = cache.shape[0]
    capacity = 2 * cache_rows // devices
    slot_count = capacity * devices

    place, bias, back_bias = prepare(routes, doc_ids, n_z, devices, seg_rows)
    slots, kv1, kv2, qg1 = memory_slots(
        cache,
        w_kv,
        place,
        capacity,
        jnp.stack([keys, values], 0),
        jnp.stack([queries, grad_out], 0),
    )
    memory = lax.all_to_all(slots, SEQ, split_axis=0, concat_axis=0, tiled=True)
    memory = memory.reshape(n_z, slot_count, slots.shape[-1])

    qg2 = shifted(qg1, -1)
    output, grad_q, stats = attend(queries, grad_out, keys, values, kv1, kv2, memory, bias)
    all_stats = [stats, shifted(stats, -1), shifted(stats, -2)]
    grad_k, grad_v = key_grads(
        keys, values, queries, grad_out, qg1, qg2, all_stats, back_bias
    )
    return (output, grad_q, grad_k, grad_v)


def solution(mesh):
    n_seq, n_head = mesh.devices.shape
    grid = Mesh(mesh.devices.reshape(GROUPS, n_seq // GROUPS, n_head), ("z", "p", "head"))
    rows = P(SEQ, "head")
    return jax.shard_map(
        body,
        mesh=grid,
        in_specs=(rows, rows, rows, rows, rows, P(None, SEQ, "head"), P(), P()),
        out_specs=(rows, rows, rows, rows),
        check_vma=False,
    )
```

```python
import functools

import jax
import jax.numpy as jnp
from jax import lax
from jax.experimental import pallas as pl
from jax.experimental.pallas import tpu as pltpu
from jax.sharding import Mesh, PartitionSpec as P

HD = 128
GROUPS = 4
SEQ = ("z", "p")
ROW_TILE = 16
RING = [0, 1, 3, 2]
VMEM = 24 * 1024 * 1024
SMALL_VMEM = 4 * 1024 * 1024
STATS = 16


def shifted(value, by):
    length = lax.axis_size("z") * lax.axis_size("p")
    pairs = [(i, i + by) for i in range(length) if 0 <= i + by < length]
    return lax.ppermute(value, SEQ, pairs)


def swapped(value, axis, mask):
    return lax.ppermute(value, axis, [(i, i ^ mask) for i in range(lax.axis_size(axis))])


def in_vmem(*arrays):
    return [pltpu.with_memory_space_constraint(array, pltpu.VMEM) for array in arrays]


def in_hbm(*arrays):
    return [pltpu.with_memory_space_constraint(array, pltpu.HBM) for array in arrays]


def dot_t(a, b, dims):
    return lax.dot_general(a, b, (dims, ((), ())), preferred_element_type=jnp.float32)


def attend_kernel(
    q_ref, g_ref, k_ref, v_ref, kv1_ref, kv2_ref, mem_ref, bias_ref, out_ref, gq_ref, stats_ref
):
    rows, width = out_ref.shape
    scaling = HD ** (-0.5)
    bias = bias_ref[...].astype(jnp.float32)
    step = pl.program_id(0)
    picked = [pl.ds(pl.multiple_of(step * width + i * HD, HD), HD) for i in range(width // HD)]
    heads = [slice(i * HD, (i + 1) * HD) for i in range(width // HD)]
    ks, vs = (
        [
            jnp.concatenate(
                [
                    mem_ref[2 * step + which, :, cols],
                    kv2_ref[which, :, cols],
                    kv1_ref[which, :, cols],
                    own_ref[:, wide],
                ],
                0,
            )
            for cols, wide in zip(heads, picked)
        ]
        for which, own_ref in enumerate((k_ref, v_ref))
    )
    scores = [dot_t(q_ref[:, wide], kh, ((1,), (1,))) + bias for wide, kh in zip(picked, ks)]
    dprobs = [dot_t(g_ref[:, wide], vh, ((1,), (1,))) for wide, vh in zip(picked, vs)]
    tops, shares, probs = [], [], []
    for score in scores:
        top = jnp.max(score, axis=-1, keepdims=True)
        weights = jnp.exp((score - top) * scaling)
        share = 1.0 / jnp.sum(weights, axis=-1, keepdims=True)
        tops.append(top)
        shares.append(share)
        probs.append(weights * share)
    outs = [
        dot_t(prob.astype(jnp.bfloat16), vh, ((1,), (0,))).astype(jnp.bfloat16)
        for prob, vh in zip(probs, vs)
    ]
    deltas, dscores = [], []
    for cols, wide, out_b, prob, dprob in zip(heads, picked, outs, probs, dprobs):
        out_ref[:, cols] = out_b
        delta = jnp.sum(
            g_ref[:, wide].astype(jnp.float32) * out_b.astype(jnp.float32), axis=-1, keepdims=True
        )
        deltas.append(delta)
        dscores.append((prob * ((dprob - delta) * scaling)).astype(jnp.bfloat16))
    lane = lax.broadcasted_iota(jnp.int32, (rows, HD), 1)
    stats = jnp.zeros((rows, HD), jnp.float32)
    for i, column in enumerate(tops + shares + deltas):
        stats = jnp.where(lane == i, column, stats)
    stats_ref[0] = stats.T[:STATS]
    for cols, kh, dscore in zip(heads, ks, dscores):
        gq_ref[:, cols] = dot_t(dscore, kh, ((1,), (0,))).astype(jnp.bfloat16)


def attend(queries, grad_out, keys, values, kv1, kv2, memory, bias):
    rows, features = queries.shape
    steps = memory.shape[0] // 2
    slots, block = memory.shape[1:]
    heads = steps * block // HD
    flat = pl.BlockSpec((rows, block), lambda i: (0, i))
    pair = pl.BlockSpec((2, rows, block), lambda i: (0, 0, i))
    whole = pl.BlockSpec(memory_space=pltpu.VMEM)
    keys_all = slots + 3 * rows
    return pl.pallas_call(
        attend_kernel,
        grid=(steps,),
        in_specs=[
            whole, whole, whole, whole, pair, pair, whole,
            pl.BlockSpec((rows, keys_all), lambda i: (0, 0)),
        ],
        out_specs=[flat, flat, pl.BlockSpec((1, STATS, rows), lambda i: (i, 0, 0))],
        out_shape=[
            jax.ShapeDtypeStruct((rows, features), jnp.bfloat16),
            jax.ShapeDtypeStruct((rows, features), jnp.bfloat16),
            jax.ShapeDtypeStruct((steps, STATS, rows), jnp.float32),
        ],
        compiler_params=pltpu.CompilerParams(vmem_limit_bytes=VMEM),
        cost_estimate=pl.CostEstimate(
            flops=2 * 4 * rows * keys_all * HD * heads,
            bytes_accessed=6 * 1024 * 1024,
            transcendentals=rows * keys_all * heads,
        ),
        name="attend",
    )(
        *in_vmem(queries, grad_out, keys, values),
        *in_hbm(kv1, kv2),
        *in_vmem(memory),
        *in_hbm(bias),
    )


def key_grads_kernel(
    k_ref, v_ref, q_ref, g_ref, qg1_ref, qg2_ref, st0_ref, st1_ref, st2_ref, bias_ref,
    gk_ref, gv_ref,
):
    width = gk_ref.shape[1]
    scaling = HD ** (-0.5)
    bias = bias_ref[...]
    heads = [slice(i * HD, (i + 1) * HD) for i in range(width // HD)]
    start = pl.program_id(0) * width
    picked = [pl.ds(pl.multiple_of(start + i * HD, HD), HD) for i in range(len(heads))]
    stats = jnp.concatenate([st0_ref[0], st1_ref[0], st2_ref[0]], 1)
    qs = [
        jnp.concatenate([q_ref[:, wide], qg1_ref[0, :, cols], qg2_ref[0, :, wide]], 0)
        for cols, wide in zip(heads, picked)
    ]
    gs = [
        jnp.concatenate([g_ref[:, wide], qg1_ref[1, :, cols], qg2_ref[1, :, wide]], 0)
        for cols, wide in zip(heads, picked)
    ]
    scores = [dot_t(k_ref[:, wide], qh, ((1,), (1,))) + bias for wide, qh in zip(picked, qs)]
    dprobs = [dot_t(v_ref[:, wide], gh, ((1,), (1,))) for wide, gh in zip(picked, gs)]
    probs, dscores = [], []
    for i, (score, dprob) in enumerate(zip(scores, dprobs)):
        top, share, delta = (stats[i + j * len(heads) : i + j * len(heads) + 1] for j in range(3))
        prob = jnp.exp((score - top) * scaling) * share
        probs.append(prob.astype(jnp.bfloat16))
        dscores.append((prob * ((dprob - delta) * scaling)).astype(jnp.bfloat16))
    for cols, qh, gh, prob, dscore in zip(heads, qs, gs, probs, dscores):
        gk_ref[:, cols] = dot_t(dscore, qh, ((1,), (0,))).astype(jnp.bfloat16)
        gv_ref[:, cols] = dot_t(prob, gh, ((1,), (0,))).astype(jnp.bfloat16)


def key_grads(keys, values, queries, grad_out, qg1, qg2, stats, bias):
    rows, features = keys.shape
    steps = stats[0].shape[0]
    block = features // steps
    flat = pl.BlockSpec((rows, block), lambda i: (0, i))
    pair = pl.BlockSpec((2, rows, block), lambda i: (0, 0, i))
    whole = pl.BlockSpec(memory_space=pltpu.VMEM)
    stat = pl.BlockSpec((1, STATS, rows), lambda i: (i, 0, 0))
    heads = features // HD
    return pl.pallas_call(
        key_grads_kernel,
        grid=(steps,),
        in_specs=[
            whole, whole, whole, whole, pair, whole, stat, stat, stat, whole,
        ],
        out_specs=[flat, flat],
        out_shape=[jax.ShapeDtypeStruct((rows, features), jnp.bfloat16)] * 2,
        compiler_params=pltpu.CompilerParams(vmem_limit_bytes=VMEM),
        cost_estimate=pl.CostEstimate(
            flops=2 * 4 * rows * 3 * rows * HD * heads,
            bytes_accessed=4 * 1024 * 1024,
            transcendentals=rows * 3 * rows * heads,
        ),
        name="key_grads",
    )(
        *in_vmem(keys, values, queries, grad_out),
        *in_hbm(qg1),
        *in_vmem(qg2),
        *stats,
        *in_vmem(bias),
    )


def project_kernel(layout, place_ref, *refs):
    n_z, _, cache_rows = place_ref.shape
    out_ref, w_ref, a_ref = refs[-3:]
    rows, pieces = refs[: 2 * n_z], refs[2 * n_z : -3]
    w_rows, block = pieces[0].shape[1:]
    depth = rows[0].shape[1]
    devices, _, capacity, _ = out_ref.shape
    z, p, y = (lax.axis_index(name) for name in ("z", "p", "head"))
    place_in_ring = z ^ (z >> 1)
    for i, ref in enumerate(rows):
        source = (place_in_ring - i % n_z + n_z) & (n_z - 1)
        a_ref[y ^ (i // n_z), source ^ (source >> 1)] = ref[...]
    for (m, first), piece in zip(layout, pieces):
        for k in range(piece.shape[0]):
            w_ref[z ^ (n_z - 1 - first - k), p ^ m] = piece[k]
    half = n_z // 2
    proj = sum(
        jnp.dot(
            a_ref[i].reshape(n_z * cache_rows, depth),
            w_ref[i * half : (i + 1) * half].reshape(depth, block),
            preferred_element_type=jnp.float32,
        )
        for i in range(2)
    ).astype(jnp.bfloat16)
    slot_ids = lax.broadcasted_iota(jnp.int32, (devices * capacity, cache_rows), 0)
    for z in range(n_z):
        chosen = jnp.where(slot_ids == place_ref[z], 1.0, 0.0).astype(jnp.bfloat16)
        slots = jnp.dot(
            chosen,
            proj[z * cache_rows : (z + 1) * cache_rows],
            preferred_element_type=jnp.float32,
        ).astype(jnp.bfloat16)
        out_ref[:, z] = slots.reshape(devices, capacity, block)


def project(place, rows, pieces, devices, capacity):
    n_z, _, cache_rows = place.shape
    depth = rows[0].shape[1]
    layout, pieces = [piece[:2] for piece in pieces], [piece[2] for piece in pieces]
    n_p = devices // n_z
    w_rows, block = pieces[0].shape[1:]
    whole = pl.BlockSpec(memory_space=pltpu.VMEM)
    return pl.pallas_call(
        functools.partial(project_kernel, layout),
        in_specs=[whole] * (1 + len(rows) + len(pieces)),
        out_specs=whole,
        out_shape=pltpu.VMEM((devices, n_z, capacity, block), jnp.bfloat16),
        scratch_shapes=[
            pltpu.VMEM((n_z, n_p, w_rows, block), jnp.bfloat16),
            pltpu.VMEM((2, n_z, cache_rows, depth), jnp.bfloat16),
        ],
        compiler_params=pltpu.CompilerParams(vmem_limit_bytes=VMEM),
        cost_estimate=pl.CostEstimate(
            flops=4 * n_z * cache_rows * depth * block,
            bytes_accessed=1024 * 1024,
            transcendentals=0,
        ),
        name="project",
    )(*in_vmem(place, *rows, *pieces))


def prepare_kernel(routes_ref, ids_ref, place_ref, bias_ref, back_ref):
    n_z, _, rows = place_ref.shape
    devices = routes_ref.shape[0]
    n_p = devices // n_z
    capacity = 2 * rows // devices
    slots = bias_ref.shape[1] - 3 * rows
    p = lax.axis_index("p")
    me = lax.axis_index("z") * n_p + p
    row = lax.broadcasted_iota(jnp.int32, (rows, rows), 0)
    lane = lax.broadcasted_iota(jnp.int32, (rows, rows), 1)

    def both_ways(line):
        wide = jnp.broadcast_to(line.astype(jnp.float32), (rows, rows))
        return wide, wide.T

    for z in range(n_z):
        across, down = both_ways(routes_ref[pl.ds(z * n_p + p, 1), :])
        ranks = jnp.sum(
            jnp.where((across == down) & (row < lane), 1.0, 0.0), axis=0, keepdims=True
        )
        place_ref[z] = (across[:1] * capacity + ranks).astype(jnp.int32)

    def ids_of(segment):
        return ids_ref[pl.ds(jnp.clip(segment, 0, devices - 1), 1), :].astype(jnp.float32)

    _, own = both_ways(ids_ref[pl.ds(me, 1), :])
    for i in range(3):
        earlier, later = me - 2 + i, me + i
        same = (own == ids_of(earlier)) & (earlier >= 0)
        same_back = (own == ids_of(later)) & (later < devices)
        if i == 2:
            same = same & (lane <= row)
        if i == 0:
            same_back = same_back & (lane >= row)
        bias_ref[:, slots + i * rows : slots + (i + 1) * rows] = jnp.where(same, 0.0, -1e30).astype(
            jnp.bfloat16
        )
        back_ref[:, i * rows : (i + 1) * rows] = jnp.where(same_back, 0.0, -1e30)

    mine = jnp.where(routes_ref[...] == me, 1.0, 0.0).astype(jnp.bfloat16)
    counts = dot_t(jnp.ones((8, rows), jnp.bfloat16), mine, ((1,), (1,))).astype(jnp.bfloat16)
    source = lax.broadcasted_iota(jnp.int32, (devices, slots), 0)
    slot = lax.broadcasted_iota(jnp.int32, (devices, slots), 1) // capacity
    expand = jnp.where(source == (slot % n_z) * n_p + slot // n_z, 1.0, 0.0).astype(jnp.bfloat16)
    filled = jnp.dot(counts, expand, preferred_element_type=jnp.float32)[:1]
    rank = lax.broadcasted_iota(jnp.int32, (1, slots), 1) % capacity
    live = jnp.where(rank.astype(jnp.float32) < filled, 0.0, -1e30)
    bias_ref[:, :slots] = jnp.broadcast_to(live, (rows, slots)).astype(jnp.bfloat16)


def prepare(routes, doc_ids, n_z, devices, rows):
    slots = 2 * rows
    return pl.pallas_call(
        prepare_kernel,
        out_shape=[
            jax.ShapeDtypeStruct((n_z, 1, rows), jnp.int32),
            jax.ShapeDtypeStruct((rows, slots + 3 * rows), jnp.bfloat16),
            jax.ShapeDtypeStruct((rows, 3 * rows), jnp.float32),
        ],
        compiler_params=pltpu.CompilerParams(vmem_limit_bytes=SMALL_VMEM),
        name="prepare",
    )(routes.reshape(devices, rows), doc_ids.reshape(devices, rows))


def column_block(w_kv, target):
    _, w_rows, features = w_kv.shape
    half = features // (GROUPS // 2)
    start = (target & 1, 0, (target >> 1) * half)
    return lax.dynamic_slice(w_kv, start, (1, w_rows, half))[0]


def ring_step(value, back=False):
    pairs = list(zip(RING, RING[1:] + RING[:1]))
    return lax.ppermute(value, "z", [(b, a) for a, b in pairs] if back else pairs)


def memory_slots(cache, w_kv, place, capacity, stream, back):
    n_z, n_p = lax.axis_size("z"), lax.axis_size("p")
    devices = n_z * n_p
    cache_rows, depth = cache.shape
    _, w_rows, features = w_kv.shape
    z = lax.axis_index("z")
    if n_p == 4 and capacity % ROW_TILE == 0 and w_rows % ROW_TILE == 0:
        blocks = [column_block(w_kv, z ^ mask) for mask in range(n_z)]
        own = jnp.stack(
            [swapped(blocks[mask], "z", mask) for mask in range(n_z - 1, 0, -1)] + [blocks[0]], 0
        )
        other0 = swapped(cache, "head", 1)
        own, other0, cache = lax.optimization_barrier((own, other0, cache))
        across, beside = swapped(own, "p", 2), swapped(own, "p", 1)
        row1, row3 = ring_step(cache), ring_step(cache, back=True)
        beside, stream, back = lax.optimization_barrier((beside, stream, back))
        near, back1 = shifted(stream, 1), shifted(back, -1)
        row1 = lax.optimization_barrier(row1)
        row2, other1 = ring_step(row1), swapped(row1, "head", 1)
        row3, other1 = lax.optimization_barrier((row3, other1))
        other3 = swapped(row3, "head", 1)
        row2 = lax.optimization_barrier(row2)
        other2 = swapped(row2, "head", 1)
        near, other3 = lax.optimization_barrier((near, other3))
        far = shifted(near, 1)
        parts = [across[k : k + 1] for k in range(n_z)]
        parts, other2, other3, back1 = lax.optimization_barrier((parts, other2, other3, back1))
        pieces = [
            (0, 0, own), (1, 0, beside), (2, 0, across),
            *((3, k, swapped(part, "p", 1)) for k, part in enumerate(parts)),
        ]
        rows = [cache, row1, row2, row3, other0, other1, other2, other3]
        slots = project(place, rows, pieces, devices, capacity)
        slots, far = lax.optimization_barrier((slots, far))
        return slots, near, far, back1
    near, back1 = shifted(stream, 1), shifted(back, -1)
    far = shifted(near, 1)
    targets = [column_block(w_kv, jnp.int32(i)) for i in range(n_z)]
    w_z = lax.all_to_all(jnp.stack(targets, 0), "z", split_axis=0, concat_axis=0, tiled=True)
    w_all = lax.all_gather(w_z, "p", axis=1, tiled=True).reshape(devices * w_rows, -1)
    rows = lax.all_gather(cache, ("head", "z"), axis=0, tiled=False)
    rows = rows.reshape(-1, n_z * cache_rows, depth)
    proj = sum(
        jnp.dot(
            rows[i], w_all[i * depth : (i + 1) * depth], preferred_element_type=jnp.float32
        )
        for i in range(rows.shape[0])
    ).astype(jnp.bfloat16)
    slot_ids = jnp.arange(devices * capacity, dtype=jnp.int32)
    chosen = (slot_ids[None, :, None] == place).astype(jnp.bfloat16)
    slots = jnp.einsum(
        "zsi,zic->zsc",
        chosen,
        proj.reshape(n_z, cache_rows, -1),
        preferred_element_type=jnp.float32,
    ).astype(jnp.bfloat16)
    slots = slots.reshape(n_z, devices, capacity, -1).transpose(1, 0, 2, 3)
    return slots, near, far, back1


def body(queries, keys, values, grad_out, cache, w_kv, doc_ids, routes):
    n_z, n_p = lax.axis_size("z"), lax.axis_size("p")
    devices = n_z * n_p
    seg_rows = queries.shape[0]
    cache_rows = cache.shape[0]
    capacity = 2 * cache_rows // devices
    slot_count = capacity * devices

    place, bias, back_bias = prepare(routes, doc_ids, n_z, devices, seg_rows)
    slots, kv1, kv2, qg1 = memory_slots(
        cache,
        w_kv,
        place,
        capacity,
        jnp.stack([keys, values], 0),
        jnp.stack([queries, grad_out], 0),
    )
    memory = lax.all_to_all(slots, SEQ, split_axis=0, concat_axis=0, tiled=True)
    memory = memory.reshape(n_z, slot_count, slots.shape[-1])

    qg2 = shifted(qg1, -1)
    output, grad_q, stats = attend(queries, grad_out, keys, values, kv1, kv2, memory, bias)
    all_stats = [stats, shifted(stats, -1), shifted(stats, -2)]
    grad_k, grad_v = key_grads(
        keys, values, queries, grad_out, qg1, qg2, all_stats, back_bias
    )
    return (output, grad_q, grad_k, grad_v)


def solution(mesh):
    n_seq, n_head = mesh.devices.shape
    grid = Mesh(mesh.devices.reshape(GROUPS, n_seq // GROUPS, n_head), ("z", "p", "head"))
    rows = P(SEQ, "head")
    return jax.shard_map(
        body,
        mesh=grid,
        in_specs=(rows, rows, rows, rows, rows, P(None, SEQ, "head"), P(), P()),
        out_specs=(rows, rows, rows, rows),
        check_vma=False,
    )
```

```python
import jax
import jax.numpy as jnp
from jax import lax
from jax.experimental import pallas as pl
from jax.experimental.pallas import tpu as pltpu
from jax.sharding import Mesh, PartitionSpec as P

HD = 128
GROUPS = 4
SEQ = ("z", "p")
ROW_TILE = 16
RING = [0, 1, 3, 2]
VMEM = 24 * 1024 * 1024
SMALL_VMEM = 4 * 1024 * 1024
STATS = 16


def shifted(value, by):
    length = lax.axis_size("z") * lax.axis_size("p")
    pairs = [(i, i + by) for i in range(length) if 0 <= i + by < length]
    return lax.ppermute(value, SEQ, pairs)


def swapped(value, axis, mask):
    return lax.ppermute(value, axis, [(i, i ^ mask) for i in range(lax.axis_size(axis))])


def in_vmem(*arrays):
    return [pltpu.with_memory_space_constraint(array, pltpu.VMEM) for array in arrays]


def in_hbm(*arrays):
    return [pltpu.with_memory_space_constraint(array, pltpu.HBM) for array in arrays]


def dot_t(a, b, dims):
    return lax.dot_general(a, b, (dims, ((), ())), preferred_element_type=jnp.float32)


def attend_kernel(
    q_ref, g_ref, k_ref, v_ref, kv1_ref, kv2_ref, mem_ref, bias_ref, out_ref, gq_ref, stats_ref
):
    rows, width = out_ref.shape
    scaling = HD ** (-0.5)
    bias = bias_ref[...].astype(jnp.float32)
    step = pl.program_id(0)
    picked = [pl.ds(pl.multiple_of(step * width + i * HD, HD), HD) for i in range(width // HD)]
    heads = [slice(i * HD, (i + 1) * HD) for i in range(width // HD)]
    ks, vs = (
        [
            jnp.concatenate(
                [
                    mem_ref[2 * step + which, :, cols],
                    kv2_ref[which, :, cols],
                    kv1_ref[which, :, cols],
                    own_ref[:, wide],
                ],
                0,
            )
            for cols, wide in zip(heads, picked)
        ]
        for which, own_ref in enumerate((k_ref, v_ref))
    )
    scores = [dot_t(q_ref[:, wide], kh, ((1,), (1,))) + bias for wide, kh in zip(picked, ks)]
    dprobs = [dot_t(g_ref[:, wide], vh, ((1,), (1,))) for wide, vh in zip(picked, vs)]
    tops, shares, probs = [], [], []
    for score in scores:
        top = jnp.max(score, axis=-1, keepdims=True)
        weights = jnp.exp((score - top) * scaling)
        share = 1.0 / jnp.sum(weights, axis=-1, keepdims=True)
        tops.append(top)
        shares.append(share)
        probs.append(weights * share)
    outs = [
        dot_t(prob.astype(jnp.bfloat16), vh, ((1,), (0,))).astype(jnp.bfloat16)
        for prob, vh in zip(probs, vs)
    ]
    deltas, dscores = [], []
    for cols, wide, out_b, prob, dprob in zip(heads, picked, outs, probs, dprobs):
        out_ref[:, cols] = out_b
        delta = jnp.sum(
            g_ref[:, wide].astype(jnp.float32) * out_b.astype(jnp.float32), axis=-1, keepdims=True
        )
        deltas.append(delta)
        dscores.append((prob * ((dprob - delta) * scaling)).astype(jnp.bfloat16))
    lane = lax.broadcasted_iota(jnp.int32, (rows, HD), 1)
    stats = jnp.zeros((rows, HD), jnp.float32)
    for i, column in enumerate(tops + shares + deltas):
        stats = jnp.where(lane == i, column, stats)
    stats_ref[0] = stats.T[:STATS]
    for cols, kh, dscore in zip(heads, ks, dscores):
        gq_ref[:, cols] = dot_t(dscore, kh, ((1,), (0,))).astype(jnp.bfloat16)


def attend(queries, grad_out, keys, values, kv1, kv2, memory, bias):
    rows, features = queries.shape
    steps = memory.shape[0] // 2
    slots, block = memory.shape[1:]
    heads = steps * block // HD
    flat = pl.BlockSpec((rows, block), lambda i: (0, i))
    pair = pl.BlockSpec((2, rows, block), lambda i: (0, 0, i))
    whole = pl.BlockSpec(memory_space=pltpu.VMEM)
    keys_all = slots + 3 * rows
    return pl.pallas_call(
        attend_kernel,
        grid=(steps,),
        in_specs=[
            whole, whole, whole, whole, pair, pair, whole,
            pl.BlockSpec((rows, keys_all), lambda i: (0, 0)),
        ],
        out_specs=[flat, flat, pl.BlockSpec((1, STATS, rows), lambda i: (i, 0, 0))],
        out_shape=[
            jax.ShapeDtypeStruct((rows, features), jnp.bfloat16),
            jax.ShapeDtypeStruct((rows, features), jnp.bfloat16),
            jax.ShapeDtypeStruct((steps, STATS, rows), jnp.float32),
        ],
        compiler_params=pltpu.CompilerParams(vmem_limit_bytes=VMEM),
        cost_estimate=pl.CostEstimate(
            flops=2 * 4 * rows * keys_all * HD * heads,
            bytes_accessed=6 * 1024 * 1024,
            transcendentals=rows * keys_all * heads,
        ),
        name="attend",
    )(
        *in_vmem(queries, grad_out, keys, values),
        *in_hbm(kv1, kv2),
        *in_vmem(memory),
        *in_hbm(bias),
    )


def key_grads_kernel(
    k_ref, v_ref, q_ref, g_ref, qg1_ref, qg2_ref, st0_ref, st1_ref, st2_ref, bias_ref,
    gk_ref, gv_ref,
):
    width = gk_ref.shape[1]
    scaling = HD ** (-0.5)
    bias = bias_ref[...]
    heads = [slice(i * HD, (i + 1) * HD) for i in range(width // HD)]
    start = pl.program_id(0) * width
    picked = [pl.ds(pl.multiple_of(start + i * HD, HD), HD) for i in range(len(heads))]
    stats = jnp.concatenate([st0_ref[0], st1_ref[0], st2_ref[0]], 1)
    qs = [
        jnp.concatenate([q_ref[:, wide], qg1_ref[0, :, cols], qg2_ref[0, :, wide]], 0)
        for cols, wide in zip(heads, picked)
    ]
    gs = [
        jnp.concatenate([g_ref[:, wide], qg1_ref[1, :, cols], qg2_ref[1, :, wide]], 0)
        for cols, wide in zip(heads, picked)
    ]
    scores = [dot_t(k_ref[:, wide], qh, ((1,), (1,))) + bias for wide, qh in zip(picked, qs)]
    dprobs = [dot_t(v_ref[:, wide], gh, ((1,), (1,))) for wide, gh in zip(picked, gs)]
    probs, dscores = [], []
    for i, (score, dprob) in enumerate(zip(scores, dprobs)):
        top, share, delta = (stats[i + j * len(heads) : i + j * len(heads) + 1] for j in range(3))
        prob = jnp.exp((score - top) * scaling) * share
        probs.append(prob.astype(jnp.bfloat16))
        dscores.append((prob * ((dprob - delta) * scaling)).astype(jnp.bfloat16))
    for cols, qh, gh, prob, dscore in zip(heads, qs, gs, probs, dscores):
        gk_ref[:, cols] = dot_t(dscore, qh, ((1,), (0,))).astype(jnp.bfloat16)
        gv_ref[:, cols] = dot_t(prob, gh, ((1,), (0,))).astype(jnp.bfloat16)


def key_grads(keys, values, queries, grad_out, qg1, qg2, stats, bias):
    rows, features = keys.shape
    steps = stats[0].shape[0]
    block = features // steps
    flat = pl.BlockSpec((rows, block), lambda i: (0, i))
    pair = pl.BlockSpec((2, rows, block), lambda i: (0, 0, i))
    whole = pl.BlockSpec(memory_space=pltpu.VMEM)
    stat = pl.BlockSpec((1, STATS, rows), lambda i: (i, 0, 0))
    heads = features // HD
    return pl.pallas_call(
        key_grads_kernel,
        grid=(steps,),
        in_specs=[
            whole, whole, whole, whole, pair, whole, stat, stat, stat, whole,
        ],
        out_specs=[flat, flat],
        out_shape=[jax.ShapeDtypeStruct((rows, features), jnp.bfloat16)] * 2,
        compiler_params=pltpu.CompilerParams(vmem_limit_bytes=VMEM),
        cost_estimate=pl.CostEstimate(
            flops=2 * 4 * rows * 3 * rows * HD * heads,
            bytes_accessed=4 * 1024 * 1024,
            transcendentals=rows * 3 * rows * heads,
        ),
        name="key_grads",
    )(
        *in_vmem(keys, values, queries, grad_out),
        *in_hbm(qg1),
        *in_vmem(qg2),
        *stats,
        *in_vmem(bias),
    )


def project_kernel(place_ref, *refs):
    n_z, _, cache_rows = place_ref.shape
    out_ref, w_ref, a_ref = refs[-3:]
    rows, pieces = refs[: 2 * n_z], refs[2 * n_z : -3]
    n_p, (_, w_rows, block) = len(pieces), pieces[0].shape
    depth = rows[0].shape[1]
    devices, _, capacity, _ = out_ref.shape
    z, p, y = (lax.axis_index(name) for name in ("z", "p", "head"))
    place_in_ring = z ^ (z >> 1)
    for i, ref in enumerate(rows):
        source = (place_in_ring - i % n_z + n_z) & (n_z - 1)
        columns = pl.ds(pl.multiple_of((y ^ (i // n_z)) * depth, HD), depth)
        a_ref[source ^ (source >> 1), :, columns] = ref[...]
    for m in range(n_p):
        for k in range(n_z):
            w_ref[z ^ k, p ^ m] = pieces[m][k]
    proj = jnp.dot(
        a_ref[...].reshape(n_z * cache_rows, 2 * depth),
        w_ref[...].reshape(2 * depth, block),
        preferred_element_type=jnp.float32,
    ).astype(jnp.bfloat16)
    slot_ids = lax.broadcasted_iota(jnp.int32, (devices * capacity, cache_rows), 0)
    for z in range(n_z):
        chosen = jnp.where(slot_ids == place_ref[z], 1.0, 0.0).astype(jnp.bfloat16)
        slots = jnp.dot(
            chosen,
            proj[z * cache_rows : (z + 1) * cache_rows],
            preferred_element_type=jnp.float32,
        ).astype(jnp.bfloat16)
        out_ref[:, z] = slots.reshape(devices, capacity, block)


def project(place, rows, pieces, devices, capacity):
    n_z, _, cache_rows = place.shape
    depth = rows[0].shape[1]
    n_p = len(pieces)
    _, w_rows, block = pieces[0].shape
    whole = pl.BlockSpec(memory_space=pltpu.VMEM)
    return pl.pallas_call(
        project_kernel,
        in_specs=[whole] * (1 + len(rows) + n_p),
        out_specs=whole,
        out_shape=pltpu.VMEM((devices, n_z, capacity, block), jnp.bfloat16),
        scratch_shapes=[
            pltpu.VMEM((n_z, n_p, w_rows, block), jnp.bfloat16),
            pltpu.VMEM((n_z, cache_rows, 2 * depth), jnp.bfloat16),
        ],
        compiler_params=pltpu.CompilerParams(vmem_limit_bytes=VMEM),
        cost_estimate=pl.CostEstimate(
            flops=4 * n_z * cache_rows * depth * block,
            bytes_accessed=8 * 1024 * 1024,
            transcendentals=0,
        ),
        name="project",
    )(*in_vmem(place, *rows, *pieces))


def prepare_kernel(routes_ref, ids_ref, place_ref, bias_ref, back_ref):
    n_z, _, rows = place_ref.shape
    devices = routes_ref.shape[0]
    n_p = devices // n_z
    capacity = 2 * rows // devices
    slots = bias_ref.shape[1] - 3 * rows
    p = lax.axis_index("p")
    me = lax.axis_index("z") * n_p + p
    row = lax.broadcasted_iota(jnp.int32, (rows, rows), 0)
    lane = lax.broadcasted_iota(jnp.int32, (rows, rows), 1)

    def both_ways(line):
        wide = jnp.broadcast_to(line.astype(jnp.float32), (rows, rows))
        return wide, wide.T

    for z in range(n_z):
        across, down = both_ways(routes_ref[pl.ds(z * n_p + p, 1), :])
        ranks = jnp.sum(
            jnp.where((across == down) & (row < lane), 1.0, 0.0), axis=0, keepdims=True
        )
        place_ref[z] = (across[:1] * capacity + ranks).astype(jnp.int32)

    def ids_of(segment):
        return ids_ref[pl.ds(jnp.clip(segment, 0, devices - 1), 1), :].astype(jnp.float32)

    _, own = both_ways(ids_ref[pl.ds(me, 1), :])
    for i in range(3):
        earlier, later = me - 2 + i, me + i
        same = (own == ids_of(earlier)) & (earlier >= 0)
        same_back = (own == ids_of(later)) & (later < devices)
        if i == 2:
            same = same & (lane <= row)
        if i == 0:
            same_back = same_back & (lane >= row)
        bias_ref[:, slots + i * rows : slots + (i + 1) * rows] = jnp.where(same, 0.0, -1e30).astype(
            jnp.bfloat16
        )
        back_ref[:, i * rows : (i + 1) * rows] = jnp.where(same_back, 0.0, -1e30)

    mine = jnp.where(routes_ref[...] == me, 1.0, 0.0).astype(jnp.bfloat16)
    counts = dot_t(jnp.ones((8, rows), jnp.bfloat16), mine, ((1,), (1,))).astype(jnp.bfloat16)
    source = lax.broadcasted_iota(jnp.int32, (devices, slots), 0)
    slot = lax.broadcasted_iota(jnp.int32, (devices, slots), 1) // capacity
    expand = jnp.where(source == (slot % n_z) * n_p + slot // n_z, 1.0, 0.0).astype(jnp.bfloat16)
    filled = jnp.dot(counts, expand, preferred_element_type=jnp.float32)[:1]
    rank = lax.broadcasted_iota(jnp.int32, (1, slots), 1) % capacity
    live = jnp.where(rank.astype(jnp.float32) < filled, 0.0, -1e30)
    bias_ref[:, :slots] = jnp.broadcast_to(live, (rows, slots)).astype(jnp.bfloat16)


def prepare(routes, doc_ids, n_z, devices, rows):
    slots = 2 * rows
    return pl.pallas_call(
        prepare_kernel,
        out_shape=[
            jax.ShapeDtypeStruct((n_z, 1, rows), jnp.int32),
            jax.ShapeDtypeStruct((rows, slots + 3 * rows), jnp.bfloat16),
            jax.ShapeDtypeStruct((rows, 3 * rows), jnp.float32),
        ],
        compiler_params=pltpu.CompilerParams(vmem_limit_bytes=SMALL_VMEM),
        name="prepare",
    )(routes.reshape(devices, rows), doc_ids.reshape(devices, rows))


def column_block(w_kv, target):
    _, w_rows, features = w_kv.shape
    half = features // (GROUPS // 2)
    start = (target & 1, 0, (target >> 1) * half)
    return lax.dynamic_slice(w_kv, start, (1, w_rows, half))[0]


def ring_step(value, back=False):
    pairs = list(zip(RING, RING[1:] + RING[:1]))
    return lax.ppermute(value, "z", [(b, a) for a, b in pairs] if back else pairs)


def memory_slots(cache, w_kv, place, capacity, stream, back):
    n_z, n_p = lax.axis_size("z"), lax.axis_size("p")
    devices = n_z * n_p
    cache_rows, depth = cache.shape
    _, w_rows, features = w_kv.shape
    z = lax.axis_index("z")
    if n_p == 4 and capacity % ROW_TILE == 0 and w_rows % ROW_TILE == 0:
        blocks = [column_block(w_kv, z ^ mask) for mask in range(n_z)]
        own = jnp.stack(
            [blocks[0]] + [swapped(blocks[mask], "z", mask) for mask in range(1, n_z)], 0
        )
        other0 = swapped(cache, "head", 1)
        own, other0, cache = lax.optimization_barrier((own, other0, cache))
        across, beside = swapped(own, "p", 2), swapped(own, "p", 1)
        row1, row3 = ring_step(cache), ring_step(cache, back=True)
        beside, stream, back = lax.optimization_barrier((beside, stream, back))
        near, back1 = shifted(stream, 1), shifted(back, -1)
        row1 = lax.optimization_barrier(row1)
        row2, other1 = ring_step(row1), swapped(row1, "head", 1)
        row3, other1 = lax.optimization_barrier((row3, other1))
        other3 = swapped(row3, "head", 1)
        row2 = lax.optimization_barrier(row2)
        other2 = swapped(row2, "head", 1)
        across, other2, other3, near, back1 = lax.optimization_barrier(
            (across, other2, other3, near, back1)
        )
        pieces = [own, beside, across, swapped(across, "p", 1)]
        far = shifted(near, 1)
        rows = [cache, row1, row2, row3, other0, other1, other2, other3]
        slots = project(place, rows, pieces, devices, capacity)
        slots, far = lax.optimization_barrier((slots, far))
        return slots, near, far, back1
    near, back1 = shifted(stream, 1), shifted(back, -1)
    far = shifted(near, 1)
    targets = [column_block(w_kv, jnp.int32(i)) for i in range(n_z)]
    w_z = lax.all_to_all(jnp.stack(targets, 0), "z", split_axis=0, concat_axis=0, tiled=True)
    w_all = lax.all_gather(w_z, "p", axis=1, tiled=True).reshape(devices * w_rows, -1)
    rows = lax.all_gather(cache, ("head", "z"), axis=0, tiled=False)
    rows = rows.reshape(-1, n_z * cache_rows, depth)
    proj = sum(
        jnp.dot(
            rows[i], w_all[i * depth : (i + 1) * depth], preferred_element_type=jnp.float32
        )
        for i in range(rows.shape[0])
    ).astype(jnp.bfloat16)
    slot_ids = jnp.arange(devices * capacity, dtype=jnp.int32)
    chosen = (slot_ids[None, :, None] == place).astype(jnp.bfloat16)
    slots = jnp.einsum(
        "zsi,zic->zsc",
        chosen,
        proj.reshape(n_z, cache_rows, -1),
        preferred_element_type=jnp.float32,
    ).astype(jnp.bfloat16)
    slots = slots.reshape(n_z, devices, capacity, -1).transpose(1, 0, 2, 3)
    return slots, near, far, back1


def body(queries, keys, values, grad_out, cache, w_kv, doc_ids, routes):
    n_z, n_p = lax.axis_size("z"), lax.axis_size("p")
    devices = n_z * n_p
    seg_rows = queries.shape[0]
    cache_rows = cache.shape[0]
    capacity = 2 * cache_rows // devices
    slot_count = capacity * devices

    place, bias, back_bias = prepare(routes, doc_ids, n_z, devices, seg_rows)
    slots, kv1, kv2, qg1 = memory_slots(
        cache,
        w_kv,
        place,
        capacity,
        jnp.stack([keys, values], 0),
        jnp.stack([queries, grad_out], 0),
    )
    memory = lax.all_to_all(slots, SEQ, split_axis=0, concat_axis=0, tiled=True)
    memory = memory.reshape(n_z, slot_count, slots.shape[-1])

    qg2 = shifted(qg1, -1)
    output, grad_q, stats = attend(queries, grad_out, keys, values, kv1, kv2, memory, bias)
    all_stats = [stats, shifted(stats, -1), shifted(stats, -2)]
    grad_k, grad_v = key_grads(
        keys, values, queries, grad_out, qg1, qg2, all_stats, back_bias
    )
    return (output, grad_q, grad_k, grad_v)


def solution(mesh):
    n_seq, n_head = mesh.devices.shape
    grid = Mesh(mesh.devices.reshape(GROUPS, n_seq // GROUPS, n_head), ("z", "p", "head"))
    rows = P(SEQ, "head")
    return jax.shard_map(
        body,
        mesh=grid,
        in_specs=(rows, rows, rows, rows, rows, P(None, SEQ, "head"), P(), P()),
        out_specs=(rows, rows, rows, rows),
        check_vma=False,
    )
```

```python
import jax
import jax.numpy as jnp
from jax import lax
from jax.experimental import pallas as pl
from jax.experimental.pallas import tpu as pltpu
from jax.sharding import Mesh, PartitionSpec as P

HD = 128
GROUPS = 4
SEQ = ("z", "p")
ROW_TILE = 16
RING = [0, 1, 3, 2]
VMEM = 24 * 1024 * 1024
SMALL_VMEM = 4 * 1024 * 1024
STATS = 16


def shifted(value, by):
    length = lax.axis_size("z") * lax.axis_size("p")
    pairs = [(i, i + by) for i in range(length) if 0 <= i + by < length]
    return lax.ppermute(value, SEQ, pairs)


def swapped(value, axis, mask):
    return lax.ppermute(value, axis, [(i, i ^ mask) for i in range(lax.axis_size(axis))])


def in_vmem(*arrays):
    return [pltpu.with_memory_space_constraint(array, pltpu.VMEM) for array in arrays]


def in_hbm(*arrays):
    return [pltpu.with_memory_space_constraint(array, pltpu.HBM) for array in arrays]


def dot_t(a, b, dims):
    return lax.dot_general(a, b, (dims, ((), ())), preferred_element_type=jnp.float32)


def attend_kernel(
    q_ref, g_ref, k_ref, v_ref, kv1_ref, kv2_ref, mem_ref, bias_ref, out_ref, gq_ref, stats_ref
):
    rows, width = out_ref.shape
    scaling = HD ** (-0.5)
    bias = bias_ref[...].astype(jnp.float32)
    step = pl.program_id(0)
    picked = [pl.ds(pl.multiple_of(step * width + i * HD, HD), HD) for i in range(width // HD)]
    heads = [slice(i * HD, (i + 1) * HD) for i in range(width // HD)]
    ks, vs = (
        [
            jnp.concatenate(
                [
                    mem_ref[2 * step + which, :, cols],
                    kv2_ref[which, :, cols],
                    kv1_ref[which, :, cols],
                    own_ref[:, wide],
                ],
                0,
            )
            for cols, wide in zip(heads, picked)
        ]
        for which, own_ref in enumerate((k_ref, v_ref))
    )
    scores = [dot_t(q_ref[:, wide], kh, ((1,), (1,))) + bias for wide, kh in zip(picked, ks)]
    dprobs = [dot_t(g_ref[:, wide], vh, ((1,), (1,))) for wide, vh in zip(picked, vs)]
    tops, shares, probs = [], [], []
    for score in scores:
        top = jnp.max(score, axis=-1, keepdims=True)
        weights = jnp.exp((score - top) * scaling)
        share = 1.0 / jnp.sum(weights, axis=-1, keepdims=True)
        tops.append(top)
        shares.append(share)
        probs.append(weights * share)
    outs = [
        dot_t(prob.astype(jnp.bfloat16), vh, ((1,), (0,))).astype(jnp.bfloat16)
        for prob, vh in zip(probs, vs)
    ]
    deltas, dscores = [], []
    for cols, wide, out_b, prob, dprob in zip(heads, picked, outs, probs, dprobs):
        out_ref[:, cols] = out_b
        delta = jnp.sum(
            g_ref[:, wide].astype(jnp.float32) * out_b.astype(jnp.float32), axis=-1, keepdims=True
        )
        deltas.append(delta)
        dscores.append((prob * ((dprob - delta) * scaling)).astype(jnp.bfloat16))
    lane = lax.broadcasted_iota(jnp.int32, (rows, HD), 1)
    stats = jnp.zeros((rows, HD), jnp.float32)
    for i, column in enumerate(tops + shares + deltas):
        stats = jnp.where(lane == i, column, stats)
    stats_ref[0] = stats.T[:STATS]
    for cols, kh, dscore in zip(heads, ks, dscores):
        gq_ref[:, cols] = dot_t(dscore, kh, ((1,), (0,))).astype(jnp.bfloat16)


def attend(queries, grad_out, keys, values, kv1, kv2, memory, bias):
    rows, features = queries.shape
    steps = memory.shape[0] // 2
    slots, block = memory.shape[1:]
    heads = steps * block // HD
    flat = pl.BlockSpec((rows, block), lambda i: (0, i))
    pair = pl.BlockSpec((2, rows, block), lambda i: (0, 0, i))
    whole = pl.BlockSpec(memory_space=pltpu.VMEM)
    keys_all = slots + 3 * rows
    return pl.pallas_call(
        attend_kernel,
        grid=(steps,),
        in_specs=[
            whole, whole, whole, whole, pair, pair, whole,
            pl.BlockSpec((rows, keys_all), lambda i: (0, 0)),
        ],
        out_specs=[flat, flat, pl.BlockSpec((1, STATS, rows), lambda i: (i, 0, 0))],
        out_shape=[
            jax.ShapeDtypeStruct((rows, features), jnp.bfloat16),
            jax.ShapeDtypeStruct((rows, features), jnp.bfloat16),
            jax.ShapeDtypeStruct((steps, STATS, rows), jnp.float32),
        ],
        compiler_params=pltpu.CompilerParams(vmem_limit_bytes=VMEM),
        cost_estimate=pl.CostEstimate(
            flops=2 * 4 * rows * keys_all * HD * heads,
            bytes_accessed=6 * 1024 * 1024,
            transcendentals=rows * keys_all * heads,
        ),
        name="attend",
    )(
        *in_vmem(queries, grad_out, keys, values),
        *in_hbm(kv1, kv2),
        *in_vmem(memory),
        *in_hbm(bias),
    )


def key_grads_kernel(
    k_ref, v_ref, q_ref, g_ref, qg1_ref, qg2_ref, st0_ref, st1_ref, st2_ref, bias_ref,
    gk_ref, gv_ref,
):
    width = gk_ref.shape[1]
    scaling = HD ** (-0.5)
    bias = bias_ref[...]
    heads = [slice(i * HD, (i + 1) * HD) for i in range(width // HD)]
    start = pl.program_id(0) * width
    picked = [pl.ds(pl.multiple_of(start + i * HD, HD), HD) for i in range(len(heads))]
    stats = jnp.concatenate([st0_ref[0], st1_ref[0], st2_ref[0]], 1)
    qs = [
        jnp.concatenate([q_ref[:, wide], qg1_ref[0, :, cols], qg2_ref[0, :, wide]], 0)
        for cols, wide in zip(heads, picked)
    ]
    gs = [
        jnp.concatenate([g_ref[:, wide], qg1_ref[1, :, cols], qg2_ref[1, :, wide]], 0)
        for cols, wide in zip(heads, picked)
    ]
    scores = [dot_t(k_ref[:, wide], qh, ((1,), (1,))) + bias for wide, qh in zip(picked, qs)]
    dprobs = [dot_t(v_ref[:, wide], gh, ((1,), (1,))) for wide, gh in zip(picked, gs)]
    probs, dscores = [], []
    for i, (score, dprob) in enumerate(zip(scores, dprobs)):
        top, share, delta = (stats[i + j * len(heads) : i + j * len(heads) + 1] for j in range(3))
        prob = jnp.exp((score - top) * scaling) * share
        probs.append(prob.astype(jnp.bfloat16))
        dscores.append((prob * ((dprob - delta) * scaling)).astype(jnp.bfloat16))
    for cols, qh, gh, prob, dscore in zip(heads, qs, gs, probs, dscores):
        gk_ref[:, cols] = dot_t(dscore, qh, ((1,), (0,))).astype(jnp.bfloat16)
        gv_ref[:, cols] = dot_t(prob, gh, ((1,), (0,))).astype(jnp.bfloat16)


def key_grads(keys, values, queries, grad_out, qg1, qg2, stats, bias):
    rows, features = keys.shape
    steps = stats[0].shape[0]
    block = features // steps
    flat = pl.BlockSpec((rows, block), lambda i: (0, i))
    pair = pl.BlockSpec((2, rows, block), lambda i: (0, 0, i))
    whole = pl.BlockSpec(memory_space=pltpu.VMEM)
    stat = pl.BlockSpec((1, STATS, rows), lambda i: (i, 0, 0))
    heads = features // HD
    return pl.pallas_call(
        key_grads_kernel,
        grid=(steps,),
        in_specs=[
            whole, whole, whole, whole, pair, whole, stat, stat, stat, whole,
        ],
        out_specs=[flat, flat],
        out_shape=[jax.ShapeDtypeStruct((rows, features), jnp.bfloat16)] * 2,
        compiler_params=pltpu.CompilerParams(vmem_limit_bytes=VMEM),
        cost_estimate=pl.CostEstimate(
            flops=2 * 4 * rows * 3 * rows * HD * heads,
            bytes_accessed=4 * 1024 * 1024,
            transcendentals=rows * 3 * rows * heads,
        ),
        name="key_grads",
    )(
        *in_vmem(keys, values, queries, grad_out),
        *in_hbm(qg1),
        *in_vmem(qg2),
        *stats,
        *in_vmem(bias),
    )


def project_kernel(place_ref, *refs):
    n_z, _, cache_rows = place_ref.shape
    out_ref, w_ref, a_ref = refs[-3:]
    rows, pieces = refs[: 2 * n_z], refs[2 * n_z : -3]
    n_p, (_, w_rows, block) = len(pieces), pieces[0].shape
    depth = rows[0].shape[1]
    devices, _, capacity, _ = out_ref.shape
    z, p, y = (lax.axis_index(name) for name in ("z", "p", "head"))
    place_in_ring = z ^ (z >> 1)
    for i, ref in enumerate(rows):
        source = (place_in_ring - i % n_z + n_z) & (n_z - 1)
        a_ref[y ^ (i // n_z), source ^ (source >> 1)] = ref[...]
    for m in range(n_p):
        for k in range(n_z):
            w_ref[z ^ k, p ^ m] = pieces[m][k]
    half = n_z // 2
    proj = sum(
        jnp.dot(
            a_ref[i].reshape(n_z * cache_rows, depth),
            w_ref[i * half : (i + 1) * half].reshape(depth, block),
            preferred_element_type=jnp.float32,
        )
        for i in range(2)
    ).astype(jnp.bfloat16)
    slot_ids = lax.broadcasted_iota(jnp.int32, (devices * capacity, cache_rows), 0)
    for z in range(n_z):
        chosen = jnp.where(slot_ids == place_ref[z], 1.0, 0.0).astype(jnp.bfloat16)
        slots = jnp.dot(
            chosen,
            proj[z * cache_rows : (z + 1) * cache_rows],
            preferred_element_type=jnp.float32,
        ).astype(jnp.bfloat16)
        out_ref[:, z] = slots.reshape(devices, capacity, block)


def project(place, rows, pieces, devices, capacity):
    n_z, _, cache_rows = place.shape
    depth = rows[0].shape[1]
    n_p = len(pieces)
    _, w_rows, block = pieces[0].shape
    whole = pl.BlockSpec(memory_space=pltpu.VMEM)
    return pl.pallas_call(
        project_kernel,
        in_specs=[whole] * (1 + len(rows) + n_p),
        out_specs=whole,
        out_shape=pltpu.VMEM((devices, n_z, capacity, block), jnp.bfloat16),
        scratch_shapes=[
            pltpu.VMEM((n_z, n_p, w_rows, block), jnp.bfloat16),
            pltpu.VMEM((2, n_z, cache_rows, depth), jnp.bfloat16),
        ],
        compiler_params=pltpu.CompilerParams(vmem_limit_bytes=VMEM),
        cost_estimate=pl.CostEstimate(
            flops=4 * n_z * cache_rows * depth * block,
            bytes_accessed=8 * 1024 * 1024,
            transcendentals=0,
        ),
        name="project",
    )(*in_vmem(place, *rows, *pieces))


def prepare_kernel(routes_ref, ids_ref, place_ref, bias_ref, back_ref):
    n_z, _, rows = place_ref.shape
    devices = routes_ref.shape[0]
    n_p = devices // n_z
    capacity = 2 * rows // devices
    slots = bias_ref.shape[1] - 3 * rows
    p = lax.axis_index("p")
    me = lax.axis_index("z") * n_p + p
    row = lax.broadcasted_iota(jnp.int32, (rows, rows), 0)
    lane = lax.broadcasted_iota(jnp.int32, (rows, rows), 1)

    def both_ways(line):
        wide = jnp.broadcast_to(line.astype(jnp.float32), (rows, rows))
        return wide, wide.T

    for z in range(n_z):
        across, down = both_ways(routes_ref[pl.ds(z * n_p + p, 1), :])
        ranks = jnp.sum(
            jnp.where((across == down) & (row < lane), 1.0, 0.0), axis=0, keepdims=True
        )
        place_ref[z] = (across[:1] * capacity + ranks).astype(jnp.int32)

    def ids_of(segment):
        return ids_ref[pl.ds(jnp.clip(segment, 0, devices - 1), 1), :].astype(jnp.float32)

    _, own = both_ways(ids_ref[pl.ds(me, 1), :])
    for i in range(3):
        earlier, later = me - 2 + i, me + i
        same = (own == ids_of(earlier)) & (earlier >= 0)
        same_back = (own == ids_of(later)) & (later < devices)
        if i == 2:
            same = same & (lane <= row)
        if i == 0:
            same_back = same_back & (lane >= row)
        bias_ref[:, slots + i * rows : slots + (i + 1) * rows] = jnp.where(same, 0.0, -1e30).astype(
            jnp.bfloat16
        )
        back_ref[:, i * rows : (i + 1) * rows] = jnp.where(same_back, 0.0, -1e30)

    mine = jnp.where(routes_ref[...] == me, 1.0, 0.0).astype(jnp.bfloat16)
    counts = dot_t(jnp.ones((8, rows), jnp.bfloat16), mine, ((1,), (1,))).astype(jnp.bfloat16)
    source = lax.broadcasted_iota(jnp.int32, (devices, slots), 0)
    slot = lax.broadcasted_iota(jnp.int32, (devices, slots), 1) // capacity
    expand = jnp.where(source == (slot % n_z) * n_p + slot // n_z, 1.0, 0.0).astype(jnp.bfloat16)
    filled = jnp.dot(counts, expand, preferred_element_type=jnp.float32)[:1]
    rank = lax.broadcasted_iota(jnp.int32, (1, slots), 1) % capacity
    live = jnp.where(rank.astype(jnp.float32) < filled, 0.0, -1e30)
    bias_ref[:, :slots] = jnp.broadcast_to(live, (rows, slots)).astype(jnp.bfloat16)


def prepare(routes, doc_ids, n_z, devices, rows):
    slots = 2 * rows
    return pl.pallas_call(
        prepare_kernel,
        out_shape=[
            jax.ShapeDtypeStruct((n_z, 1, rows), jnp.int32),
            jax.ShapeDtypeStruct((rows, slots + 3 * rows), jnp.bfloat16),
            jax.ShapeDtypeStruct((rows, 3 * rows), jnp.float32),
        ],
        compiler_params=pltpu.CompilerParams(vmem_limit_bytes=SMALL_VMEM),
        name="prepare",
    )(routes.reshape(devices, rows), doc_ids.reshape(devices, rows))


def column_block(w_kv, target):
    _, w_rows, features = w_kv.shape
    half = features // (GROUPS // 2)
    start = (target & 1, 0, (target >> 1) * half)
    return lax.dynamic_slice(w_kv, start, (1, w_rows, half))[0]


def ring_step(value, back=False):
    pairs = list(zip(RING, RING[1:] + RING[:1]))
    return lax.ppermute(value, "z", [(b, a) for a, b in pairs] if back else pairs)


def memory_slots(cache, w_kv, place, capacity, stream, back):
    n_z, n_p = lax.axis_size("z"), lax.axis_size("p")
    devices = n_z * n_p
    cache_rows, depth = cache.shape
    _, w_rows, features = w_kv.shape
    z = lax.axis_index("z")
    if n_p == 4 and capacity % ROW_TILE == 0 and w_rows % ROW_TILE == 0:
        blocks = [column_block(w_kv, z ^ mask) for mask in range(n_z)]
        own = jnp.stack(
            [blocks[0]] + [swapped(blocks[mask], "z", mask) for mask in range(1, n_z)], 0
        )
        other0 = swapped(cache, "head", 1)
        own, other0, cache = lax.optimization_barrier((own, other0, cache))
        across, beside = swapped(own, "p", 2), swapped(own, "p", 1)
        row1, row3 = ring_step(cache), ring_step(cache, back=True)
        beside, stream, back = lax.optimization_barrier((beside, stream, back))
        near, back1 = shifted(stream, 1), shifted(back, -1)
        row1 = lax.optimization_barrier(row1)
        row2, other1 = ring_step(row1), swapped(row1, "head", 1)
        row3, other1 = lax.optimization_barrier((row3, other1))
        other3 = swapped(row3, "head", 1)
        row2 = lax.optimization_barrier(row2)
        other2 = swapped(row2, "head", 1)
        across, other2, other3, near = lax.optimization_barrier((across, other2, other3, near))
        pieces = [own, beside, across, swapped(across, "p", 1)]
        far = shifted(near, 1)
        rows = [cache, row1, row2, row3, other0, other1, other2, other3]
        slots = project(place, rows, pieces, devices, capacity)
        slots, far, back1 = lax.optimization_barrier((slots, far, back1))
        return slots, near, far, back1
    near, back1 = shifted(stream, 1), shifted(back, -1)
    far = shifted(near, 1)
    targets = [column_block(w_kv, jnp.int32(i)) for i in range(n_z)]
    w_z = lax.all_to_all(jnp.stack(targets, 0), "z", split_axis=0, concat_axis=0, tiled=True)
    w_all = lax.all_gather(w_z, "p", axis=1, tiled=True).reshape(devices * w_rows, -1)
    rows = lax.all_gather(cache, ("head", "z"), axis=0, tiled=False)
    rows = rows.reshape(-1, n_z * cache_rows, depth)
    proj = sum(
        jnp.dot(
            rows[i], w_all[i * depth : (i + 1) * depth], preferred_element_type=jnp.float32
        )
        for i in range(rows.shape[0])
    ).astype(jnp.bfloat16)
    slot_ids = jnp.arange(devices * capacity, dtype=jnp.int32)
    chosen = (slot_ids[None, :, None] == place).astype(jnp.bfloat16)
    slots = jnp.einsum(
        "zsi,zic->zsc",
        chosen,
        proj.reshape(n_z, cache_rows, -1),
        preferred_element_type=jnp.float32,
    ).astype(jnp.bfloat16)
    slots = slots.reshape(n_z, devices, capacity, -1).transpose(1, 0, 2, 3)
    return slots, near, far, back1


def body(queries, keys, values, grad_out, cache, w_kv, doc_ids, routes):
    n_z, n_p = lax.axis_size("z"), lax.axis_size("p")
    devices = n_z * n_p
    seg_rows = queries.shape[0]
    cache_rows = cache.shape[0]
    capacity = 2 * cache_rows // devices
    slot_count = capacity * devices

    place, bias, back_bias = prepare(routes, doc_ids, n_z, devices, seg_rows)
    slots, kv1, kv2, qg1 = memory_slots(
        cache,
        w_kv,
        place,
        capacity,
        jnp.stack([keys, values], 0),
        jnp.stack([queries, grad_out], 0),
    )
    memory = lax.all_to_all(slots, SEQ, split_axis=0, concat_axis=0, tiled=True)
    memory = memory.reshape(n_z, slot_count, slots.shape[-1])

    qg2 = shifted(qg1, -1)
    output, grad_q, stats = attend(queries, grad_out, keys, values, kv1, kv2, memory, bias)
    all_stats = [stats, shifted(stats, -1), shifted(stats, -2)]
    grad_k, grad_v = key_grads(
        keys, values, queries, grad_out, qg1, qg2, all_stats, back_bias
    )
    return (output, grad_q, grad_k, grad_v)


def solution(mesh):
    n_seq, n_head = mesh.devices.shape
    grid = Mesh(mesh.devices.reshape(GROUPS, n_seq // GROUPS, n_head), ("z", "p", "head"))
    rows = P(SEQ, "head")
    return jax.shard_map(
        body,
        mesh=grid,
        in_specs=(rows, rows, rows, rows, rows, P(None, SEQ, "head"), P(), P()),
        out_specs=(rows, rows, rows, rows),
        check_vma=False,
    )
```
